32 devices in a mesh: seq: 8 (over z, y), head: 4 (over x, core).
Axes of the slice: x: 2, y: 2, z: 4, core: 2. Of those that a mesh axis runs over, the one named last changes fastest.
Arguments:
- queries_first: bfloat16 [4096, 1024], P('seq', 'head'), may hold values from -4.4 to 4.4
- keys_first: bfloat16 [4096, 1024], P('seq', 'head'), may hold values from -4.4 to 4.4
- values_first: bfloat16 [4096, 1024], P('seq', 'head'), may hold values from -6 to 6
- input_map: bfloat16 [4, 256, 512], P('head'), may hold values from -0.375 to 0.375
- fast_keys: bfloat16 [4096, 2048], P('seq', 'head'), may hold values from -6 to 6
- fast_values: bfloat16 [4096, 2048], P('seq', 'head'), may hold values from -6 to 6
- step_rates: float32 [4096, 4], P('seq', 'head'), may hold values from 0.1 to 1
- fast_weights: bfloat16 [4, 512, 3, 512], P('head'), may hold values from -6 to 6
- output_map: bfloat16 [2048, 1024], P('head'), may hold values from -0.25 to 0.25
- queries_second: bfloat16 [4096, 1024], P('seq', 'head'), may hold values from -4.4 to 4.4
- keys_second: bfloat16 [4096, 1024], P('seq', 'head'), may hold values from -4.4 to 4.4
- values_second: bfloat16 [4096, 1024], P('seq', 'head'), may hold values from -6 to 6
Outputs:
- block_output: bfloat16 [4096, 1024], P('seq', 'head')
- new_weights: bfloat16 [4, 512, 3, 512], P('head', 'seq')
The draws below stay inside these ranges and needn't reach their ends.
All inputs are finite; a program needn't handle non-finite values.
Results may differ from the reference program's by a relative error of at most 0.034.
Values may be sent and summed in bfloat16 or wider, within the bound.
No kernel may reach another device: no remote copies, remote signals or barrier semaphores. Data moves between devices by JAX's collectives and lax.ppermute only.
A program may use at most 64 MiB of HBM per device.

```python
import math
import jax
import jax.numpy as jnp
from jax import lax

HALF_WIN = 512
HEAD_DIM = 128
HEADS_GRP = 2
FAST_DIM = 512
FAST_HIDDEN = 512
GROUPS = 4
TOKENS = 4096


def qk_pair(key, salt):
    base = jax.random.fold_in(key, salt)
    key_query, key_keys = jax.random.split(base, 2)
    array_shape = (TOKENS, GROUPS * HEADS_GRP * HEAD_DIM)
    queries = jnp.clip(jax.random.normal(key_query, array_shape, jnp.float32), -4.375, 4.375)
    key_rows = jnp.clip(jax.random.normal(key_keys, array_shape, jnp.float32), -4.375, 4.375)
    return (queries, key_rows)


def draw_queries_first(key, part):
    return qk_pair(key, 11)[0].astype(jnp.bfloat16)


def draw_keys_first(key, part):
    return qk_pair(key, 11)[1].astype(jnp.bfloat16)


def draw_queries_second(key, part):
    return qk_pair(key, 23)[0].astype(jnp.bfloat16)


def draw_keys_second(key, part):
    return qk_pair(key, 23)[1].astype(jnp.bfloat16)


def draw_fast_weights(key, part):
    base = jax.random.fold_in(key, 37)
    key_rows, key_cols, key_main = jax.random.split(base, 3)
    array_shape = (GROUPS, FAST_HIDDEN, 3, FAST_DIM)
    row_scale = jnp.exp(jax.random.uniform(key_rows, (GROUPS, FAST_HIDDEN, 3, 1), jnp.float32) * 2.302585) / 3.16
    col_scale = jnp.exp(jax.random.uniform(key_cols, (GROUPS, 1, 3, FAST_DIM), jnp.float32) * 2.302585) / 4.64
    entries = jnp.clip(jax.random.normal(key_main, array_shape, jnp.float32), -4.0, 4.0)
    return jnp.clip(entries * row_scale * col_scale, -6.0, 6.0).astype(jnp.bfloat16)


def raised(array, rng, source, target, blocks, factor):
    owner, partner = [(jnp.arange(array.shape[dim]) // (array.shape[dim] // blocks)).reshape([-1 if axis == dim else 1 for axis in range(array.ndim)]) for dim in (source, target)]
    chosen = jax.random.permutation(rng, blocks)[partner]
    strong = (owner == chosen) | (owner == (partner + blocks // 2) % blocks)
    return jnp.where(strong, factor * array, array)


def steps_of(own_key, extent, shards, smallest, largest):
    def one(position, blocks):
        heights = jax.random.uniform(jax.random.fold_in(jax.random.fold_in(own_key, 6), position), (blocks,), jnp.float32, smallest / len(shards), largest / len(shards))
        return jnp.repeat(jnp.exp(heights), extent[position] // blocks).reshape((-1,) + (1,) * (len(extent) - position - 1))

    level = one(*shards[0])
    for cut in shards[1:]:
        level = level * one(*cut)
    return level


def noise(own_key, shape, spread, most, cuts=(), kind=jnp.bfloat16):
    level = steps_of(own_key, shape, cuts, -0.22, 0.18) if cuts else 1.0
    array = jax.random.normal(own_key, shape, jnp.float32) * spread * level
    return jnp.minimum(jnp.maximum(array, -most), most).astype(kind)


def gaussian_with(own_key, extent, width, reach, pieces, heavy, kind=jnp.bfloat16):
    values = width * jax.random.normal(own_key, extent, jnp.float32)
    if pieces:
        values = values * steps_of(own_key, extent, pieces, -0.22, 0.18)
    return jnp.clip(raised(values, jax.random.fold_in(own_key, 3), *heavy), -reach, reach).astype(kind)


def setup_inputs(seed: int = 0) -> dict:
    streams_of = jax.random.split(jax.random.key(seed), 13)
    queries_first = draw_queries_first(jax.random.fold_in(streams_of[12], 71), 0)
    keys_first = draw_keys_first(jax.random.fold_in(streams_of[12], 71), 0)
    values_first = noise(streams_of[2], (TOKENS, GROUPS * HEADS_GRP * HEAD_DIM), 1.0, 6.0, ((0, 8), (1, 4)))
    input_map = noise(streams_of[3], (GROUPS, HEADS_GRP * HEAD_DIM, FAST_DIM), (HEADS_GRP * HEAD_DIM) ** -0.5, 0.375, ((0, 4),))
    fast_keys = noise(streams_of[4], (TOKENS, GROUPS * FAST_DIM), 1.0, 6.0, ((0, 8), (1, 4)))
    fast_values = gaussian_with(streams_of[5], (TOKENS, GROUPS * FAST_DIM), 1.0, 6.0, ((0, 8), (1, 4)), (0, 1, 8, 2.0))
    step_rates = jnp.clip(jnp.exp(math.log(1.0) - 2.3025851 * jax.random.uniform(streams_of[6], (TOKENS, GROUPS), jnp.float32) ** steps_of(streams_of[6], (TOKENS, GROUPS), ((0, 8), (1, 4)), -0.2, 0.2)), 0.1, 1.0)
    fast_weights = draw_fast_weights(jax.random.fold_in(streams_of[12], 71), 0)
    output_map = noise(streams_of[8], (GROUPS * FAST_DIM, GROUPS * HEADS_GRP * HEAD_DIM), FAST_DIM ** -0.5, 0.25, ((0, 4),))
    queries_second = draw_queries_second(jax.random.fold_in(streams_of[12], 71), 0)
    keys_second = draw_keys_second(jax.random.fold_in(streams_of[12], 71), 0)
    values_second = noise(streams_of[11], (TOKENS, GROUPS * HEADS_GRP * HEAD_DIM), 1.0, 6.0, ((0, 8), (1, 4)))
    return dict(queries_first=queries_first, keys_first=keys_first, values_first=values_first, input_map=input_map, fast_keys=fast_keys, fast_values=fast_values, step_rates=step_rates, fast_weights=fast_weights, output_map=output_map, queries_second=queries_second, keys_second=keys_second, values_second=values_second)


def rms_round(matrix):
    return (matrix * lax.rsqrt(lax.optimization_barrier(jnp.mean(matrix * matrix, axis=-1, keepdims=True)) + 1e-05)).astype(jnp.bfloat16)

def window_attend(queries, key_rows, value_rows):
    block_rows = min(512, TOKENS)
    span_rows = block_rows + 2 * HALF_WIN
    keys_ext = jnp.pad(key_rows, ((HALF_WIN, HALF_WIN), (0, 0)))
    values_ext = jnp.pad(value_rows, ((HALF_WIN, HALF_WIN), (0, 0)))
    inverse_root = 1.0 / math.sqrt(HEAD_DIM)

    def attend_block(block_index):
        start_row = (block_index * block_rows).astype(jnp.int32)
        query_block = lax.dynamic_slice_in_dim(queries, start_row, block_rows, 0).reshape(block_rows, HEADS_GRP, HEAD_DIM)
        key_block = lax.dynamic_slice_in_dim(keys_ext, start_row, span_rows, 0).reshape(span_rows, HEADS_GRP, HEAD_DIM)
        value_block = lax.dynamic_slice_in_dim(values_ext, start_row, span_rows, 0).reshape(span_rows, HEADS_GRP, HEAD_DIM)
        scores = jnp.einsum('qhd,khd->hqk', query_block.astype(jnp.float32), key_block.astype(jnp.float32)) * inverse_root
        query_pos = jnp.arange(block_rows, dtype=jnp.int32)[:, None]
        key_pos = jnp.arange(span_rows, dtype=jnp.int32)[None, :]
        global_pos = start_row + key_pos - HALF_WIN
        allowed = (key_pos >= query_pos) & (key_pos <= query_pos + 2 * HALF_WIN) & (global_pos >= 0) & (global_pos < TOKENS)
        scores = jnp.where(allowed[None], scores, -jnp.inf)
        highest = lax.optimization_barrier(jnp.max(scores, axis=-1, keepdims=True))
        weights_exp = jnp.exp(scores - highest)
        weights_bf = (weights_exp / lax.optimization_barrier(jnp.sum(weights_exp, axis=-1, keepdims=True))).astype(jnp.bfloat16)
        attended = jnp.einsum('hqk,khd->qhd', weights_bf.astype(jnp.float32), value_block.astype(jnp.float32))
        return rms_round(attended.reshape(block_rows, HEADS_GRP * HEAD_DIM))
    outputs = lax.map(attend_block, jnp.arange(TOKENS // block_rows, dtype=jnp.int32))
    return outputs.reshape(TOKENS, HEADS_GRP * HEAD_DIM)

def swiglu_apply(fast_query, weights_rows):
    inverse = 1.0 / math.sqrt(FAST_DIM)
    gate_part = jnp.dot(fast_query, weights_rows[:, 0, :].T, preferred_element_type=jnp.float32) * inverse
    up_part = jnp.dot(fast_query, weights_rows[:, 1, :].T, preferred_element_type=jnp.float32) * inverse
    hidden_query = (jax.nn.silu(gate_part) * up_part).astype(jnp.bfloat16)
    return jnp.dot(hidden_query, weights_rows[:, 2, :], preferred_element_type=jnp.float32)

def renormalize(old_rows, gradient_rows, factor):
    old_float = old_rows.astype(jnp.float32)
    stepped = old_float + factor * gradient_rows
    old_norm = jnp.sqrt(lax.optimization_barrier(jnp.sum(old_float * old_float, axis=-1, keepdims=True)))
    return (stepped * old_norm * lax.rsqrt(lax.optimization_barrier(jnp.sum(stepped * stepped, axis=-1, keepdims=True)) + 1e-06)).astype(jnp.bfloat16)

def reference(queries_first, keys_first, values_first, input_map, fast_keys, fast_values, step_rates, fast_weights, output_map, queries_second, keys_second, values_second):
    group_width = HEADS_GRP * HEAD_DIM
    inverse = 1.0 / math.sqrt(FAST_DIM)
    limit_norm = math.sqrt(FAST_HIDDEN * FAST_DIM) / 2.0
    fast_list = []
    weight_list = []
    for group in range(GROUPS):
        low_col = group * group_width
        normed_first = window_attend(queries_first[:, low_col:low_col + group_width], keys_first[:, low_col:low_col + group_width], values_first[:, low_col:low_col + group_width])
        fast_query = jnp.dot(normed_first, input_map[group], preferred_element_type=jnp.float32).astype(jnp.bfloat16)
        weights_local = fast_weights[group]
        keys_fast = fast_keys[:, group * FAST_DIM:(group + 1) * FAST_DIM]
        values_fast = fast_values[:, group * FAST_DIM:(group + 1) * FAST_DIM]
        rates_col = step_rates[:, group:group + 1]
        gate_keys = jnp.dot(keys_fast, weights_local[:, 0, :].T, preferred_element_type=jnp.float32) * inverse
        up_keys = jnp.dot(keys_fast, weights_local[:, 1, :].T, preferred_element_type=jnp.float32) * inverse
        sigmoid_gate = jax.nn.sigmoid(gate_keys)
        silu_gate = gate_keys * sigmoid_gate
        hidden_keys = (rates_col * silu_gate * up_keys).astype(jnp.bfloat16)
        backward = rates_col * jnp.dot(values_fast, weights_local[:, 2, :].T, preferred_element_type=jnp.float32)
        d_gate = (backward * up_keys * sigmoid_gate * (1.0 + gate_keys * (1.0 - sigmoid_gate)) * inverse).astype(jnp.bfloat16)
        d_up = (backward * silu_gate * inverse).astype(jnp.bfloat16)
        gradient = jnp.stack([jnp.dot(d_gate.T, keys_fast, preferred_element_type=jnp.float32), jnp.dot(d_up.T, keys_fast, preferred_element_type=jnp.float32), jnp.dot(hidden_keys.T, values_fast, preferred_element_type=jnp.float32)], axis=1)
        factor = jnp.minimum(1.0, limit_norm * lax.rsqrt(jnp.sum(gradient * gradient) + 1e-06))
        updated = renormalize(weights_local, gradient, factor)
        fast_list.append(rms_round(swiglu_apply(fast_query, updated)))
        weight_list.append(updated)
    mixed = jnp.zeros((TOKENS, GROUPS * group_width), jnp.float32)
    for group in range(GROUPS):
        product = jnp.dot(fast_list[group], output_map[group * FAST_DIM:(group + 1) * FAST_DIM], preferred_element_type=jnp.float32)
        mixed = mixed + lax.optimization_barrier(product.astype(jnp.bfloat16)).astype(jnp.float32)
    query_two = (queries_second.astype(jnp.float32) + mixed).astype(jnp.bfloat16)
    out_list = []
    for group in range(GROUPS):
        low_col = group * group_width
        out_list.append(window_attend(query_two[:, low_col:low_col + group_width], keys_second[:, low_col:low_col + group_width], values_second[:, low_col:low_col + group_width]))
    return (jnp.concatenate(out_list, axis=1), jnp.stack(weight_list))
```

```python
import functools
import math

import jax
import jax.numpy as jnp
from jax import lax
from jax.experimental import pallas as pl
from jax.experimental.pallas import tpu as pltpu
from jax.sharding import PartitionSpec as P

HALF_WIN = 512
HEAD_DIM = 128
HEADS_GRP = 2
FAST_DIM = 512
FAST_HIDDEN = 512
TILE = 128
VMEM_LIMIT = 48 * 1024 * 1024

BF16 = jnp.bfloat16
F32 = jnp.float32
INVERSE = 1.0 / math.sqrt(FAST_DIM)


def dot_nn(left, right):
    return lax.dot_general(left, right, (((1,), (0,)), ((), ())), preferred_element_type=F32)


def dot_nt(left, right):
    return lax.dot_general(left, right, (((1,), (1,)), ((), ())), preferred_element_type=F32)


def call(body, out_shapes, operands, flops, moved, scalars=0, scratch=()):
    in_specs = [pl.BlockSpec(memory_space=pltpu.SMEM)] * scalars + [
        pl.BlockSpec(memory_space=pltpu.VMEM)
    ] * (len(operands) - scalars)
    return pl.pallas_call(
        body,
        out_shape=out_shapes,
        in_specs=in_specs,
        out_specs=jax.tree.map(lambda _: pl.BlockSpec(memory_space=pltpu.VMEM), out_shapes),
        scratch_shapes=scratch,
        compiler_params=pltpu.CompilerParams(vmem_limit_bytes=VMEM_LIMIT),
        cost_estimate=pl.CostEstimate(flops=flops, bytes_accessed=moved, transcendentals=0),
    )(*operands)


def gradient_kernel(rates_ref, keys_ref, values_ref, weights_ref, out_ref):
    rates = rates_ref[...]
    keys = keys_ref[...]
    values = values_ref[...]
    step = 128
    for low in range(0, weights_ref.shape[1], step):
        rows = slice(low, low + step)
        gate = dot_nt(weights_ref[0, rows, :], keys) * INVERSE
        up = dot_nt(weights_ref[1, rows, :], keys) * INVERSE
        sigmoid = jax.nn.sigmoid(gate)
        silu = gate * sigmoid
        hidden = (rates * silu * up).astype(BF16)
        backward = rates * dot_nt(weights_ref[2, rows, :], values)
        d_gate = (
            backward * up * sigmoid * (1.0 + gate * (1.0 - sigmoid)) * INVERSE
        ).astype(BF16)
        d_up = (backward * silu * INVERSE).astype(BF16)
        out_ref[0, rows, :] = dot_nn(d_gate, keys).astype(BF16)
        out_ref[1, rows, :] = dot_nn(d_up, keys).astype(BF16)
        out_ref[2, rows, :] = dot_nn(hidden, values).astype(BF16)


def attend_rows(edge_ref, index, query_tile, keys_prev, keys_own, keys_next,
                values_prev, values_own, values_next):
    scale = 1.0 / math.sqrt(HEAD_DIM)
    row = lax.broadcasted_iota(jnp.int32, (TILE, TILE), 0)
    col = lax.broadcasted_iota(jnp.int32, (TILE, TILE), 1)
    minus = jnp.float32(-jnp.inf)
    edge_prev = edge_ref[0, 0]
    edge_next = edge_ref[0, 1]
    score_prev = dot_nt(query_tile, keys_prev)
    score_own = dot_nt(query_tile, keys_own)
    score_next = dot_nt(query_tile, keys_next)
    first = score_prev[:, :TILE] + jnp.where(col >= row, edge_prev, minus)
    parts = [first]
    if score_prev.shape[1] > TILE:
        parts.append(score_prev[:, TILE:] + edge_prev)
    parts.append(score_own)
    if score_next.shape[1] > TILE:
        parts.append(score_next[:, :-TILE] + edge_next)
    parts.append(score_next[:, -TILE:] + jnp.where(col <= row, edge_next, minus))
    scores = jnp.concatenate(parts, axis=1)
    highest = jnp.max(scores, axis=1, keepdims=True)
    weights = jnp.exp((scores - highest) * scale)
    total = jnp.sum(weights, axis=1, keepdims=True)
    weights = weights.astype(BF16)
    width_prev, width_own = score_prev.shape[1], score_own.shape[1]
    attended = (
        dot_nn(weights[:, :width_prev], values_prev)
        + dot_nn(weights[:, width_prev:width_prev + width_own], values_own)
        + dot_nn(weights[:, width_prev + width_own:], values_next)
    )
    return attended / total


def window_tile(edge_ref, index, query_tile, prev_ref, keys_ref, values_ref, next_ref):
    reach = keys_ref.shape[0]
    heads = []
    for head in range(HEADS_GRP):
        cols = slice(head * HEAD_DIM, (head + 1) * HEAD_DIM)
        low, high = index * TILE, (index + 1) * TILE
        heads.append(
            attend_rows(
                edge_ref, index, query_tile[:, cols],
                prev_ref[low:reach, cols], keys_ref[:, cols], next_ref[:high, cols],
                prev_ref[reach + low:, cols], values_ref[:, cols],
                next_ref[reach:reach + high, cols],
            )
        )
    both = jnp.concatenate(heads, axis=1)
    mean = jnp.mean(both * both, axis=1, keepdims=True)
    return (both * lax.rsqrt(mean + 1e-05)).astype(BF16)


def first_kernel(edge_ref, queries_ref, prev_ref, keys_ref, values_ref, next_ref, map_ref, out_ref):
    for index in range(queries_ref.shape[0] // TILE):
        rows = slice(index * TILE, (index + 1) * TILE)
        normed = window_tile(
            edge_ref, index, queries_ref[rows, :], prev_ref, keys_ref, values_ref, next_ref
        )
        out_ref[rows, :] = dot_nn(normed, map_ref[...]).astype(BF16)


def second_kernel(edge_ref, queries_ref, keep_ref, near_ref, far_ref,
                  prev_ref, keys_ref, values_ref, next_ref, out_ref):
    for index in range(queries_ref.shape[0] // TILE):
        rows = slice(index * TILE, (index + 1) * TILE)
        mixed = (
            keep_ref[1, rows, :].astype(F32)
            + near_ref[1, rows, :].astype(F32)
            + far_ref[rows, :].astype(F32)
        )
        query = (queries_ref[rows, :].astype(F32) + mixed).astype(BF16)
        out_ref[rows, :] = window_tile(
            edge_ref, index, query, prev_ref, keys_ref, values_ref, next_ref
        )


def renew_kernel(gradient_ref, weights_ref, query_ref, new_ref, fast_ref):
    limit_norm = math.sqrt(FAST_HIDDEN * FAST_DIM) / 2.0
    square = jnp.zeros((1, weights_ref.shape[2]), F32)
    step = 64
    for matrix in range(3):
        for low in range(0, weights_ref.shape[1], step):
            part = gradient_ref[matrix, low:low + step, :].astype(F32)
            square = square + jnp.sum(part * part, axis=0, keepdims=True)
    square = jnp.sum(square, axis=1, keepdims=True)
    factor = jnp.minimum(1.0, limit_norm * lax.rsqrt(square + 1e-06))
    for matrix in range(3):
        for low in range(0, weights_ref.shape[1], step):
            rows = slice(low, low + step)
            old = weights_ref[matrix, rows, :].astype(F32)
            stepped = old + factor * gradient_ref[matrix, rows, :].astype(F32)
            norm = jnp.sqrt(jnp.sum(old * old, axis=1, keepdims=True))
            size = jnp.sum(stepped * stepped, axis=1, keepdims=True)
            new_ref[matrix, rows, :] = (stepped * norm * lax.rsqrt(size + 1e-06)).astype(BF16)
    step = 128
    for low in range(0, query_ref.shape[0], step):
        rows = slice(low, low + step)
        query = query_ref[rows, :]
        gate = dot_nt(query, new_ref[0]) * INVERSE
        up = dot_nt(query, new_ref[1]) * INVERSE
        hidden = (jax.nn.silu(gate) * up).astype(BF16)
        raw = dot_nn(hidden, new_ref[2])
        mean = jnp.mean(raw * raw, axis=1, keepdims=True)
        fast_ref[rows, :] = (raw * lax.rsqrt(mean + 1e-05)).astype(BF16)


def mix_kernel(place_ref, fast_ref, map_ref, out_ref):
    width = out_ref.shape[2]
    for slot in range(2):
        start = pl.multiple_of(place_ref[0, slot] * width, width)
        columns = map_ref[:, pl.ds(start, width)]
        out_ref[slot] = dot_nn(fast_ref[...], columns).astype(BF16)


def seq_shift(value, up):
    peers = lax.axis_size("seq")
    pairs = [(i, i + 1) for i in range(peers - 1)]
    return lax.ppermute(value, "seq", pairs if up else [(j, i) for i, j in pairs])


def head_swap(value, bit):
    return lax.ppermute(value, "head", [(i, i ^ bit) for i in range(lax.axis_size("head"))])


def local(
    queries_first,
    keys_first,
    values_first,
    input_map,
    fast_keys,
    fast_values,
    step_rates,
    fast_weights,
    output_map,
    queries_second,
    keys_second,
    values_second,
):
    rows, width = queries_first.shape
    seq_count = lax.axis_size("seq")
    seq_place = lax.axis_index("seq")
    head_place = lax.axis_index("head")
    weights = jnp.transpose(fast_weights[0], (1, 0, 2))
    hidden_size, fast_width = weights.shape[1:]
    shape = jax.ShapeDtypeStruct
    minus = jnp.float32(-jnp.inf)
    edges = jnp.stack(
        [
            jnp.where(seq_place > 0, 0.0, minus),
            jnp.where(seq_place < seq_count - 1, 0.0, minus),
        ]
    ).reshape(1, 2)

    gradient = call(
        gradient_kernel,
        shape(weights.shape, BF16),
        (step_rates.reshape(1, rows), fast_keys, fast_values, weights),
        12 * rows * hidden_size * fast_width,
        8 * rows * fast_width,
    )
    share = lax.psum_scatter(gradient, "seq", scatter_dimension=1, tiled=True)
    gathered = lax.all_gather(share, "seq", axis=1, tiled=True)

    both_first = jnp.concatenate([keys_first, values_first])
    prev_first = seq_shift(both_first, True)
    next_first = seq_shift(both_first, False)
    attend_flops = 12 * rows * rows * width
    fast_query = call(
        first_kernel,
        shape((rows, fast_width), BF16),
        (edges, queries_first, prev_first, keys_first, values_first, next_first, input_map[0]),
        attend_flops,
        16 * rows * width,
        scalars=1,
    )
    both_second = jnp.concatenate([keys_second, values_second])
    prev_second = seq_shift(both_second, True)
    next_second = seq_shift(both_second, False)

    updated, fast_out = call(
        renew_kernel,
        (shape(weights.shape, BF16), shape((rows, fast_width), BF16)),
        (gathered, weights, fast_query),
        6 * rows * hidden_size * fast_width,
        12 * hidden_size * fast_width,
    )
    share_rows = hidden_size // seq_count
    own_new = lax.dynamic_slice_in_dim(updated, seq_place * share_rows, share_rows, 1)

    def mixed_for(low_bit):
        far = (head_place // 2) ^ 1
        near = head_place // 2
        places = jnp.stack([far * 2 + low_bit, near * 2 + low_bit]).reshape(1, 2)
        return call(
            mix_kernel,
            shape((2, rows, width), BF16),
            (places, fast_out, output_map),
            4 * rows * fast_width * width,
            8 * rows * width,
            scalars=1,
        )

    my_bit = head_place % 2
    near_part = head_swap(mixed_for(1 - my_bit), 1)
    keep_part = mixed_for(my_bit)
    to_send = (keep_part[0].astype(F32) + near_part[0].astype(F32)).astype(BF16)
    far_part = head_swap(to_send, 2)

    normed_second = call(
        second_kernel,
        shape((rows, width), BF16),
        (edges, queries_second, keep_part, near_part, far_part,
         prev_second, keys_second, values_second, next_second),
        attend_flops,
        16 * rows * width,
        scalars=1,
    )
    return (normed_second, jnp.transpose(own_new, (1, 0, 2))[None])


def solution(mesh):
    return jax.shard_map(
        local,
        mesh=mesh,
        in_specs=(
            P("seq", "head"),
            P("seq", "head"),
            P("seq", "head"),
            P("head", None, None),
            P("seq", "head"),
            P("seq", "head"),
            P("seq", "head"),
            P("head", None, None, None),
            P("head", None),
            P("seq", "head"),
            P("seq", "head"),
            P("seq", "head"),
        ),
        out_specs=(P("seq", "head"), P("head", "seq", None, None)),
        check_vma=False,
    )
```

```python
import functools
import math

import jax
import jax.numpy as jnp
from jax import lax
from jax.experimental import pallas as pl
from jax.experimental.pallas import tpu as pltpu
from jax.sharding import PartitionSpec as P

HALF_WIN = 512
HEAD_DIM = 128
HEADS_GRP = 2
FAST_DIM = 512
FAST_HIDDEN = 512
TILE = 128
VMEM_LIMIT = 48 * 1024 * 1024

BF16 = jnp.bfloat16
F32 = jnp.float32
INVERSE = 1.0 / math.sqrt(FAST_DIM)


def dot_nn(left, right):
    return lax.dot_general(left, right, (((1,), (0,)), ((), ())), preferred_element_type=F32)


def dot_nt(left, right):
    return lax.dot_general(left, right, (((1,), (1,)), ((), ())), preferred_element_type=F32)


def call(body, out_shapes, operands, flops, moved, scalars=0, scratch=()):
    in_specs = [pl.BlockSpec(memory_space=pltpu.SMEM)] * scalars + [
        pl.BlockSpec(memory_space=pltpu.VMEM)
    ] * (len(operands) - scalars)
    return pl.pallas_call(
        body,
        out_shape=out_shapes,
        in_specs=in_specs,
        out_specs=jax.tree.map(lambda _: pl.BlockSpec(memory_space=pltpu.VMEM), out_shapes),
        scratch_shapes=scratch,
        compiler_params=pltpu.CompilerParams(vmem_limit_bytes=VMEM_LIMIT),
        cost_estimate=pl.CostEstimate(flops=flops, bytes_accessed=moved, transcendentals=0),
    )(*operands)


def slot_of(block, order):
    slot = 0
    for bit in order:
        slot = slot * 2 + ((block >> bit) & 1)
    return slot


def block_at(slot, order):
    block = 0
    for place, bit in enumerate(reversed(order)):
        block |= ((slot >> place) & 1) << bit
    return block


def gradient_kernel(orders, place_ref, rates_ref, keys_ref, values_ref, weights_ref, *out_refs):
    place = place_ref[0, 0]
    rates = rates_ref[...]
    keys = keys_ref[...]
    values = values_ref[...]
    hidden_size = weights_ref.shape[1]
    step = 128

    def put(matrix, low, product):
        order = orders[matrix]
        block_rows = hidden_size >> len(order)
        for start in range(0, step, block_rows):
            if not order:
                out_refs[matrix][low:low + step, :] = product.astype(BF16)
                break
            slot = slot_of(((low + start) // block_rows) ^ place, order)
            rows = pl.ds(pl.multiple_of(slot * block_rows, block_rows), block_rows)
            out_refs[matrix][rows, :] = product[start:start + block_rows].astype(BF16)

    for low in range(0, hidden_size, step):
        rows = slice(low, low + step)
        gate = dot_nt(weights_ref[0, rows, :], keys) * INVERSE
        up = dot_nt(weights_ref[1, rows, :], keys) * INVERSE
        sigmoid = jax.nn.sigmoid(gate)
        silu = gate * sigmoid
        hidden = (rates * silu * up).astype(BF16)
        backward = rates * dot_nt(weights_ref[2, rows, :], values)
        d_gate = (
            backward * up * sigmoid * (1.0 + gate * (1.0 - sigmoid)) * INVERSE
        ).astype(BF16)
        d_up = (backward * silu * INVERSE).astype(BF16)
        put(0, low, dot_nn(d_gate, keys))
        put(1, low, dot_nn(d_up, keys))
        put(2, low, dot_nn(hidden, values))


def attend_rows(edge_ref, index, query_tile, keys_prev, keys_own, keys_next,
                values_prev, values_own, values_next):
    scale = 1.0 / math.sqrt(HEAD_DIM)
    row = lax.broadcasted_iota(jnp.int32, (TILE, TILE), 0)
    col = lax.broadcasted_iota(jnp.int32, (TILE, TILE), 1)
    minus = jnp.float32(-jnp.inf)
    edge_prev = edge_ref[0, 0]
    edge_next = edge_ref[0, 1]
    score_prev = dot_nt(query_tile, keys_prev)
    score_own = dot_nt(query_tile, keys_own)
    score_next = dot_nt(query_tile, keys_next)
    first = score_prev[:, :TILE] + jnp.where(col >= row, edge_prev, minus)
    parts = [first]
    if score_prev.shape[1] > TILE:
        parts.append(score_prev[:, TILE:] + edge_prev)
    parts.append(score_own)
    if score_next.shape[1] > TILE:
        parts.append(score_next[:, :-TILE] + edge_next)
    parts.append(score_next[:, -TILE:] + jnp.where(col <= row, edge_next, minus))
    scores = jnp.concatenate(parts, axis=1)
    highest = jnp.max(scores, axis=1, keepdims=True)
    weights = jnp.exp((scores - highest) * scale)
    total = jnp.sum(weights, axis=1, keepdims=True)
    weights = weights.astype(BF16)
    width_prev, width_own = score_prev.shape[1], score_own.shape[1]
    attended = (
        dot_nn(weights[:, :width_prev], values_prev)
        + dot_nn(weights[:, width_prev:width_prev + width_own], values_own)
        + dot_nn(weights[:, width_prev + width_own:], values_next)
    )
    return attended / total


def window_tile(edge_ref, index, query_tile, prev_ref, keys_ref, values_ref, next_ref):
    reach = keys_ref.shape[0]
    heads = []
    for head in range(HEADS_GRP):
        cols = slice(head * HEAD_DIM, (head + 1) * HEAD_DIM)
        low, high = index * TILE, (index + 1) * TILE
        heads.append(
            attend_rows(
                edge_ref, index, query_tile[:, cols],
                prev_ref[low:reach, cols], keys_ref[:, cols], next_ref[:high, cols],
                prev_ref[reach + low:, cols], values_ref[:, cols],
                next_ref[reach:reach + high, cols],
            )
        )
    both = jnp.concatenate(heads, axis=1)
    mean = jnp.mean(both * both, axis=1, keepdims=True)
    return (both * lax.rsqrt(mean + 1e-05)).astype(BF16)


def first_kernel(edge_ref, queries_ref, prev_ref, keys_ref, values_ref, next_ref, map_ref, out_ref):
    for index in range(queries_ref.shape[0] // TILE):
        rows = slice(index * TILE, (index + 1) * TILE)
        normed = window_tile(
            edge_ref, index, queries_ref[rows, :], prev_ref, keys_ref, values_ref, next_ref
        )
        out_ref[rows, :] = dot_nn(normed, map_ref[...]).astype(BF16)


def second_kernel(edge_ref, queries_ref, keep_ref, near_ref, far_ref,
                  prev_ref, keys_ref, values_ref, next_ref, out_ref):
    for index in range(queries_ref.shape[0] // TILE):
        rows = slice(index * TILE, (index + 1) * TILE)
        mixed = (
            keep_ref[1, rows, :].astype(F32)
            + near_ref[1, rows, :].astype(F32)
            + far_ref[rows, :].astype(F32)
        )
        query = (queries_ref[rows, :].astype(F32) + mixed).astype(BF16)
        out_ref[rows, :] = window_tile(
            edge_ref, index, query, prev_ref, keys_ref, values_ref, next_ref
        )


def renew_kernel(orders, place_ref, weights_ref, query_ref, *refs):
    pieces, (own_ref, fast_ref, new_ref) = refs[:-3], refs[-3:]
    place = place_ref[0, 0]
    limit_norm = math.sqrt(FAST_HIDDEN * FAST_DIM) / 2.0
    square = jnp.zeros((1, weights_ref.shape[2]), F32)
    step = 64
    for piece in pieces:
        for low in range(0, piece.shape[0], step):
            part = piece[low:low + step, :].astype(F32)
            square = square + jnp.sum(part * part, axis=0, keepdims=True)
    square = jnp.sum(square, axis=1, keepdims=True)
    factor = jnp.minimum(1.0, limit_norm * lax.rsqrt(square + 1e-06))
    per_matrix = len(pieces) // 3
    for matrix, order in enumerate(orders):
        block_rows = weights_ref.shape[1] >> len(order)
        slots = 1 << len(order)
        for slot in range(slots):
            piece = pieces[matrix * per_matrix + slot * per_matrix // slots]
            inside = slot % (slots // per_matrix)
            block = block_at(slot, order) ^ place if order else 0
            for low in range(0, block_rows, step):
                count = min(step, block_rows)
                rows = pl.ds(pl.multiple_of(block * block_rows + low, count), count)
                old = weights_ref[matrix, rows, :].astype(F32)
                part = piece[inside * block_rows + low:inside * block_rows + low + count, :]
                stepped = old + factor * part.astype(F32)
                norm = jnp.sqrt(jnp.sum(old * old, axis=1, keepdims=True))
                size = jnp.sum(stepped * stepped, axis=1, keepdims=True)
                fresh = (stepped * norm * lax.rsqrt(size + 1e-06)).astype(BF16)
                new_ref[matrix, rows, :] = fresh
                if slot == 0:
                    own_ref[matrix, low:low + count, :] = fresh
    step = 128
    for low in range(0, query_ref.shape[0], step):
        rows = slice(low, low + step)
        query = query_ref[rows, :]
        gate = dot_nt(query, new_ref[0]) * INVERSE
        up = dot_nt(query, new_ref[1]) * INVERSE
        hidden = (jax.nn.silu(gate) * up).astype(BF16)
        raw = dot_nn(hidden, new_ref[2])
        mean = jnp.mean(raw * raw, axis=1, keepdims=True)
        fast_ref[rows, :] = (raw * lax.rsqrt(mean + 1e-05)).astype(BF16)


def mix_kernel(place_ref, fast_ref, map_ref, out_ref):
    width = out_ref.shape[2]
    for slot in range(2):
        start = pl.multiple_of(place_ref[0, slot] * width, width)
        columns = map_ref[:, pl.ds(start, width)]
        out_ref[slot] = dot_nn(fast_ref[...], columns).astype(BF16)


def seq_shift(value, up):
    peers = lax.axis_size("seq")
    pairs = [(i, i + 1) for i in range(peers - 1)]
    return lax.ppermute(value, "seq", pairs if up else [(j, i) for i, j in pairs])


def head_swap(value, bit):
    return lax.ppermute(value, "head", [(i, i ^ bit) for i in range(lax.axis_size("head"))])


def seq_swap(value, bit):
    step = 1 << bit
    return lax.ppermute(value, "seq", [(i, i ^ step) for i in range(lax.axis_size("seq"))])


def sum_over_seq(chunks, orders):
    keeps = [[chunk] for chunk in chunks]
    for turn in range(len(orders[0])):
        swapped = []
        for keep, order in zip(keeps, orders):
            half = keep[0].shape[0] // 2
            total = sum(part[half:].astype(F32) for part in keep).astype(BF16)
            swapped.append(seq_swap(total, order[turn]))
        keeps = [
            [part[:part.shape[0] // 2] for part in keep] + [new]
            for keep, new in zip(keeps, swapped)
        ]
    held = [(sum(part.astype(F32) for part in keep).astype(BF16),) for keep in keeps]
    for turn in reversed(range(len(orders[0]))):
        whole = [jnp.concatenate(parts) if len(parts) > 1 else parts[0] for parts in held]
        held = [(own, seq_swap(own, order[turn])) for own, order in zip(whole, orders)]
    return [part for parts in held for part in parts]


def local(
    queries_first,
    keys_first,
    values_first,
    input_map,
    fast_keys,
    fast_values,
    step_rates,
    fast_weights,
    output_map,
    queries_second,
    keys_second,
    values_second,
):
    rows, width = queries_first.shape
    seq_count = lax.axis_size("seq")
    seq_place = lax.axis_index("seq")
    head_place = lax.axis_index("head")
    weights = jnp.transpose(fast_weights[0], (1, 0, 2))
    hidden_size, fast_width = weights.shape[1:]
    shape = jax.ShapeDtypeStruct
    minus = jnp.float32(-jnp.inf)
    edges = jnp.stack(
        [
            jnp.where(seq_place > 0, 0.0, minus),
            jnp.where(seq_place < seq_count - 1, 0.0, minus),
        ]
    ).reshape(1, 2)

    bits = tuple(range(seq_count.bit_length() - 1))
    halving = seq_count == 1 << len(bits) and len(bits) > 1 and hidden_size >> len(bits) >= 16
    if halving:
        orders = (bits, bits, bits[1:] + bits[:1])
    else:
        orders = ((), (), ())
    place = seq_place.astype(jnp.int32).reshape(1, 1)
    gradients = call(
        functools.partial(gradient_kernel, orders),
        [shape(weights.shape[1:], BF16)] * 3,
        (place, step_rates.reshape(1, rows), fast_keys, fast_values, weights),
        12 * rows * hidden_size * fast_width,
        8 * rows * fast_width,
        scalars=1,
    )
    if halving:
        gathered = sum_over_seq(gradients, orders)
    else:
        gathered = lax.psum(gradients, "seq")

    both_first = jnp.concatenate([keys_first, values_first])
    prev_first = seq_shift(both_first, True)
    next_first = seq_shift(both_first, False)
    attend_flops = 12 * rows * rows * width
    fast_query = call(
        first_kernel,
        shape((rows, fast_width), BF16),
        (edges, queries_first, prev_first, keys_first, values_first, next_first, input_map[0]),
        attend_flops,
        16 * rows * width,
        scalars=1,
    )
    both_second = jnp.concatenate([keys_second, values_second])
    prev_second = seq_shift(both_second, True)
    next_second = seq_shift(both_second, False)

    own_rows = hidden_size >> len(orders[0])
    own_new, fast_out = call(
        functools.partial(renew_kernel, orders),
        [shape((3, own_rows, fast_width), BF16), shape((rows, fast_width), BF16)],
        (place, weights, fast_query, *gathered),
        6 * rows * hidden_size * fast_width,
        12 * hidden_size * fast_width,
        scalars=1,
        scratch=[pltpu.VMEM(weights.shape, BF16)],
    )
    if not halving:
        share_rows = hidden_size // seq_count
        own_new = lax.dynamic_slice_in_dim(own_new, seq_place * share_rows, share_rows, 1)

    def mixed_for(low_bit):
        far = (head_place // 2) ^ 1
        near = head_place // 2
        places = jnp.stack([far * 2 + low_bit, near * 2 + low_bit]).reshape(1, 2)
        return call(
            mix_kernel,
            shape((2, rows, width), BF16),
            (places, fast_out, output_map),
            4 * rows * fast_width * width,
            8 * rows * width,
            scalars=1,
        )

    my_bit = head_place % 2
    near_part = head_swap(mixed_for(1 - my_bit), 1)
    keep_part = mixed_for(my_bit)
    to_send = (keep_part[0].astype(F32) + near_part[0].astype(F32)).astype(BF16)
    far_part = head_swap(to_send, 2)

    normed_second = call(
        second_kernel,
        shape((rows, width), BF16),
        (edges, queries_second, keep_part, near_part, far_part,
         prev_second, keys_second, values_second, next_second),
        attend_flops,
        16 * rows * width,
        scalars=1,
    )
    return (normed_second, jnp.transpose(own_new, (1, 0, 2))[None])


def solution(mesh):
    return jax.shard_map(
        local,
        mesh=mesh,
        in_specs=(
            P("seq", "head"),
            P("seq", "head"),
            P("seq", "head"),
            P("head", None, None),
            P("seq", "head"),
            P("seq", "head"),
            P("seq", "head"),
            P("head", None, None, None),
            P("head", None),
            P("seq", "head"),
            P("seq", "head"),
            P("seq", "head"),
        ),
        out_specs=(P("seq", "head"), P("head", "seq", None, None)),
        check_vma=False,
    )
```

```python
import functools
import math

import jax
import jax.numpy as jnp
from jax import lax
from jax.experimental import pallas as pl
from jax.experimental.pallas import tpu as pltpu
from jax.sharding import PartitionSpec as P

HALF_WIN = 512
HEAD_DIM = 128
HEADS_GRP = 2
FAST_DIM = 512
FAST_HIDDEN = 512
TILE = 128
VMEM_LIMIT = 48 * 1024 * 1024

BF16 = jnp.bfloat16
F32 = jnp.float32
INVERSE = 1.0 / math.sqrt(FAST_DIM)


def dot_nn(left, right):
    return lax.dot_general(left, right, (((1,), (0,)), ((), ())), preferred_element_type=F32)


def dot_nt(left, right):
    return lax.dot_general(left, right, (((1,), (1,)), ((), ())), preferred_element_type=F32)


def call(body, out_shapes, operands, scalars=0, anywhere=0, scratch=(), cost=None):
    vmem = pl.BlockSpec(memory_space=pltpu.VMEM)
    in_specs = (
        [pl.BlockSpec(memory_space=pltpu.SMEM)] * scalars
        + [vmem] * (len(operands) - scalars - anywhere)
        + [pl.BlockSpec(memory_space=pl.ANY)] * anywhere
    )
    flops, moved = cost or (1000, 1000)
    return pl.pallas_call(
        body,
        out_shape=out_shapes,
        in_specs=in_specs,
        out_specs=jax.tree.map(lambda _: vmem, out_shapes),
        scratch_shapes=scratch,
        compiler_params=pltpu.CompilerParams(vmem_limit_bytes=VMEM_LIMIT),
        cost_estimate=pl.CostEstimate(flops=flops, bytes_accessed=moved, transcendentals=0),
    )(*operands)


def block_at(slot, order):
    block = 0
    for place, bit in enumerate(reversed(order)):
        block |= ((slot >> place) & 1) << bit
    return block


def load_rows(order, place, source, target, sems, first):
    block_rows = target.shape[0] >> len(order)
    copies = []
    for slot in range(1 << len(order)):
        block = (block_at(slot, order) ^ place) if order else 0
        start = pl.multiple_of(block * block_rows, block_rows)
        copies.append(
            pltpu.make_async_copy(
                source.at[pl.ds(start, block_rows), :],
                target.at[pl.ds(slot * block_rows, block_rows), :],
                sems.at[first + slot],
            )
        )
    for copy in copies:
        copy.start()
    return copies


def gradient_kernel(order, down, place_ref, rates_ref, keys_hbm, values_hbm, weights_hbm, *refs):
    out_refs, (keys_ref, values_ref, weights_ref, sems) = refs[:-4], refs[-4:]
    place = place_ref[0, 0]
    slots = 1 << len(order)
    matrices = weights_ref.shape[0]
    hidden_size = weights_ref.shape[1]
    keys_copy = pltpu.make_async_copy(keys_hbm, keys_ref, sems.at[matrices * slots])
    keys_copy.start()
    copies = [keys_copy]
    for matrix in range(matrices):
        copies += load_rows(
            order, place, weights_hbm.at[matrix], weights_ref.at[matrix], sems, matrix * slots
        )
    values_copy = pltpu.make_async_copy(values_hbm, values_ref, sems.at[matrices * slots + 1])
    values_copy.start()
    for copy in copies + [values_copy]:
        copy.wait()
    rates = rates_ref[...]
    keys = keys_ref[...]
    values = values_ref[...]
    step = 128
    halves = 2 if order else 1
    half_rows = hidden_size // halves
    for low in range(0, hidden_size, step):
        rows = slice(low, low + step)
        half, start = low // half_rows, low % half_rows
        target = slice(start, start + step)
        gate = dot_nt(weights_ref[0, rows, :], keys) * INVERSE
        up = dot_nt(weights_ref[1, rows, :], keys) * INVERSE
        sigmoid = jax.nn.sigmoid(gate)
        silu = gate * sigmoid
        if down:
            hidden = (rates * silu * up).astype(BF16)
            out_refs[half][target, :] = dot_nn(hidden, values).astype(BF16)
            continue
        backward = rates * dot_nt(weights_ref[2, rows, :], values)
        d_gate = (
            backward * up * sigmoid * (1.0 + gate * (1.0 - sigmoid)) * INVERSE
        ).astype(BF16)
        d_up = (backward * silu * INVERSE).astype(BF16)
        out_refs[half][target, :] = dot_nn(d_gate, keys).astype(BF16)
        out_refs[halves + half][target, :] = dot_nn(d_up, keys).astype(BF16)


def attend_rows(edge_prev, edge_next, query_tile, keys_prev, keys_own, keys_next,
                values_prev, values_own, values_next):
    scale = 1.0 / math.sqrt(HEAD_DIM)
    row = lax.broadcasted_iota(jnp.int32, (TILE, TILE), 0)
    col = lax.broadcasted_iota(jnp.int32, (TILE, TILE), 1)
    minus = jnp.float32(-jnp.inf)
    score_prev = dot_nt(query_tile, keys_prev)
    score_own = dot_nt(query_tile, keys_own)
    score_next = dot_nt(query_tile, keys_next)
    parts = [score_prev[:, :TILE] + jnp.where(col >= row, edge_prev, minus)]
    if score_prev.shape[1] > TILE:
        parts.append(score_prev[:, TILE:] + edge_prev)
    parts.append(score_own)
    if score_next.shape[1] > TILE:
        parts.append(score_next[:, :-TILE] + edge_next)
    parts.append(score_next[:, -TILE:] + jnp.where(col <= row, edge_next, minus))
    scores = jnp.concatenate(parts, axis=1)
    highest = jnp.max(scores, axis=1, keepdims=True)
    weights = jnp.exp((scores - highest) * scale)
    total = jnp.sum(weights, axis=1, keepdims=True)
    weights = weights.astype(BF16)
    width_prev, width_own = score_prev.shape[1], score_own.shape[1]
    attended = (
        dot_nn(weights[:, :width_prev], values_prev)
        + dot_nn(weights[:, width_prev:width_prev + width_own], values_own)
        + dot_nn(weights[:, width_prev + width_own:], values_next)
    )
    return attended / total


def pack_kernel(side_ref, queries_ref, keys_ref, values_ref, out_ref):
    count = queries_ref.shape[0]
    start = pl.multiple_of((1 - side_ref[0, 0]) * HEAD_DIM, HEAD_DIM)
    for index, ref in enumerate((queries_ref, keys_ref, values_ref)):
        out_ref[index * count:(index + 1) * count, :] = ref[:, pl.ds(start, HEAD_DIM)]


def border_kernel(side_ref, keys_ref, values_ref, other_ref, low_ref, high_ref):
    count = keys_ref.shape[0]
    side = side_ref[0, 0]
    start = pl.multiple_of(side * HEAD_DIM, HEAD_DIM)

    def fill(own_ref, other_out_ref):
        own_ref[:count, :] = keys_ref[:, pl.ds(start, HEAD_DIM)]
        own_ref[count:, :] = values_ref[:, pl.ds(start, HEAD_DIM)]
        other_out_ref[...] = other_ref[count:, :]

    @pl.when(side == 0)
    def _():
        fill(low_ref, high_ref)

    @pl.when(side != 0)
    def _():
        fill(high_ref, low_ref)


def first_kernel(edge_ref, side_ref, queries_ref, other_ref, prev_ref, low_ref, high_ref, next_ref,
                 keep_ref, send_ref, keys_ref, values_ref):
    count = queries_ref.shape[0]
    side = side_ref[0, 0]
    for index, ref in enumerate((prev_ref, low_ref, high_ref, next_ref)):
        rows = slice(index * count, (index + 1) * count)
        keys_ref[rows, :] = ref[:count, :]
        values_ref[rows, :] = ref[count:, :]
    start = pl.multiple_of(side * HEAD_DIM, HEAD_DIM)
    for turn, out_ref in enumerate((keep_ref, send_ref)):
        base = (side if turn == 0 else 1 - side) * count

        def span(ref, low, length):
            return ref[pl.ds(pl.multiple_of(base + low, TILE), length), :]

        for index in range(count // TILE):
            low, high = index * TILE, (index + 1) * TILE
            query = queries_ref[low:high, pl.ds(start, HEAD_DIM)] if turn == 0 else other_ref[low:high, :]
            out_ref[low:high, :] = attend_rows(
                edge_ref[turn, 0], edge_ref[turn, 1], query,
                span(keys_ref, low, count - low), span(keys_ref, count, count),
                span(keys_ref, 2 * count, high),
                span(values_ref, low, count - low), span(values_ref, count, count),
                span(values_ref, 2 * count, high),
            ).astype(BF16)


def query_kernel(side_ref, keep_ref, other_ref, map_ref, out_ref):
    side = side_ref[0, 0]
    own = keep_ref[...].astype(F32)
    other = other_ref[...].astype(F32)
    square = jnp.sum(own * own + other * other, axis=1, keepdims=True)
    norm = lax.rsqrt(square / (HEADS_GRP * HEAD_DIM) + 1e-05)
    own_map = map_ref[pl.ds(pl.multiple_of(side * HEAD_DIM, HEAD_DIM), HEAD_DIM), :]
    other_map = map_ref[pl.ds(pl.multiple_of((1 - side) * HEAD_DIM, HEAD_DIM), HEAD_DIM), :]
    out_ref[...] = (
        dot_nn((own * norm).astype(BF16), own_map) + dot_nn((other * norm).astype(BF16), other_map)
    ).astype(BF16)


def second_kernel(edge_ref, queries_ref, keep_ref, near_ref, far_ref, keys_prev_ref, keys_ref, keys_next_ref,
                  values_prev_ref, values_ref, values_next_ref, out_ref):
    count = keys_ref.shape[0]
    for index in range(count // TILE):
        low, high = index * TILE, (index + 1) * TILE
        rows = slice(low, high)
        mixed = (
            keep_ref[1, rows, :].astype(F32)
            + near_ref[1, rows, :].astype(F32)
            + far_ref[rows, :].astype(F32)
        )
        query = (queries_ref[rows, :].astype(F32) + mixed).astype(BF16)
        heads = []
        for head in range(HEADS_GRP):
            cols = slice(head * HEAD_DIM, (head + 1) * HEAD_DIM)
            heads.append(
                attend_rows(
                    edge_ref[0, 0], edge_ref[0, 1], query[:, cols],
                    keys_prev_ref[low:, cols], keys_ref[:, cols], keys_next_ref[:high, cols],
                    values_prev_ref[low:, cols], values_ref[:, cols], values_next_ref[:high, cols],
                )
            )
        both = jnp.concatenate(heads, axis=1)
        mean = jnp.mean(both * both, axis=1, keepdims=True)
        out_ref[rows, :] = (both * lax.rsqrt(mean + 1e-05)).astype(BF16)


def renew_kernel(orders, place_ref, weights_ref, query_ref, *refs):
    pieces, (own_ref, fast_ref, new_ref) = refs[:-3], refs[-3:]
    place = place_ref[0, 0]
    limit_norm = math.sqrt(FAST_HIDDEN * FAST_DIM) / 2.0
    square = jnp.zeros((1, weights_ref.shape[2]), F32)
    step = 64
    for piece in pieces:
        for low in range(0, piece.shape[0], step):
            part = piece[low:low + step, :].astype(F32)
            square = square + jnp.sum(part * part, axis=0, keepdims=True)
    square = jnp.sum(square, axis=1, keepdims=True)
    factor = jnp.minimum(1.0, limit_norm * lax.rsqrt(square + 1e-06))
    per_matrix = len(pieces) // 3
    for matrix, order in enumerate(orders):
        block_rows = weights_ref.shape[1] >> len(order)
        slots = 1 << len(order)
        for slot in range(slots):
            piece = pieces[matrix * per_matrix + slot * per_matrix // slots]
            inside = slot % (slots // per_matrix)
            block = block_at(slot, order) ^ place if order else 0
            for low in range(0, block_rows, step):
                count = min(step, block_rows)
                rows = pl.ds(pl.multiple_of(block * block_rows + low, count), count)
                old = weights_ref[matrix, rows, :].astype(F32)
                part = piece[inside * block_rows + low:inside * block_rows + low + count, :]
                stepped = old + factor * part.astype(F32)
                norm = jnp.sqrt(jnp.sum(old * old, axis=1, keepdims=True))
                size = jnp.sum(stepped * stepped, axis=1, keepdims=True)
                fresh = (stepped * norm * lax.rsqrt(size + 1e-06)).astype(BF16)
                new_ref[matrix, rows, :] = fresh
                if slot == 0:
                    own_ref[matrix, low:low + count, :] = fresh
    step = 128
    for low in range(0, query_ref.shape[0], step):
        rows = slice(low, low + step)
        query = query_ref[rows, :]
        gate = dot_nt(query, new_ref[0]) * INVERSE
        up = dot_nt(query, new_ref[1]) * INVERSE
        hidden = (jax.nn.silu(gate) * up).astype(BF16)
        raw = dot_nn(hidden, new_ref[2])
        mean = jnp.mean(raw * raw, axis=1, keepdims=True)
        fast_ref[rows, :] = (raw * lax.rsqrt(mean + 1e-05)).astype(BF16)


def mix_kernel(place_ref, fast_ref, map_ref, out_ref):
    width = out_ref.shape[2]
    for slot in range(2):
        start = pl.multiple_of(place_ref[0, slot] * width, width)
        columns = map_ref[:, pl.ds(start, width)]
        out_ref[slot] = dot_nn(fast_ref[...], columns).astype(BF16)


def seq_shift(value, step):
    peers = lax.axis_size("seq")
    return lax.ppermute(
        value, "seq", [(i, i + step) for i in range(peers) if 0 <= i + step < peers]
    )


def head_swap(value, bit):
    return lax.ppermute(value, "head", [(i, i ^ bit) for i in range(lax.axis_size("head"))])


def seq_swap(value, bit):
    step = 1 << bit
    return lax.ppermute(value, "seq", [(i, i ^ step) for i in range(lax.axis_size("seq"))])


def sum_over_seq(chunks, orders):
    keeps = [[keep] for keep, _ in chunks]
    for turn in range(len(orders[0])):
        swapped = []
        for index, order in enumerate(orders):
            if turn == 0:
                total = chunks[index][1]
            else:
                half = keeps[index][0].shape[0] // 2
                total = sum(part[half:].astype(F32) for part in keeps[index]).astype(BF16)
                keeps[index] = [part[:half] for part in keeps[index]]
            swapped.append(seq_swap(total, order[turn]))
        keeps = [keep + [new] for keep, new in zip(keeps, swapped)]
    held = [(sum(part.astype(F32) for part in keep).astype(BF16),) for keep in keeps]
    for turn in reversed(range(len(orders[0]))):
        whole = [jnp.concatenate(parts) if len(parts) > 1 else parts[0] for parts in held]
        held = [(own, seq_swap(own, order[turn])) for own, order in zip(whole, orders)]
    return [part for parts in held for part in parts]


def local(
    queries_first,
    keys_first,
    values_first,
    input_map,
    fast_keys,
    fast_values,
    step_rates,
    fast_weights,
    output_map,
    queries_second,
    keys_second,
    values_second,
):
    rows, width = queries_first.shape
    seq_count = lax.axis_size("seq")
    seq_place = lax.axis_index("seq")
    head_place = lax.axis_index("head")
    weights = jnp.transpose(fast_weights[0], (1, 0, 2))
    hidden_size, fast_width = weights.shape[1:]
    shape = jax.ShapeDtypeStruct
    minus = jnp.float32(-jnp.inf)
    side = seq_place % 2

    def edges_of(block):
        return [jnp.where(block > 0, 0.0, minus), jnp.where(block < seq_count - 1, 0.0, minus)]

    edges = jnp.stack(edges_of(seq_place) + edges_of(seq_place ^ 1)).reshape(2, 2)
    side_scalar = side.astype(jnp.int32).reshape(1, 1)
    place = seq_place.astype(jnp.int32).reshape(1, 1)

    packed = call(
        pack_kernel,
        shape((3 * rows, HEAD_DIM), BF16),
        (side_scalar, queries_first, keys_first, values_first),
        scalars=1,
    )
    other_first = seq_swap(packed, 0)

    bits = tuple(range(seq_count.bit_length() - 1))
    halving = seq_count == 1 << len(bits) and len(bits) > 1 and hidden_size >> len(bits) >= 16
    order, down_order = (bits, bits[1:] + bits[:1]) if halving else ((), ())
    orders = (order, order, down_order)
    halves = 2 if halving else 1

    def gradient_of(order, down):
        matrices, chunks = (2, 1) if down else (3, 2)
        return call(
            functools.partial(gradient_kernel, order, down),
            [shape((hidden_size // halves, fast_width), BF16)] * (halves * chunks),
            (place, step_rates.reshape(1, rows), fast_keys, fast_values, weights),
            scalars=1,
            anywhere=3,
            scratch=[
                pltpu.VMEM(fast_keys.shape, BF16),
                pltpu.VMEM(fast_values.shape, BF16),
                pltpu.VMEM((matrices, hidden_size, fast_width), BF16),
                pltpu.SemaphoreType.DMA((matrices * (1 << len(order)) + 2,)),
            ],
        )

    down_halves = gradient_of(down_order, True)
    gate_up_halves = gradient_of(order, False)
    halves_of = [gate_up_halves[:halves], gate_up_halves[halves:], down_halves]
    if halving:
        gathered = sum_over_seq(halves_of, orders)
    else:
        gathered = lax.psum([part for (part,) in halves_of], "seq")

    low_block, high_block = call(
        border_kernel,
        [shape((2 * rows, HEAD_DIM), BF16)] * 2,
        (side_scalar, keys_first, values_first, other_first),
        scalars=1,
    )
    prev_first = seq_shift(high_block, 2)
    next_first = seq_shift(low_block, -2)
    keep_first, send_first = call(
        first_kernel,
        [shape((rows, HEAD_DIM), BF16)] * 2,
        (edges, side_scalar, queries_first, other_first, prev_first, low_block, high_block, next_first),
        scalars=2,
        scratch=[pltpu.VMEM((4 * rows, HEAD_DIM), BF16)] * 2,
        cost=(12 * rows * rows * width, 16 * rows * width),
    )
    fast_query = call(
        query_kernel,
        shape((rows, fast_width), BF16),
        (side_scalar, keep_first, seq_swap(send_first, 0), input_map[0]),
        scalars=1,
    )

    keys_prev, keys_next = seq_shift(keys_second, 1), seq_shift(keys_second, -1)
    values_prev, values_next = seq_shift(values_second, 1), seq_shift(values_second, -1)
    fast_query, keys_prev, keys_next = lax.optimization_barrier((fast_query, keys_prev, keys_next))

    own_rows = hidden_size >> len(orders[0])
    own_new, fast_out = call(
        functools.partial(renew_kernel, orders),
        [shape((3, own_rows, fast_width), BF16), shape((rows, fast_width), BF16)],
        (place, weights, fast_query, *gathered),
        scalars=1,
        scratch=[pltpu.VMEM(weights.shape, BF16)],
    )
    if not halving:
        share_rows = hidden_size // seq_count
        own_new = lax.dynamic_slice_in_dim(own_new, seq_place * share_rows, share_rows, 1)

    def mixed_for(low_bit):
        far = (head_place // 2) ^ 1
        near = head_place // 2
        places = jnp.stack([far * 2 + low_bit, near * 2 + low_bit]).reshape(1, 2)
        return call(
            mix_kernel,
            shape((2, rows, width), BF16),
            (places, fast_out, output_map),
            scalars=1,
        )

    my_bit = head_place % 2
    near_part = head_swap(mixed_for(1 - my_bit), 1)
    keep_part = mixed_for(my_bit)
    to_send = (keep_part[0].astype(F32) + near_part[0].astype(F32)).astype(BF16)
    far_part = head_swap(to_send, 2)

    normed_second = call(
        second_kernel,
        shape((rows, width), BF16),
        (edges, queries_second, keep_part, near_part, far_part,
         keys_prev, keys_second, keys_next, values_prev, values_second, values_next),
        scalars=1,
        cost=(12 * rows * rows * width, 16 * rows * width),
    )
    return (normed_second, jnp.transpose(own_new, (1, 0, 2))[None])


def solution(mesh):
    return jax.shard_map(
        local,
        mesh=mesh,
        in_specs=(
            P("seq", "head"),
            P("seq", "head"),
            P("seq", "head"),
            P("head", None, None),
            P("seq", "head"),
            P("seq", "head"),
            P("seq", "head"),
            P("head", None, None, None),
            P("head", None),
            P("seq", "head"),
            P("seq", "head"),
            P("seq", "head"),
        ),
        out_specs=(P("seq", "head"), P("head", "seq", None, None)),
        check_vma=False,
    )
```

```python
import functools
import math

import jax
import jax.numpy as jnp
from jax import lax
from jax.experimental import pallas as pl
from jax.experimental.pallas import tpu as pltpu
from jax.sharding import PartitionSpec as P

HALF_WIN = 512
HEAD_DIM = 128
HEADS_GRP = 2
FAST_DIM = 512
FAST_HIDDEN = 512
TILE = 128
VMEM_LIMIT = 48 * 1024 * 1024

BF16 = jnp.bfloat16
F32 = jnp.float32
INVERSE = 1.0 / math.sqrt(FAST_DIM)


def dot_nn(left, right):
    return lax.dot_general(left, right, (((1,), (0,)), ((), ())), preferred_element_type=F32)


def dot_nt(left, right):
    return lax.dot_general(left, right, (((1,), (1,)), ((), ())), preferred_element_type=F32)


def call(body, out_shapes, operands, scalars=0, anywhere=0, scratch=(), cost=None):
    vmem = pl.BlockSpec(memory_space=pltpu.VMEM)
    in_specs = (
        [pl.BlockSpec(memory_space=pltpu.SMEM)] * scalars
        + [vmem] * (len(operands) - scalars - anywhere)
        + [pl.BlockSpec(memory_space=pl.ANY)] * anywhere
    )
    flops, moved = cost or (1000, 1000)
    return pl.pallas_call(
        body,
        out_shape=out_shapes,
        in_specs=in_specs,
        out_specs=jax.tree.map(lambda _: vmem, out_shapes),
        scratch_shapes=scratch,
        compiler_params=pltpu.CompilerParams(vmem_limit_bytes=VMEM_LIMIT),
        cost_estimate=pl.CostEstimate(flops=flops, bytes_accessed=moved, transcendentals=0),
    )(*operands)


def slot_of(block, order):
    slot = 0
    for bit in order:
        slot = slot * 2 + ((block >> bit) & 1)
    return slot


def gradient_kernel(orders, place_ref, rates_ref, keys_ref, values_ref, weights_ref, *refs):
    out_refs, chunk_refs = refs[:-2], refs[-2:]
    place = place_ref[0, 0]
    rates = rates_ref[...]
    keys = keys_ref[...]
    values = values_ref[...]
    hidden_size, width = weights_ref.shape[1:]
    step = 128

    def put(chunk, low, columns, product):
        order = orders[chunk]
        block_rows = min(step, hidden_size >> len(order))
        for start in range(0, step, block_rows):
            row = low + start
            if order:
                slot = slot_of((row // block_rows) ^ place, order)
                row = pl.multiple_of(slot * block_rows, block_rows)
            chunk_refs[chunk][pl.ds(row, block_rows), columns] = product[start:start + block_rows]

    for low in range(0, hidden_size, step):
        rows = slice(low, low + step)
        gate = dot_nt(weights_ref[0, rows, :], keys) * INVERSE
        up = dot_nt(weights_ref[1, rows, :], keys) * INVERSE
        sigmoid = jax.nn.sigmoid(gate)
        silu = gate * sigmoid
        hidden = (rates * silu * up).astype(BF16)
        backward = rates * dot_nt(weights_ref[2, rows, :], values)
        d_gate = (
            backward * up * sigmoid * (1.0 + gate * (1.0 - sigmoid)) * INVERSE
        ).astype(BF16)
        d_up = (backward * silu * INVERSE).astype(BF16)
        up_part = dot_nn(d_up, keys).astype(BF16)
        put(0, low, slice(0, width), dot_nn(d_gate, keys).astype(BF16))
        put(0, low, slice(width, width + width // 2), up_part[:, :width // 2])
        put(1, low, slice(0, width), dot_nn(hidden, values).astype(BF16))
        put(1, low, slice(width, width + width // 2), up_part[:, width // 2:])
    halves = len(out_refs) // 2
    half_rows = hidden_size // halves
    for index, out_ref in enumerate(out_refs):
        half = index % halves
        out_ref[...] = chunk_refs[index // halves][half * half_rows:(half + 1) * half_rows, :]


def attend_rows(edge_prev, edge_next, query_tile, keys_prev, keys_own, keys_next,
                values_prev, values_own, values_next):
    scale = 1.0 / math.sqrt(HEAD_DIM)
    row = lax.broadcasted_iota(jnp.int32, (TILE, TILE), 0)
    col = lax.broadcasted_iota(jnp.int32, (TILE, TILE), 1)
    minus = jnp.float32(-jnp.inf)
    score_prev = dot_nt(query_tile, keys_prev)
    score_own = dot_nt(query_tile, keys_own)
    score_next = dot_nt(query_tile, keys_next)
    parts = [score_prev[:, :TILE] + jnp.where(col >= row, edge_prev, minus)]
    if score_prev.shape[1] > TILE:
        parts.append(score_prev[:, TILE:] + edge_prev)
    parts.append(score_own)
    if score_next.shape[1] > TILE:
        parts.append(score_next[:, :-TILE] + edge_next)
    parts.append(score_next[:, -TILE:] + jnp.where(col <= row, edge_next, minus))
    scores = jnp.concatenate(parts, axis=1)
    highest = jnp.max(scores, axis=1, keepdims=True)
    weights = jnp.exp((scores - highest) * scale)
    total = jnp.sum(weights, axis=1, keepdims=True)
    weights = weights.astype(BF16)
    width_prev, width_own = score_prev.shape[1], score_own.shape[1]
    attended = (
        dot_nn(weights[:, :width_prev], values_prev)
        + dot_nn(weights[:, width_prev:width_prev + width_own], values_own)
        + dot_nn(weights[:, width_prev + width_own:], values_next)
    )
    return attended / total


def pack_kernel(side_ref, queries_ref, keys_ref, values_ref, out_ref):
    count = queries_ref.shape[0]
    start = pl.multiple_of((1 - side_ref[0, 0]) * HEAD_DIM, HEAD_DIM)
    for index, ref in enumerate((queries_ref, keys_ref, values_ref)):
        out_ref[index * count:(index + 1) * count, :] = ref[:, pl.ds(start, HEAD_DIM)]


def border_kernel(side_ref, keys_ref, values_ref, other_ref, low_ref, high_ref):
    count = keys_ref.shape[0]
    side = side_ref[0, 0]
    start = pl.multiple_of(side * HEAD_DIM, HEAD_DIM)

    def fill(own_ref, other_out_ref):
        own_ref[:count, :] = keys_ref[:, pl.ds(start, HEAD_DIM)]
        own_ref[count:, :] = values_ref[:, pl.ds(start, HEAD_DIM)]
        other_out_ref[...] = other_ref[count:, :]

    @pl.when(side == 0)
    def _():
        fill(low_ref, high_ref)

    @pl.when(side != 0)
    def _():
        fill(high_ref, low_ref)


def first_kernel(edge_ref, side_ref, queries_ref, other_ref, prev_ref, low_ref, high_ref, next_ref,
                 keep_ref, send_ref, keys_ref, values_ref):
    count = queries_ref.shape[0]
    side = side_ref[0, 0]
    for index, ref in enumerate((prev_ref, low_ref, high_ref, next_ref)):
        rows = slice(index * count, (index + 1) * count)
        keys_ref[rows, :] = ref[:count, :]
        values_ref[rows, :] = ref[count:, :]
    start = pl.multiple_of(side * HEAD_DIM, HEAD_DIM)
    for turn, out_ref in enumerate((keep_ref, send_ref)):
        base = (side if turn == 0 else 1 - side) * count

        def span(ref, low, length):
            return ref[pl.ds(pl.multiple_of(base + low, TILE), length), :]

        for index in range(count // TILE):
            low, high = index * TILE, (index + 1) * TILE
            query = queries_ref[low:high, pl.ds(start, HEAD_DIM)] if turn == 0 else other_ref[low:high, :]
            out_ref[low:high, :] = attend_rows(
                edge_ref[turn, 0], edge_ref[turn, 1], query,
                span(keys_ref, low, count - low), span(keys_ref, count, count),
                span(keys_ref, 2 * count, high),
                span(values_ref, low, count - low), span(values_ref, count, count),
                span(values_ref, 2 * count, high),
            ).astype(BF16)


def query_kernel(side_ref, keep_ref, other_ref, map_ref, out_ref):
    side = side_ref[0, 0]
    own = keep_ref[...].astype(F32)
    other = other_ref[...].astype(F32)
    square = jnp.sum(own * own + other * other, axis=1, keepdims=True)
    norm = lax.rsqrt(square / (HEADS_GRP * HEAD_DIM) + 1e-05)
    own_map = map_ref[pl.ds(pl.multiple_of(side * HEAD_DIM, HEAD_DIM), HEAD_DIM), :]
    other_map = map_ref[pl.ds(pl.multiple_of((1 - side) * HEAD_DIM, HEAD_DIM), HEAD_DIM), :]
    out_ref[...] = (
        dot_nn((own * norm).astype(BF16), own_map) + dot_nn((other * norm).astype(BF16), other_map)
    ).astype(BF16)


def second_kernel(edge_ref, queries_ref, keep_ref, near_ref, far_ref, keys_prev_ref, keys_ref, keys_next_ref,
                  values_prev_ref, values_ref, values_next_ref, out_ref):
    count = keys_ref.shape[0]
    for index in range(count // TILE):
        low, high = index * TILE, (index + 1) * TILE
        rows = slice(low, high)
        mixed = (
            keep_ref[1, rows, :].astype(F32)
            + near_ref[1, rows, :].astype(F32)
            + far_ref[rows, :].astype(F32)
        )
        query = (queries_ref[rows, :].astype(F32) + mixed).astype(BF16)
        heads = []
        for head in range(HEADS_GRP):
            cols = slice(head * HEAD_DIM, (head + 1) * HEAD_DIM)
            heads.append(
                attend_rows(
                    edge_ref[0, 0], edge_ref[0, 1], query[:, cols],
                    keys_prev_ref[low:, cols], keys_ref[:, cols], keys_next_ref[:high, cols],
                    values_prev_ref[low:, cols], values_ref[:, cols], values_next_ref[:high, cols],
                )
            )
        both = jnp.concatenate(heads, axis=1)
        mean = jnp.mean(both * both, axis=1, keepdims=True)
        out_ref[rows, :] = (both * lax.rsqrt(mean + 1e-05)).astype(BF16)


def renew_kernel(orders, place_ref, weights_ref, query_ref, *refs):
    pieces, (own_ref, fast_ref, new_ref) = refs[:-3], refs[-3:]
    place = place_ref[0, 0]
    hidden_size, width = weights_ref.shape[1:]
    limit_norm = math.sqrt(FAST_HIDDEN * FAST_DIM) / 2.0
    step = 64
    square = jnp.zeros((1, pieces[0].shape[1]), F32)
    for piece in pieces:
        for low in range(0, piece.shape[0], step):
            part = piece[low:low + step, :].astype(F32)
            square = square + jnp.sum(part * part, axis=0, keepdims=True)
    square = jnp.sum(square, axis=1, keepdims=True)
    factor = jnp.minimum(1.0, limit_norm * lax.rsqrt(square + 1e-06))
    per_chunk = len(pieces) // 2
    piece_rows = pieces[0].shape[0]
    blocks = 1 << len(orders[0])
    block_rows = hidden_size // blocks
    count = min(step, block_rows)
    for block in range(blocks):
        starts = [slot_of(block, order) * block_rows for order in orders]
        for low in range(0, block_rows, count):
            found = []
            for chunk, start in enumerate(starts):
                piece = pieces[chunk * per_chunk + start // piece_rows]
                inside = start % piece_rows + low
                found.append(piece[inside:inside + count, :].astype(F32))
            parts = [
                found[0][:, :width],
                jnp.concatenate([found[0][:, width:], found[1][:, width:]], axis=1),
                found[1][:, :width],
            ]
            rows = slice(low, low + count)
            if blocks > 1:
                rows = pl.ds(pl.multiple_of((block ^ place) * block_rows + low, count), count)
            for matrix, part in enumerate(parts):
                old = weights_ref[matrix, rows, :].astype(F32)
                stepped = old + factor * part
                norm = jnp.sqrt(jnp.sum(old * old, axis=1, keepdims=True))
                size = jnp.sum(stepped * stepped, axis=1, keepdims=True)
                fresh = (stepped * norm * lax.rsqrt(size + 1e-06)).astype(BF16)
                new_ref[matrix, rows, :] = fresh
                if block == 0:
                    own_ref[matrix, low:low + count, :] = fresh
    step = 128
    for low in range(0, query_ref.shape[0], step):
        rows = slice(low, low + step)
        query = query_ref[rows, :]
        gate = dot_nt(query, new_ref[0]) * INVERSE
        up = dot_nt(query, new_ref[1]) * INVERSE
        hidden = (jax.nn.silu(gate) * up).astype(BF16)
        raw = dot_nn(hidden, new_ref[2])
        mean = jnp.mean(raw * raw, axis=1, keepdims=True)
        fast_ref[rows, :] = (raw * lax.rsqrt(mean + 1e-05)).astype(BF16)


def mix_kernel(place_ref, fast_ref, map_ref, out_ref):
    width = out_ref.shape[2]
    for slot in range(2):
        start = pl.multiple_of(place_ref[0, slot] * width, width)
        columns = map_ref[:, pl.ds(start, width)]
        out_ref[slot] = dot_nn(fast_ref[...], columns).astype(BF16)


def seq_shift(value, step):
    peers = lax.axis_size("seq")
    return lax.ppermute(
        value, "seq", [(i, i + step) for i in range(peers) if 0 <= i + step < peers]
    )


def head_swap(value, bit):
    return lax.ppermute(value, "head", [(i, i ^ bit) for i in range(lax.axis_size("head"))])


def seq_swap(value, bit):
    step = 1 << bit
    return lax.ppermute(value, "seq", [(i, i ^ step) for i in range(lax.axis_size("seq"))])


def sum_over_seq(chunks, orders):
    keeps = [[keep] for keep, _ in chunks]
    for turn in range(len(orders[0])):
        swapped = []
        for index, order in enumerate(orders):
            if turn == 0:
                total = chunks[index][1]
            else:
                half = keeps[index][0].shape[0] // 2
                total = sum(part[half:].astype(F32) for part in keeps[index]).astype(BF16)
                keeps[index] = [part[:half] for part in keeps[index]]
            swapped.append(seq_swap(total, order[turn]))
        keeps = [keep + [new] for keep, new in zip(keeps, swapped)]
    held = [(sum(part.astype(F32) for part in keep).astype(BF16),) for keep in keeps]
    for turn in reversed(range(len(orders[0]))):
        whole = [jnp.concatenate(parts) if len(parts) > 1 else parts[0] for parts in held]
        held = [(own, seq_swap(own, order[turn])) for own, order in zip(whole, orders)]
    return [part for parts in held for part in parts]


def local(
    queries_first,
    keys_first,
    values_first,
    input_map,
    fast_keys,
    fast_values,
    step_rates,
    fast_weights,
    output_map,
    queries_second,
    keys_second,
    values_second,
):
    rows, width = queries_first.shape
    seq_count = lax.axis_size("seq")
    seq_place = lax.axis_index("seq")
    head_place = lax.axis_index("head")
    weights = jnp.transpose(fast_weights[0], (1, 0, 2))
    hidden_size, fast_width = weights.shape[1:]
    shape = jax.ShapeDtypeStruct
    minus = jnp.float32(-jnp.inf)
    side = seq_place % 2

    def edges_of(block):
        return [jnp.where(block > 0, 0.0, minus), jnp.where(block < seq_count - 1, 0.0, minus)]

    edges = jnp.stack(edges_of(seq_place) + edges_of(seq_place ^ 1)).reshape(2, 2)
    side_scalar = side.astype(jnp.int32).reshape(1, 1)
    place = seq_place.astype(jnp.int32).reshape(1, 1)

    packed = call(
        pack_kernel,
        shape((3 * rows, HEAD_DIM), BF16),
        (side_scalar, queries_first, keys_first, values_first),
        scalars=1,
    )
    other_first = seq_swap(packed, 0)

    bits = tuple(range(seq_count.bit_length() - 1))
    halving = seq_count == 1 << len(bits) and len(bits) > 1 and hidden_size >> len(bits) >= 16
    orders = (bits, bits[1:] + bits[:1]) if halving else ((), ())
    halves = 2 if halving else 1
    chunk_width = fast_width + fast_width // 2
    gradients = call(
        functools.partial(gradient_kernel, orders),
        [shape((hidden_size // halves, chunk_width), BF16)] * (2 * halves),
        (place, step_rates.reshape(1, rows), fast_keys, fast_values, weights),
        scalars=1,
        scratch=[pltpu.VMEM((hidden_size, chunk_width), BF16)] * 2,
    )
    if halving:
        gathered = sum_over_seq([gradients[:2], gradients[2:]], orders)
    else:
        gathered = lax.psum(gradients, "seq")

    low_block, high_block = call(
        border_kernel,
        [shape((2 * rows, HEAD_DIM), BF16)] * 2,
        (side_scalar, keys_first, values_first, other_first),
        scalars=1,
    )
    prev_first = seq_shift(high_block, 2)
    next_first = seq_shift(low_block, -2)
    keep_first, send_first = call(
        first_kernel,
        [shape((rows, HEAD_DIM), BF16)] * 2,
        (edges, side_scalar, queries_first, other_first, prev_first, low_block, high_block, next_first),
        scalars=2,
        scratch=[pltpu.VMEM((4 * rows, HEAD_DIM), BF16)] * 2,
        cost=(12 * rows * rows * width, 16 * rows * width),
    )
    fast_query = call(
        query_kernel,
        shape((rows, fast_width), BF16),
        (side_scalar, keep_first, seq_swap(send_first, 0), input_map[0]),
        scalars=1,
    )

    keys_prev, keys_next = seq_shift(keys_second, 1), seq_shift(keys_second, -1)
    values_prev, values_next = seq_shift(values_second, 1), seq_shift(values_second, -1)
    fast_query, keys_prev, keys_next = lax.optimization_barrier((fast_query, keys_prev, keys_next))

    own_rows = hidden_size >> len(orders[0])
    own_new, fast_out = call(
        functools.partial(renew_kernel, orders),
        [shape((3, own_rows, fast_width), BF16), shape((rows, fast_width), BF16)],
        (place, weights, fast_query, *gathered),
        scalars=1,
        scratch=[pltpu.VMEM(weights.shape, BF16)],
    )
    if not halving:
        share_rows = hidden_size // seq_count
        own_new = lax.dynamic_slice_in_dim(own_new, seq_place * share_rows, share_rows, 1)

    def mixed_for(low_bit):
        far = (head_place // 2) ^ 1
        near = head_place // 2
        places = jnp.stack([far * 2 + low_bit, near * 2 + low_bit]).reshape(1, 2)
        return call(
            mix_kernel,
            shape((2, rows, width), BF16),
            (places, fast_out, output_map),
            scalars=1,
        )

    my_bit = head_place % 2
    near_part = head_swap(mixed_for(1 - my_bit), 1)
    keep_part = mixed_for(my_bit)
    to_send = (keep_part[0].astype(F32) + near_part[0].astype(F32)).astype(BF16)
    far_part = head_swap(to_send, 2)

    normed_second = call(
        second_kernel,
        shape((rows, width), BF16),
        (edges, queries_second, keep_part, near_part, far_part,
         keys_prev, keys_second, keys_next, values_prev, values_second, values_next),
        scalars=1,
        cost=(12 * rows * rows * width, 16 * rows * width),
    )
    return (normed_second, jnp.transpose(own_new, (1, 0, 2))[None])


def solution(mesh):
    return jax.shard_map(
        local,
        mesh=mesh,
        in_specs=(
            P("seq", "head"),
            P("seq", "head"),
            P("seq", "head"),
            P("head", None, None),
            P("seq", "head"),
            P("seq", "head"),
            P("seq", "head"),
            P("head", None, None, None),
            P("head", None),
            P("seq", "head"),
            P("seq", "head"),
            P("seq", "head"),
        ),
        out_specs=(P("seq", "head"), P("head", "seq", None, None)),
        check_vma=False,
    )
```

```python
import functools
import math

import jax
import jax.numpy as jnp
from jax import lax
from jax.experimental import pallas as pl
from jax.experimental.pallas import tpu as pltpu
from jax.sharding import PartitionSpec as P

HALF_WIN = 512
HEAD_DIM = 128
HEADS_GRP = 2
FAST_DIM = 512
FAST_HIDDEN = 512
TILE = 128
VMEM_LIMIT = 24 * 1024 * 1024
VMEM_MOST = 60 * 1024 * 1024

BF16 = jnp.bfloat16
F32 = jnp.float32
INVERSE = 1.0 / math.sqrt(FAST_DIM)


def dot_nn(left, right):
    return lax.dot_general(left, right, (((1,), (0,)), ((), ())), preferred_element_type=F32)


def dot_nt(left, right):
    return lax.dot_general(left, right, (((1,), (1,)), ((), ())), preferred_element_type=F32)


def call(body, out_shapes, operands, scalars=0, anywhere=0, scratch=(), cost=None, limit=VMEM_LIMIT):
    vmem = pl.BlockSpec(memory_space=pltpu.VMEM)
    in_specs = (
        [pl.BlockSpec(memory_space=pltpu.SMEM)] * scalars
        + [vmem] * (len(operands) - scalars - anywhere)
        + [pl.BlockSpec(memory_space=pl.ANY)] * anywhere
    )
    flops, moved = cost or (1000, 1000)
    return pl.pallas_call(
        body,
        out_shape=out_shapes,
        in_specs=in_specs,
        out_specs=jax.tree.map(lambda _: vmem, out_shapes),
        scratch_shapes=scratch,
        compiler_params=pltpu.CompilerParams(vmem_limit_bytes=limit),
        cost_estimate=pl.CostEstimate(flops=flops, bytes_accessed=moved, transcendentals=0),
    )(*operands)


def slot_of(block, order):
    slot = 0
    for bit in order:
        slot = slot * 2 + ((block >> bit) & 1)
    return slot


def gradient_kernel(orders, place_ref, rates_ref, keys_ref, values_ref, weights_ref, *refs):
    out_refs, chunk_refs = refs[:-2], refs[-2:]
    place = place_ref[0, 0]
    rates = rates_ref[...]
    keys = keys_ref[...]
    values = values_ref[...]
    hidden_size, width = weights_ref.shape[1:]
    step = 128

    def put(chunk, low, columns, product):
        order = orders[chunk]
        block_rows = min(step, hidden_size >> len(order))
        for start in range(0, step, block_rows):
            row = low + start
            if order:
                slot = slot_of((row // block_rows) ^ place, order)
                row = pl.multiple_of(slot * block_rows, block_rows)
            chunk_refs[chunk][pl.ds(row, block_rows), columns] = product[start:start + block_rows]

    for low in range(0, hidden_size, step):
        rows = slice(low, low + step)
        gate = dot_nt(weights_ref[0, rows, :], keys) * INVERSE
        up = dot_nt(weights_ref[1, rows, :], keys) * INVERSE
        sigmoid = jax.nn.sigmoid(gate)
        silu = gate * sigmoid
        hidden = (rates * silu * up).astype(BF16)
        backward = rates * dot_nt(weights_ref[2, rows, :], values)
        d_gate = (
            backward * up * sigmoid * (1.0 + gate * (1.0 - sigmoid)) * INVERSE
        ).astype(BF16)
        d_up = (backward * silu * INVERSE).astype(BF16)
        up_part = dot_nn(d_up, keys).astype(BF16)
        put(0, low, slice(0, width), dot_nn(d_gate, keys).astype(BF16))
        put(0, low, slice(width, width + width // 2), up_part[:, :width // 2])
        put(1, low, slice(0, width), dot_nn(hidden, values).astype(BF16))
        put(1, low, slice(width, width + width // 2), up_part[:, width // 2:])
    halves = len(out_refs) // 2
    half_rows = hidden_size // halves
    for index, out_ref in enumerate(out_refs):
        half = index % halves
        out_ref[...] = chunk_refs[index // halves][half * half_rows:(half + 1) * half_rows, :]


def attend_rows(edge_prev, edge_next, query_tile, keys_prev, keys_own, keys_next,
                values_prev, values_own, values_next):
    scale = 1.0 / math.sqrt(HEAD_DIM)
    row = lax.broadcasted_iota(jnp.int32, (TILE, TILE), 0)
    col = lax.broadcasted_iota(jnp.int32, (TILE, TILE), 1)
    minus = jnp.float32(-jnp.inf)
    score_prev = dot_nt(query_tile, keys_prev)
    score_own = dot_nt(query_tile, keys_own)
    score_next = dot_nt(query_tile, keys_next)
    parts = [score_prev[:, :TILE] + jnp.where(col >= row, edge_prev, minus)]
    if score_prev.shape[1] > TILE:
        parts.append(score_prev[:, TILE:] + edge_prev)
    parts.append(score_own)
    if score_next.shape[1] > TILE:
        parts.append(score_next[:, :-TILE] + edge_next)
    parts.append(score_next[:, -TILE:] + jnp.where(col <= row, edge_next, minus))
    scores = jnp.concatenate(parts, axis=1)
    highest = jnp.max(scores, axis=1, keepdims=True)
    weights = jnp.exp((scores - highest) * scale)
    total = jnp.sum(weights, axis=1, keepdims=True)
    weights = weights.astype(BF16)
    width_prev, width_own = score_prev.shape[1], score_own.shape[1]
    attended = (
        dot_nn(weights[:, :width_prev], values_prev)
        + dot_nn(weights[:, width_prev:width_prev + width_own], values_own)
        + dot_nn(weights[:, width_prev + width_own:], values_next)
    )
    return attended / total


def pack_kernel(side_ref, queries_ref, keys_ref, values_ref, out_ref):
    count = queries_ref.shape[0]
    start = pl.multiple_of((1 - side_ref[0, 0]) * HEAD_DIM, HEAD_DIM)
    for index, ref in enumerate((queries_ref, keys_ref, values_ref)):
        out_ref[index * count:(index + 1) * count, :] = ref[:, pl.ds(start, HEAD_DIM)]


def border_kernel(side_ref, keys_ref, values_ref, other_ref, low_ref, high_ref):
    count = keys_ref.shape[0]
    side = side_ref[0, 0]
    start = pl.multiple_of(side * HEAD_DIM, HEAD_DIM)

    def fill(own_ref, other_out_ref):
        own_ref[:count, :] = keys_ref[:, pl.ds(start, HEAD_DIM)]
        own_ref[count:, :] = values_ref[:, pl.ds(start, HEAD_DIM)]
        other_out_ref[...] = other_ref[count:, :]

    @pl.when(side == 0)
    def _():
        fill(low_ref, high_ref)

    @pl.when(side != 0)
    def _():
        fill(high_ref, low_ref)


def first_kernel(edge_ref, side_ref, queries_ref, other_ref, prev_ref, low_ref, high_ref, next_ref,
                 keep_ref, send_ref, keys_ref, values_ref):
    count = queries_ref.shape[0]
    side = side_ref[0, 0]
    for index, ref in enumerate((prev_ref, low_ref, high_ref, next_ref)):
        rows = slice(index * count, (index + 1) * count)
        keys_ref[rows, :] = ref[:count, :]
        values_ref[rows, :] = ref[count:, :]
    start = pl.multiple_of(side * HEAD_DIM, HEAD_DIM)
    for turn, out_ref in enumerate((keep_ref, send_ref)):
        base = (side if turn == 0 else 1 - side) * count

        def span(ref, low, length):
            return ref[pl.ds(pl.multiple_of(base + low, TILE), length), :]

        for index in range(count // TILE):
            low, high = index * TILE, (index + 1) * TILE
            query = queries_ref[low:high, pl.ds(start, HEAD_DIM)] if turn == 0 else other_ref[low:high, :]
            out_ref[low:high, :] = attend_rows(
                edge_ref[turn, 0], edge_ref[turn, 1], query,
                span(keys_ref, low, count - low), span(keys_ref, count, count),
                span(keys_ref, 2 * count, high),
                span(values_ref, low, count - low), span(values_ref, count, count),
                span(values_ref, 2 * count, high),
            ).astype(BF16)


def query_kernel(side_ref, keep_ref, other_ref, map_ref, out_ref):
    side = side_ref[0, 0]
    own = keep_ref[...].astype(F32)
    other = other_ref[...].astype(F32)
    square = jnp.sum(own * own + other * other, axis=1, keepdims=True)
    norm = lax.rsqrt(square / (HEADS_GRP * HEAD_DIM) + 1e-05)
    own_map = map_ref[pl.ds(pl.multiple_of(side * HEAD_DIM, HEAD_DIM), HEAD_DIM), :]
    other_map = map_ref[pl.ds(pl.multiple_of((1 - side) * HEAD_DIM, HEAD_DIM), HEAD_DIM), :]
    out_ref[...] = (
        dot_nn((own * norm).astype(BF16), own_map) + dot_nn((other * norm).astype(BF16), other_map)
    ).astype(BF16)


def second_kernel(edge_ref, queries_ref, keep_ref, near_ref, far_ref, keys_prev_ref, keys_ref, keys_next_ref,
                  values_prev_ref, values_ref, values_next_ref, out_ref):
    count = keys_ref.shape[0]
    for index in range(count // TILE):
        low, high = index * TILE, (index + 1) * TILE
        rows = slice(low, high)
        mixed = (
            keep_ref[1, rows, :].astype(F32)
            + near_ref[1, rows, :].astype(F32)
            + far_ref[rows, :].astype(F32)
        )
        query = (queries_ref[rows, :].astype(F32) + mixed).astype(BF16)
        heads = []
        for head in range(HEADS_GRP):
            cols = slice(head * HEAD_DIM, (head + 1) * HEAD_DIM)
            heads.append(
                attend_rows(
                    edge_ref[0, 0], edge_ref[0, 1], query[:, cols],
                    keys_prev_ref[low:, cols], keys_ref[:, cols], keys_next_ref[:high, cols],
                    values_prev_ref[low:, cols], values_ref[:, cols], values_next_ref[:high, cols],
                )
            )
        both = jnp.concatenate(heads, axis=1)
        mean = jnp.mean(both * both, axis=1, keepdims=True)
        out_ref[rows, :] = (both * lax.rsqrt(mean + 1e-05)).astype(BF16)


def renew_kernel(orders, place_ref, weights_ref, query_ref, *refs):
    pieces, (own_ref, fast_ref, new_ref) = refs[:-3], refs[-3:]
    place = place_ref[0, 0]
    hidden_size, width = weights_ref.shape[1:]
    limit_norm = math.sqrt(FAST_HIDDEN * FAST_DIM) / 2.0
    step = 64
    square = jnp.zeros((1, pieces[0].shape[1]), F32)
    for piece in pieces:
        for low in range(0, piece.shape[0], step):
            part = piece[low:low + step, :].astype(F32)
            square = square + jnp.sum(part * part, axis=0, keepdims=True)
    square = jnp.sum(square, axis=1, keepdims=True)
    factor = jnp.minimum(1.0, limit_norm * lax.rsqrt(square + 1e-06))
    per_chunk = len(pieces) // 2
    piece_rows = pieces[0].shape[0]
    blocks = 1 << len(orders[0])
    block_rows = hidden_size // blocks
    count = min(step, block_rows)
    for block in range(blocks):
        starts = [slot_of(block, order) * block_rows for order in orders]
        for low in range(0, block_rows, count):
            found = []
            for chunk, start in enumerate(starts):
                piece = pieces[chunk * per_chunk + start // piece_rows]
                inside = start % piece_rows + low
                found.append(piece[inside:inside + count, :].astype(F32))
            parts = [
                found[0][:, :width],
                jnp.concatenate([found[0][:, width:], found[1][:, width:]], axis=1),
                found[1][:, :width],
            ]
            rows = slice(low, low + count)
            if blocks > 1:
                rows = pl.ds(pl.multiple_of((block ^ place) * block_rows + low, count), count)
            for matrix, part in enumerate(parts):
                old = weights_ref[matrix, rows, :].astype(F32)
                stepped = old + factor * part
                norm = jnp.sqrt(jnp.sum(old * old, axis=1, keepdims=True))
                size = jnp.sum(stepped * stepped, axis=1, keepdims=True)
                fresh = (stepped * norm * lax.rsqrt(size + 1e-06)).astype(BF16)
                new_ref[matrix, rows, :] = fresh
                if block == 0:
                    own_ref[matrix, low:low + count, :] = fresh
    step = 128
    for low in range(0, query_ref.shape[0], step):
        rows = slice(low, low + step)
        query = query_ref[rows, :]
        gate = dot_nt(query, new_ref[0]) * INVERSE
        up = dot_nt(query, new_ref[1]) * INVERSE
        hidden = (jax.nn.silu(gate) * up).astype(BF16)
        raw = dot_nn(hidden, new_ref[2])
        mean = jnp.mean(raw * raw, axis=1, keepdims=True)
        fast_ref[rows, :] = (raw * lax.rsqrt(mean + 1e-05)).astype(BF16)


def mix_kernel(place_ref, fast_ref, map_ref, out_ref):
    width = out_ref.shape[2]
    for slot in range(2):
        start = pl.multiple_of(place_ref[0, slot] * width, width)
        columns = map_ref[:, pl.ds(start, width)]
        out_ref[slot] = dot_nn(fast_ref[...], columns).astype(BF16)


def seq_shift(value, step):
    peers = lax.axis_size("seq")
    return lax.ppermute(
        value, "seq", [(i, i + step) for i in range(peers) if 0 <= i + step < peers]
    )


def head_swap(value, bit):
    return lax.ppermute(value, "head", [(i, i ^ bit) for i in range(lax.axis_size("head"))])


def seq_swap(value, bit):
    step = 1 << bit
    return lax.ppermute(value, "seq", [(i, i ^ step) for i in range(lax.axis_size("seq"))])


def after(value, others):
    return lax.optimization_barrier((value, others))[0]


def sum_over_seq(chunks, orders, waits):
    turns = len(orders[0])

    def swapped(values, stage, turn):
        values = list(values)
        if stage in waits:
            values[0] = after(values[0], waits[stage])
        return [seq_swap(value, order[turn]) for value, order in zip(values, orders)]

    keeps = [keep for keep, _ in chunks]
    sends = [send for _, send in chunks]
    for turn in range(turns):
        found = swapped(sends, turn, turn)
        sends, rest = [], []
        for keep, new in zip(keeps, found):
            if turn == turns - 1:
                rest.append((keep.astype(F32) + new.astype(F32)).astype(BF16))
                continue
            half = keep.shape[0] // 2
            sends.append((keep[half:].astype(F32) + new[half:].astype(F32)).astype(BF16))
            rest.append(lax.optimization_barrier(keep[:half].astype(F32) + new[:half].astype(F32)))
        keeps = rest
    held = [(keep,) for keep in keeps]
    for turn in reversed(range(turns)):
        whole = [jnp.concatenate(parts) if len(parts) > 1 else parts[0] for parts in held]
        found = swapped(whole, 2 * turns - 1 - turn, turn)
        held = list(zip(whole, found))
    return [part for parts in held for part in parts]


def local(
    queries_first,
    keys_first,
    values_first,
    input_map,
    fast_keys,
    fast_values,
    step_rates,
    fast_weights,
    output_map,
    queries_second,
    keys_second,
    values_second,
):
    rows, width = queries_first.shape
    seq_count = lax.axis_size("seq")
    seq_place = lax.axis_index("seq")
    head_place = lax.axis_index("head")
    weights = jnp.transpose(fast_weights[0], (1, 0, 2))
    hidden_size, fast_width = weights.shape[1:]
    shape = jax.ShapeDtypeStruct
    minus = jnp.float32(-jnp.inf)
    side = seq_place % 2

    def edges_of(block):
        return [jnp.where(block > 0, 0.0, minus), jnp.where(block < seq_count - 1, 0.0, minus)]

    edges = jnp.stack(edges_of(seq_place) + edges_of(seq_place ^ 1)).reshape(2, 2)
    side_scalar = side.astype(jnp.int32).reshape(1, 1)
    place = seq_place.astype(jnp.int32).reshape(1, 1)

    packed = call(
        pack_kernel,
        shape((3 * rows, HEAD_DIM), BF16),
        (side_scalar, queries_first, keys_first, values_first),
        scalars=1,
    )
    other_first = seq_swap(packed, 0)

    bits = tuple(range(seq_count.bit_length() - 1))
    halving = seq_count == 1 << len(bits) and len(bits) > 1 and hidden_size >> len(bits) >= 16
    orders = (bits, bits[1:] + bits[:1]) if halving else ((), ())
    halves = 2 if halving else 1
    chunk_width = fast_width + fast_width // 2
    gradients = call(
        functools.partial(gradient_kernel, orders),
        [shape((hidden_size // halves, chunk_width), BF16)] * (2 * halves),
        (place, step_rates.reshape(1, rows), fast_keys, fast_values, weights),
        scalars=1,
        scratch=[pltpu.VMEM((hidden_size, chunk_width), BF16)] * 2,
        limit=VMEM_MOST,
    )
    low_block, high_block = call(
        border_kernel,
        [shape((2 * rows, HEAD_DIM), BF16)] * 2,
        (side_scalar, keys_first, values_first, other_first),
        scalars=1,
    )
    prev_first = seq_shift(high_block, 2)
    next_first = seq_shift(low_block, -2)
    keep_first, send_first = call(
        first_kernel,
        [shape((rows, HEAD_DIM), BF16)] * 2,
        (edges, side_scalar, queries_first, other_first, prev_first, low_block, high_block, next_first),
        scalars=2,
        scratch=[pltpu.VMEM((4 * rows, HEAD_DIM), BF16)] * 2,
        cost=(12 * rows * rows * width, 16 * rows * width),
    )
    fast_query = call(
        query_kernel,
        shape((rows, fast_width), BF16),
        (side_scalar, keep_first, seq_swap(send_first, 0), input_map[0]),
        scalars=1,
    )

    keys_prev, keys_next = seq_shift(keys_second, 1), seq_shift(keys_second, -1)
    values_prev, values_next = seq_shift(values_second, 1), seq_shift(values_second, -1)
    if halving:
        stages = 2 * len(bits)
        waits = {
            len(bits) - 1: (low_block, high_block),
            stages - 2: (prev_first, next_first),
            stages - 1: (keep_first, send_first, keys_prev, keys_next),
        }
        gathered = sum_over_seq([gradients[:2], gradients[2:]], orders, waits)
    else:
        gathered = lax.psum(gradients, "seq")

    own_rows = hidden_size >> len(orders[0])
    own_new, fast_out = call(
        functools.partial(renew_kernel, orders),
        [shape((3, own_rows, fast_width), BF16), shape((rows, fast_width), BF16)],
        (place, weights, fast_query, *gathered),
        scalars=1,
        scratch=[pltpu.VMEM(weights.shape, BF16)],
    )
    if not halving:
        share_rows = hidden_size // seq_count
        own_new = lax.dynamic_slice_in_dim(own_new, seq_place * share_rows, share_rows, 1)

    fast_out = after(fast_out, (values_prev, values_next))

    def mixed_for(low_bit):
        far = (head_place // 2) ^ 1
        near = head_place // 2
        places = jnp.stack([far * 2 + low_bit, near * 2 + low_bit]).reshape(1, 2)
        return call(
            mix_kernel,
            shape((2, rows, width), BF16),
            (places, fast_out, output_map),
            scalars=1,
        )

    my_bit = head_place % 2
    near_part = head_swap(mixed_for(1 - my_bit), 1)
    keep_part = mixed_for(my_bit)
    to_send = (keep_part[0].astype(F32) + near_part[0].astype(F32)).astype(BF16)
    far_part = head_swap(to_send, 2)

    normed_second = call(
        second_kernel,
        shape((rows, width), BF16),
        (edges, queries_second, keep_part, near_part, far_part,
         keys_prev, keys_second, keys_next, values_prev, values_second, values_next),
        scalars=1,
        cost=(12 * rows * rows * width, 16 * rows * width),
    )
    return (normed_second, jnp.transpose(own_new, (1, 0, 2))[None])


def solution(mesh):
    return jax.shard_map(
        local,
        mesh=mesh,
        in_specs=(
            P("seq", "head"),
            P("seq", "head"),
            P("seq", "head"),
            P("head", None, None),
            P("seq", "head"),
            P("seq", "head"),
            P("seq", "head"),
            P("head", None, None, None),
            P("head", None),
            P("seq", "head"),
            P("seq", "head"),
            P("seq", "head"),
        ),
        out_specs=(P("seq", "head"), P("head", "seq", None, None)),
        check_vma=False,
    )
```

```python
import functools
import math

import jax
import jax.numpy as jnp
from jax import lax
from jax.experimental import pallas as pl
from jax.experimental.pallas import tpu as pltpu
from jax.sharding import PartitionSpec as P

HALF_WIN = 512
HEAD_DIM = 128
HEADS_GRP = 2
FAST_DIM = 512
FAST_HIDDEN = 512
TILE = 128
VMEM_LIMIT = 24 * 1024 * 1024
VMEM_MOST = 60 * 1024 * 1024

BF16 = jnp.bfloat16
F32 = jnp.float32
INVERSE = 1.0 / math.sqrt(FAST_DIM)


def dot_nn(left, right):
    return lax.dot_general(left, right, (((1,), (0,)), ((), ())), preferred_element_type=F32)


def dot_nt(left, right):
    return lax.dot_general(left, right, (((1,), (1,)), ((), ())), preferred_element_type=F32)


def call(body, out_shapes, operands, scalars=0, anywhere=0, scratch=(), cost=None, limit=VMEM_LIMIT):
    vmem = pl.BlockSpec(memory_space=pltpu.VMEM)
    in_specs = (
        [pl.BlockSpec(memory_space=pltpu.SMEM)] * scalars
        + [vmem] * (len(operands) - scalars - anywhere)
        + [pl.BlockSpec(memory_space=pl.ANY)] * anywhere
    )
    flops, moved = cost or (1000, 1000)
    return pl.pallas_call(
        body,
        out_shape=out_shapes,
        in_specs=in_specs,
        out_specs=jax.tree.map(lambda _: vmem, out_shapes),
        scratch_shapes=scratch,
        compiler_params=pltpu.CompilerParams(vmem_limit_bytes=limit),
        cost_estimate=pl.CostEstimate(flops=flops, bytes_accessed=moved, transcendentals=0),
    )(*operands)


def slot_of(block, order):
    slot = 0
    for bit in order:
        slot = slot * 2 + ((block >> bit) & 1)
    return slot


def gradient_kernel(orders, place_ref, rates_ref, keys_ref, values_ref, weights_ref, *refs):
    out_refs, chunk_refs = refs[:-2], refs[-2:]
    place = place_ref[0, 0]
    rates = rates_ref[...]
    keys = keys_ref[...]
    values = values_ref[...]
    hidden_size, width = weights_ref.shape[1:]
    step = 128

    def put(chunk, low, columns, product):
        order = orders[chunk]
        block_rows = min(step, hidden_size >> len(order))
        for start in range(0, step, block_rows):
            row = low + start
            if order:
                slot = slot_of((row // block_rows) ^ place, order)
                row = pl.multiple_of(slot * block_rows, block_rows)
            chunk_refs[chunk][pl.ds(row, block_rows), columns] = product[start:start + block_rows]

    for low in range(0, hidden_size, step):
        rows = slice(low, low + step)
        gate = dot_nt(weights_ref[0, rows, :], keys) * INVERSE
        up = dot_nt(weights_ref[1, rows, :], keys) * INVERSE
        sigmoid = jax.nn.sigmoid(gate)
        silu = gate * sigmoid
        hidden = (rates * silu * up).astype(BF16)
        backward = rates * dot_nt(weights_ref[2, rows, :], values)
        d_gate = (
            backward * up * sigmoid * (1.0 + gate * (1.0 - sigmoid)) * INVERSE
        ).astype(BF16)
        d_up = (backward * silu * INVERSE).astype(BF16)
        up_part = dot_nn(d_up, keys).astype(BF16)
        put(0, low, slice(0, width), dot_nn(d_gate, keys).astype(BF16))
        put(0, low, slice(width, width + width // 2), up_part[:, :width // 2])
        put(1, low, slice(0, width), dot_nn(hidden, values).astype(BF16))
        put(1, low, slice(width, width + width // 2), up_part[:, width // 2:])
    halves = len(out_refs) // 2
    half_rows = hidden_size // halves
    for index, out_ref in enumerate(out_refs):
        half = index % halves
        out_ref[...] = chunk_refs[index // halves][half * half_rows:(half + 1) * half_rows, :]


def attend_rows(edge_prev, edge_next, query_tile, keys_prev, keys_own, keys_next,
                values_prev, values_own, values_next):
    scale = 1.0 / math.sqrt(HEAD_DIM)
    row = lax.broadcasted_iota(jnp.int32, (TILE, TILE), 0)
    col = lax.broadcasted_iota(jnp.int32, (TILE, TILE), 1)
    minus = jnp.float32(-jnp.inf)
    score_prev = dot_nt(query_tile, keys_prev)
    score_own = dot_nt(query_tile, keys_own)
    score_next = dot_nt(query_tile, keys_next)
    parts = [score_prev[:, :TILE] + jnp.where(col >= row, edge_prev, minus)]
    if score_prev.shape[1] > TILE:
        parts.append(score_prev[:, TILE:] + edge_prev)
    parts.append(score_own)
    if score_next.shape[1] > TILE:
        parts.append(score_next[:, :-TILE] + edge_next)
    parts.append(score_next[:, -TILE:] + jnp.where(col <= row, edge_next, minus))
    scores = jnp.concatenate(parts, axis=1)
    highest = jnp.max(scores, axis=1, keepdims=True)
    weights = jnp.exp((scores - highest) * scale)
    total = jnp.sum(weights, axis=1, keepdims=True)
    weights = weights.astype(BF16)
    width_prev, width_own = score_prev.shape[1], score_own.shape[1]
    attended = (
        dot_nn(weights[:, :width_prev], values_prev)
        + dot_nn(weights[:, width_prev:width_prev + width_own], values_own)
        + dot_nn(weights[:, width_prev + width_own:], values_next)
    )
    return attended / total


def pack_kernel(side_ref, queries_ref, keys_ref, values_ref, out_ref):
    count = queries_ref.shape[0]
    start = pl.multiple_of((1 - side_ref[0, 0]) * HEAD_DIM, HEAD_DIM)
    for index, ref in enumerate((queries_ref, keys_ref, values_ref)):
        out_ref[index * count:(index + 1) * count, :] = ref[:, pl.ds(start, HEAD_DIM)]


def border_kernel(side_ref, keys_ref, values_ref, other_ref, low_ref, high_ref):
    count = keys_ref.shape[0]
    side = side_ref[0, 0]
    start = pl.multiple_of(side * HEAD_DIM, HEAD_DIM)

    def fill(own_ref, other_out_ref):
        own_ref[:count, :] = keys_ref[:, pl.ds(start, HEAD_DIM)]
        own_ref[count:, :] = values_ref[:, pl.ds(start, HEAD_DIM)]
        other_out_ref[...] = other_ref[count:, :]

    @pl.when(side == 0)
    def _():
        fill(low_ref, high_ref)

    @pl.when(side != 0)
    def _():
        fill(high_ref, low_ref)


def first_kernel(edge_ref, side_ref, queries_ref, other_ref, prev_ref, low_ref, high_ref, next_ref,
                 keep_ref, send_ref, keys_ref, values_ref):
    count = queries_ref.shape[0]
    side = side_ref[0, 0]
    for index, ref in enumerate((prev_ref, low_ref, high_ref, next_ref)):
        rows = slice(index * count, (index + 1) * count)
        keys_ref[rows, :] = ref[:count, :]
        values_ref[rows, :] = ref[count:, :]
    start = pl.multiple_of(side * HEAD_DIM, HEAD_DIM)
    for turn, out_ref in enumerate((keep_ref, send_ref)):
        base = (side if turn == 0 else 1 - side) * count

        def span(ref, low, length):
            return ref[pl.ds(pl.multiple_of(base + low, TILE), length), :]

        for index in range(count // TILE):
            low, high = index * TILE, (index + 1) * TILE
            query = queries_ref[low:high, pl.ds(start, HEAD_DIM)] if turn == 0 else other_ref[low:high, :]
            out_ref[low:high, :] = attend_rows(
                edge_ref[turn, 0], edge_ref[turn, 1], query,
                span(keys_ref, low, count - low), span(keys_ref, count, count),
                span(keys_ref, 2 * count, high),
                span(values_ref, low, count - low), span(values_ref, count, count),
                span(values_ref, 2 * count, high),
            ).astype(BF16)


def query_kernel(side_ref, keep_ref, other_ref, map_ref, out_ref):
    side = side_ref[0, 0]
    own = keep_ref[...].astype(F32)
    other = other_ref[...].astype(F32)
    square = jnp.sum(own * own + other * other, axis=1, keepdims=True)
    norm = lax.rsqrt(square / (HEADS_GRP * HEAD_DIM) + 1e-05)
    own_map = map_ref[pl.ds(pl.multiple_of(side * HEAD_DIM, HEAD_DIM), HEAD_DIM), :]
    other_map = map_ref[pl.ds(pl.multiple_of((1 - side) * HEAD_DIM, HEAD_DIM), HEAD_DIM), :]
    out_ref[...] = (
        dot_nn((own * norm).astype(BF16), own_map) + dot_nn((other * norm).astype(BF16), other_map)
    ).astype(BF16)


def second_kernel(edge_ref, queries_ref, keep_ref, near_ref, far_ref, prev_ref, keys_ref, values_ref, next_ref,
                  out_ref):
    count = keys_ref.shape[0]
    for index in range(count // TILE):
        low, high = index * TILE, (index + 1) * TILE
        rows = slice(low, high)
        mixed = (
            keep_ref[1, rows, :].astype(F32)
            + near_ref[1, rows, :].astype(F32)
            + far_ref[rows, :].astype(F32)
        )
        query = (queries_ref[rows, :].astype(F32) + mixed).astype(BF16)
        heads = []
        for head in range(HEADS_GRP):
            cols = slice(head * HEAD_DIM, (head + 1) * HEAD_DIM)
            heads.append(
                attend_rows(
                    edge_ref[0, 0], edge_ref[0, 1], query[:, cols],
                    prev_ref[low:count, cols], keys_ref[:, cols], next_ref[:high, cols],
                    prev_ref[count + low:, cols], values_ref[:, cols], next_ref[count:count + high, cols],
                )
            )
        both = jnp.concatenate(heads, axis=1)
        mean = jnp.mean(both * both, axis=1, keepdims=True)
        out_ref[rows, :] = (both * lax.rsqrt(mean + 1e-05)).astype(BF16)


def renew_kernel(orders, place_ref, weights_ref, query_ref, *refs):
    pieces, (own_ref, fast_ref, new_ref) = refs[:-3], refs[-3:]
    place = place_ref[0, 0]
    hidden_size, width = weights_ref.shape[1:]
    limit_norm = math.sqrt(FAST_HIDDEN * FAST_DIM) / 2.0
    step = 64
    square = jnp.zeros((1, pieces[0].shape[1]), F32)
    for piece in pieces:
        for low in range(0, piece.shape[0], step):
            part = piece[low:low + step, :].astype(F32)
            square = square + jnp.sum(part * part, axis=0, keepdims=True)
    square = jnp.sum(square, axis=1, keepdims=True)
    factor = jnp.minimum(1.0, limit_norm * lax.rsqrt(square + 1e-06))
    per_chunk = len(pieces) // 2
    piece_rows = pieces[0].shape[0]
    blocks = 1 << len(orders[0])
    block_rows = hidden_size // blocks
    count = min(step, block_rows)
    for block in range(blocks):
        starts = [slot_of(block, order) * block_rows for order in orders]
        for low in range(0, block_rows, count):
            found = []
            for chunk, start in enumerate(starts):
                piece = pieces[chunk * per_chunk + start // piece_rows]
                inside = start % piece_rows + low
                found.append(piece[inside:inside + count, :].astype(F32))
            parts = [
                found[0][:, :width],
                jnp.concatenate([found[0][:, width:], found[1][:, width:]], axis=1),
                found[1][:, :width],
            ]
            rows = slice(low, low + count)
            if blocks > 1:
                rows = pl.ds(pl.multiple_of((block ^ place) * block_rows + low, count), count)
            for matrix, part in enumerate(parts):
                old = weights_ref[matrix, rows, :].astype(F32)
                stepped = old + factor * part
                norm = jnp.sqrt(jnp.sum(old * old, axis=1, keepdims=True))
                size = jnp.sum(stepped * stepped, axis=1, keepdims=True)
                fresh = (stepped * norm * lax.rsqrt(size + 1e-06)).astype(BF16)
                new_ref[matrix, rows, :] = fresh
                if block == 0:
                    own_ref[matrix, low:low + count, :] = fresh
    step = 128
    for low in range(0, query_ref.shape[0], step):
        rows = slice(low, low + step)
        query = query_ref[rows, :]
        gate = dot_nt(query, new_ref[0]) * INVERSE
        up = dot_nt(query, new_ref[1]) * INVERSE
        hidden = (jax.nn.silu(gate) * up).astype(BF16)
        raw = dot_nn(hidden, new_ref[2])
        mean = jnp.mean(raw * raw, axis=1, keepdims=True)
        fast_ref[rows, :] = (raw * lax.rsqrt(mean + 1e-05)).astype(BF16)


def mix_kernel(place_ref, fast_ref, map_ref, out_ref):
    width = out_ref.shape[2]
    for slot in range(2):
        start = pl.multiple_of(place_ref[0, slot] * width, width)
        columns = map_ref[:, pl.ds(start, width)]
        out_ref[slot] = dot_nn(fast_ref[...], columns).astype(BF16)


def seq_shift(value, step):
    peers = lax.axis_size("seq")
    return lax.ppermute(
        value, "seq", [(i, i + step) for i in range(peers) if 0 <= i + step < peers]
    )


def head_swap(value, bit):
    return lax.ppermute(value, "head", [(i, i ^ bit) for i in range(lax.axis_size("head"))])


def seq_swap(value, bit):
    step = 1 << bit
    return lax.ppermute(value, "seq", [(i, i ^ step) for i in range(lax.axis_size("seq"))])


def after(value, others):
    return lax.optimization_barrier((value, others))[0]


def sum_started(chunks, orders):
    return [keep for keep, _ in chunks], [
        seq_swap(send, order[0]) for (_, send), order in zip(chunks, orders)
    ]


def sum_over_seq(keeps, found, orders, waits):
    turns = len(orders[0])

    def swapped(values, stage, turn):
        values = list(values)
        if stage in waits:
            values[0] = after(values[0], waits[stage])
        return [seq_swap(value, order[turn]) for value, order in zip(values, orders)]

    for turn in range(1, turns):
        sends, rest = [], []
        for keep, new in zip(keeps, found):
            half = keep.shape[0] // 2
            sends.append((keep[half:].astype(F32) + new[half:].astype(F32)).astype(BF16))
            rest.append(lax.optimization_barrier(keep[:half].astype(F32) + new[:half].astype(F32)))
        keeps = rest
        found = swapped(sends, turn, turn)
    held = [((keep.astype(F32) + new.astype(F32)).astype(BF16),) for keep, new in zip(keeps, found)]
    for turn in reversed(range(turns)):
        whole = [jnp.concatenate(parts) if len(parts) > 1 else parts[0] for parts in held]
        found = swapped(whole, 2 * turns - 1 - turn, turn)
        held = list(zip(whole, found))
    return [part for parts in held for part in parts]


def local(
    queries_first,
    keys_first,
    values_first,
    input_map,
    fast_keys,
    fast_values,
    step_rates,
    fast_weights,
    output_map,
    queries_second,
    keys_second,
    values_second,
):
    rows, width = queries_first.shape
    seq_count = lax.axis_size("seq")
    seq_place = lax.axis_index("seq")
    head_place = lax.axis_index("head")
    weights = jnp.transpose(fast_weights[0], (1, 0, 2))
    hidden_size, fast_width = weights.shape[1:]
    shape = jax.ShapeDtypeStruct
    minus = jnp.float32(-jnp.inf)
    side = seq_place % 2

    def edges_of(block):
        return [jnp.where(block > 0, 0.0, minus), jnp.where(block < seq_count - 1, 0.0, minus)]

    edges = jnp.stack(edges_of(seq_place) + edges_of(seq_place ^ 1)).reshape(2, 2)
    side_scalar = side.astype(jnp.int32).reshape(1, 1)
    place = seq_place.astype(jnp.int32).reshape(1, 1)

    packed = call(
        pack_kernel,
        shape((3 * rows, HEAD_DIM), BF16),
        (side_scalar, queries_first, keys_first, values_first),
        scalars=1,
    )
    other_first = seq_swap(packed, 0)

    bits = tuple(range(seq_count.bit_length() - 1))
    halving = seq_count == 1 << len(bits) and len(bits) > 1 and hidden_size >> len(bits) >= 16
    orders = (bits, bits[1:] + bits[:1]) if halving else ((), ())
    halves = 2 if halving else 1
    chunk_width = fast_width + fast_width // 2
    gradients = call(
        functools.partial(gradient_kernel, orders),
        [shape((hidden_size // halves, chunk_width), BF16)] * (2 * halves),
        (place, step_rates.reshape(1, rows), fast_keys, fast_values, weights),
        scalars=1,
        scratch=[pltpu.VMEM((hidden_size, chunk_width), BF16)] * 2,
        limit=VMEM_MOST,
    )
    low_block, high_block = call(
        border_kernel,
        [shape((2 * rows, HEAD_DIM), BF16)] * 2,
        (side_scalar, keys_first, values_first, other_first),
        scalars=1,
    )
    prev_first = seq_shift(high_block, 2)
    next_first = seq_shift(low_block, -2)
    keep_first, send_first = call(
        first_kernel,
        [shape((rows, HEAD_DIM), BF16)] * 2,
        (edges, side_scalar, queries_first, other_first, prev_first, low_block, high_block, next_first),
        scalars=2,
        scratch=[pltpu.VMEM((4 * rows, HEAD_DIM), BF16)] * 2,
        cost=(12 * rows * rows * width, 16 * rows * width),
    )
    fast_query = call(
        query_kernel,
        shape((rows, fast_width), BF16),
        (side_scalar, keep_first, seq_swap(send_first, 0), input_map[0]),
        scalars=1,
    )

    both_second = jnp.concatenate([keys_second, values_second])
    if halving:
        stages = 2 * len(bits)
        started = sum_started([gradients[:2], gradients[2:]], orders)
        both_second = after(both_second, started[1])
        prev_second, next_second = seq_shift(both_second, 1), seq_shift(both_second, -1)
        waits = {
            stages - 2: (prev_first, next_first, prev_second),
            stages - 1: (keep_first, send_first, next_second),
        }
        gathered = sum_over_seq(*started, orders, waits)
    else:
        prev_second, next_second = seq_shift(both_second, 1), seq_shift(both_second, -1)
        gathered = lax.psum(gradients, "seq")

    own_rows = hidden_size >> len(orders[0])
    own_new, fast_out = call(
        functools.partial(renew_kernel, orders),
        [shape((3, own_rows, fast_width), BF16), shape((rows, fast_width), BF16)],
        (place, weights, fast_query, *gathered),
        scalars=1,
        scratch=[pltpu.VMEM(weights.shape, BF16)],
    )
    if not halving:
        share_rows = hidden_size // seq_count
        own_new = lax.dynamic_slice_in_dim(own_new, seq_place * share_rows, share_rows, 1)

    def mixed_for(low_bit):
        far = (head_place // 2) ^ 1
        near = head_place // 2
        places = jnp.stack([far * 2 + low_bit, near * 2 + low_bit]).reshape(1, 2)
        return call(
            mix_kernel,
            shape((2, rows, width), BF16),
            (places, fast_out, output_map),
            scalars=1,
        )

    my_bit = head_place % 2
    near_part = head_swap(mixed_for(1 - my_bit), 1)
    keep_part = mixed_for(my_bit)
    to_send = (keep_part[0].astype(F32) + near_part[0].astype(F32)).astype(BF16)
    far_part = head_swap(to_send, 2)

    normed_second = call(
        second_kernel,
        shape((rows, width), BF16),
        (edges, queries_second, keep_part, near_part, far_part,
         prev_second, keys_second, values_second, next_second),
        scalars=1,
        cost=(12 * rows * rows * width, 16 * rows * width),
    )
    return (normed_second, jnp.transpose(own_new, (1, 0, 2))[None])


def solution(mesh):
    return jax.shard_map(
        local,
        mesh=mesh,
        in_specs=(
            P("seq", "head"),
            P("seq", "head"),
            P("seq", "head"),
            P("head", None, None),
            P("seq", "head"),
            P("seq", "head"),
            P("seq", "head"),
            P("head", None, None, None),
            P("head", None),
            P("seq", "head"),
            P("seq", "head"),
            P("seq", "head"),
        ),
        out_specs=(P("seq", "head"), P("head", "seq", None, None)),
        check_vma=False,
    )
```

```python
import functools
import math

import jax
import jax.numpy as jnp
from jax import lax
from jax.experimental import pallas as pl
from jax.experimental.pallas import tpu as pltpu
from jax.sharding import PartitionSpec as P

HALF_WIN = 512
HEAD_DIM = 128
HEADS_GRP = 2
FAST_DIM = 512
FAST_HIDDEN = 512
TILE = 128
VMEM_LIMIT = 24 * 1024 * 1024
VMEM_MOST = 60 * 1024 * 1024

BF16 = jnp.bfloat16
F32 = jnp.float32
INVERSE = 1.0 / math.sqrt(FAST_DIM)


def dot_nn(left, right):
    return lax.dot_general(left, right, (((1,), (0,)), ((), ())), preferred_element_type=F32)


def dot_nt(left, right):
    return lax.dot_general(left, right, (((1,), (1,)), ((), ())), preferred_element_type=F32)


def call(body, out_shapes, operands, scalars=0, anywhere=0, scratch=(), cost=None, limit=VMEM_LIMIT):
    vmem = pl.BlockSpec(memory_space=pltpu.VMEM)
    in_specs = (
        [pl.BlockSpec(memory_space=pltpu.SMEM)] * scalars
        + [vmem] * (len(operands) - scalars - anywhere)
        + [pl.BlockSpec(memory_space=pl.ANY)] * anywhere
    )
    flops, moved = cost or (1000, 1000)
    return pl.pallas_call(
        body,
        out_shape=out_shapes,
        in_specs=in_specs,
        out_specs=jax.tree.map(lambda _: vmem, out_shapes),
        scratch_shapes=scratch,
        compiler_params=pltpu.CompilerParams(vmem_limit_bytes=limit),
        cost_estimate=pl.CostEstimate(flops=flops, bytes_accessed=moved, transcendentals=0),
    )(*operands)


def slot_of(block, order):
    slot = 0
    for bit in order:
        slot = slot * 2 + ((block >> bit) & 1)
    return slot


def gradient_kernel(orders, place_ref, rates_ref, keys_ref, values_ref, weights_ref, *refs):
    out_refs, chunk_refs = refs[:-2], refs[-2:]
    place = place_ref[0, 0]
    rates = rates_ref[...]
    keys = keys_ref[...]
    values = values_ref[...]
    hidden_size, width = weights_ref.shape[1:]
    step = 128

    def put(chunk, low, columns, product):
        order = orders[chunk]
        block_rows = min(step, hidden_size >> len(order))
        for start in range(0, step, block_rows):
            row = low + start
            if order:
                slot = slot_of((row // block_rows) ^ place, order)
                row = pl.multiple_of(slot * block_rows, block_rows)
            chunk_refs[chunk][pl.ds(row, block_rows), columns] = product[start:start + block_rows]

    for low in range(0, hidden_size, step):
        rows = slice(low, low + step)
        gate = dot_nt(weights_ref[0, rows, :], keys) * INVERSE
        up = dot_nt(weights_ref[1, rows, :], keys) * INVERSE
        sigmoid = jax.nn.sigmoid(gate)
        silu = gate * sigmoid
        hidden = (rates * silu * up).astype(BF16)
        backward = rates * dot_nt(weights_ref[2, rows, :], values)
        d_gate = (
            backward * up * sigmoid * (1.0 + gate * (1.0 - sigmoid)) * INVERSE
        ).astype(BF16)
        d_up = (backward * silu * INVERSE).astype(BF16)
        up_part = dot_nn(d_up, keys).astype(BF16)
        put(0, low, slice(0, width), dot_nn(d_gate, keys).astype(BF16))
        put(0, low, slice(width, width + width // 2), up_part[:, :width // 2])
        put(1, low, slice(0, width), dot_nn(hidden, values).astype(BF16))
        put(1, low, slice(width, width + width // 2), up_part[:, width // 2:])
    halves = len(out_refs) // 2
    half_rows = hidden_size // halves
    for index, out_ref in enumerate(out_refs):
        half = index % halves
        out_ref[...] = chunk_refs[index // halves][half * half_rows:(half + 1) * half_rows, :]


def attend_rows(edge_prev, edge_next, query_tile, keys_prev, keys_own, keys_next,
                values_prev, values_own, values_next):
    scale = 1.0 / math.sqrt(HEAD_DIM)
    row = lax.broadcasted_iota(jnp.int32, (TILE, TILE), 0)
    col = lax.broadcasted_iota(jnp.int32, (TILE, TILE), 1)
    minus = jnp.float32(-jnp.inf)
    score_prev = dot_nt(query_tile, keys_prev)
    score_own = dot_nt(query_tile, keys_own)
    score_next = dot_nt(query_tile, keys_next)
    parts = [score_prev[:, :TILE] + jnp.where(col >= row, edge_prev, minus)]
    if score_prev.shape[1] > TILE:
        parts.append(score_prev[:, TILE:] + edge_prev)
    parts.append(score_own)
    if score_next.shape[1] > TILE:
        parts.append(score_next[:, :-TILE] + edge_next)
    parts.append(score_next[:, -TILE:] + jnp.where(col <= row, edge_next, minus))
    scores = jnp.concatenate(parts, axis=1)
    highest = jnp.max(scores, axis=1, keepdims=True)
    weights = jnp.exp((scores - highest) * scale)
    total = jnp.sum(weights, axis=1, keepdims=True)
    weights = weights.astype(BF16)
    width_prev, width_own = score_prev.shape[1], score_own.shape[1]
    attended = (
        dot_nn(weights[:, :width_prev], values_prev)
        + dot_nn(weights[:, width_prev:width_prev + width_own], values_own)
        + dot_nn(weights[:, width_prev + width_own:], values_next)
    )
    return attended / total


def pack_kernel(side_ref, queries_ref, keys_ref, values_ref, out_ref):
    count = queries_ref.shape[0]
    start = pl.multiple_of((1 - side_ref[0, 0]) * HEAD_DIM, HEAD_DIM)
    for index, ref in enumerate((queries_ref, keys_ref, values_ref)):
        out_ref[index * count:(index + 1) * count, :] = ref[:, pl.ds(start, HEAD_DIM)]


def border_kernel(side_ref, keys_ref, values_ref, other_ref, low_ref, high_ref):
    count = keys_ref.shape[0]
    side = side_ref[0, 0]
    start = pl.multiple_of(side * HEAD_DIM, HEAD_DIM)

    def fill(own_ref, other_out_ref):
        own_ref[:count, :] = keys_ref[:, pl.ds(start, HEAD_DIM)]
        own_ref[count:, :] = values_ref[:, pl.ds(start, HEAD_DIM)]
        other_out_ref[...] = other_ref[count:, :]

    @pl.when(side == 0)
    def _():
        fill(low_ref, high_ref)

    @pl.when(side != 0)
    def _():
        fill(high_ref, low_ref)


def first_kernel(edge_ref, side_ref, queries_ref, other_ref, prev_ref, low_ref, high_ref, next_ref,
                 keep_ref, send_ref, keys_ref, values_ref):
    count = queries_ref.shape[0]
    side = side_ref[0, 0]
    for index, ref in enumerate((prev_ref, low_ref, high_ref, next_ref)):
        rows = slice(index * count, (index + 1) * count)
        keys_ref[rows, :] = ref[:count, :]
        values_ref[rows, :] = ref[count:, :]
    start = pl.multiple_of(side * HEAD_DIM, HEAD_DIM)
    for turn, out_ref in enumerate((keep_ref, send_ref)):
        base = (side if turn == 0 else 1 - side) * count

        def span(ref, low, length):
            return ref[pl.ds(pl.multiple_of(base + low, TILE), length), :]

        for index in range(count // TILE):
            low, high = index * TILE, (index + 1) * TILE
            query = queries_ref[low:high, pl.ds(start, HEAD_DIM)] if turn == 0 else other_ref[low:high, :]
            out_ref[low:high, :] = attend_rows(
                edge_ref[turn, 0], edge_ref[turn, 1], query,
                span(keys_ref, low, count - low), span(keys_ref, count, count),
                span(keys_ref, 2 * count, high),
                span(values_ref, low, count - low), span(values_ref, count, count),
                span(values_ref, 2 * count, high),
            ).astype(BF16)


def query_kernel(side_ref, keep_ref, other_ref, map_ref, out_ref):
    side = side_ref[0, 0]
    own = keep_ref[...].astype(F32)
    other = other_ref[...].astype(F32)
    square = jnp.sum(own * own + other * other, axis=1, keepdims=True)
    norm = lax.rsqrt(square / (HEADS_GRP * HEAD_DIM) + 1e-05)
    own_map = map_ref[pl.ds(pl.multiple_of(side * HEAD_DIM, HEAD_DIM), HEAD_DIM), :]
    other_map = map_ref[pl.ds(pl.multiple_of((1 - side) * HEAD_DIM, HEAD_DIM), HEAD_DIM), :]
    out_ref[...] = (
        dot_nn((own * norm).astype(BF16), own_map) + dot_nn((other * norm).astype(BF16), other_map)
    ).astype(BF16)


def second_kernel(edge_ref, queries_ref, keep_ref, near_ref, far_ref, keys_prev_ref, keys_ref, keys_next_ref,
                  values_prev_ref, values_ref, values_next_ref, out_ref):
    count = keys_ref.shape[0]
    for index in range(count // TILE):
        low, high = index * TILE, (index + 1) * TILE
        rows = slice(low, high)
        mixed = (
            keep_ref[1, rows, :].astype(F32)
            + near_ref[1, rows, :].astype(F32)
            + far_ref[rows, :].astype(F32)
        )
        query = (queries_ref[rows, :].astype(F32) + mixed).astype(BF16)
        heads = []
        for head in range(HEADS_GRP):
            cols = slice(head * HEAD_DIM, (head + 1) * HEAD_DIM)
            heads.append(
                attend_rows(
                    edge_ref[0, 0], edge_ref[0, 1], query[:, cols],
                    keys_prev_ref[low:, cols], keys_ref[:, cols], keys_next_ref[:high, cols],
                    values_prev_ref[low:, cols], values_ref[:, cols], values_next_ref[:high, cols],
                )
            )
        both = jnp.concatenate(heads, axis=1)
        mean = jnp.mean(both * both, axis=1, keepdims=True)
        out_ref[rows, :] = (both * lax.rsqrt(mean + 1e-05)).astype(BF16)


def renew_kernel(orders, place_ref, weights_ref, query_ref, *refs):
    pieces, (own_ref, fast_ref, new_ref) = refs[:-3], refs[-3:]
    place = place_ref[0, 0]
    hidden_size, width = weights_ref.shape[1:]
    limit_norm = math.sqrt(FAST_HIDDEN * FAST_DIM) / 2.0
    step = 64
    square = jnp.zeros((1, pieces[0].shape[1]), F32)
    for piece in pieces:
        for low in range(0, piece.shape[0], step):
            part = piece[low:low + step, :].astype(F32)
            square = square + jnp.sum(part * part, axis=0, keepdims=True)
    square = jnp.sum(square, axis=1, keepdims=True)
    factor = jnp.minimum(1.0, limit_norm * lax.rsqrt(square + 1e-06))
    per_chunk = len(pieces) // 2
    piece_rows = pieces[0].shape[0]
    blocks = 1 << len(orders[0])
    block_rows = hidden_size // blocks
    count = min(step, block_rows)
    for block in range(blocks):
        starts = [slot_of(block, order) * block_rows for order in orders]
        for low in range(0, block_rows, count):
            found = []
            for chunk, start in enumerate(starts):
                piece = pieces[chunk * per_chunk + start // piece_rows]
                inside = start % piece_rows + low
                found.append(piece[inside:inside + count, :].astype(F32))
            parts = [
                found[0][:, :width],
                jnp.concatenate([found[0][:, width:], found[1][:, width:]], axis=1),
                found[1][:, :width],
            ]
            rows = slice(low, low + count)
            if blocks > 1:
                rows = pl.ds(pl.multiple_of((block ^ place) * block_rows + low, count), count)
            for matrix, part in enumerate(parts):
                old = weights_ref[matrix, rows, :].astype(F32)
                stepped = old + factor * part
                norm = jnp.sqrt(jnp.sum(old * old, axis=1, keepdims=True))
                size = jnp.sum(stepped * stepped, axis=1, keepdims=True)
                fresh = (stepped * norm * lax.rsqrt(size + 1e-06)).astype(BF16)
                new_ref[matrix, rows, :] = fresh
                if block == 0:
                    own_ref[matrix, low:low + count, :] = fresh
    step = 128
    for low in range(0, query_ref.shape[0], step):
        rows = slice(low, low + step)
        query = query_ref[rows, :]
        gate = dot_nt(query, new_ref[0]) * INVERSE
        up = dot_nt(query, new_ref[1]) * INVERSE
        hidden = (jax.nn.silu(gate) * up).astype(BF16)
        raw = dot_nn(hidden, new_ref[2])
        mean = jnp.mean(raw * raw, axis=1, keepdims=True)
        fast_ref[rows, :] = (raw * lax.rsqrt(mean + 1e-05)).astype(BF16)


def mix_kernel(place_ref, fast_ref, map_ref, out_ref):
    width = out_ref.shape[2]
    for slot in range(2):
        start = pl.multiple_of(place_ref[0, slot] * width, width)
        columns = map_ref[:, pl.ds(start, width)]
        out_ref[slot] = dot_nn(fast_ref[...], columns).astype(BF16)


def seq_shift(value, step):
    peers = lax.axis_size("seq")
    return lax.ppermute(
        value, "seq", [(i, i + step) for i in range(peers) if 0 <= i + step < peers]
    )


def head_swap(value, bit):
    return lax.ppermute(value, "head", [(i, i ^ bit) for i in range(lax.axis_size("head"))])


def seq_swap(value, bit):
    step = 1 << bit
    return lax.ppermute(value, "seq", [(i, i ^ step) for i in range(lax.axis_size("seq"))])


def after(value, others):
    return lax.optimization_barrier((value, others))[0]


def halving_start(chunks, orders):
    keeps = [keep for keep, _ in chunks]
    return keeps, [seq_swap(send, order[0]) for (_, send), order in zip(chunks, orders)]


def halving_step(keeps, found, orders, turn, wait=()):
    sends, rest = [], []
    for keep, new in zip(keeps, found):
        half = keep.shape[0] // 2
        sends.append((keep[half:].astype(F32) + new[half:].astype(F32)).astype(BF16))
        rest.append(lax.optimization_barrier(keep[:half].astype(F32) + new[:half].astype(F32)))
    sends = after(sends, wait) if wait else sends
    return rest, [seq_swap(send, order[turn]) for send, order in zip(sends, orders)]


def doubling_step(held, orders, turn, wait=()):
    whole = [jnp.concatenate(parts) if len(parts) > 1 else parts[0] for parts in held]
    whole = after(whole, wait) if wait else whole
    return [(own, seq_swap(own, order[turn])) for own, order in zip(whole, orders)]


def local(
    queries_first,
    keys_first,
    values_first,
    input_map,
    fast_keys,
    fast_values,
    step_rates,
    fast_weights,
    output_map,
    queries_second,
    keys_second,
    values_second,
):
    rows, width = queries_first.shape
    seq_count = lax.axis_size("seq")
    seq_place = lax.axis_index("seq")
    head_place = lax.axis_index("head")
    weights = jnp.transpose(fast_weights[0], (1, 0, 2))
    hidden_size, fast_width = weights.shape[1:]
    shape = jax.ShapeDtypeStruct
    minus = jnp.float32(-jnp.inf)
    side = seq_place % 2

    def edges_of(block):
        return [jnp.where(block > 0, 0.0, minus), jnp.where(block < seq_count - 1, 0.0, minus)]

    edges = jnp.stack(edges_of(seq_place) + edges_of(seq_place ^ 1)).reshape(2, 2)
    side_scalar = side.astype(jnp.int32).reshape(1, 1)
    place = seq_place.astype(jnp.int32).reshape(1, 1)

    packed = call(
        pack_kernel,
        shape((3 * rows, HEAD_DIM), BF16),
        (side_scalar, queries_first, keys_first, values_first),
        scalars=1,
    )
    other_first = seq_swap(packed, 0)

    bits = tuple(range(seq_count.bit_length() - 1))
    halving = seq_count == 1 << len(bits) and len(bits) > 1 and hidden_size >> len(bits) >= 16
    orders = (bits, bits[1:] + bits[:1]) if halving else ((), ())
    halves = 2 if halving else 1
    chunk_width = fast_width + fast_width // 2
    gradients = call(
        functools.partial(gradient_kernel, orders),
        [shape((hidden_size // halves, chunk_width), BF16)] * (2 * halves),
        (place, step_rates.reshape(1, rows), fast_keys, fast_values, weights),
        scalars=1,
        scratch=[pltpu.VMEM((hidden_size, chunk_width), BF16)] * 2,
        limit=VMEM_MOST,
    )
    low_block, high_block = call(
        border_kernel,
        [shape((2 * rows, HEAD_DIM), BF16)] * 2,
        (side_scalar, keys_first, values_first, other_first),
        scalars=1,
    )

    def first_halos(low_block, high_block):
        return seq_shift(high_block, 2), seq_shift(low_block, -2)

    def first_attention(prev_first, next_first):
        keep_first, send_first = call(
            first_kernel,
            [shape((rows, HEAD_DIM), BF16)] * 2,
            (edges, side_scalar, queries_first, other_first, prev_first, low_block, high_block, next_first),
            scalars=2,
            scratch=[pltpu.VMEM((4 * rows, HEAD_DIM), BF16)] * 2,
            cost=(12 * rows * rows * width, 16 * rows * width),
        )
        return keep_first, seq_swap(send_first, 0)

    def second_halos(array):
        return seq_shift(array, 1), seq_shift(array, -1)

    if halving:
        turns = len(bits)
        keeps, found = halving_start([gradients[:2], gradients[2:]], orders)
        for turn in range(1, turns):
            if turn == turns - 1:
                prev_first, next_first = first_halos(*after((low_block, high_block), found))
            keeps, found = halving_step(keeps, found, orders, turn)
        held = [((keep.astype(F32) + new.astype(F32)).astype(BF16),) for keep, new in zip(keeps, found)]
        keys_prev, keys_next = second_halos(after(keys_second, found))
        for turn in reversed(range(turns)):
            wait = ()
            if turn == 1:
                wait = (prev_first, next_first)
            if turn == 0:
                keep_first, back_first = first_attention(prev_first, next_first)
                wait = (keep_first, keys_prev, keys_next)
            held = doubling_step(held, orders, turn, wait)
        gathered = [part for parts in held for part in parts]
        values_prev, values_next = second_halos(after(values_second, gathered))
    else:
        gathered = lax.psum(gradients, "seq")
        keep_first, back_first = first_attention(*first_halos(low_block, high_block))
        keys_prev, keys_next = second_halos(keys_second)
        values_prev, values_next = second_halos(values_second)
    fast_query = call(
        query_kernel,
        shape((rows, fast_width), BF16),
        (side_scalar, keep_first, back_first, input_map[0]),
        scalars=1,
    )

    own_rows = hidden_size >> len(orders[0])
    own_new, fast_out = call(
        functools.partial(renew_kernel, orders),
        [shape((3, own_rows, fast_width), BF16), shape((rows, fast_width), BF16)],
        (place, weights, fast_query, *gathered),
        scalars=1,
        scratch=[pltpu.VMEM(weights.shape, BF16)],
    )
    if not halving:
        share_rows = hidden_size // seq_count
        own_new = lax.dynamic_slice_in_dim(own_new, seq_place * share_rows, share_rows, 1)

    fast_out = after(fast_out, (values_prev, values_next))

    def mixed_for(low_bit):
        far = (head_place // 2) ^ 1
        near = head_place // 2
        places = jnp.stack([far * 2 + low_bit, near * 2 + low_bit]).reshape(1, 2)
        return call(
            mix_kernel,
            shape((2, rows, width), BF16),
            (places, fast_out, output_map),
            scalars=1,
        )

    my_bit = head_place % 2
    near_part = head_swap(mixed_for(1 - my_bit), 1)
    keep_part = mixed_for(my_bit)
    to_send = (keep_part[0].astype(F32) + near_part[0].astype(F32)).astype(BF16)
    far_part = head_swap(to_send, 2)

    normed_second = call(
        second_kernel,
        shape((rows, width), BF16),
        (edges, queries_second, keep_part, near_part, far_part,
         keys_prev, keys_second, keys_next, values_prev, values_second, values_next),
        scalars=1,
        cost=(12 * rows * rows * width, 16 * rows * width),
    )
    return (normed_second, jnp.transpose(own_new, (1, 0, 2))[None])


def solution(mesh):
    return jax.shard_map(
        local,
        mesh=mesh,
        in_specs=(
            P("seq", "head"),
            P("seq", "head"),
            P("seq", "head"),
            P("head", None, None),
            P("seq", "head"),
            P("seq", "head"),
            P("seq", "head"),
            P("head", None, None, None),
            P("head", None),
            P("seq", "head"),
            P("seq", "head"),
            P("seq", "head"),
        ),
        out_specs=(P("seq", "head"), P("head", "seq", None, None)),
        check_vma=False,
    )
```

```python
import functools
import math

import jax
import jax.numpy as jnp
from jax import lax
from jax.experimental import pallas as pl
from jax.experimental.pallas import tpu as pltpu
from jax.sharding import PartitionSpec as P

HALF_WIN = 512
HEAD_DIM = 128
HEADS_GRP = 2
FAST_DIM = 512
FAST_HIDDEN = 512
TILE = 128
VMEM_LIMIT = 24 * 1024 * 1024
VMEM_MOST = 60 * 1024 * 1024

BF16 = jnp.bfloat16
F32 = jnp.float32
INVERSE = 1.0 / math.sqrt(FAST_DIM)


def dot_nn(left, right):
    return lax.dot_general(left, right, (((1,), (0,)), ((), ())), preferred_element_type=F32)


def dot_nt(left, right):
    return lax.dot_general(left, right, (((1,), (1,)), ((), ())), preferred_element_type=F32)


def call(body, out_shapes, operands, scalars=0, anywhere=0, scratch=(), cost=None, limit=VMEM_LIMIT):
    vmem = pl.BlockSpec(memory_space=pltpu.VMEM)
    in_specs = (
        [pl.BlockSpec(memory_space=pltpu.SMEM)] * scalars
        + [vmem] * (len(operands) - scalars - anywhere)
        + [pl.BlockSpec(memory_space=pl.ANY)] * anywhere
    )
    flops, moved = cost or (1000, 1000)
    return pl.pallas_call(
        body,
        out_shape=out_shapes,
        in_specs=in_specs,
        out_specs=jax.tree.map(lambda _: vmem, out_shapes),
        scratch_shapes=scratch,
        compiler_params=pltpu.CompilerParams(vmem_limit_bytes=limit),
        cost_estimate=pl.CostEstimate(flops=flops, bytes_accessed=moved, transcendentals=0),
    )(*operands)


def slot_of(block, order):
    slot = 0
    for bit in order:
        slot = slot * 2 + ((block >> bit) & 1)
    return slot


def gradient_kernel(orders, place_ref, rates_ref, keys_ref, values_ref, weights_ref, *refs):
    out_refs, chunk_refs = refs[:-2], refs[-2:]
    place = place_ref[0, 0]
    rates = rates_ref[...]
    keys = keys_ref[...]
    values = values_ref[...]
    hidden_size = chunk_refs[0].shape[0]
    width = weights_ref.shape[2]
    turn = pl.program_id(0)
    step = weights_ref.shape[1]

    def put(chunk, columns, product):
        order = orders[chunk]
        block_rows = min(step, hidden_size >> len(order))
        for start in range(0, step, block_rows):
            row = turn * step + start
            if order:
                block = turn * (step // block_rows) + start // block_rows
                row = slot_of(block ^ place, order) * block_rows
            row = pl.multiple_of(row, block_rows)
            chunk_refs[chunk][pl.ds(row, block_rows), columns] = product[start:start + block_rows]

    gate = dot_nt(weights_ref[0], keys) * INVERSE
    up = dot_nt(weights_ref[1], keys) * INVERSE
    sigmoid = jax.nn.sigmoid(gate)
    silu = gate * sigmoid
    hidden = (rates * silu * up).astype(BF16)
    backward = rates * dot_nt(weights_ref[2], values)
    d_gate = (backward * up * sigmoid * (1.0 + gate * (1.0 - sigmoid)) * INVERSE).astype(BF16)
    d_up = (backward * silu * INVERSE).astype(BF16)
    up_part = dot_nn(d_up, keys).astype(BF16)
    put(0, slice(0, width), dot_nn(d_gate, keys).astype(BF16))
    put(0, slice(width, width + width // 2), up_part[:, :width // 2])
    put(1, slice(0, width), dot_nn(hidden, values).astype(BF16))
    put(1, slice(width, width + width // 2), up_part[:, width // 2:])

    @pl.when(turn == pl.num_programs(0) - 1)
    def _():
        halves = len(out_refs) // 2
        half_rows = hidden_size // halves
        for index, out_ref in enumerate(out_refs):
            half = index % halves
            out_ref[...] = chunk_refs[index // halves][half * half_rows:(half + 1) * half_rows, :]


def attend_rows(edge_prev, edge_next, query_tile, keys_prev, keys_own, keys_next,
                values_prev, values_own, values_next):
    scale = 1.0 / math.sqrt(HEAD_DIM)
    row = lax.broadcasted_iota(jnp.int32, (TILE, TILE), 0)
    col = lax.broadcasted_iota(jnp.int32, (TILE, TILE), 1)
    minus = jnp.float32(-jnp.inf)
    score_prev = dot_nt(query_tile, keys_prev)
    score_own = dot_nt(query_tile, keys_own)
    score_next = dot_nt(query_tile, keys_next)
    parts = [score_prev[:, :TILE] + jnp.where(col >= row, edge_prev, minus)]
    if score_prev.shape[1] > TILE:
        parts.append(score_prev[:, TILE:] + edge_prev)
    parts.append(score_own)
    if score_next.shape[1] > TILE:
        parts.append(score_next[:, :-TILE] + edge_next)
    parts.append(score_next[:, -TILE:] + jnp.where(col <= row, edge_next, minus))
    scores = jnp.concatenate(parts, axis=1)
    highest = jnp.max(scores, axis=1, keepdims=True)
    weights = jnp.exp((scores - highest) * scale)
    total = jnp.sum(weights, axis=1, keepdims=True)
    weights = weights.astype(BF16)
    width_prev, width_own = score_prev.shape[1], score_own.shape[1]
    attended = (
        dot_nn(weights[:, :width_prev], values_prev)
        + dot_nn(weights[:, width_prev:width_prev + width_own], values_own)
        + dot_nn(weights[:, width_prev + width_own:], values_next)
    )
    return attended / total


def pack_kernel(side_ref, queries_ref, keys_ref, values_ref, out_ref):
    count = queries_ref.shape[0]
    start = pl.multiple_of((1 - side_ref[0, 0]) * HEAD_DIM, HEAD_DIM)
    for index, ref in enumerate((queries_ref, keys_ref, values_ref)):
        out_ref[index * count:(index + 1) * count, :] = ref[:, pl.ds(start, HEAD_DIM)]


def border_kernel(side_ref, keys_ref, values_ref, other_ref, low_ref, high_ref):
    count = keys_ref.shape[0]
    side = side_ref[0, 0]
    start = pl.multiple_of(side * HEAD_DIM, HEAD_DIM)

    def fill(own_ref, other_out_ref):
        own_ref[:count, :] = keys_ref[:, pl.ds(start, HEAD_DIM)]
        own_ref[count:, :] = values_ref[:, pl.ds(start, HEAD_DIM)]
        other_out_ref[...] = other_ref[count:, :]

    @pl.when(side == 0)
    def _():
        fill(low_ref, high_ref)

    @pl.when(side != 0)
    def _():
        fill(high_ref, low_ref)


def first_kernel(edge_ref, side_ref, queries_ref, other_ref, prev_ref, low_ref, high_ref, next_ref,
                 keep_ref, send_ref, keys_ref, values_ref):
    count = queries_ref.shape[0]
    side = side_ref[0, 0]
    for index, ref in enumerate((prev_ref, low_ref, high_ref, next_ref)):
        rows = slice(index * count, (index + 1) * count)
        keys_ref[rows, :] = ref[:count, :]
        values_ref[rows, :] = ref[count:, :]
    start = pl.multiple_of(side * HEAD_DIM, HEAD_DIM)
    for turn, out_ref in enumerate((keep_ref, send_ref)):
        base = (side if turn == 0 else 1 - side) * count

        def span(ref, low, length):
            return ref[pl.ds(pl.multiple_of(base + low, TILE), length), :]

        for index in range(count // TILE):
            low, high = index * TILE, (index + 1) * TILE
            query = queries_ref[low:high, pl.ds(start, HEAD_DIM)] if turn == 0 else other_ref[low:high, :]
            out_ref[low:high, :] = attend_rows(
                edge_ref[turn, 0], edge_ref[turn, 1], query,
                span(keys_ref, low, count - low), span(keys_ref, count, count),
                span(keys_ref, 2 * count, high),
                span(values_ref, low, count - low), span(values_ref, count, count),
                span(values_ref, 2 * count, high),
            ).astype(BF16)


def query_kernel(side_ref, keep_ref, other_ref, map_ref, out_ref):
    side = side_ref[0, 0]
    own = keep_ref[...].astype(F32)
    other = other_ref[...].astype(F32)
    square = jnp.sum(own * own + other * other, axis=1, keepdims=True)
    norm = lax.rsqrt(square / (HEADS_GRP * HEAD_DIM) + 1e-05)
    own_map = map_ref[pl.ds(pl.multiple_of(side * HEAD_DIM, HEAD_DIM), HEAD_DIM), :]
    other_map = map_ref[pl.ds(pl.multiple_of((1 - side) * HEAD_DIM, HEAD_DIM), HEAD_DIM), :]
    out_ref[...] = (
        dot_nn((own * norm).astype(BF16), own_map) + dot_nn((other * norm).astype(BF16), other_map)
    ).astype(BF16)


def second_kernel(edge_ref, queries_ref, keep_ref, near_ref, far_ref, prev_ref, keys_ref, values_ref, next_ref,
                  out_ref):
    count = keys_ref.shape[0]
    for index in range(count // TILE):
        low, high = index * TILE, (index + 1) * TILE
        rows = slice(low, high)
        mixed = (
            keep_ref[1, rows, :].astype(F32)
            + near_ref[1, rows, :].astype(F32)
            + far_ref[rows, :].astype(F32)
        )
        query = (queries_ref[rows, :].astype(F32) + mixed).astype(BF16)
        heads = []
        for head in range(HEADS_GRP):
            cols = slice(head * HEAD_DIM, (head + 1) * HEAD_DIM)
            heads.append(
                attend_rows(
                    edge_ref[0, 0], edge_ref[0, 1], query[:, cols],
                    prev_ref[low:count, cols], keys_ref[:, cols], next_ref[:high, cols],
                    prev_ref[count + low:, cols], values_ref[:, cols], next_ref[count:count + high, cols],
                )
            )
        both = jnp.concatenate(heads, axis=1)
        mean = jnp.mean(both * both, axis=1, keepdims=True)
        out_ref[rows, :] = (both * lax.rsqrt(mean + 1e-05)).astype(BF16)


def renew_kernel(orders, place_ref, weights_ref, query_ref, *refs):
    pieces, (own_ref, fast_ref, new_ref) = refs[:-3], refs[-3:]
    place = place_ref[0, 0]
    hidden_size, width = weights_ref.shape[1:]
    limit_norm = math.sqrt(FAST_HIDDEN * FAST_DIM) / 2.0
    step = 64
    square = jnp.zeros((1, pieces[0].shape[1]), F32)
    for piece in pieces:
        for low in range(0, piece.shape[0], step):
            part = piece[low:low + step, :].astype(F32)
            square = square + jnp.sum(part * part, axis=0, keepdims=True)
    square = jnp.sum(square, axis=1, keepdims=True)
    factor = jnp.minimum(1.0, limit_norm * lax.rsqrt(square + 1e-06))
    per_chunk = len(pieces) // 2
    piece_rows = pieces[0].shape[0]
    blocks = 1 << len(orders[0])
    block_rows = hidden_size // blocks
    count = min(step, block_rows)
    for block in range(blocks):
        starts = [slot_of(block, order) * block_rows for order in orders]
        for low in range(0, block_rows, count):
            found = []
            for chunk, start in enumerate(starts):
                piece = pieces[chunk * per_chunk + start // piece_rows]
                inside = start % piece_rows + low
                found.append(piece[inside:inside + count, :].astype(F32))
            parts = [
                found[0][:, :width],
                jnp.concatenate([found[0][:, width:], found[1][:, width:]], axis=1),
                found[1][:, :width],
            ]
            rows = slice(low, low + count)
            if blocks > 1:
                rows = pl.ds(pl.multiple_of((block ^ place) * block_rows + low, count), count)
            for matrix, part in enumerate(parts):
                old = weights_ref[matrix, rows, :].astype(F32)
                stepped = old + factor * part
                norm = jnp.sqrt(jnp.sum(old * old, axis=1, keepdims=True))
                size = jnp.sum(stepped * stepped, axis=1, keepdims=True)
                fresh = (stepped * norm * lax.rsqrt(size + 1e-06)).astype(BF16)
                new_ref[matrix, rows, :] = fresh
                if block == 0:
                    own_ref[matrix, low:low + count, :] = fresh
    step = 128
    for low in range(0, query_ref.shape[0], step):
        rows = slice(low, low + step)
        query = query_ref[rows, :]
        gate = dot_nt(query, new_ref[0]) * INVERSE
        up = dot_nt(query, new_ref[1]) * INVERSE
        hidden = (jax.nn.silu(gate) * up).astype(BF16)
        raw = dot_nn(hidden, new_ref[2])
        mean = jnp.mean(raw * raw, axis=1, keepdims=True)
        fast_ref[rows, :] = (raw * lax.rsqrt(mean + 1e-05)).astype(BF16)


def mix_kernel(place_ref, fast_ref, map_ref, out_ref):
    width = out_ref.shape[2]
    for slot in range(2):
        start = pl.multiple_of(place_ref[0, slot] * width, width)
        columns = map_ref[:, pl.ds(start, width)]
        out_ref[slot] = dot_nn(fast_ref[...], columns).astype(BF16)


def seq_shift(value, step):
    peers = lax.axis_size("seq")
    return lax.ppermute(
        value, "seq", [(i, i + step) for i in range(peers) if 0 <= i + step < peers]
    )


def head_swap(value, bit):
    return lax.ppermute(value, "head", [(i, i ^ bit) for i in range(lax.axis_size("head"))])


def seq_swap(value, bit):
    step = 1 << bit
    return lax.ppermute(value, "seq", [(i, i ^ step) for i in range(lax.axis_size("seq"))])


def after(value, others):
    return lax.optimization_barrier((value, others))[0]


def halving_start(chunks, orders):
    keeps = [keep for keep, _ in chunks]
    return keeps, [seq_swap(send, order[0]) for (_, send), order in zip(chunks, orders)]


def halving_step(keeps, found, orders, turn, wait=()):
    sends, rest = [], []
    for keep, new in zip(keeps, found):
        half = keep.shape[0] // 2
        sends.append((keep[half:].astype(F32) + new[half:].astype(F32)).astype(BF16))
        rest.append(lax.optimization_barrier(keep[:half].astype(F32) + new[:half].astype(F32)))
    sends = after(sends, wait) if wait else sends
    return rest, [seq_swap(send, order[turn]) for send, order in zip(sends, orders)]


def doubling_step(held, orders, turn, wait=()):
    whole = [jnp.concatenate(parts) if len(parts) > 1 else parts[0] for parts in held]
    whole = after(whole, wait) if wait else whole
    return [(own, seq_swap(own, order[turn])) for own, order in zip(whole, orders)]


def local(
    queries_first,
    keys_first,
    values_first,
    input_map,
    fast_keys,
    fast_values,
    step_rates,
    fast_weights,
    output_map,
    queries_second,
    keys_second,
    values_second,
):
    rows, width = queries_first.shape
    seq_count = lax.axis_size("seq")
    seq_place = lax.axis_index("seq")
    head_place = lax.axis_index("head")
    weights = jnp.transpose(fast_weights[0], (1, 0, 2))
    hidden_size, fast_width = weights.shape[1:]
    shape = jax.ShapeDtypeStruct
    minus = jnp.float32(-jnp.inf)
    side = seq_place % 2

    def edges_of(block):
        return [jnp.where(block > 0, 0.0, minus), jnp.where(block < seq_count - 1, 0.0, minus)]

    edges = jnp.stack(edges_of(seq_place) + edges_of(seq_place ^ 1)).reshape(2, 2)
    side_scalar = side.astype(jnp.int32).reshape(1, 1)
    place = seq_place.astype(jnp.int32).reshape(1, 1)

    packed = call(
        pack_kernel,
        shape((3 * rows, HEAD_DIM), BF16),
        (side_scalar, queries_first, keys_first, values_first),
        scalars=1,
    )
    other_first = seq_swap(packed, 0)

    bits = tuple(range(seq_count.bit_length() - 1))
    halving = seq_count == 1 << len(bits) and len(bits) > 1 and hidden_size >> len(bits) >= 16
    orders = (bits, bits[1:] + bits[:1]) if halving else ((), ())
    halves = 2 if halving else 1
    chunk_width = fast_width + fast_width // 2
    out_shapes = [shape((hidden_size // halves, chunk_width), BF16)] * (2 * halves)
    whole = pl.BlockSpec(memory_space=pltpu.VMEM)
    gradients = pl.pallas_call(
        functools.partial(gradient_kernel, orders),
        grid=(hidden_size // TILE,),
        out_shape=out_shapes,
        in_specs=[
            pl.BlockSpec(memory_space=pltpu.SMEM),
            whole,
            whole,
            whole,
            pl.BlockSpec((3, TILE, fast_width), lambda turn: (0, turn, 0)),
        ],
        out_specs=[whole] * len(out_shapes),
        scratch_shapes=[pltpu.VMEM((hidden_size, chunk_width), BF16)] * 2,
        compiler_params=pltpu.CompilerParams(vmem_limit_bytes=VMEM_MOST),
        cost_estimate=pl.CostEstimate(flops=1000, bytes_accessed=1000, transcendentals=0),
    )(place, step_rates.reshape(1, rows), fast_keys, fast_values, weights)

    low_block, high_block = call(
        border_kernel,
        [shape((2 * rows, HEAD_DIM), BF16)] * 2,
        (side_scalar, keys_first, values_first, other_first),
        scalars=1,
    )

    def first_halos(low_block, high_block):
        return seq_shift(high_block, 2), seq_shift(low_block, -2)

    def first_attention(prev_first, next_first):
        keep_first, send_first = call(
            first_kernel,
            [shape((rows, HEAD_DIM), BF16)] * 2,
            (edges, side_scalar, queries_first, other_first, prev_first, low_block, high_block, next_first),
            scalars=2,
            scratch=[pltpu.VMEM((4 * rows, HEAD_DIM), BF16)] * 2,
            cost=(12 * rows * rows * width, 16 * rows * width),
        )
        return keep_first, seq_swap(send_first, 0)

    both_second = jnp.concatenate([keys_second, values_second])

    def second_halos(array):
        return seq_shift(array, 1), seq_shift(array, -1)

    if halving:
        turns = len(bits)
        keeps, found = halving_start([gradients[:2], gradients[2:]], orders)
        for turn in range(1, turns):
            if turn == turns - 1:
                prev_first, next_first = first_halos(*after((low_block, high_block), found))
            keeps, found = halving_step(keeps, found, orders, turn)
        held = [((keep.astype(F32) + new.astype(F32)).astype(BF16),) for keep, new in zip(keeps, found)]
        for turn in reversed(range(turns)):
            wait = ()
            if turn == 1:
                wait = (prev_first, next_first)
            if turn == 0:
                keep_first, back_first = first_attention(prev_first, next_first)
                wait = (keep_first,)
            held = doubling_step(held, orders, turn, wait)
        gathered = [part for parts in held for part in parts]
        prev_second, next_second = second_halos(after(both_second, (gathered, back_first)))
    else:
        gathered = lax.psum(gradients, "seq")
        keep_first, back_first = first_attention(*first_halos(low_block, high_block))
        prev_second, next_second = second_halos(both_second)
    fast_query = call(
        query_kernel,
        shape((rows, fast_width), BF16),
        (side_scalar, keep_first, back_first, input_map[0]),
        scalars=1,
    )

    own_rows = hidden_size >> len(orders[0])
    own_new, fast_out = call(
        functools.partial(renew_kernel, orders),
        [shape((3, own_rows, fast_width), BF16), shape((rows, fast_width), BF16)],
        (place, weights, fast_query, *gathered),
        scalars=1,
        scratch=[pltpu.VMEM(weights.shape, BF16)],
    )
    if not halving:
        share_rows = hidden_size // seq_count
        own_new = lax.dynamic_slice_in_dim(own_new, seq_place * share_rows, share_rows, 1)

    def mixed_for(low_bit):
        far = (head_place // 2) ^ 1
        near = head_place // 2
        places = jnp.stack([far * 2 + low_bit, near * 2 + low_bit]).reshape(1, 2)
        return call(
            mix_kernel,
            shape((2, rows, width), BF16),
            (places, fast_out, output_map),
            scalars=1,
        )

    my_bit = head_place % 2
    near_part = head_swap(mixed_for(1 - my_bit), 1)
    keep_part = mixed_for(my_bit)
    to_send = (keep_part[0].astype(F32) + near_part[0].astype(F32)).astype(BF16)
    far_part = head_swap(to_send, 2)

    normed_second = call(
        second_kernel,
        shape((rows, width), BF16),
        (edges, queries_second, keep_part, near_part, far_part,
         prev_second, keys_second, values_second, next_second),
        scalars=1,
        cost=(12 * rows * rows * width, 16 * rows * width),
    )
    return (normed_second, jnp.transpose(own_new, (1, 0, 2))[None])


def solution(mesh):
    return jax.shard_map(
        local,
        mesh=mesh,
        in_specs=(
            P("seq", "head"),
            P("seq", "head"),
            P("seq", "head"),
            P("head", None, None),
            P("seq", "head"),
            P("seq", "head"),
            P("seq", "head"),
            P("head", None, None, None),
            P("head", None),
            P("seq", "head"),
            P("seq", "head"),
            P("seq", "head"),
        ),
        out_specs=(P("seq", "head"), P("head", "seq", None, None)),
        check_vma=False,
    )
```

```python
import functools
import math

import jax
import jax.numpy as jnp
from jax import lax
from jax.experimental import pallas as pl
from jax.experimental.pallas import tpu as pltpu
from jax.sharding import PartitionSpec as P

HALF_WIN = 512
HEAD_DIM = 128
HEADS_GRP = 2
FAST_DIM = 512
FAST_HIDDEN = 512
TILE = 128
VMEM_LIMIT = 24 * 1024 * 1024
VMEM_MOST = 60 * 1024 * 1024

BF16 = jnp.bfloat16
F32 = jnp.float32
INVERSE = 1.0 / math.sqrt(FAST_DIM)


def dot_nn(left, right):
    return lax.dot_general(left, right, (((1,), (0,)), ((), ())), preferred_element_type=F32)


def dot_nt(left, right):
    return lax.dot_general(left, right, (((1,), (1,)), ((), ())), preferred_element_type=F32)


def call(body, out_shapes, operands, scalars=0, anywhere=0, scratch=(), cost=None, limit=VMEM_LIMIT):
    vmem = pl.BlockSpec(memory_space=pltpu.VMEM)
    in_specs = (
        [pl.BlockSpec(memory_space=pltpu.SMEM)] * scalars
        + [vmem] * (len(operands) - scalars - anywhere)
        + [pl.BlockSpec(memory_space=pl.ANY)] * anywhere
    )
    flops, moved = cost or (1000, 1000)
    return pl.pallas_call(
        body,
        out_shape=out_shapes,
        in_specs=in_specs,
        out_specs=jax.tree.map(lambda _: vmem, out_shapes),
        scratch_shapes=scratch,
        compiler_params=pltpu.CompilerParams(vmem_limit_bytes=limit),
        cost_estimate=pl.CostEstimate(flops=flops, bytes_accessed=moved, transcendentals=0),
    )(*operands)


def slot_of(block, order):
    slot = 0
    for bit in order:
        slot = slot * 2 + ((block >> bit) & 1)
    return slot


def gradient_kernel(orders, place_ref, rates_ref, keys_ref, values_ref, weights_ref, *refs):
    out_refs, chunk_refs = refs[:-2], refs[-2:]
    place = place_ref[0, 0]
    rates = rates_ref[...]
    keys = keys_ref[...]
    values = values_ref[...]
    hidden_size = chunk_refs[0].shape[0]
    width = weights_ref.shape[2]
    turn = pl.program_id(0)
    step = weights_ref.shape[1]

    def put(chunk, columns, product):
        order = orders[chunk]
        block_rows = min(step, hidden_size >> len(order))
        for start in range(0, step, block_rows):
            row = turn * step + start
            if order:
                block = turn * (step // block_rows) + start // block_rows
                row = slot_of(block ^ place, order) * block_rows
            row = pl.multiple_of(row, block_rows)
            chunk_refs[chunk][pl.ds(row, block_rows), columns] = product[start:start + block_rows]

    gate = dot_nt(weights_ref[0], keys) * INVERSE
    up = dot_nt(weights_ref[1], keys) * INVERSE
    sigmoid = jax.nn.sigmoid(gate)
    silu = gate * sigmoid
    hidden = (rates * silu * up).astype(BF16)
    backward = rates * dot_nt(weights_ref[2], values)
    d_gate = (backward * up * sigmoid * (1.0 + gate * (1.0 - sigmoid)) * INVERSE).astype(BF16)
    d_up = (backward * silu * INVERSE).astype(BF16)
    up_part = dot_nn(d_up, keys).astype(BF16)
    put(0, slice(0, width), dot_nn(d_gate, keys).astype(BF16))
    put(0, slice(width, width + width // 2), up_part[:, :width // 2])
    put(1, slice(0, width), dot_nn(hidden, values).astype(BF16))
    put(1, slice(width, width + width // 2), up_part[:, width // 2:])

    @pl.when(turn == pl.num_programs(0) - 1)
    def _():
        halves = len(out_refs) // 2
        half_rows = hidden_size // halves
        for index, out_ref in enumerate(out_refs):
            half = index % halves
            out_ref[...] = chunk_refs[index // halves][half * half_rows:(half + 1) * half_rows, :]


def attend_rows(edge_prev, edge_next, query_tile, keys_prev, keys_own, keys_next,
                values_prev, values_own, values_next):
    scale = 1.0 / math.sqrt(HEAD_DIM)
    row = lax.broadcasted_iota(jnp.int32, (TILE, TILE), 0)
    col = lax.broadcasted_iota(jnp.int32, (TILE, TILE), 1)
    minus = jnp.float32(-jnp.inf)
    score_prev = dot_nt(query_tile, keys_prev)
    score_own = dot_nt(query_tile, keys_own)
    score_next = dot_nt(query_tile, keys_next)
    parts = [score_prev[:, :TILE] + jnp.where(col >= row, edge_prev, minus)]
    if score_prev.shape[1] > TILE:
        parts.append(score_prev[:, TILE:] + edge_prev)
    parts.append(score_own)
    if score_next.shape[1] > TILE:
        parts.append(score_next[:, :-TILE] + edge_next)
    parts.append(score_next[:, -TILE:] + jnp.where(col <= row, edge_next, minus))
    scores = jnp.concatenate(parts, axis=1)
    highest = jnp.max(scores, axis=1, keepdims=True)
    weights = jnp.exp((scores - highest) * scale)
    total = jnp.sum(weights, axis=1, keepdims=True)
    weights = weights.astype(BF16)
    width_prev, width_own = score_prev.shape[1], score_own.shape[1]
    attended = (
        dot_nn(weights[:, :width_prev], values_prev)
        + dot_nn(weights[:, width_prev:width_prev + width_own], values_own)
        + dot_nn(weights[:, width_prev + width_own:], values_next)
    )
    return attended / total


def pack_kernel(side_ref, queries_ref, keys_ref, values_ref, out_ref):
    count = queries_ref.shape[0]
    start = pl.multiple_of((1 - side_ref[0, 0]) * HEAD_DIM, HEAD_DIM)
    for index, ref in enumerate((queries_ref, keys_ref, values_ref)):
        out_ref[index * count:(index + 1) * count, :] = ref[:, pl.ds(start, HEAD_DIM)]


def border_kernel(side_ref, keys_ref, values_ref, other_ref, low_ref, high_ref):
    count = keys_ref.shape[0]
    side = side_ref[0, 0]
    start = pl.multiple_of(side * HEAD_DIM, HEAD_DIM)

    def fill(own_ref, other_out_ref):
        own_ref[:count, :] = keys_ref[:, pl.ds(start, HEAD_DIM)]
        own_ref[count:, :] = values_ref[:, pl.ds(start, HEAD_DIM)]
        other_out_ref[...] = other_ref[count:, :]

    @pl.when(side == 0)
    def _():
        fill(low_ref, high_ref)

    @pl.when(side != 0)
    def _():
        fill(high_ref, low_ref)


def first_kernel(edge_ref, side_ref, queries_ref, other_ref, prev_ref, low_ref, high_ref, next_ref,
                 keep_ref, send_ref, keys_ref, values_ref):
    count = queries_ref.shape[0]
    side = side_ref[0, 0]
    for index, ref in enumerate((prev_ref, low_ref, high_ref, next_ref)):
        rows = slice(index * count, (index + 1) * count)
        keys_ref[rows, :] = ref[:count, :]
        values_ref[rows, :] = ref[count:, :]
    start = pl.multiple_of(side * HEAD_DIM, HEAD_DIM)
    for turn, out_ref in enumerate((keep_ref, send_ref)):
        base = (side if turn == 0 else 1 - side) * count

        def span(ref, low, length):
            return ref[pl.ds(pl.multiple_of(base + low, TILE), length), :]

        for index in range(count // TILE):
            low, high = index * TILE, (index + 1) * TILE
            query = queries_ref[low:high, pl.ds(start, HEAD_DIM)] if turn == 0 else other_ref[low:high, :]
            out_ref[low:high, :] = attend_rows(
                edge_ref[turn, 0], edge_ref[turn, 1], query,
                span(keys_ref, low, count - low), span(keys_ref, count, count),
                span(keys_ref, 2 * count, high),
                span(values_ref, low, count - low), span(values_ref, count, count),
                span(values_ref, 2 * count, high),
            ).astype(BF16)


def query_kernel(side_ref, keep_ref, other_ref, map_ref, out_ref):
    side = side_ref[0, 0]
    own = keep_ref[...].astype(F32)
    other = other_ref[...].astype(F32)
    square = jnp.sum(own * own + other * other, axis=1, keepdims=True)
    norm = lax.rsqrt(square / (HEADS_GRP * HEAD_DIM) + 1e-05)
    own_map = map_ref[pl.ds(pl.multiple_of(side * HEAD_DIM, HEAD_DIM), HEAD_DIM), :]
    other_map = map_ref[pl.ds(pl.multiple_of((1 - side) * HEAD_DIM, HEAD_DIM), HEAD_DIM), :]
    out_ref[...] = (
        dot_nn((own * norm).astype(BF16), own_map) + dot_nn((other * norm).astype(BF16), other_map)
    ).astype(BF16)


def second_kernel(edge_ref, queries_ref, keep_ref, near_ref, far_ref, prev_ref, keys_ref, values_ref, next_ref,
                  out_ref):
    count = keys_ref.shape[0]
    for index in range(count // TILE):
        low, high = index * TILE, (index + 1) * TILE
        rows = slice(low, high)
        mixed = (
            keep_ref[1, rows, :].astype(F32)
            + near_ref[1, rows, :].astype(F32)
            + far_ref[rows, :].astype(F32)
        )
        query = (queries_ref[rows, :].astype(F32) + mixed).astype(BF16)
        heads = []
        for head in range(HEADS_GRP):
            cols = slice(head * HEAD_DIM, (head + 1) * HEAD_DIM)
            heads.append(
                attend_rows(
                    edge_ref[0, 0], edge_ref[0, 1], query[:, cols],
                    prev_ref[low:count, cols], keys_ref[:, cols], next_ref[:high, cols],
                    prev_ref[count + low:, cols], values_ref[:, cols], next_ref[count:count + high, cols],
                )
            )
        both = jnp.concatenate(heads, axis=1)
        mean = jnp.mean(both * both, axis=1, keepdims=True)
        out_ref[rows, :] = (both * lax.rsqrt(mean + 1e-05)).astype(BF16)


def renew_kernel(orders, place_ref, weights_ref, query_ref, *refs):
    pieces, (own_ref, fast_ref, new_ref) = refs[:-3], refs[-3:]
    place = place_ref[0, 0]
    hidden_size, width = weights_ref.shape[1:]
    limit_norm = math.sqrt(FAST_HIDDEN * FAST_DIM) / 2.0
    step = 64
    square = jnp.zeros((1, pieces[0].shape[1]), F32)
    for piece in pieces:
        for low in range(0, piece.shape[0], step):
            part = piece[low:low + step, :].astype(F32)
            square = square + jnp.sum(part * part, axis=0, keepdims=True)
    square = jnp.sum(square, axis=1, keepdims=True)
    factor = jnp.minimum(1.0, limit_norm * lax.rsqrt(square + 1e-06))
    per_chunk = len(pieces) // 2
    piece_rows = pieces[0].shape[0]
    blocks = 1 << len(orders[0])
    block_rows = hidden_size // blocks
    count = min(step, block_rows)
    for block in range(blocks):
        starts = [slot_of(block, order) * block_rows for order in orders]
        for low in range(0, block_rows, count):
            found = []
            for chunk, start in enumerate(starts):
                piece = pieces[chunk * per_chunk + start // piece_rows]
                inside = start % piece_rows + low
                found.append(piece[inside:inside + count, :].astype(F32))
            parts = [
                found[0][:, :width],
                jnp.concatenate([found[0][:, width:], found[1][:, width:]], axis=1),
                found[1][:, :width],
            ]
            rows = slice(low, low + count)
            if blocks > 1:
                rows = pl.ds(pl.multiple_of((block ^ place) * block_rows + low, count), count)
            for matrix, part in enumerate(parts):
                old = weights_ref[matrix, rows, :].astype(F32)
                stepped = old + factor * part
                norm = jnp.sqrt(jnp.sum(old * old, axis=1, keepdims=True))
                size = jnp.sum(stepped * stepped, axis=1, keepdims=True)
                fresh = (stepped * norm * lax.rsqrt(size + 1e-06)).astype(BF16)
                new_ref[matrix, rows, :] = fresh
                if block == 0:
                    own_ref[matrix, low:low + count, :] = fresh
    step = 128
    for low in range(0, query_ref.shape[0], step):
        rows = slice(low, low + step)
        query = query_ref[rows, :]
        gate = dot_nt(query, new_ref[0]) * INVERSE
        up = dot_nt(query, new_ref[1]) * INVERSE
        hidden = (jax.nn.silu(gate) * up).astype(BF16)
        raw = dot_nn(hidden, new_ref[2])
        mean = jnp.mean(raw * raw, axis=1, keepdims=True)
        fast_ref[rows, :] = (raw * lax.rsqrt(mean + 1e-05)).astype(BF16)


def mix_kernel(place_ref, fast_ref, map_ref, out_ref):
    width = out_ref.shape[2]
    for slot in range(2):
        start = pl.multiple_of(place_ref[0, slot] * width, width)
        columns = map_ref[:, pl.ds(start, width)]
        out_ref[slot] = dot_nn(fast_ref[...], columns).astype(BF16)


def seq_shift(value, step):
    peers = lax.axis_size("seq")
    return lax.ppermute(
        value, "seq", [(i, i + step) for i in range(peers) if 0 <= i + step < peers]
    )


def head_swap(value, bit):
    return lax.ppermute(value, "head", [(i, i ^ bit) for i in range(lax.axis_size("head"))])


def seq_swap(value, bit):
    step = 1 << bit
    return lax.ppermute(value, "seq", [(i, i ^ step) for i in range(lax.axis_size("seq"))])


def after(value, others):
    return lax.optimization_barrier((value, others))[0]


def halving_start(chunks, orders):
    keeps = [keep for keep, _ in chunks]
    return keeps, [seq_swap(send, order[0]) for (_, send), order in zip(chunks, orders)]


def halving_step(keeps, found, orders, turn, wait=()):
    sends, rest = [], []
    for keep, new in zip(keeps, found):
        half = keep.shape[0] // 2
        sends.append((keep[half:].astype(F32) + new[half:].astype(F32)).astype(BF16))
        rest.append(lax.optimization_barrier(keep[:half].astype(F32) + new[:half].astype(F32)))
    sends = after(sends, wait) if wait else sends
    return rest, [seq_swap(send, order[turn]) for send, order in zip(sends, orders)]


def doubling_step(held, orders, turn, wait=()):
    whole = [jnp.concatenate(parts) if len(parts) > 1 else parts[0] for parts in held]
    whole = after(whole, wait) if wait else whole
    return [(own, seq_swap(own, order[turn])) for own, order in zip(whole, orders)]


def local(
    queries_first,
    keys_first,
    values_first,
    input_map,
    fast_keys,
    fast_values,
    step_rates,
    fast_weights,
    output_map,
    queries_second,
    keys_second,
    values_second,
):
    rows, width = queries_first.shape
    seq_count = lax.axis_size("seq")
    seq_place = lax.axis_index("seq")
    head_place = lax.axis_index("head")
    weights = jnp.transpose(fast_weights[0], (1, 0, 2))
    hidden_size, fast_width = weights.shape[1:]
    shape = jax.ShapeDtypeStruct
    minus = jnp.float32(-jnp.inf)
    side = seq_place % 2

    def edges_of(block):
        return [jnp.where(block > 0, 0.0, minus), jnp.where(block < seq_count - 1, 0.0, minus)]

    edges = jnp.stack(edges_of(seq_place) + edges_of(seq_place ^ 1)).reshape(2, 2)
    side_scalar = side.astype(jnp.int32).reshape(1, 1)
    place = seq_place.astype(jnp.int32).reshape(1, 1)

    packed = call(
        pack_kernel,
        shape((3 * rows, HEAD_DIM), BF16),
        (side_scalar, queries_first, keys_first, values_first),
        scalars=1,
    )
    other_first = seq_swap(packed, 0)

    bits = tuple(range(seq_count.bit_length() - 1))
    halving = seq_count == 1 << len(bits) and len(bits) > 1 and hidden_size >> len(bits) >= 16
    orders = (bits, bits[1:] + bits[:1]) if halving else ((), ())
    halves = 2 if halving else 1
    chunk_width = fast_width + fast_width // 2
    out_shapes = [shape((hidden_size // halves, chunk_width), BF16)] * (2 * halves)
    whole = pl.BlockSpec(memory_space=pltpu.VMEM)
    gradients = pl.pallas_call(
        functools.partial(gradient_kernel, orders),
        grid=(hidden_size // TILE,),
        out_shape=out_shapes,
        in_specs=[
            pl.BlockSpec(memory_space=pltpu.SMEM),
            whole,
            whole,
            whole,
            pl.BlockSpec((3, TILE, fast_width), lambda turn: (0, turn, 0)),
        ],
        out_specs=[whole] * len(out_shapes),
        scratch_shapes=[pltpu.VMEM((hidden_size, chunk_width), BF16)] * 2,
        compiler_params=pltpu.CompilerParams(vmem_limit_bytes=VMEM_MOST),
        cost_estimate=pl.CostEstimate(flops=1000, bytes_accessed=1000, transcendentals=0),
    )(place, step_rates.reshape(1, rows), fast_keys, fast_values, weights)

    low_block, high_block = call(
        border_kernel,
        [shape((2 * rows, HEAD_DIM), BF16)] * 2,
        (side_scalar, keys_first, values_first, other_first),
        scalars=1,
    )

    def first_halos(low_block, high_block):
        return seq_shift(high_block, 2), seq_shift(low_block, -2)

    def first_attention(prev_first, next_first):
        keep_first, send_first = call(
            first_kernel,
            [shape((rows, HEAD_DIM), BF16)] * 2,
            (edges, side_scalar, queries_first, other_first, prev_first, low_block, high_block, next_first),
            scalars=2,
            scratch=[pltpu.VMEM((4 * rows, HEAD_DIM), BF16)] * 2,
            cost=(12 * rows * rows * width, 16 * rows * width),
        )
        return keep_first, seq_swap(send_first, 0)

    both_second = jnp.concatenate([keys_second, values_second])

    if halving:
        turns = len(bits)
        keeps, found = halving_start([gradients[:2], gradients[2:]], orders)
        for turn in range(1, turns):
            if turn == turns - 1:
                prev_first, next_first = first_halos(*after((low_block, high_block), found))
                prev_second = seq_shift(after(both_second, found), 1)
            keeps, found = halving_step(keeps, found, orders, turn)
        held = [((keep.astype(F32) + new.astype(F32)).astype(BF16),) for keep, new in zip(keeps, found)]
        for turn in reversed(range(turns)):
            wait = ()
            if turn == 1:
                wait = (prev_first, next_first, prev_second)
            if turn == 0:
                keep_first, back_first = first_attention(prev_first, next_first)
                wait = (keep_first,)
            held = doubling_step(held, orders, turn, wait)
        gathered = [part for parts in held for part in parts]
        next_second = seq_shift(after(both_second, (gathered, back_first)), -1)
    else:
        gathered = lax.psum(gradients, "seq")
        keep_first, back_first = first_attention(*first_halos(low_block, high_block))
        prev_second, next_second = seq_shift(both_second, 1), seq_shift(both_second, -1)
    fast_query = call(
        query_kernel,
        shape((rows, fast_width), BF16),
        (side_scalar, keep_first, back_first, input_map[0]),
        scalars=1,
    )

    own_rows = hidden_size >> len(orders[0])
    own_new, fast_out = call(
        functools.partial(renew_kernel, orders),
        [shape((3, own_rows, fast_width), BF16), shape((rows, fast_width), BF16)],
        (place, weights, fast_query, *gathered),
        scalars=1,
        scratch=[pltpu.VMEM(weights.shape, BF16)],
    )
    if not halving:
        share_rows = hidden_size // seq_count
        own_new = lax.dynamic_slice_in_dim(own_new, seq_place * share_rows, share_rows, 1)

    def mixed_for(low_bit):
        far = (head_place // 2) ^ 1
        near = head_place // 2
        places = jnp.stack([far * 2 + low_bit, near * 2 + low_bit]).reshape(1, 2)
        return call(
            mix_kernel,
            shape((2, rows, width), BF16),
            (places, fast_out, output_map),
            scalars=1,
        )

    my_bit = head_place % 2
    near_part = head_swap(mixed_for(1 - my_bit), 1)
    keep_part = mixed_for(my_bit)
    to_send = (keep_part[0].astype(F32) + near_part[0].astype(F32)).astype(BF16)
    far_part = head_swap(to_send, 2)

    normed_second = call(
        second_kernel,
        shape((rows, width), BF16),
        (edges, queries_second, keep_part, near_part, far_part,
         prev_second, keys_second, values_second, next_second),
        scalars=1,
        cost=(12 * rows * rows * width, 16 * rows * width),
    )
    return (normed_second, jnp.transpose(own_new, (1, 0, 2))[None])


def solution(mesh):
    return jax.shard_map(
        local,
        mesh=mesh,
        in_specs=(
            P("seq", "head"),
            P("seq", "head"),
            P("seq", "head"),
            P("head", None, None),
            P("seq", "head"),
            P("seq", "head"),
            P("seq", "head"),
            P("head", None, None, None),
            P("head", None),
            P("seq", "head"),
            P("seq", "head"),
            P("seq", "head"),
        ),
        out_specs=(P("seq", "head"), P("head", "seq", None, None)),
        check_vma=False,
    )
```

```python
import functools
import math

import jax
import jax.numpy as jnp
from jax import lax
from jax.experimental import pallas as pl
from jax.experimental.pallas import tpu as pltpu
from jax.sharding import PartitionSpec as P

HALF_WIN = 512
HEAD_DIM = 128
HEADS_GRP = 2
FAST_DIM = 512
FAST_HIDDEN = 512
TILE = 128
VMEM_LIMIT = 24 * 1024 * 1024
VMEM_MOST = 60 * 1024 * 1024

BF16 = jnp.bfloat16
F32 = jnp.float32
INVERSE = 1.0 / math.sqrt(FAST_DIM)


def dot_nn(left, right):
    return lax.dot_general(left, right, (((1,), (0,)), ((), ())), preferred_element_type=F32)


def dot_nt(left, right):
    return lax.dot_general(left, right, (((1,), (1,)), ((), ())), preferred_element_type=F32)


def call(body, out_shapes, operands, scalars=0, anywhere=0, scratch=(), cost=None, limit=VMEM_LIMIT):
    vmem = pl.BlockSpec(memory_space=pltpu.VMEM)
    in_specs = (
        [pl.BlockSpec(memory_space=pltpu.SMEM)] * scalars
        + [vmem] * (len(operands) - scalars - anywhere)
        + [pl.BlockSpec(memory_space=pl.ANY)] * anywhere
    )
    flops, moved = cost or (1000, 1000)
    return pl.pallas_call(
        body,
        out_shape=out_shapes,
        in_specs=in_specs,
        out_specs=jax.tree.map(lambda _: vmem, out_shapes),
        scratch_shapes=scratch,
        compiler_params=pltpu.CompilerParams(vmem_limit_bytes=limit),
        cost_estimate=pl.CostEstimate(flops=flops, bytes_accessed=moved, transcendentals=0),
    )(*operands)


def slot_of(block, order):
    slot = 0
    for bit in order:
        slot = slot * 2 + ((block >> bit) & 1)
    return slot


def gradient_kernel(orders, place_ref, rates_ref, keys_ref, values_ref, weights_ref, *refs):
    out_refs, chunk_refs = refs[:-2], refs[-2:]
    place = place_ref[0, 0]
    rates = rates_ref[...]
    keys = keys_ref[...]
    values = values_ref[...]
    hidden_size = chunk_refs[0].shape[0]
    width = weights_ref.shape[2]
    turn = pl.program_id(0)
    step = weights_ref.shape[1]

    def put(chunk, columns, product):
        order = orders[chunk]
        block_rows = min(step, hidden_size >> len(order))
        for start in range(0, step, block_rows):
            row = turn * step + start
            if order:
                block = turn * (step // block_rows) + start // block_rows
                row = slot_of(block ^ place, order) * block_rows
            row = pl.multiple_of(row, block_rows)
            chunk_refs[chunk][pl.ds(row, block_rows), columns] = product[start:start + block_rows]

    gate = dot_nt(weights_ref[0], keys) * INVERSE
    up = dot_nt(weights_ref[1], keys) * INVERSE
    sigmoid = jax.nn.sigmoid(gate)
    silu = gate * sigmoid
    hidden = (rates * silu * up).astype(BF16)
    backward = rates * dot_nt(weights_ref[2], values)
    d_gate = (backward * up * sigmoid * (1.0 + gate * (1.0 - sigmoid)) * INVERSE).astype(BF16)
    d_up = (backward * silu * INVERSE).astype(BF16)
    up_part = dot_nn(d_up, keys).astype(BF16)
    put(0, slice(0, width), dot_nn(d_gate, keys).astype(BF16))
    put(0, slice(width, width + width // 2), up_part[:, :width // 2])
    put(1, slice(0, width), dot_nn(hidden, values).astype(BF16))
    put(1, slice(width, width + width // 2), up_part[:, width // 2:])

    @pl.when(turn == pl.num_programs(0) - 1)
    def _():
        halves = len(out_refs) // 2
        half_rows = hidden_size // halves
        for index, out_ref in enumerate(out_refs):
            half = index % halves
            out_ref[...] = chunk_refs[index // halves][half * half_rows:(half + 1) * half_rows, :]


def attend_rows(edge_prev, edge_next, query_tile, keys_prev, keys_own, keys_next,
                values_prev, values_own, values_next):
    scale = 1.0 / math.sqrt(HEAD_DIM)
    row = lax.broadcasted_iota(jnp.int32, (TILE, TILE), 0)
    col = lax.broadcasted_iota(jnp.int32, (TILE, TILE), 1)
    minus = jnp.float32(-jnp.inf)
    score_prev = dot_nt(query_tile, keys_prev)
    score_own = dot_nt(query_tile, keys_own)
    score_next = dot_nt(query_tile, keys_next)
    parts = [score_prev[:, :TILE] + jnp.where(col >= row, edge_prev, minus)]
    if score_prev.shape[1] > TILE:
        parts.append(score_prev[:, TILE:] + edge_prev)
    parts.append(score_own)
    if score_next.shape[1] > TILE:
        parts.append(score_next[:, :-TILE] + edge_next)
    parts.append(score_next[:, -TILE:] + jnp.where(col <= row, edge_next, minus))
    scores = jnp.concatenate(parts, axis=1)
    highest = jnp.max(scores, axis=1, keepdims=True)
    weights = jnp.exp((scores - highest) * scale)
    total = jnp.sum(weights, axis=1, keepdims=True)
    weights = weights.astype(BF16)
    width_prev, width_own = score_prev.shape[1], score_own.shape[1]
    attended = (
        dot_nn(weights[:, :width_prev], values_prev)
        + dot_nn(weights[:, width_prev:width_prev + width_own], values_own)
        + dot_nn(weights[:, width_prev + width_own:], values_next)
    )
    return attended / total


def pack_kernel(side_ref, queries_ref, keys_ref, values_ref, out_ref):
    count = queries_ref.shape[0]
    start = pl.multiple_of((1 - side_ref[0, 0]) * HEAD_DIM, HEAD_DIM)
    for index, ref in enumerate((queries_ref, keys_ref, values_ref)):
        out_ref[index * count:(index + 1) * count, :] = ref[:, pl.ds(start, HEAD_DIM)]


def border_kernel(side_ref, keys_ref, values_ref, other_ref, low_ref, high_ref):
    count = keys_ref.shape[0]
    side = side_ref[0, 0]
    start = pl.multiple_of(side * HEAD_DIM, HEAD_DIM)

    def fill(own_ref, other_out_ref):
        own_ref[:count, :] = keys_ref[:, pl.ds(start, HEAD_DIM)]
        own_ref[count:, :] = values_ref[:, pl.ds(start, HEAD_DIM)]
        other_out_ref[...] = other_ref[count:, :]

    @pl.when(side == 0)
    def _():
        fill(low_ref, high_ref)

    @pl.when(side != 0)
    def _():
        fill(high_ref, low_ref)


def first_kernel(edge_ref, side_ref, queries_ref, other_ref, prev_ref, low_ref, high_ref, next_ref,
                 keep_ref, send_ref, keys_ref, values_ref):
    count = queries_ref.shape[0]
    side = side_ref[0, 0]
    for index, ref in enumerate((prev_ref, low_ref, high_ref, next_ref)):
        rows = slice(index * count, (index + 1) * count)
        keys_ref[rows, :] = ref[:count, :]
        values_ref[rows, :] = ref[count:, :]
    start = pl.multiple_of(side * HEAD_DIM, HEAD_DIM)
    for turn, out_ref in enumerate((keep_ref, send_ref)):
        base = (side if turn == 0 else 1 - side) * count

        def span(ref, low, length):
            return ref[pl.ds(pl.multiple_of(base + low, TILE), length), :]

        for index in range(count // TILE):
            low, high = index * TILE, (index + 1) * TILE
            query = queries_ref[low:high, pl.ds(start, HEAD_DIM)] if turn == 0 else other_ref[low:high, :]
            out_ref[low:high, :] = attend_rows(
                edge_ref[turn, 0], edge_ref[turn, 1], query,
                span(keys_ref, low, count - low), span(keys_ref, count, count),
                span(keys_ref, 2 * count, high),
                span(values_ref, low, count - low), span(values_ref, count, count),
                span(values_ref, 2 * count, high),
            ).astype(BF16)


def query_kernel(side_ref, keep_ref, other_ref, map_ref, out_ref):
    side = side_ref[0, 0]
    own = keep_ref[...].astype(F32)
    other = other_ref[...].astype(F32)
    square = jnp.sum(own * own + other * other, axis=1, keepdims=True)
    norm = lax.rsqrt(square / (HEADS_GRP * HEAD_DIM) + 1e-05)
    own_map = map_ref[pl.ds(pl.multiple_of(side * HEAD_DIM, HEAD_DIM), HEAD_DIM), :]
    other_map = map_ref[pl.ds(pl.multiple_of((1 - side) * HEAD_DIM, HEAD_DIM), HEAD_DIM), :]
    out_ref[...] = (
        dot_nn((own * norm).astype(BF16), own_map) + dot_nn((other * norm).astype(BF16), other_map)
    ).astype(BF16)


def second_kernel(edge_ref, queries_ref, keep_ref, near_ref, far_ref, prev_ref, keys_ref, values_ref, next_ref,
                  out_ref):
    count = keys_ref.shape[0]
    for index in range(count // TILE):
        low, high = index * TILE, (index + 1) * TILE
        rows = slice(low, high)
        mixed = (
            keep_ref[1, rows, :].astype(F32)
            + near_ref[1, rows, :].astype(F32)
            + far_ref[rows, :].astype(F32)
        )
        query = (queries_ref[rows, :].astype(F32) + mixed).astype(BF16)
        heads = []
        for head in range(HEADS_GRP):
            cols = slice(head * HEAD_DIM, (head + 1) * HEAD_DIM)
            heads.append(
                attend_rows(
                    edge_ref[0, 0], edge_ref[0, 1], query[:, cols],
                    prev_ref[low:count, cols], keys_ref[:, cols], next_ref[:high, cols],
                    prev_ref[count + low:, cols], values_ref[:, cols], next_ref[count:count + high, cols],
                )
            )
        both = jnp.concatenate(heads, axis=1)
        mean = jnp.mean(both * both, axis=1, keepdims=True)
        out_ref[rows, :] = (both * lax.rsqrt(mean + 1e-05)).astype(BF16)


def renew_kernel(orders, place_ref, weights_ref, query_ref, *refs):
    pieces, (own_ref, fast_ref, new_ref) = refs[:-3], refs[-3:]
    place = place_ref[0, 0]
    hidden_size, width = weights_ref.shape[1:]
    limit_norm = math.sqrt(FAST_HIDDEN * FAST_DIM) / 2.0
    step = 64
    square = jnp.zeros((1, pieces[0].shape[1]), F32)
    for piece in pieces:
        for low in range(0, piece.shape[0], step):
            part = piece[low:low + step, :].astype(F32)
            square = square + jnp.sum(part * part, axis=0, keepdims=True)
    square = jnp.sum(square, axis=1, keepdims=True)
    factor = jnp.minimum(1.0, limit_norm * lax.rsqrt(square + 1e-06))
    per_chunk = len(pieces) // 2
    piece_rows = pieces[0].shape[0]
    blocks = 1 << len(orders[0])
    block_rows = hidden_size // blocks
    count = min(step, block_rows)
    for block in range(blocks):
        starts = [slot_of(block, order) * block_rows for order in orders]
        for low in range(0, block_rows, count):
            found = []
            for chunk, start in enumerate(starts):
                piece = pieces[chunk * per_chunk + start // piece_rows]
                inside = start % piece_rows + low
                found.append(piece[inside:inside + count, :].astype(F32))
            parts = [
                found[0][:, :width],
                jnp.concatenate([found[0][:, width:], found[1][:, width:]], axis=1),
                found[1][:, :width],
            ]
            rows = slice(low, low + count)
            if blocks > 1:
                rows = pl.ds(pl.multiple_of((block ^ place) * block_rows + low, count), count)
            for matrix, part in enumerate(parts):
                old = weights_ref[matrix, rows, :].astype(F32)
                stepped = old + factor * part
                norm = jnp.sqrt(jnp.sum(old * old, axis=1, keepdims=True))
                size = jnp.sum(stepped * stepped, axis=1, keepdims=True)
                fresh = (stepped * norm * lax.rsqrt(size + 1e-06)).astype(BF16)
                new_ref[matrix, rows, :] = fresh
                if block == 0:
                    own_ref[matrix, low:low + count, :] = fresh
    step = 128
    for low in range(0, query_ref.shape[0], step):
        rows = slice(low, low + step)
        query = query_ref[rows, :]
        gate = dot_nt(query, new_ref[0]) * INVERSE
        up = dot_nt(query, new_ref[1]) * INVERSE
        hidden = (jax.nn.silu(gate) * up).astype(BF16)
        raw = dot_nn(hidden, new_ref[2])
        mean = jnp.mean(raw * raw, axis=1, keepdims=True)
        fast_ref[rows, :] = (raw * lax.rsqrt(mean + 1e-05)).astype(BF16)


def mix_kernel(place_ref, fast_ref, map_ref, out_ref):
    width = out_ref.shape[2]
    for slot in range(2):
        start = pl.multiple_of(place_ref[0, slot] * width, width)
        columns = map_ref[:, pl.ds(start, width)]
        out_ref[slot] = dot_nn(fast_ref[...], columns).astype(BF16)


def seq_shift(value, step):
    peers = lax.axis_size("seq")
    return lax.ppermute(
        value, "seq", [(i, i + step) for i in range(peers) if 0 <= i + step < peers]
    )


def head_swap(value, bit):
    return lax.ppermute(value, "head", [(i, i ^ bit) for i in range(lax.axis_size("head"))])


def seq_swap(value, bit):
    step = 1 << bit
    return lax.ppermute(value, "seq", [(i, i ^ step) for i in range(lax.axis_size("seq"))])


def after(value, others):
    return lax.optimization_barrier((value, others))[0]


def halving_start(chunks, orders):
    keeps = [keep for keep, _ in chunks]
    return keeps, [seq_swap(send, order[0]) for (_, send), order in zip(chunks, orders)]


def halving_step(keeps, found, orders, turn, wait=()):
    sends, rest = [], []
    for keep, new in zip(keeps, found):
        half = keep.shape[0] // 2
        sends.append((keep[half:].astype(F32) + new[half:].astype(F32)).astype(BF16))
        rest.append(lax.optimization_barrier(keep[:half].astype(F32) + new[:half].astype(F32)))
    sends = after(sends, wait) if wait else sends
    return rest, [seq_swap(send, order[turn]) for send, order in zip(sends, orders)]


def doubling_step(held, orders, turn, wait=()):
    whole = [jnp.concatenate(parts) if len(parts) > 1 else parts[0] for parts in held]
    whole = after(whole, wait) if wait else whole
    return [(own, seq_swap(own, order[turn])) for own, order in zip(whole, orders)]


def local(
    queries_first,
    keys_first,
    values_first,
    input_map,
    fast_keys,
    fast_values,
    step_rates,
    fast_weights,
    output_map,
    queries_second,
    keys_second,
    values_second,
):
    rows, width = queries_first.shape
    seq_count = lax.axis_size("seq")
    seq_place = lax.axis_index("seq")
    head_place = lax.axis_index("head")
    weights = jnp.transpose(fast_weights[0], (1, 0, 2))
    hidden_size, fast_width = weights.shape[1:]
    shape = jax.ShapeDtypeStruct
    minus = jnp.float32(-jnp.inf)
    side = seq_place % 2

    def edges_of(block):
        return [jnp.where(block > 0, 0.0, minus), jnp.where(block < seq_count - 1, 0.0, minus)]

    edges = jnp.stack(edges_of(seq_place) + edges_of(seq_place ^ 1)).reshape(2, 2)
    side_scalar = side.astype(jnp.int32).reshape(1, 1)
    place = seq_place.astype(jnp.int32).reshape(1, 1)

    packed = call(
        pack_kernel,
        shape((3 * rows, HEAD_DIM), BF16),
        (side_scalar, queries_first, keys_first, values_first),
        scalars=1,
    )
    other_first = seq_swap(packed, 0)

    bits = tuple(range(seq_count.bit_length() - 1))
    halving = seq_count == 1 << len(bits) and len(bits) > 1 and hidden_size >> len(bits) >= 16
    orders = (bits, bits[1:] + bits[:1]) if halving else ((), ())
    halves = 2 if halving else 1
    chunk_width = fast_width + fast_width // 2
    out_shapes = [shape((hidden_size // halves, chunk_width), BF16)] * (2 * halves)
    whole = pl.BlockSpec(memory_space=pltpu.VMEM)
    gradients = pl.pallas_call(
        functools.partial(gradient_kernel, orders),
        grid=(hidden_size // TILE,),
        out_shape=out_shapes,
        in_specs=[
            pl.BlockSpec(memory_space=pltpu.SMEM),
            whole,
            whole,
            whole,
            pl.BlockSpec((3, TILE, fast_width), lambda turn: (0, turn, 0)),
        ],
        out_specs=[whole] * len(out_shapes),
        scratch_shapes=[pltpu.VMEM((hidden_size, chunk_width), BF16)] * 2,
        compiler_params=pltpu.CompilerParams(vmem_limit_bytes=VMEM_MOST),
        cost_estimate=pl.CostEstimate(flops=1000, bytes_accessed=1000, transcendentals=0),
    )(place, step_rates.reshape(1, rows), fast_keys, fast_values, weights)

    low_block, high_block = call(
        border_kernel,
        [shape((2 * rows, HEAD_DIM), BF16)] * 2,
        (side_scalar, keys_first, values_first, other_first),
        scalars=1,
    )

    def first_halos(low_block, high_block):
        return seq_shift(high_block, 2), seq_shift(low_block, -2)

    def first_attention(prev_first, next_first):
        keep_first, send_first = call(
            first_kernel,
            [shape((rows, HEAD_DIM), BF16)] * 2,
            (edges, side_scalar, queries_first, other_first, prev_first, low_block, high_block, next_first),
            scalars=2,
            scratch=[pltpu.VMEM((4 * rows, HEAD_DIM), BF16)] * 2,
            cost=(12 * rows * rows * width, 16 * rows * width),
        )
        return keep_first, seq_swap(send_first, 0)

    both_second = jnp.concatenate([keys_second, values_second])

    if halving:
        turns = len(bits)
        keeps, found = halving_start([gradients[:2], gradients[2:]], orders)
        for turn in range(1, turns):
            if turn == turns - 1:
                prev_first, next_first = first_halos(*after((low_block, high_block), found))
                both_second = after(both_second, found)
                prev_second, next_second = seq_shift(both_second, 1), seq_shift(both_second, -1)
            keeps, found = halving_step(keeps, found, orders, turn)
        held = [((keep.astype(F32) + new.astype(F32)).astype(BF16),) for keep, new in zip(keeps, found)]
        for turn in reversed(range(turns)):
            wait = ()
            if turn == 1:
                wait = (prev_first, next_first, prev_second, next_second)
            if turn == 0:
                keep_first, back_first = first_attention(prev_first, next_first)
                wait = (keep_first,)
            held = doubling_step(held, orders, turn, wait)
        gathered = [part for parts in held for part in parts]
    else:
        gathered = lax.psum(gradients, "seq")
        keep_first, back_first = first_attention(*first_halos(low_block, high_block))
        prev_second, next_second = seq_shift(both_second, 1), seq_shift(both_second, -1)
    fast_query = call(
        query_kernel,
        shape((rows, fast_width), BF16),
        (side_scalar, keep_first, back_first, input_map[0]),
        scalars=1,
    )

    own_rows = hidden_size >> len(orders[0])
    own_new, fast_out = call(
        functools.partial(renew_kernel, orders),
        [shape((3, own_rows, fast_width), BF16), shape((rows, fast_width), BF16)],
        (place, weights, fast_query, *gathered),
        scalars=1,
        scratch=[pltpu.VMEM(weights.shape, BF16)],
    )
    if not halving:
        share_rows = hidden_size // seq_count
        own_new = lax.dynamic_slice_in_dim(own_new, seq_place * share_rows, share_rows, 1)

    def mixed_for(low_bit):
        far = (head_place // 2) ^ 1
        near = head_place // 2
        places = jnp.stack([far * 2 + low_bit, near * 2 + low_bit]).reshape(1, 2)
        return call(
            mix_kernel,
            shape((2, rows, width), BF16),
            (places, fast_out, output_map),
            scalars=1,
        )

    my_bit = head_place % 2
    near_part = head_swap(mixed_for(1 - my_bit), 1)
    keep_part = mixed_for(my_bit)
    to_send = (keep_part[0].astype(F32) + near_part[0].astype(F32)).astype(BF16)
    far_part = head_swap(to_send, 2)

    normed_second = call(
        second_kernel,
        shape((rows, width), BF16),
        (edges, queries_second, keep_part, near_part, far_part,
         prev_second, keys_second, values_second, next_second),
        scalars=1,
        cost=(12 * rows * rows * width, 16 * rows * width),
    )
    return (normed_second, jnp.transpose(own_new, (1, 0, 2))[None])


def solution(mesh):
    return jax.shard_map(
        local,
        mesh=mesh,
        in_specs=(
            P("seq", "head"),
            P("seq", "head"),
            P("seq", "head"),
            P("head", None, None),
            P("seq", "head"),
            P("seq", "head"),
            P("seq", "head"),
            P("head", None, None, None),
            P("head", None),
            P("seq", "head"),
            P("seq", "head"),
            P("seq", "head"),
        ),
        out_specs=(P("seq", "head"), P("head", "seq", None, None)),
        check_vma=False,
    )
```

```python
import functools
import math

import jax
import jax.numpy as jnp
from jax import lax
from jax.experimental import pallas as pl
from jax.experimental.pallas import tpu as pltpu
from jax.sharding import PartitionSpec as P

HALF_WIN = 512
HEAD_DIM = 128
HEADS_GRP = 2
FAST_DIM = 512
FAST_HIDDEN = 512
TILE = 128
VMEM_LIMIT = 24 * 1024 * 1024
VMEM_MOST = 60 * 1024 * 1024

BF16 = jnp.bfloat16
F32 = jnp.float32
INVERSE = 1.0 / math.sqrt(FAST_DIM)


def dot_nn(left, right):
    return lax.dot_general(left, right, (((1,), (0,)), ((), ())), preferred_element_type=F32)


def dot_nt(left, right):
    return lax.dot_general(left, right, (((1,), (1,)), ((), ())), preferred_element_type=F32)


def call(body, out_shapes, operands, scalars=0, anywhere=0, scratch=(), cost=None, limit=VMEM_LIMIT):
    vmem = pl.BlockSpec(memory_space=pltpu.VMEM)
    in_specs = (
        [pl.BlockSpec(memory_space=pltpu.SMEM)] * scalars
        + [vmem] * (len(operands) - scalars - anywhere)
        + [pl.BlockSpec(memory_space=pl.ANY)] * anywhere
    )
    flops, moved = cost or (1000, 1000)
    return pl.pallas_call(
        body,
        out_shape=out_shapes,
        in_specs=in_specs,
        out_specs=jax.tree.map(lambda _: vmem, out_shapes),
        scratch_shapes=scratch,
        compiler_params=pltpu.CompilerParams(vmem_limit_bytes=limit),
        cost_estimate=pl.CostEstimate(flops=flops, bytes_accessed=moved, transcendentals=0),
    )(*operands)


def slot_of(block, order):
    slot = 0
    for bit in order:
        slot = slot * 2 + ((block >> bit) & 1)
    return slot


def gradient_kernel(orders, place_ref, rates_ref, keys_ref, values_ref, weights_ref, *refs):
    out_refs, chunk_refs = refs[:-2], refs[-2:]
    place = place_ref[0, 0]
    rates = rates_ref[...]
    keys = keys_ref[...]
    values = values_ref[...]
    hidden_size = chunk_refs[0].shape[0]
    width = weights_ref.shape[2]
    turn = pl.program_id(0)
    step = weights_ref.shape[1]

    def put(chunk, columns, product):
        order = orders[chunk]
        block_rows = min(step, hidden_size >> len(order))
        for start in range(0, step, block_rows):
            row = turn * step + start
            if order:
                block = turn * (step // block_rows) + start // block_rows
                row = slot_of(block ^ place, order) * block_rows
            row = pl.multiple_of(row, block_rows)
            chunk_refs[chunk][pl.ds(row, block_rows), columns] = product[start:start + block_rows]

    gate = dot_nt(weights_ref[0], keys) * INVERSE
    up = dot_nt(weights_ref[1], keys) * INVERSE
    sigmoid = jax.nn.sigmoid(gate)
    silu = gate * sigmoid
    hidden = (rates * silu * up).astype(BF16)
    backward = rates * dot_nt(weights_ref[2], values)
    d_gate = (backward * up * sigmoid * (1.0 + gate * (1.0 - sigmoid)) * INVERSE).astype(BF16)
    d_up = (backward * silu * INVERSE).astype(BF16)
    up_part = dot_nn(d_up, keys).astype(BF16)
    put(0, slice(0, width), dot_nn(d_gate, keys).astype(BF16))
    put(0, slice(width, width + width // 2), up_part[:, :width // 2])
    put(1, slice(0, width), dot_nn(hidden, values).astype(BF16))
    put(1, slice(width, width + width // 2), up_part[:, width // 2:])

    @pl.when(turn == pl.num_programs(0) - 1)
    def _():
        halves = len(out_refs) // 2
        half_rows = hidden_size // halves
        for index, out_ref in enumerate(out_refs):
            half = index % halves
            out_ref[...] = chunk_refs[index // halves][half * half_rows:(half + 1) * half_rows, :]


def attend_rows(edge_prev, edge_next, query_tile, keys_prev, keys_own, keys_next,
                values_prev, values_own, values_next):
    scale = 1.0 / math.sqrt(HEAD_DIM)
    row = lax.broadcasted_iota(jnp.int32, (TILE, TILE), 0)
    col = lax.broadcasted_iota(jnp.int32, (TILE, TILE), 1)
    minus = jnp.float32(-jnp.inf)
    score_prev = dot_nt(query_tile, keys_prev)
    score_own = dot_nt(query_tile, keys_own)
    score_next = dot_nt(query_tile, keys_next)
    parts = [score_prev[:, :TILE] + jnp.where(col >= row, edge_prev, minus)]
    if score_prev.shape[1] > TILE:
        parts.append(score_prev[:, TILE:] + edge_prev)
    parts.append(score_own)
    if score_next.shape[1] > TILE:
        parts.append(score_next[:, :-TILE] + edge_next)
    parts.append(score_next[:, -TILE:] + jnp.where(col <= row, edge_next, minus))
    scores = jnp.concatenate(parts, axis=1)
    highest = jnp.max(scores, axis=1, keepdims=True)
    weights = jnp.exp((scores - highest) * scale)
    total = jnp.sum(weights, axis=1, keepdims=True)
    weights = weights.astype(BF16)
    width_prev, width_own = score_prev.shape[1], score_own.shape[1]
    attended = (
        dot_nn(weights[:, :width_prev], values_prev)
        + dot_nn(weights[:, width_prev:width_prev + width_own], values_own)
        + dot_nn(weights[:, width_prev + width_own:], values_next)
    )
    return attended / total


def pack_kernel(side_ref, queries_ref, keys_ref, values_ref, out_ref):
    count = queries_ref.shape[0]
    start = pl.multiple_of((1 - side_ref[0, 0]) * HEAD_DIM, HEAD_DIM)
    for index, ref in enumerate((queries_ref, keys_ref, values_ref)):
        out_ref[index * count:(index + 1) * count, :] = ref[:, pl.ds(start, HEAD_DIM)]


def border_kernel(side_ref, keys_ref, values_ref, other_ref, low_ref, high_ref):
    count = keys_ref.shape[0]
    side = side_ref[0, 0]
    start = pl.multiple_of(side * HEAD_DIM, HEAD_DIM)

    def fill(own_ref, other_out_ref):
        own_ref[:count, :] = keys_ref[:, pl.ds(start, HEAD_DIM)]
        own_ref[count:, :] = values_ref[:, pl.ds(start, HEAD_DIM)]
        other_out_ref[...] = other_ref[count:, :]

    @pl.when(side == 0)
    def _():
        fill(low_ref, high_ref)

    @pl.when(side != 0)
    def _():
        fill(high_ref, low_ref)


def first_kernel(edge_ref, side_ref, queries_ref, other_ref, prev_ref, low_ref, high_ref, next_ref,
                 keep_ref, send_ref, keys_ref, values_ref):
    count = queries_ref.shape[0]
    side = side_ref[0, 0]
    for index, ref in enumerate((prev_ref, low_ref, high_ref, next_ref)):
        rows = slice(index * count, (index + 1) * count)
        keys_ref[rows, :] = ref[:count, :]
        values_ref[rows, :] = ref[count:, :]
    start = pl.multiple_of(side * HEAD_DIM, HEAD_DIM)
    for turn, out_ref in enumerate((keep_ref, send_ref)):
        base = (side if turn == 0 else 1 - side) * count

        def span(ref, low, length):
            return ref[pl.ds(pl.multiple_of(base + low, TILE), length), :]

        for index in range(count // TILE):
            low, high = index * TILE, (index + 1) * TILE
            query = queries_ref[low:high, pl.ds(start, HEAD_DIM)] if turn == 0 else other_ref[low:high, :]
            out_ref[low:high, :] = attend_rows(
                edge_ref[turn, 0], edge_ref[turn, 1], query,
                span(keys_ref, low, count - low), span(keys_ref, count, count),
                span(keys_ref, 2 * count, high),
                span(values_ref, low, count - low), span(values_ref, count, count),
                span(values_ref, 2 * count, high),
            ).astype(BF16)


def query_kernel(side_ref, keep_ref, other_ref, map_ref, out_ref):
    side = side_ref[0, 0]
    own = keep_ref[...].astype(F32)
    other = other_ref[...].astype(F32)
    square = jnp.sum(own * own + other * other, axis=1, keepdims=True)
    norm = lax.rsqrt(square / (HEADS_GRP * HEAD_DIM) + 1e-05)
    own_map = map_ref[pl.ds(pl.multiple_of(side * HEAD_DIM, HEAD_DIM), HEAD_DIM), :]
    other_map = map_ref[pl.ds(pl.multiple_of((1 - side) * HEAD_DIM, HEAD_DIM), HEAD_DIM), :]
    out_ref[...] = (
        dot_nn((own * norm).astype(BF16), own_map) + dot_nn((other * norm).astype(BF16), other_map)
    ).astype(BF16)


def second_kernel(edge_ref, queries_ref, keep_ref, near_ref, far_ref, prev_ref, keys_ref, values_ref, next_ref,
                  *refs):
    done_refs, out_ref = refs[:-1], refs[-1]
    count = keys_ref.shape[0]
    half = far_ref.shape[0]
    offset = half if done_refs else 0
    if done_refs:
        out_ref[:half, :] = done_refs[0][...]
    for low in range(offset, offset + half, TILE):
        high = low + TILE
        rows = slice(low, high)
        mixed = (
            keep_ref[rows, :].astype(F32)
            + near_ref[rows, :].astype(F32)
            + far_ref[low - offset:high - offset, :].astype(F32)
        )
        query = (queries_ref[rows, :].astype(F32) + mixed).astype(BF16)
        heads = []
        for head in range(HEADS_GRP):
            cols = slice(head * HEAD_DIM, (head + 1) * HEAD_DIM)
            heads.append(
                attend_rows(
                    edge_ref[0, 0], edge_ref[0, 1], query[:, cols],
                    prev_ref[low:count, cols], keys_ref[:, cols], next_ref[:high, cols],
                    prev_ref[count + low:, cols], values_ref[:, cols], next_ref[count:count + high, cols],
                )
            )
        both = jnp.concatenate(heads, axis=1)
        mean = jnp.mean(both * both, axis=1, keepdims=True)
        out_ref[rows, :] = (both * lax.rsqrt(mean + 1e-05)).astype(BF16)


def renew_kernel(orders, place_ref, places_ref, weights_ref, query_ref, map_ref, *refs):
    pieces, (own_ref, fast_ref, send_ref, keep_ref, new_ref) = refs[:-5], refs[-5:]
    place = place_ref[0, 0]
    hidden_size, width = weights_ref.shape[1:]
    limit_norm = math.sqrt(FAST_HIDDEN * FAST_DIM) / 2.0
    step = 64
    square = jnp.zeros((1, pieces[0].shape[1]), F32)
    for piece in pieces:
        for low in range(0, piece.shape[0], step):
            part = piece[low:low + step, :].astype(F32)
            square = square + jnp.sum(part * part, axis=0, keepdims=True)
    square = jnp.sum(square, axis=1, keepdims=True)
    factor = jnp.minimum(1.0, limit_norm * lax.rsqrt(square + 1e-06))
    per_chunk = len(pieces) // 2
    piece_rows = pieces[0].shape[0]
    blocks = 1 << len(orders[0])
    block_rows = hidden_size // blocks
    count = min(step, block_rows)
    for block in range(blocks):
        starts = [slot_of(block, order) * block_rows for order in orders]
        for low in range(0, block_rows, count):
            found = []
            for chunk, start in enumerate(starts):
                piece = pieces[chunk * per_chunk + start // piece_rows]
                inside = start % piece_rows + low
                found.append(piece[inside:inside + count, :].astype(F32))
            parts = [
                found[0][:, :width],
                jnp.concatenate([found[0][:, width:], found[1][:, width:]], axis=1),
                found[1][:, :width],
            ]
            rows = slice(low, low + count)
            if blocks > 1:
                rows = pl.ds(pl.multiple_of((block ^ place) * block_rows + low, count), count)
            for matrix, part in enumerate(parts):
                old = weights_ref[matrix, rows, :].astype(F32)
                stepped = old + factor * part
                norm = jnp.sqrt(jnp.sum(old * old, axis=1, keepdims=True))
                size = jnp.sum(stepped * stepped, axis=1, keepdims=True)
                fresh = (stepped * norm * lax.rsqrt(size + 1e-06)).astype(BF16)
                new_ref[matrix, rows, :] = fresh
                if block == 0:
                    own_ref[matrix, low:low + count, :] = fresh
    step = 128
    for low in range(0, query_ref.shape[0], step):
        rows = slice(low, low + step)
        query = query_ref[rows, :]
        gate = dot_nt(query, new_ref[0]) * INVERSE
        up = dot_nt(query, new_ref[1]) * INVERSE
        hidden = (jax.nn.silu(gate) * up).astype(BF16)
        raw = dot_nn(hidden, new_ref[2])
        mean = jnp.mean(raw * raw, axis=1, keepdims=True)
        fast_ref[rows, :] = (raw * lax.rsqrt(mean + 1e-05)).astype(BF16)
    mix([places_ref[0, 0], places_ref[0, 1]], fast_ref[...], map_ref, [send_ref, keep_ref])


def mix(places, fast, map_ref, out_refs):
    for place, out_ref in zip(places, out_refs):
        width = out_ref.shape[1]
        columns = map_ref[:, pl.ds(pl.multiple_of(place * width, width), width)]
        out_ref[...] = dot_nn(fast, columns).astype(BF16)


def mix_kernel(places_ref, fast_ref, map_ref, *out_refs):
    mix([places_ref[0, 2], places_ref[0, 3]], fast_ref[...], map_ref, out_refs)


def seq_shift(value, step):
    peers = lax.axis_size("seq")
    return lax.ppermute(
        value, "seq", [(i, i + step) for i in range(peers) if 0 <= i + step < peers]
    )


def head_swap(value, bit):
    return lax.ppermute(value, "head", [(i, i ^ bit) for i in range(lax.axis_size("head"))])


def seq_swap(value, bit):
    step = 1 << bit
    return lax.ppermute(value, "seq", [(i, i ^ step) for i in range(lax.axis_size("seq"))])


def after(value, others):
    return lax.optimization_barrier((value, others))[0]


def halving_start(chunks, orders):
    keeps = [keep for keep, _ in chunks]
    return keeps, [seq_swap(send, order[0]) for (_, send), order in zip(chunks, orders)]


def halving_step(keeps, found, orders, turn, wait=()):
    sends, rest = [], []
    for keep, new in zip(keeps, found):
        half = keep.shape[0] // 2
        sends.append((keep[half:].astype(F32) + new[half:].astype(F32)).astype(BF16))
        rest.append(lax.optimization_barrier(keep[:half].astype(F32) + new[:half].astype(F32)))
    sends = after(sends, wait) if wait else sends
    return rest, [seq_swap(send, order[turn]) for send, order in zip(sends, orders)]


def doubling_step(held, orders, turn, wait=()):
    whole = [jnp.concatenate(parts) if len(parts) > 1 else parts[0] for parts in held]
    whole = after(whole, wait) if wait else whole
    return [(own, seq_swap(own, order[turn])) for own, order in zip(whole, orders)]


def local(
    queries_first,
    keys_first,
    values_first,
    input_map,
    fast_keys,
    fast_values,
    step_rates,
    fast_weights,
    output_map,
    queries_second,
    keys_second,
    values_second,
):
    rows, width = queries_first.shape
    seq_count = lax.axis_size("seq")
    seq_place = lax.axis_index("seq")
    head_place = lax.axis_index("head")
    weights = jnp.transpose(fast_weights[0], (1, 0, 2))
    hidden_size, fast_width = weights.shape[1:]
    shape = jax.ShapeDtypeStruct
    minus = jnp.float32(-jnp.inf)
    side = seq_place % 2

    def edges_of(block):
        return [jnp.where(block > 0, 0.0, minus), jnp.where(block < seq_count - 1, 0.0, minus)]

    edges = jnp.stack(edges_of(seq_place) + edges_of(seq_place ^ 1)).reshape(2, 2)
    side_scalar = side.astype(jnp.int32).reshape(1, 1)
    place = seq_place.astype(jnp.int32).reshape(1, 1)

    packed = call(
        pack_kernel,
        shape((3 * rows, HEAD_DIM), BF16),
        (side_scalar, queries_first, keys_first, values_first),
        scalars=1,
    )
    other_first = seq_swap(packed, 0)

    bits = tuple(range(seq_count.bit_length() - 1))
    halving = seq_count == 1 << len(bits) and len(bits) > 1 and hidden_size >> len(bits) >= 16
    orders = (bits, bits[1:] + bits[:1]) if halving else ((), ())
    halves = 2 if halving else 1
    chunk_width = fast_width + fast_width // 2
    out_shapes = [shape((hidden_size // halves, chunk_width), BF16)] * (2 * halves)
    whole = pl.BlockSpec(memory_space=pltpu.VMEM)
    gradients = pl.pallas_call(
        functools.partial(gradient_kernel, orders),
        grid=(hidden_size // TILE,),
        out_shape=out_shapes,
        in_specs=[
            pl.BlockSpec(memory_space=pltpu.SMEM),
            whole,
            whole,
            whole,
            pl.BlockSpec((3, TILE, fast_width), lambda turn: (0, turn, 0)),
        ],
        out_specs=[whole] * len(out_shapes),
        scratch_shapes=[pltpu.VMEM((hidden_size, chunk_width), BF16)] * 2,
        compiler_params=pltpu.CompilerParams(vmem_limit_bytes=VMEM_MOST),
        cost_estimate=pl.CostEstimate(flops=1000, bytes_accessed=1000, transcendentals=0),
    )(place, step_rates.reshape(1, rows), fast_keys, fast_values, weights)

    low_block, high_block = call(
        border_kernel,
        [shape((2 * rows, HEAD_DIM), BF16)] * 2,
        (side_scalar, keys_first, values_first, other_first),
        scalars=1,
    )

    def first_halos(low_block, high_block):
        return seq_shift(high_block, 2), seq_shift(low_block, -2)

    def first_attention(prev_first, next_first):
        keep_first, send_first = call(
            first_kernel,
            [shape((rows, HEAD_DIM), BF16)] * 2,
            (edges, side_scalar, queries_first, other_first, prev_first, low_block, high_block, next_first),
            scalars=2,
            scratch=[pltpu.VMEM((4 * rows, HEAD_DIM), BF16)] * 2,
            cost=(12 * rows * rows * width, 16 * rows * width),
        )
        return keep_first, seq_swap(send_first, 0)

    both_second = jnp.concatenate([keys_second, values_second])

    if halving:
        turns = len(bits)
        keeps, found = halving_start([gradients[:2], gradients[2:]], orders)
        for turn in range(1, turns):
            if turn == turns - 1:
                prev_first, next_first = first_halos(*after((low_block, high_block), found))
                prev_second = seq_shift(after(both_second, found), 1)
            keeps, found = halving_step(keeps, found, orders, turn)
        held = [((keep.astype(F32) + new.astype(F32)).astype(BF16),) for keep, new in zip(keeps, found)]
        for turn in reversed(range(turns)):
            wait = ()
            if turn == 1:
                wait = (prev_first, next_first, prev_second)
            if turn == 0:
                keep_first, back_first = first_attention(prev_first, next_first)
                wait = (keep_first,)
            held = doubling_step(held, orders, turn, wait)
        gathered = [part for parts in held for part in parts]
        next_second = seq_shift(after(both_second, (gathered, back_first)), -1)
    else:
        gathered = lax.psum(gradients, "seq")
        keep_first, back_first = first_attention(*first_halos(low_block, high_block))
        prev_second, next_second = seq_shift(both_second, 1), seq_shift(both_second, -1)
    fast_query = call(
        query_kernel,
        shape((rows, fast_width), BF16),
        (side_scalar, keep_first, back_first, input_map[0]),
        scalars=1,
    )

    own_rows = hidden_size >> len(orders[0])
    my_bit, near = head_place % 2, head_place // 2
    places = jnp.stack(
        [2 * pair + bit for pair in (near ^ 1, near) for bit in (1 - my_bit, my_bit)]
    ).astype(jnp.int32).reshape(1, 4)
    share = shape((rows, width), BF16)
    own_new, fast_out, far_send, far_keep = call(
        functools.partial(renew_kernel, orders),
        [shape((3, own_rows, fast_width), BF16), shape((rows, fast_width), BF16), share, share],
        (place, places, weights, fast_query, output_map, *gathered),
        scalars=2,
        scratch=[pltpu.VMEM(weights.shape, BF16)],
    )
    far_near = head_swap(far_send, 1)
    near_send, near_keep = call(
        mix_kernel, [share, share], (places, fast_out, output_map), scalars=1
    )
    near_near = head_swap(near_send, 1)
    half = rows // 2
    far_parts = []
    for part in (slice(0, half), slice(half, rows)):
        far_sum = far_keep[part].astype(F32) + far_near[part].astype(F32)
        far_parts.append(head_swap(far_sum.astype(BF16), 2))
    if not halving:
        share_rows = hidden_size // seq_count
        own_new = lax.dynamic_slice_in_dim(own_new, seq_place * share_rows, share_rows, 1)

    def second_attention(part, *done):
        return call(
            second_kernel,
            shape((half * (1 + len(done)), width), BF16),
            (edges, queries_second, near_keep, near_near, far_parts[part],
             prev_second, keys_second, values_second, next_second, *done),
            scalars=1,
            cost=(6 * rows * rows * width, 16 * rows * width),
        )

    normed_second = second_attention(1, second_attention(0))
    return (normed_second, jnp.transpose(own_new, (1, 0, 2))[None])


def solution(mesh):
    return jax.shard_map(
        local,
        mesh=mesh,
        in_specs=(
            P("seq", "head"),
            P("seq", "head"),
            P("seq", "head"),
            P("head", None, None),
            P("seq", "head"),
            P("seq", "head"),
            P("seq", "head"),
            P("head", None, None, None),
            P("head", None),
            P("seq", "head"),
            P("seq", "head"),
            P("seq", "head"),
        ),
        out_specs=(P("seq", "head"), P("head", "seq", None, None)),
        check_vma=False,
    )
```

```python
import functools
import math

import jax
import jax.numpy as jnp
from jax import lax
from jax.experimental import pallas as pl
from jax.experimental.pallas import tpu as pltpu
from jax.sharding import PartitionSpec as P

HALF_WIN = 512
HEAD_DIM = 128
HEADS_GRP = 2
FAST_DIM = 512
FAST_HIDDEN = 512
TILE = 128
VMEM_LIMIT = 16 * 1024 * 1024
VMEM_MOST = 60 * 1024 * 1024

BF16 = jnp.bfloat16
F32 = jnp.float32
INVERSE = 1.0 / math.sqrt(FAST_DIM)


def dot_nn(left, right):
    return lax.dot_general(left, right, (((1,), (0,)), ((), ())), preferred_element_type=F32)


def dot_nt(left, right):
    return lax.dot_general(left, right, (((1,), (1,)), ((), ())), preferred_element_type=F32)


def call(body, out_shapes, operands, scalars=0, anywhere=0, scratch=(), cost=None, limit=VMEM_LIMIT):
    vmem = pl.BlockSpec(memory_space=pltpu.VMEM)
    in_specs = (
        [pl.BlockSpec(memory_space=pltpu.SMEM)] * scalars
        + [vmem] * (len(operands) - scalars - anywhere)
        + [pl.BlockSpec(memory_space=pl.ANY)] * anywhere
    )
    flops, moved = cost or (1000, 1000)
    return pl.pallas_call(
        body,
        out_shape=out_shapes,
        in_specs=in_specs,
        out_specs=jax.tree.map(lambda _: vmem, out_shapes),
        scratch_shapes=scratch,
        compiler_params=pltpu.CompilerParams(vmem_limit_bytes=limit),
        cost_estimate=pl.CostEstimate(flops=flops, bytes_accessed=moved, transcendentals=0),
    )(*operands)


def slot_of(block, order):
    slot = 0
    for bit in order:
        slot = slot * 2 + ((block >> bit) & 1)
    return slot


def gradient_kernel(orders, place_ref, rates_ref, keys_ref, values_ref, weights_ref, *refs):
    out_refs, chunk_refs = refs[:-2], refs[-2:]
    place = place_ref[0, 0]
    rates = rates_ref[...]
    keys = keys_ref[...]
    values = values_ref[...]
    hidden_size = chunk_refs[0].shape[0]
    width = weights_ref.shape[2]
    turn = pl.program_id(0)
    step = weights_ref.shape[1]

    def put(chunk, columns, product):
        order = orders[chunk]
        block_rows = min(step, hidden_size >> len(order))
        for start in range(0, step, block_rows):
            row = turn * step + start
            if order:
                block = turn * (step // block_rows) + start // block_rows
                row = slot_of(block ^ place, order) * block_rows
            row = pl.multiple_of(row, block_rows)
            chunk_refs[chunk][pl.ds(row, block_rows), columns] = product[start:start + block_rows]

    gate = dot_nt(weights_ref[0], keys) * INVERSE
    up = dot_nt(weights_ref[1], keys) * INVERSE
    sigmoid = jax.nn.sigmoid(gate)
    silu = gate * sigmoid
    hidden = (rates * silu * up).astype(BF16)
    backward = rates * dot_nt(weights_ref[2], values)
    d_gate = (backward * up * sigmoid * (1.0 + gate * (1.0 - sigmoid)) * INVERSE).astype(BF16)
    d_up = (backward * silu * INVERSE).astype(BF16)
    up_part = dot_nn(d_up, keys).astype(BF16)
    put(0, slice(0, width), dot_nn(d_gate, keys).astype(BF16))
    put(0, slice(width, width + width // 2), up_part[:, :width // 2])
    put(1, slice(0, width), dot_nn(hidden, values).astype(BF16))
    put(1, slice(width, width + width // 2), up_part[:, width // 2:])

    @pl.when(turn == pl.num_programs(0) - 1)
    def _():
        halves = len(out_refs) // 2
        half_rows = hidden_size // halves
        for index, out_ref in enumerate(out_refs):
            half = index % halves
            out_ref[...] = chunk_refs[index // halves][half * half_rows:(half + 1) * half_rows, :]


def attend_rows(edge_prev, edge_next, query_tile, keys_prev, keys_own, keys_next,
                values_prev, values_own, values_next):
    scale = 1.0 / math.sqrt(HEAD_DIM)
    row = lax.broadcasted_iota(jnp.int32, (TILE, TILE), 0)
    col = lax.broadcasted_iota(jnp.int32, (TILE, TILE), 1)
    minus = jnp.float32(-jnp.inf)
    score_prev = dot_nt(query_tile, keys_prev)
    score_own = dot_nt(query_tile, keys_own)
    score_next = dot_nt(query_tile, keys_next)
    parts = [score_prev[:, :TILE] + jnp.where(col >= row, edge_prev, minus)]
    if score_prev.shape[1] > TILE:
        parts.append(score_prev[:, TILE:] + edge_prev)
    parts.append(score_own)
    if score_next.shape[1] > TILE:
        parts.append(score_next[:, :-TILE] + edge_next)
    parts.append(score_next[:, -TILE:] + jnp.where(col <= row, edge_next, minus))
    scores = jnp.concatenate(parts, axis=1)
    highest = jnp.max(scores, axis=1, keepdims=True)
    weights = jnp.exp((scores - highest) * scale)
    total = jnp.sum(weights, axis=1, keepdims=True)
    weights = weights.astype(BF16)
    width_prev, width_own = score_prev.shape[1], score_own.shape[1]
    attended = (
        dot_nn(weights[:, :width_prev], values_prev)
        + dot_nn(weights[:, width_prev:width_prev + width_own], values_own)
        + dot_nn(weights[:, width_prev + width_own:], values_next)
    )
    return attended / total


def pack_kernel(side_ref, queries_ref, keys_ref, values_ref, out_ref):
    count = queries_ref.shape[0]
    start = pl.multiple_of((1 - side_ref[0, 0]) * HEAD_DIM, HEAD_DIM)
    for index, ref in enumerate((queries_ref, keys_ref, values_ref)):
        out_ref[index * count:(index + 1) * count, :] = ref[:, pl.ds(start, HEAD_DIM)]


def border_kernel(side_ref, keys_ref, values_ref, other_ref, low_ref, high_ref):
    count = keys_ref.shape[0]
    side = side_ref[0, 0]
    start = pl.multiple_of(side * HEAD_DIM, HEAD_DIM)

    def fill(own_ref, other_out_ref):
        own_ref[:count, :] = keys_ref[:, pl.ds(start, HEAD_DIM)]
        own_ref[count:, :] = values_ref[:, pl.ds(start, HEAD_DIM)]
        other_out_ref[...] = other_ref[count:, :]

    @pl.when(side == 0)
    def _():
        fill(low_ref, high_ref)

    @pl.when(side != 0)
    def _():
        fill(high_ref, low_ref)


def first_kernel(edge_ref, side_ref, queries_ref, other_ref, prev_ref, low_ref, high_ref, next_ref,
                 keep_ref, send_ref, keys_ref, values_ref):
    count = queries_ref.shape[0]
    side = side_ref[0, 0]
    for index, ref in enumerate((prev_ref, low_ref, high_ref, next_ref)):
        rows = slice(index * count, (index + 1) * count)
        keys_ref[rows, :] = ref[:count, :]
        values_ref[rows, :] = ref[count:, :]
    start = pl.multiple_of(side * HEAD_DIM, HEAD_DIM)
    for turn, out_ref in enumerate((keep_ref, send_ref)):
        base = (side if turn == 0 else 1 - side) * count

        def span(ref, low, length):
            return ref[pl.ds(pl.multiple_of(base + low, TILE), length), :]

        for index in range(count // TILE):
            low, high = index * TILE, (index + 1) * TILE
            query = queries_ref[low:high, pl.ds(start, HEAD_DIM)] if turn == 0 else other_ref[low:high, :]
            out_ref[low:high, :] = attend_rows(
                edge_ref[turn, 0], edge_ref[turn, 1], query,
                span(keys_ref, low, count - low), span(keys_ref, count, count),
                span(keys_ref, 2 * count, high),
                span(values_ref, low, count - low), span(values_ref, count, count),
                span(values_ref, 2 * count, high),
            ).astype(BF16)


def query_kernel(side_ref, keep_ref, other_ref, map_ref, out_ref):
    side = side_ref[0, 0]
    own = keep_ref[...].astype(F32)
    other = other_ref[...].astype(F32)
    square = jnp.sum(own * own + other * other, axis=1, keepdims=True)
    norm = lax.rsqrt(square / (HEADS_GRP * HEAD_DIM) + 1e-05)
    own_map = map_ref[pl.ds(pl.multiple_of(side * HEAD_DIM, HEAD_DIM), HEAD_DIM), :]
    other_map = map_ref[pl.ds(pl.multiple_of((1 - side) * HEAD_DIM, HEAD_DIM), HEAD_DIM), :]
    out_ref[...] = (
        dot_nn((own * norm).astype(BF16), own_map) + dot_nn((other * norm).astype(BF16), other_map)
    ).astype(BF16)


def second_kernel(edge_ref, queries_ref, keep_ref, near_ref, far_ref, prev_ref, keys_ref, values_ref, next_ref,
                  *refs):
    done_refs, out_ref = refs[:-1], refs[-1]
    count = keys_ref.shape[0]
    half = far_ref.shape[0]
    offset = half if done_refs else 0
    if done_refs:
        out_ref[:half, :] = done_refs[0][...]
    for low in range(offset, offset + half, TILE):
        high = low + TILE
        rows = slice(low, high)
        mixed = (
            keep_ref[rows, :].astype(F32)
            + near_ref[rows, :].astype(F32)
            + far_ref[low - offset:high - offset, :].astype(F32)
        )
        query = (queries_ref[rows, :].astype(F32) + mixed).astype(BF16)
        heads = []
        for head in range(HEADS_GRP):
            cols = slice(head * HEAD_DIM, (head + 1) * HEAD_DIM)
            heads.append(
                attend_rows(
                    edge_ref[0, 0], edge_ref[0, 1], query[:, cols],
                    prev_ref[low:count, cols], keys_ref[:, cols], next_ref[:high, cols],
                    prev_ref[count + low:, cols], values_ref[:, cols], next_ref[count:count + high, cols],
                )
            )
        both = jnp.concatenate(heads, axis=1)
        mean = jnp.mean(both * both, axis=1, keepdims=True)
        out_ref[rows, :] = (both * lax.rsqrt(mean + 1e-05)).astype(BF16)


def renew_kernel(orders, place_ref, places_ref, weights_ref, query_ref, map_ref, *refs):
    pieces, (own_ref, fast_ref, send_ref, keep_ref, new_ref) = refs[:-5], refs[-5:]
    place = place_ref[0, 0]
    hidden_size, width = weights_ref.shape[1:]
    limit_norm = math.sqrt(FAST_HIDDEN * FAST_DIM) / 2.0
    step = 64
    square = jnp.zeros((1, pieces[0].shape[1]), F32)
    for piece in pieces:
        for low in range(0, piece.shape[0], step):
            part = piece[low:low + step, :].astype(F32)
            square = square + jnp.sum(part * part, axis=0, keepdims=True)
    square = jnp.sum(square, axis=1, keepdims=True)
    factor = jnp.minimum(1.0, limit_norm * lax.rsqrt(square + 1e-06))
    per_chunk = len(pieces) // 2
    piece_rows = pieces[0].shape[0]
    blocks = 1 << len(orders[0])
    block_rows = hidden_size // blocks
    count = min(step, block_rows)
    for block in range(blocks):
        starts = [slot_of(block, order) * block_rows for order in orders]
        for low in range(0, block_rows, count):
            found = []
            for chunk, start in enumerate(starts):
                piece = pieces[chunk * per_chunk + start // piece_rows]
                inside = start % piece_rows + low
                found.append(piece[inside:inside + count, :].astype(F32))
            parts = [
                found[0][:, :width],
                jnp.concatenate([found[0][:, width:], found[1][:, width:]], axis=1),
                found[1][:, :width],
            ]
            rows = slice(low, low + count)
            if blocks > 1:
                rows = pl.ds(pl.multiple_of((block ^ place) * block_rows + low, count), count)
            for matrix, part in enumerate(parts):
                old = weights_ref[matrix, rows, :].astype(F32)
                stepped = old + factor * part
                norm = jnp.sqrt(jnp.sum(old * old, axis=1, keepdims=True))
                size = jnp.sum(stepped * stepped, axis=1, keepdims=True)
                fresh = (stepped * norm * lax.rsqrt(size + 1e-06)).astype(BF16)
                new_ref[matrix, rows, :] = fresh
                if block == 0:
                    own_ref[matrix, low:low + count, :] = fresh
    step = 128
    for low in range(0, query_ref.shape[0], step):
        rows = slice(low, low + step)
        query = query_ref[rows, :]
        gate = dot_nt(query, new_ref[0]) * INVERSE
        up = dot_nt(query, new_ref[1]) * INVERSE
        hidden = (jax.nn.silu(gate) * up).astype(BF16)
        raw = dot_nn(hidden, new_ref[2])
        mean = jnp.mean(raw * raw, axis=1, keepdims=True)
        fast_ref[rows, :] = (raw * lax.rsqrt(mean + 1e-05)).astype(BF16)
    mix([places_ref[0, 0], places_ref[0, 1]], fast_ref[...], map_ref, [send_ref, keep_ref])


def mix(places, fast, map_ref, out_refs):
    for place, out_ref in zip(places, out_refs):
        width = out_ref.shape[1]
        columns = map_ref[:, pl.ds(pl.multiple_of(place * width, width), width)]
        out_ref[...] = dot_nn(fast, columns).astype(BF16)


def mix_kernel(places_ref, fast_ref, map_ref, *out_refs):
    mix([places_ref[0, 2], places_ref[0, 3]], fast_ref[...], map_ref, out_refs)


def seq_shift(value, step):
    peers = lax.axis_size("seq")
    return lax.ppermute(
        value, "seq", [(i, i + step) for i in range(peers) if 0 <= i + step < peers]
    )


def head_swap(value, bit):
    return lax.ppermute(value, "head", [(i, i ^ bit) for i in range(lax.axis_size("head"))])


def seq_swap(value, bit):
    step = 1 << bit
    return lax.ppermute(value, "seq", [(i, i ^ step) for i in range(lax.axis_size("seq"))])


def after(value, others):
    return lax.optimization_barrier((value, others))[0]


def halving_start(chunks, orders):
    keeps = [keep for keep, _ in chunks]
    return keeps, [seq_swap(send, order[0]) for (_, send), order in zip(chunks, orders)]


def halving_step(keeps, found, orders, turn, wait=()):
    sends, rest = [], []
    for keep, new in zip(keeps, found):
        half = keep.shape[0] // 2
        sends.append((keep[half:].astype(F32) + new[half:].astype(F32)).astype(BF16))
        rest.append(lax.optimization_barrier(keep[:half].astype(F32) + new[:half].astype(F32)))
    sends = after(sends, wait) if wait else sends
    return rest, [seq_swap(send, order[turn]) for send, order in zip(sends, orders)]


def doubling_step(held, orders, turn, wait=()):
    whole = [jnp.concatenate(parts) if len(parts) > 1 else parts[0] for parts in held]
    whole = after(whole, wait) if wait else whole
    return [(own, seq_swap(own, order[turn])) for own, order in zip(whole, orders)]


def local(
    queries_first,
    keys_first,
    values_first,
    input_map,
    fast_keys,
    fast_values,
    step_rates,
    fast_weights,
    output_map,
    queries_second,
    keys_second,
    values_second,
):
    rows, width = queries_first.shape
    seq_count = lax.axis_size("seq")
    seq_place = lax.axis_index("seq")
    head_place = lax.axis_index("head")
    weights = jnp.transpose(fast_weights[0], (1, 0, 2))
    hidden_size, fast_width = weights.shape[1:]
    shape = jax.ShapeDtypeStruct
    minus = jnp.float32(-jnp.inf)
    side = seq_place % 2

    def edges_of(block):
        return [jnp.where(block > 0, 0.0, minus), jnp.where(block < seq_count - 1, 0.0, minus)]

    edges = jnp.stack(edges_of(seq_place) + edges_of(seq_place ^ 1)).reshape(2, 2)
    side_scalar = side.astype(jnp.int32).reshape(1, 1)
    place = seq_place.astype(jnp.int32).reshape(1, 1)

    packed = call(
        pack_kernel,
        shape((3 * rows, HEAD_DIM), BF16),
        (side_scalar, queries_first, keys_first, values_first),
        scalars=1,
    )
    other_first = seq_swap(packed, 0)

    bits = tuple(range(seq_count.bit_length() - 1))
    halving = seq_count == 1 << len(bits) and len(bits) > 1 and hidden_size >> len(bits) >= 16
    orders = (bits, bits[1:] + bits[:1]) if halving else ((), ())
    halves = 2 if halving else 1
    chunk_width = fast_width + fast_width // 2
    out_shapes = [shape((hidden_size // halves, chunk_width), BF16)] * (2 * halves)
    whole = pl.BlockSpec(memory_space=pltpu.VMEM)
    gradients = pl.pallas_call(
        functools.partial(gradient_kernel, orders),
        grid=(hidden_size // TILE,),
        out_shape=out_shapes,
        in_specs=[
            pl.BlockSpec(memory_space=pltpu.SMEM),
            whole,
            whole,
            whole,
            pl.BlockSpec((3, TILE, fast_width), lambda turn: (0, turn, 0)),
        ],
        out_specs=[whole] * len(out_shapes),
        scratch_shapes=[pltpu.VMEM((hidden_size, chunk_width), BF16)] * 2,
        compiler_params=pltpu.CompilerParams(vmem_limit_bytes=VMEM_MOST),
        cost_estimate=pl.CostEstimate(flops=1000, bytes_accessed=1000, transcendentals=0),
    )(place, step_rates.reshape(1, rows), fast_keys, fast_values, weights)

    low_block, high_block = call(
        border_kernel,
        [shape((2 * rows, HEAD_DIM), BF16)] * 2,
        (side_scalar, keys_first, values_first, other_first),
        scalars=1,
    )

    def first_halos(low_block, high_block):
        return seq_shift(high_block, 2), seq_shift(low_block, -2)

    def first_attention(prev_first, next_first):
        keep_first, send_first = call(
            first_kernel,
            [shape((rows, HEAD_DIM), BF16)] * 2,
            (edges, side_scalar, queries_first, other_first, prev_first, low_block, high_block, next_first),
            scalars=2,
            scratch=[pltpu.VMEM((4 * rows, HEAD_DIM), BF16)] * 2,
            cost=(12 * rows * rows * width, 16 * rows * width),
        )
        return keep_first, seq_swap(send_first, 0)

    both_second = jnp.concatenate([keys_second, values_second])

    if halving:
        turns = len(bits)
        keeps, found = halving_start([gradients[:2], gradients[2:]], orders)
        for turn in range(1, turns):
            if turn == turns - 1:
                prev_first, next_first = first_halos(*after((low_block, high_block), found))
                prev_second = seq_shift(after(both_second, found), 1)
            keeps, found = halving_step(keeps, found, orders, turn)
        held = [((keep.astype(F32) + new.astype(F32)).astype(BF16),) for keep, new in zip(keeps, found)]
        for turn in reversed(range(turns)):
            wait = ()
            if turn == 1:
                wait = (prev_first, next_first, prev_second)
            if turn == 0:
                keep_first, back_first = first_attention(prev_first, next_first)
                wait = (keep_first,)
            held = doubling_step(held, orders, turn, wait)
        gathered = [part for parts in held for part in parts]
        next_second = seq_shift(after(both_second, (gathered, back_first)), -1)
    else:
        gathered = lax.psum(gradients, "seq")
        keep_first, back_first = first_attention(*first_halos(low_block, high_block))
        prev_second, next_second = seq_shift(both_second, 1), seq_shift(both_second, -1)
    fast_query = call(
        query_kernel,
        shape((rows, fast_width), BF16),
        (side_scalar, keep_first, back_first, input_map[0]),
        scalars=1,
    )

    own_rows = hidden_size >> len(orders[0])
    my_bit, near = head_place % 2, head_place // 2
    places = jnp.stack(
        [2 * pair + bit for pair in (near ^ 1, near) for bit in (1 - my_bit, my_bit)]
    ).astype(jnp.int32).reshape(1, 4)
    share = shape((rows, width), BF16)
    own_new, fast_out, far_send, far_keep = call(
        functools.partial(renew_kernel, orders),
        [shape((3, own_rows, fast_width), BF16), shape((rows, fast_width), BF16), share, share],
        (place, places, weights, fast_query, output_map, *gathered),
        scalars=2,
        scratch=[pltpu.VMEM(weights.shape, BF16)],
    )
    far_near = head_swap(far_send, 1)
    near_send, near_keep = call(
        mix_kernel, [share, share], (places, after(fast_out, next_second), output_map), scalars=1
    )
    near_near = head_swap(near_send, 1)
    half = rows // 2
    far_parts = []
    for part in (slice(0, half), slice(half, rows)):
        far_sum = far_keep[part].astype(F32) + far_near[part].astype(F32)
        far_parts.append(head_swap(far_sum.astype(BF16), 2))
    if not halving:
        share_rows = hidden_size // seq_count
        own_new = lax.dynamic_slice_in_dim(own_new, seq_place * share_rows, share_rows, 1)

    def second_attention(part, *done):
        return call(
            second_kernel,
            shape((half * (1 + len(done)), width), BF16),
            (edges, queries_second, near_keep, near_near, far_parts[part],
             prev_second, keys_second, values_second, next_second, *done),
            scalars=1,
            cost=(6 * rows * rows * width, 16 * rows * width),
        )

    normed_second = second_attention(1, second_attention(0))
    return (normed_second, jnp.transpose(own_new, (1, 0, 2))[None])


def solution(mesh):
    return jax.shard_map(
        local,
        mesh=mesh,
        in_specs=(
            P("seq", "head"),
            P("seq", "head"),
            P("seq", "head"),
            P("head", None, None),
            P("seq", "head"),
            P("seq", "head"),
            P("seq", "head"),
            P("head", None, None, None),
            P("head", None),
            P("seq", "head"),
            P("seq", "head"),
            P("seq", "head"),
        ),
        out_specs=(P("seq", "head"), P("head", "seq", None, None)),
        check_vma=False,
    )
```

```python
import functools
import math

import jax
import jax.numpy as jnp
from jax import lax
from jax.experimental import pallas as pl
from jax.experimental.pallas import tpu as pltpu
from jax.sharding import PartitionSpec as P

HALF_WIN = 512
HEAD_DIM = 128
HEADS_GRP = 2
FAST_DIM = 512
FAST_HIDDEN = 512
TILE = 128
VMEM_LIMIT = 24 * 1024 * 1024
VMEM_MOST = 60 * 1024 * 1024

BF16 = jnp.bfloat16
F32 = jnp.float32
INVERSE = 1.0 / math.sqrt(FAST_DIM)


def dot_nn(left, right):
    return lax.dot_general(left, right, (((1,), (0,)), ((), ())), preferred_element_type=F32)


def dot_nt(left, right):
    return lax.dot_general(left, right, (((1,), (1,)), ((), ())), preferred_element_type=F32)


def call(body, out_shapes, operands, scalars=0, anywhere=0, scratch=(), cost=None, limit=VMEM_LIMIT):
    vmem = pl.BlockSpec(memory_space=pltpu.VMEM)
    in_specs = (
        [pl.BlockSpec(memory_space=pltpu.SMEM)] * scalars
        + [vmem] * (len(operands) - scalars - anywhere)
        + [pl.BlockSpec(memory_space=pl.ANY)] * anywhere
    )
    flops, moved = cost or (1000, 1000)
    return pl.pallas_call(
        body,
        out_shape=out_shapes,
        in_specs=in_specs,
        out_specs=jax.tree.map(lambda _: vmem, out_shapes),
        scratch_shapes=scratch,
        compiler_params=pltpu.CompilerParams(vmem_limit_bytes=limit),
        cost_estimate=pl.CostEstimate(flops=flops, bytes_accessed=moved, transcendentals=0),
    )(*operands)


def slot_of(block, order):
    slot = 0
    for bit in order:
        slot = slot * 2 + ((block >> bit) & 1)
    return slot


def gradient_kernel(orders, place_ref, rates_ref, keys_ref, values_ref, weights_ref, *refs):
    out_refs, chunk_refs = refs[:-2], refs[-2:]
    place = place_ref[0, 0]
    rates = rates_ref[...]
    keys = keys_ref[...]
    values = values_ref[...]
    hidden_size = chunk_refs[0].shape[0]
    width = weights_ref.shape[2]
    turn = pl.program_id(0)
    step = weights_ref.shape[1]

    def put(chunk, columns, product):
        order = orders[chunk]
        block_rows = min(step, hidden_size >> len(order))
        for start in range(0, step, block_rows):
            row = turn * step + start
            if order:
                block = turn * (step // block_rows) + start // block_rows
                row = slot_of(block ^ place, order) * block_rows
            row = pl.multiple_of(row, block_rows)
            chunk_refs[chunk][pl.ds(row, block_rows), columns] = product[start:start + block_rows]

    gate = dot_nt(weights_ref[0], keys) * INVERSE
    up = dot_nt(weights_ref[1], keys) * INVERSE
    sigmoid = jax.nn.sigmoid(gate)
    silu = gate * sigmoid
    hidden = (rates * silu * up).astype(BF16)
    backward = rates * dot_nt(weights_ref[2], values)
    d_gate = (backward * up * sigmoid * (1.0 + gate * (1.0 - sigmoid)) * INVERSE).astype(BF16)
    d_up = (backward * silu * INVERSE).astype(BF16)
    up_part = dot_nn(d_up, keys).astype(BF16)
    put(0, slice(0, width), dot_nn(d_gate, keys).astype(BF16))
    put(0, slice(width, width + width // 2), up_part[:, :width // 2])
    put(1, slice(0, width), dot_nn(hidden, values).astype(BF16))
    put(1, slice(width, width + width // 2), up_part[:, width // 2:])

    @pl.when(turn == pl.num_programs(0) - 1)
    def _():
        halves = len(out_refs) // 2
        half_rows = hidden_size // halves
        for index, out_ref in enumerate(out_refs):
            half = index % halves
            out_ref[...] = chunk_refs[index // halves][half * half_rows:(half + 1) * half_rows, :]


def attend_rows(edge_prev, edge_next, query_tile, keys_prev, keys_own, keys_next,
                values_prev, values_own, values_next):
    scale = 1.0 / math.sqrt(HEAD_DIM)
    row = lax.broadcasted_iota(jnp.int32, (TILE, TILE), 0)
    col = lax.broadcasted_iota(jnp.int32, (TILE, TILE), 1)
    minus = jnp.float32(-jnp.inf)
    score_prev = dot_nt(query_tile, keys_prev)
    score_own = dot_nt(query_tile, keys_own)
    score_next = dot_nt(query_tile, keys_next)
    parts = [score_prev[:, :TILE] + jnp.where(col >= row, edge_prev, minus)]
    if score_prev.shape[1] > TILE:
        parts.append(score_prev[:, TILE:] + edge_prev)
    parts.append(score_own)
    if score_next.shape[1] > TILE:
        parts.append(score_next[:, :-TILE] + edge_next)
    parts.append(score_next[:, -TILE:] + jnp.where(col <= row, edge_next, minus))
    scores = jnp.concatenate(parts, axis=1)
    highest = jnp.max(scores, axis=1, keepdims=True)
    weights = jnp.exp((scores - highest) * scale)
    total = jnp.sum(weights, axis=1, keepdims=True)
    weights = weights.astype(BF16)
    width_prev, width_own = score_prev.shape[1], score_own.shape[1]
    attended = (
        dot_nn(weights[:, :width_prev], values_prev)
        + dot_nn(weights[:, width_prev:width_prev + width_own], values_own)
        + dot_nn(weights[:, width_prev + width_own:], values_next)
    )
    return attended / total


def pack_kernel(side_ref, queries_ref, keys_ref, values_ref, out_ref):
    count = queries_ref.shape[0]
    start = pl.multiple_of((1 - side_ref[0, 0]) * HEAD_DIM, HEAD_DIM)
    for index, ref in enumerate((queries_ref, keys_ref, values_ref)):
        out_ref[index * count:(index + 1) * count, :] = ref[:, pl.ds(start, HEAD_DIM)]


def border_kernel(side_ref, keys_ref, values_ref, other_ref, low_ref, high_ref):
    count = keys_ref.shape[0]
    side = side_ref[0, 0]
    start = pl.multiple_of(side * HEAD_DIM, HEAD_DIM)

    def fill(own_ref, other_out_ref):
        own_ref[:count, :] = keys_ref[:, pl.ds(start, HEAD_DIM)]
        own_ref[count:, :] = values_ref[:, pl.ds(start, HEAD_DIM)]
        other_out_ref[...] = other_ref[count:, :]

    @pl.when(side == 0)
    def _():
        fill(low_ref, high_ref)

    @pl.when(side != 0)
    def _():
        fill(high_ref, low_ref)


def first_kernel(edge_ref, side_ref, queries_ref, other_ref, prev_ref, low_ref, high_ref, next_ref,
                 keep_ref, send_ref, keys_ref, values_ref):
    count = queries_ref.shape[0]
    side = side_ref[0, 0]
    for index, ref in enumerate((prev_ref, low_ref, high_ref, next_ref)):
        rows = slice(index * count, (index + 1) * count)
        keys_ref[rows, :] = ref[:count, :]
        values_ref[rows, :] = ref[count:, :]
    start = pl.multiple_of(side * HEAD_DIM, HEAD_DIM)
    for turn, out_ref in enumerate((keep_ref, send_ref)):
        base = (side if turn == 0 else 1 - side) * count

        def span(ref, low, length):
            return ref[pl.ds(pl.multiple_of(base + low, TILE), length), :]

        for index in range(count // TILE):
            low, high = index * TILE, (index + 1) * TILE
            query = queries_ref[low:high, pl.ds(start, HEAD_DIM)] if turn == 0 else other_ref[low:high, :]
            out_ref[low:high, :] = attend_rows(
                edge_ref[turn, 0], edge_ref[turn, 1], query,
                span(keys_ref, low, count - low), span(keys_ref, count, count),
                span(keys_ref, 2 * count, high),
                span(values_ref, low, count - low), span(values_ref, count, count),
                span(values_ref, 2 * count, high),
            ).astype(BF16)


def query_kernel(side_ref, keep_ref, other_ref, map_ref, out_ref):
    side = side_ref[0, 0]
    own = keep_ref[...].astype(F32)
    other = other_ref[...].astype(F32)
    square = jnp.sum(own * own + other * other, axis=1, keepdims=True)
    norm = lax.rsqrt(square / (HEADS_GRP * HEAD_DIM) + 1e-05)
    own_map = map_ref[pl.ds(pl.multiple_of(side * HEAD_DIM, HEAD_DIM), HEAD_DIM), :]
    other_map = map_ref[pl.ds(pl.multiple_of((1 - side) * HEAD_DIM, HEAD_DIM), HEAD_DIM), :]
    out_ref[...] = (
        dot_nn((own * norm).astype(BF16), own_map) + dot_nn((other * norm).astype(BF16), other_map)
    ).astype(BF16)


def second_kernel(edge_ref, queries_ref, keep_ref, near_ref, far_ref, prev_ref, keys_ref, values_ref, next_ref,
                  *refs):
    done_refs, out_ref = refs[:-1], refs[-1]
    count = keys_ref.shape[0]
    half = far_ref.shape[0]
    offset = half if done_refs else 0
    if done_refs:
        out_ref[:half, :] = done_refs[0][...]
    for low in range(offset, offset + half, TILE):
        high = low + TILE
        rows = slice(low, high)
        mixed = (
            keep_ref[rows, :].astype(F32)
            + near_ref[rows, :].astype(F32)
            + far_ref[low - offset:high - offset, :].astype(F32)
        )
        query = (queries_ref[rows, :].astype(F32) + mixed).astype(BF16)
        heads = []
        for head in range(HEADS_GRP):
            cols = slice(head * HEAD_DIM, (head + 1) * HEAD_DIM)
            heads.append(
                attend_rows(
                    edge_ref[0, 0], edge_ref[0, 1], query[:, cols],
                    prev_ref[low:count, cols], keys_ref[:, cols], next_ref[:high, cols],
                    prev_ref[count + low:, cols], values_ref[:, cols], next_ref[count:count + high, cols],
                )
            )
        both = jnp.concatenate(heads, axis=1)
        mean = jnp.mean(both * both, axis=1, keepdims=True)
        out_ref[rows, :] = (both * lax.rsqrt(mean + 1e-05)).astype(BF16)


def renew_kernel(orders, place_ref, weights_ref, query_ref, *refs):
    pieces, (own_ref, fast_ref, new_ref) = refs[:-3], refs[-3:]
    place = place_ref[0, 0]
    hidden_size, width = weights_ref.shape[1:]
    limit_norm = math.sqrt(FAST_HIDDEN * FAST_DIM) / 2.0
    step = 64
    square = jnp.zeros((1, pieces[0].shape[1]), F32)
    for piece in pieces:
        for low in range(0, piece.shape[0], step):
            part = piece[low:low + step, :].astype(F32)
            square = square + jnp.sum(part * part, axis=0, keepdims=True)
    square = jnp.sum(square, axis=1, keepdims=True)
    factor = jnp.minimum(1.0, limit_norm * lax.rsqrt(square + 1e-06))
    per_chunk = len(pieces) // 2
    piece_rows = pieces[0].shape[0]
    blocks = 1 << len(orders[0])
    block_rows = hidden_size // blocks
    count = min(step, block_rows)
    for block in range(blocks):
        starts = [slot_of(block, order) * block_rows for order in orders]
        for low in range(0, block_rows, count):
            found = []
            for chunk, start in enumerate(starts):
                piece = pieces[chunk * per_chunk + start // piece_rows]
                inside = start % piece_rows + low
                found.append(piece[inside:inside + count, :].astype(F32))
            parts = [
                found[0][:, :width],
                jnp.concatenate([found[0][:, width:], found[1][:, width:]], axis=1),
                found[1][:, :width],
            ]
            rows = slice(low, low + count)
            if blocks > 1:
                rows = pl.ds(pl.multiple_of((block ^ place) * block_rows + low, count), count)
            for matrix, part in enumerate(parts):
                old = weights_ref[matrix, rows, :].astype(F32)
                stepped = old + factor * part
                norm = jnp.sqrt(jnp.sum(old * old, axis=1, keepdims=True))
                size = jnp.sum(stepped * stepped, axis=1, keepdims=True)
                fresh = (stepped * norm * lax.rsqrt(size + 1e-06)).astype(BF16)
                new_ref[matrix, rows, :] = fresh
                if block == 0:
                    own_ref[matrix, low:low + count, :] = fresh
    step = 128
    for low in range(0, query_ref.shape[0], step):
        rows = slice(low, low + step)
        query = query_ref[rows, :]
        gate = dot_nt(query, new_ref[0]) * INVERSE
        up = dot_nt(query, new_ref[1]) * INVERSE
        hidden = (jax.nn.silu(gate) * up).astype(BF16)
        raw = dot_nn(hidden, new_ref[2])
        mean = jnp.mean(raw * raw, axis=1, keepdims=True)
        fast_ref[rows, :] = (raw * lax.rsqrt(mean + 1e-05)).astype(BF16)


def mix_kernel(pair, places_ref, fast_ref, map_ref, *out_refs):
    for index, out_ref in enumerate(out_refs):
        width = out_ref.shape[1]
        start = pl.multiple_of(places_ref[0, 2 * pair + index] * width, width)
        out_ref[...] = dot_nn(fast_ref[...], map_ref[:, pl.ds(start, width)]).astype(BF16)


def seq_shift(value, step):
    peers = lax.axis_size("seq")
    return lax.ppermute(
        value, "seq", [(i, i + step) for i in range(peers) if 0 <= i + step < peers]
    )


def head_swap(value, bit):
    return lax.ppermute(value, "head", [(i, i ^ bit) for i in range(lax.axis_size("head"))])


def seq_swap(value, bit):
    step = 1 << bit
    return lax.ppermute(value, "seq", [(i, i ^ step) for i in range(lax.axis_size("seq"))])


def after(value, others):
    return lax.optimization_barrier((value, others))[0]


def halving_start(chunks, orders):
    keeps = [keep for keep, _ in chunks]
    return keeps, [seq_swap(send, order[0]) for (_, send), order in zip(chunks, orders)]


def halving_step(keeps, found, orders, turn, wait=()):
    sends, rest = [], []
    for keep, new in zip(keeps, found):
        half = keep.shape[0] // 2
        sends.append((keep[half:].astype(F32) + new[half:].astype(F32)).astype(BF16))
        rest.append(lax.optimization_barrier(keep[:half].astype(F32) + new[:half].astype(F32)))
    sends = after(sends, wait) if wait else sends
    return rest, [seq_swap(send, order[turn]) for send, order in zip(sends, orders)]


def doubling_step(held, orders, turn, wait=()):
    whole = [jnp.concatenate(parts) if len(parts) > 1 else parts[0] for parts in held]
    whole = after(whole, wait) if wait else whole
    return [(own, seq_swap(own, order[turn])) for own, order in zip(whole, orders)]


def local(
    queries_first,
    keys_first,
    values_first,
    input_map,
    fast_keys,
    fast_values,
    step_rates,
    fast_weights,
    output_map,
    queries_second,
    keys_second,
    values_second,
):
    rows, width = queries_first.shape
    seq_count = lax.axis_size("seq")
    seq_place = lax.axis_index("seq")
    head_place = lax.axis_index("head")
    weights = jnp.transpose(fast_weights[0], (1, 0, 2))
    hidden_size, fast_width = weights.shape[1:]
    shape = jax.ShapeDtypeStruct
    minus = jnp.float32(-jnp.inf)
    side = seq_place % 2

    def edges_of(block):
        return [jnp.where(block > 0, 0.0, minus), jnp.where(block < seq_count - 1, 0.0, minus)]

    edges = jnp.stack(edges_of(seq_place) + edges_of(seq_place ^ 1)).reshape(2, 2)
    side_scalar = side.astype(jnp.int32).reshape(1, 1)
    place = seq_place.astype(jnp.int32).reshape(1, 1)

    packed = call(
        pack_kernel,
        shape((3 * rows, HEAD_DIM), BF16),
        (side_scalar, queries_first, keys_first, values_first),
        scalars=1,
    )
    other_first = seq_swap(packed, 0)

    bits = tuple(range(seq_count.bit_length() - 1))
    halving = seq_count == 1 << len(bits) and len(bits) > 1 and hidden_size >> len(bits) >= 16
    orders = (bits, bits[1:] + bits[:1]) if halving else ((), ())
    halves = 2 if halving else 1
    chunk_width = fast_width + fast_width // 2
    out_shapes = [shape((hidden_size // halves, chunk_width), BF16)] * (2 * halves)
    whole = pl.BlockSpec(memory_space=pltpu.VMEM)
    gradients = pl.pallas_call(
        functools.partial(gradient_kernel, orders),
        grid=(hidden_size // TILE,),
        out_shape=out_shapes,
        in_specs=[
            pl.BlockSpec(memory_space=pltpu.SMEM),
            whole,
            whole,
            whole,
            pl.BlockSpec((3, TILE, fast_width), lambda turn: (0, turn, 0)),
        ],
        out_specs=[whole] * len(out_shapes),
        scratch_shapes=[pltpu.VMEM((hidden_size, chunk_width), BF16)] * 2,
        compiler_params=pltpu.CompilerParams(vmem_limit_bytes=VMEM_MOST),
        cost_estimate=pl.CostEstimate(flops=1000, bytes_accessed=1000, transcendentals=0),
    )(place, step_rates.reshape(1, rows), fast_keys, fast_values, weights)

    low_block, high_block = call(
        border_kernel,
        [shape((2 * rows, HEAD_DIM), BF16)] * 2,
        (side_scalar, keys_first, values_first, other_first),
        scalars=1,
    )

    def first_halos(low_block, high_block):
        return seq_shift(high_block, 2), seq_shift(low_block, -2)

    def first_attention(prev_first, next_first):
        keep_first, send_first = call(
            first_kernel,
            [shape((rows, HEAD_DIM), BF16)] * 2,
            (edges, side_scalar, queries_first, other_first, prev_first, low_block, high_block, next_first),
            scalars=2,
            scratch=[pltpu.VMEM((4 * rows, HEAD_DIM), BF16)] * 2,
            cost=(12 * rows * rows * width, 16 * rows * width),
        )
        return keep_first, seq_swap(send_first, 0)

    both_second = jnp.concatenate([keys_second, values_second])

    if halving:
        turns = len(bits)
        keeps, found = halving_start([gradients[:2], gradients[2:]], orders)
        for turn in range(1, turns):
            if turn == turns - 1:
                prev_first, next_first = first_halos(*after((low_block, high_block), found))
                prev_second = seq_shift(after(both_second, found), 1)
            keeps, found = halving_step(keeps, found, orders, turn)
        held = [((keep.astype(F32) + new.astype(F32)).astype(BF16),) for keep, new in zip(keeps, found)]
        for turn in reversed(range(turns)):
            wait = ()
            if turn == 1:
                wait = (prev_first, next_first, prev_second)
            if turn == 0:
                keep_first, back_first = first_attention(prev_first, next_first)
                wait = (keep_first,)
            held = doubling_step(held, orders, turn, wait)
        gathered = [part for parts in held for part in parts]
        next_second = seq_shift(after(both_second, (gathered, back_first)), -1)
    else:
        gathered = lax.psum(gradients, "seq")
        keep_first, back_first = first_attention(*first_halos(low_block, high_block))
        prev_second, next_second = seq_shift(both_second, 1), seq_shift(both_second, -1)
    fast_query = call(
        query_kernel,
        shape((rows, fast_width), BF16),
        (side_scalar, keep_first, back_first, input_map[0]),
        scalars=1,
    )

    own_rows = hidden_size >> len(orders[0])
    my_bit, near = head_place % 2, head_place // 2
    places = jnp.stack(
        [2 * pair + bit for pair in (near ^ 1, near) for bit in (1 - my_bit, my_bit)]
    ).astype(jnp.int32).reshape(1, 4)
    share = shape((rows, width), BF16)
    own_new, fast_out = call(
        functools.partial(renew_kernel, orders),
        [shape((3, own_rows, fast_width), BF16), shape((rows, fast_width), BF16)],
        (place, weights, fast_query, *gathered),
        scalars=1,
        scratch=[pltpu.VMEM(weights.shape, BF16)],
    )

    def mixed_for(pair, fast):
        return call(
            functools.partial(mix_kernel, pair), [share, share], (places, fast, output_map), scalars=1
        )

    far_send, far_keep = mixed_for(0, fast_out)
    far_near = head_swap(far_send, 1)
    near_send, near_keep = mixed_for(1, after(fast_out, next_second))
    near_near = head_swap(near_send, 1)
    half = rows // 2
    far_parts = []
    for part in (slice(0, half), slice(half, rows)):
        far_sum = far_keep[part].astype(F32) + far_near[part].astype(F32)
        far_parts.append(head_swap(far_sum.astype(BF16), 2))
    if not halving:
        share_rows = hidden_size // seq_count
        own_new = lax.dynamic_slice_in_dim(own_new, seq_place * share_rows, share_rows, 1)

    def second_attention(part, *done):
        return call(
            second_kernel,
            shape((half * (1 + len(done)), width), BF16),
            (edges, queries_second, near_keep, near_near, far_parts[part],
             prev_second, keys_second, values_second, next_second, *done),
            scalars=1,
            cost=(6 * rows * rows * width, 16 * rows * width),
        )

    normed_second = second_attention(1, second_attention(0))
    return (normed_second, jnp.transpose(own_new, (1, 0, 2))[None])


def solution(mesh):
    return jax.shard_map(
        local,
        mesh=mesh,
        in_specs=(
            P("seq", "head"),
            P("seq", "head"),
            P("seq", "head"),
            P("head", None, None),
            P("seq", "head"),
            P("seq", "head"),
            P("seq", "head"),
            P("head", None, None, None),
            P("head", None),
            P("seq", "head"),
            P("seq", "head"),
            P("seq", "head"),
        ),
        out_specs=(P("seq", "head"), P("head", "seq", None, None)),
        check_vma=False,
    )
```

```python
import functools
import math

import jax
import jax.numpy as jnp
from jax import lax
from jax.experimental import pallas as pl
from jax.experimental.pallas import tpu as pltpu
from jax.sharding import PartitionSpec as P

HALF_WIN = 512
HEAD_DIM = 128
HEADS_GRP = 2
FAST_DIM = 512
FAST_HIDDEN = 512
TILE = 128
VMEM_LIMIT = 24 * 1024 * 1024
VMEM_MOST = 60 * 1024 * 1024

BF16 = jnp.bfloat16
F32 = jnp.float32
INVERSE = 1.0 / math.sqrt(FAST_DIM)


def dot_nn(left, right):
    return lax.dot_general(left, right, (((1,), (0,)), ((), ())), preferred_element_type=F32)


def dot_nt(left, right):
    return lax.dot_general(left, right, (((1,), (1,)), ((), ())), preferred_element_type=F32)


def call(body, out_shapes, operands, scalars=0, anywhere=0, scratch=(), cost=None, limit=VMEM_LIMIT):
    vmem = pl.BlockSpec(memory_space=pltpu.VMEM)
    in_specs = (
        [pl.BlockSpec(memory_space=pltpu.SMEM)] * scalars
        + [vmem] * (len(operands) - scalars - anywhere)
        + [pl.BlockSpec(memory_space=pl.ANY)] * anywhere
    )
    flops, moved = cost or (1000, 1000)
    return pl.pallas_call(
        body,
        out_shape=out_shapes,
        in_specs=in_specs,
        out_specs=jax.tree.map(lambda _: vmem, out_shapes),
        scratch_shapes=scratch,
        compiler_params=pltpu.CompilerParams(vmem_limit_bytes=limit),
        cost_estimate=pl.CostEstimate(flops=flops, bytes_accessed=moved, transcendentals=0),
    )(*operands)


def slot_of(block, order):
    slot = 0
    for bit in order:
        slot = slot * 2 + ((block >> bit) & 1)
    return slot


def gradient_kernel(orders, place_ref, rates_ref, keys_ref, values_ref, weights_ref, *refs):
    out_refs, chunk_refs = refs[:-2], refs[-2:]
    place = place_ref[0, 0]
    rates = rates_ref[...]
    keys = keys_ref[...]
    values = values_ref[...]
    hidden_size = chunk_refs[0].shape[0]
    width = weights_ref.shape[2]
    turn = pl.program_id(0)
    step = weights_ref.shape[1]

    def put(chunk, columns, product):
        order = orders[chunk]
        block_rows = min(step, hidden_size >> len(order))
        for start in range(0, step, block_rows):
            row = turn * step + start
            if order:
                block = turn * (step // block_rows) + start // block_rows
                row = slot_of(block ^ place, order) * block_rows
            row = pl.multiple_of(row, block_rows)
            chunk_refs[chunk][pl.ds(row, block_rows), columns] = product[start:start + block_rows]

    gate = dot_nt(weights_ref[0], keys) * INVERSE
    up = dot_nt(weights_ref[1], keys) * INVERSE
    sigmoid = jax.nn.sigmoid(gate)
    silu = gate * sigmoid
    hidden = (rates * silu * up).astype(BF16)
    backward = rates * dot_nt(weights_ref[2], values)
    d_gate = (backward * up * sigmoid * (1.0 + gate * (1.0 - sigmoid)) * INVERSE).astype(BF16)
    d_up = (backward * silu * INVERSE).astype(BF16)
    up_part = dot_nn(d_up, keys).astype(BF16)
    put(0, slice(0, width), dot_nn(d_gate, keys).astype(BF16))
    put(0, slice(width, width + width // 2), up_part[:, :width // 2])
    put(1, slice(0, width), dot_nn(hidden, values).astype(BF16))
    put(1, slice(width, width + width // 2), up_part[:, width // 2:])

    @pl.when(turn == pl.num_programs(0) - 1)
    def _():
        halves = len(out_refs) // 2
        half_rows = hidden_size // halves
        for index, out_ref in enumerate(out_refs):
            half = index % halves
            out_ref[...] = chunk_refs[index // halves][half * half_rows:(half + 1) * half_rows, :]


def attend_rows(edge_prev, edge_next, query_tile, keys_prev, keys_own, keys_next,
                values_prev, values_own, values_next):
    scale = 1.0 / math.sqrt(HEAD_DIM)
    row = lax.broadcasted_iota(jnp.int32, (TILE, TILE), 0)
    col = lax.broadcasted_iota(jnp.int32, (TILE, TILE), 1)
    minus = jnp.float32(-jnp.inf)
    score_prev = dot_nt(query_tile, keys_prev)
    score_own = dot_nt(query_tile, keys_own)
    score_next = dot_nt(query_tile, keys_next)
    parts = [score_prev[:, :TILE] + jnp.where(col >= row, edge_prev, minus)]
    if score_prev.shape[1] > TILE:
        parts.append(score_prev[:, TILE:] + edge_prev)
    parts.append(score_own)
    if score_next.shape[1] > TILE:
        parts.append(score_next[:, :-TILE] + edge_next)
    parts.append(score_next[:, -TILE:] + jnp.where(col <= row, edge_next, minus))
    scores = jnp.concatenate(parts, axis=1)
    highest = jnp.max(scores, axis=1, keepdims=True)
    weights = jnp.exp((scores - highest) * scale)
    total = jnp.sum(weights, axis=1, keepdims=True)
    weights = weights.astype(BF16)
    width_prev, width_own = score_prev.shape[1], score_own.shape[1]
    attended = (
        dot_nn(weights[:, :width_prev], values_prev)
        + dot_nn(weights[:, width_prev:width_prev + width_own], values_own)
        + dot_nn(weights[:, width_prev + width_own:], values_next)
    )
    return attended / total


def pack_kernel(side_ref, queries_ref, keys_ref, values_ref, out_ref):
    count = queries_ref.shape[0]
    start = pl.multiple_of((1 - side_ref[0, 0]) * HEAD_DIM, HEAD_DIM)
    for index, ref in enumerate((queries_ref, keys_ref, values_ref)):
        out_ref[index * count:(index + 1) * count, :] = ref[:, pl.ds(start, HEAD_DIM)]


def border_kernel(side_ref, keys_ref, values_ref, other_ref, low_ref, high_ref):
    count = keys_ref.shape[0]
    side = side_ref[0, 0]
    start = pl.multiple_of(side * HEAD_DIM, HEAD_DIM)

    def fill(own_ref, other_out_ref):
        own_ref[:count, :] = keys_ref[:, pl.ds(start, HEAD_DIM)]
        own_ref[count:, :] = values_ref[:, pl.ds(start, HEAD_DIM)]
        other_out_ref[...] = other_ref[count:, :]

    @pl.when(side == 0)
    def _():
        fill(low_ref, high_ref)

    @pl.when(side != 0)
    def _():
        fill(high_ref, low_ref)


def first_kernel(edge_ref, side_ref, queries_ref, other_ref, prev_ref, low_ref, high_ref, next_ref,
                 keep_ref, send_ref, keys_ref, values_ref):
    count = queries_ref.shape[0]
    side = side_ref[0, 0]
    for index, ref in enumerate((prev_ref, low_ref, high_ref, next_ref)):
        rows = slice(index * count, (index + 1) * count)
        keys_ref[rows, :] = ref[:count, :]
        values_ref[rows, :] = ref[count:, :]
    start = pl.multiple_of(side * HEAD_DIM, HEAD_DIM)
    for turn, out_ref in enumerate((keep_ref, send_ref)):
        base = (side if turn == 0 else 1 - side) * count

        def span(ref, low, length):
            return ref[pl.ds(pl.multiple_of(base + low, TILE), length), :]

        for index in range(count // TILE):
            low, high = index * TILE, (index + 1) * TILE
            query = queries_ref[low:high, pl.ds(start, HEAD_DIM)] if turn == 0 else other_ref[low:high, :]
            out_ref[low:high, :] = attend_rows(
                edge_ref[turn, 0], edge_ref[turn, 1], query,
                span(keys_ref, low, count - low), span(keys_ref, count, count),
                span(keys_ref, 2 * count, high),
                span(values_ref, low, count - low), span(values_ref, count, count),
                span(values_ref, 2 * count, high),
            ).astype(BF16)


def second_kernel(edge_ref, queries_ref, keep_ref, near_ref, far_ref, prev_ref, keys_ref, values_ref, next_ref,
                  *refs):
    done_refs, out_ref = refs[:-1], refs[-1]
    count = keys_ref.shape[0]
    half = far_ref.shape[0]
    offset = half if done_refs else 0
    if done_refs:
        out_ref[:half, :] = done_refs[0][...]
    for low in range(offset, offset + half, TILE):
        high = low + TILE
        rows = slice(low, high)
        mixed = (
            keep_ref[rows, :].astype(F32)
            + near_ref[rows, :].astype(F32)
            + far_ref[low - offset:high - offset, :].astype(F32)
        )
        query = (queries_ref[rows, :].astype(F32) + mixed).astype(BF16)
        heads = []
        for head in range(HEADS_GRP):
            cols = slice(head * HEAD_DIM, (head + 1) * HEAD_DIM)
            heads.append(
                attend_rows(
                    edge_ref[0, 0], edge_ref[0, 1], query[:, cols],
                    prev_ref[low:count, cols], keys_ref[:, cols], next_ref[:high, cols],
                    prev_ref[count + low:, cols], values_ref[:, cols], next_ref[count:count + high, cols],
                )
            )
        both = jnp.concatenate(heads, axis=1)
        mean = jnp.mean(both * both, axis=1, keepdims=True)
        out_ref[rows, :] = (both * lax.rsqrt(mean + 1e-05)).astype(BF16)


def renew_kernel(orders, place_ref, side_ref, *refs):
    count = (len(refs) - 4) // 2
    sources, (own_ref, fast_ref), loaded = refs[:count], refs[count:count + 2], refs[count + 2:-2]
    new_ref, sems = refs[-2:]
    copies = [
        pltpu.make_async_copy(source, target, sems.at[index])
        for index, (source, target) in enumerate(zip(sources, loaded))
    ]
    for copy in copies:
        copy.start()
    pieces, (weights_ref, keep_ref, other_ref, map_ref) = loaded[:-4], loaded[-4:]
    place = place_ref[0, 0]
    side = side_ref[0, 0]
    hidden_size, width = weights_ref.shape[1:]
    for copy in copies[:-4]:
        copy.wait()
    limit_norm = math.sqrt(FAST_HIDDEN * FAST_DIM) / 2.0
    step = 64
    square = jnp.zeros((1, pieces[0].shape[1]), F32)
    for piece in pieces:
        for low in range(0, piece.shape[0], step):
            part = piece[low:low + step, :].astype(F32)
            square = square + jnp.sum(part * part, axis=0, keepdims=True)
    square = jnp.sum(square, axis=1, keepdims=True)
    factor = jnp.minimum(1.0, limit_norm * lax.rsqrt(square + 1e-06))
    copies[-4].wait()
    per_chunk = len(pieces) // 2
    piece_rows = pieces[0].shape[0]
    blocks = 1 << len(orders[0])
    block_rows = hidden_size // blocks
    count = min(step, block_rows)
    for block in range(blocks):
        starts = [slot_of(block, order) * block_rows for order in orders]
        for low in range(0, block_rows, count):
            found = []
            for chunk, start in enumerate(starts):
                piece = pieces[chunk * per_chunk + start // piece_rows]
                inside = start % piece_rows + low
                found.append(piece[inside:inside + count, :].astype(F32))
            parts = [
                found[0][:, :width],
                jnp.concatenate([found[0][:, width:], found[1][:, width:]], axis=1),
                found[1][:, :width],
            ]
            rows = slice(low, low + count)
            if blocks > 1:
                rows = pl.ds(pl.multiple_of((block ^ place) * block_rows + low, count), count)
            for matrix, part in enumerate(parts):
                old = weights_ref[matrix, rows, :].astype(F32)
                stepped = old + factor * part
                norm = jnp.sqrt(jnp.sum(old * old, axis=1, keepdims=True))
                size = jnp.sum(stepped * stepped, axis=1, keepdims=True)
                fresh = (stepped * norm * lax.rsqrt(size + 1e-06)).astype(BF16)
                new_ref[matrix, rows, :] = fresh
                if block == 0:
                    own_ref[matrix, low:low + count, :] = fresh
    for copy in copies[-3:]:
        copy.wait()
    own_map = map_ref[pl.ds(pl.multiple_of(side * HEAD_DIM, HEAD_DIM), HEAD_DIM), :]
    other_map = map_ref[pl.ds(pl.multiple_of((1 - side) * HEAD_DIM, HEAD_DIM), HEAD_DIM), :]
    for low in range(0, keep_ref.shape[0], TILE):
        rows = slice(low, low + TILE)
        own = keep_ref[rows, :].astype(F32)
        other = other_ref[rows, :].astype(F32)
        total = jnp.sum(own * own + other * other, axis=1, keepdims=True)
        norm = lax.rsqrt(total / (HEADS_GRP * HEAD_DIM) + 1e-05)
        query = (
            dot_nn((own * norm).astype(BF16), own_map) + dot_nn((other * norm).astype(BF16), other_map)
        ).astype(BF16)
        gate = dot_nt(query, new_ref[0]) * INVERSE
        up = dot_nt(query, new_ref[1]) * INVERSE
        hidden = (jax.nn.silu(gate) * up).astype(BF16)
        raw = dot_nn(hidden, new_ref[2])
        mean = jnp.mean(raw * raw, axis=1, keepdims=True)
        fast_ref[rows, :] = (raw * lax.rsqrt(mean + 1e-05)).astype(BF16)


def mix_kernel(pair, places_ref, fast_ref, map_ref, *out_refs):
    for index, out_ref in enumerate(out_refs):
        width = out_ref.shape[1]
        start = pl.multiple_of(places_ref[0, 2 * pair + index] * width, width)
        out_ref[...] = dot_nn(fast_ref[...], map_ref[:, pl.ds(start, width)]).astype(BF16)


def seq_shift(value, step):
    peers = lax.axis_size("seq")
    return lax.ppermute(
        value, "seq", [(i, i + step) for i in range(peers) if 0 <= i + step < peers]
    )


def head_swap(value, bit):
    return lax.ppermute(value, "head", [(i, i ^ bit) for i in range(lax.axis_size("head"))])


def seq_swap(value, bit):
    step = 1 << bit
    return lax.ppermute(value, "seq", [(i, i ^ step) for i in range(lax.axis_size("seq"))])


def after(value, others):
    return lax.optimization_barrier((value, others))[0]


def halving_start(chunks, orders):
    keeps = [keep for keep, _ in chunks]
    return keeps, [seq_swap(send, order[0]) for (_, send), order in zip(chunks, orders)]


def halving_step(keeps, found, orders, turn, wait=()):
    sends, rest = [], []
    for keep, new in zip(keeps, found):
        half = keep.shape[0] // 2
        sends.append((keep[half:].astype(F32) + new[half:].astype(F32)).astype(BF16))
        rest.append(lax.optimization_barrier(keep[:half].astype(F32) + new[:half].astype(F32)))
    sends = after(sends, wait) if wait else sends
    return rest, [seq_swap(send, order[turn]) for send, order in zip(sends, orders)]


def doubling_step(held, orders, turn, wait=()):
    whole = [jnp.concatenate(parts) if len(parts) > 1 else parts[0] for parts in held]
    whole = after(whole, wait) if wait else whole
    return [(own, seq_swap(own, order[turn])) for own, order in zip(whole, orders)]


def local(
    queries_first,
    keys_first,
    values_first,
    input_map,
    fast_keys,
    fast_values,
    step_rates,
    fast_weights,
    output_map,
    queries_second,
    keys_second,
    values_second,
):
    rows, width = queries_first.shape
    seq_count = lax.axis_size("seq")
    seq_place = lax.axis_index("seq")
    head_place = lax.axis_index("head")
    weights = jnp.transpose(fast_weights[0], (1, 0, 2))
    hidden_size, fast_width = weights.shape[1:]
    shape = jax.ShapeDtypeStruct
    minus = jnp.float32(-jnp.inf)
    side = seq_place % 2

    def edges_of(block):
        return [jnp.where(block > 0, 0.0, minus), jnp.where(block < seq_count - 1, 0.0, minus)]

    edges = jnp.stack(edges_of(seq_place) + edges_of(seq_place ^ 1)).reshape(2, 2)
    side_scalar = side.astype(jnp.int32).reshape(1, 1)
    place = seq_place.astype(jnp.int32).reshape(1, 1)

    packed = call(
        pack_kernel,
        shape((3 * rows, HEAD_DIM), BF16),
        (side_scalar, queries_first, keys_first, values_first),
        scalars=1,
    )
    other_first = seq_swap(packed, 0)

    bits = tuple(range(seq_count.bit_length() - 1))
    halving = seq_count == 1 << len(bits) and len(bits) > 1 and hidden_size >> len(bits) >= 16
    orders = (bits, bits[1:] + bits[:1]) if halving else ((), ())
    halves = 2 if halving else 1
    chunk_width = fast_width + fast_width // 2
    out_shapes = [shape((hidden_size // halves, chunk_width), BF16)] * (2 * halves)
    whole = pl.BlockSpec(memory_space=pltpu.VMEM)
    gradients = pl.pallas_call(
        functools.partial(gradient_kernel, orders),
        grid=(hidden_size // TILE,),
        out_shape=out_shapes,
        in_specs=[
            pl.BlockSpec(memory_space=pltpu.SMEM),
            whole,
            whole,
            whole,
            pl.BlockSpec((3, TILE, fast_width), lambda turn: (0, turn, 0)),
        ],
        out_specs=[whole] * len(out_shapes),
        scratch_shapes=[pltpu.VMEM((hidden_size, chunk_width), BF16)] * 2,
        compiler_params=pltpu.CompilerParams(vmem_limit_bytes=VMEM_MOST),
        cost_estimate=pl.CostEstimate(flops=1000, bytes_accessed=1000, transcendentals=0),
    )(place, step_rates.reshape(1, rows), fast_keys, fast_values, weights)

    low_block, high_block = call(
        border_kernel,
        [shape((2 * rows, HEAD_DIM), BF16)] * 2,
        (side_scalar, keys_first, values_first, other_first),
        scalars=1,
    )

    def first_halos(low_block, high_block):
        return seq_shift(high_block, 2), seq_shift(low_block, -2)

    def first_attention(prev_first, next_first):
        keep_first, send_first = call(
            first_kernel,
            [shape((rows, HEAD_DIM), BF16)] * 2,
            (edges, side_scalar, queries_first, other_first, prev_first, low_block, high_block, next_first),
            scalars=2,
            scratch=[pltpu.VMEM((4 * rows, HEAD_DIM), BF16)] * 2,
            cost=(12 * rows * rows * width, 16 * rows * width),
        )
        return keep_first, seq_swap(send_first, 0)

    both_second = jnp.concatenate([keys_second, values_second])

    if halving:
        turns = len(bits)
        keeps, found = halving_start([gradients[:2], gradients[2:]], orders)
        for turn in range(1, turns):
            if turn == turns - 1:
                prev_first, next_first = first_halos(*after((low_block, high_block), found))
                prev_second = seq_shift(after(both_second, found), 1)
            keeps, found = halving_step(keeps, found, orders, turn)
        held = [((keep.astype(F32) + new.astype(F32)).astype(BF16),) for keep, new in zip(keeps, found)]
        for turn in reversed(range(turns)):
            wait = ()
            if turn == 1:
                wait = (prev_first, next_first, prev_second)
            if turn == 0:
                keep_first, back_first = first_attention(prev_first, next_first)
                wait = (keep_first,)
            held = doubling_step(held, orders, turn, wait)
        gathered = [part for parts in held for part in parts]
        next_second = seq_shift(after(both_second, back_first), -1)
    else:
        gathered = lax.psum(gradients, "seq")
        keep_first, back_first = first_attention(*first_halos(low_block, high_block))
        prev_second, next_second = seq_shift(both_second, 1), seq_shift(both_second, -1)
    own_rows = hidden_size >> len(orders[0])
    my_bit, near = head_place % 2, head_place // 2
    places = jnp.stack(
        [2 * pair + bit for pair in (near ^ 1, near) for bit in (1 - my_bit, my_bit)]
    ).astype(jnp.int32).reshape(1, 4)
    share = shape((rows, width), BF16)
    operands = (*gathered, weights, keep_first, back_first, input_map[0])
    own_new, fast_out = call(
        functools.partial(renew_kernel, orders),
        [shape((3, own_rows, fast_width), BF16), shape((rows, fast_width), BF16)],
        (place, side_scalar, *operands),
        scalars=2,
        anywhere=len(operands),
        scratch=[pltpu.VMEM(operand.shape, BF16) for operand in operands]
        + [pltpu.VMEM(weights.shape, BF16), pltpu.SemaphoreType.DMA((len(operands),))],
        limit=VMEM_MOST,
    )

    def mixed_for(pair, fast):
        return call(
            functools.partial(mix_kernel, pair), [share, share], (places, fast, output_map), scalars=1
        )

    far_send, far_keep = mixed_for(0, fast_out)
    far_near = head_swap(far_send, 1)
    near_send, near_keep = mixed_for(1, after(fast_out, next_second))
    near_near = head_swap(near_send, 1)
    half = rows // 2
    far_parts = []
    for part in (slice(0, half), slice(half, rows)):
        far_sum = far_keep[part].astype(F32) + far_near[part].astype(F32)
        far_parts.append(head_swap(far_sum.astype(BF16), 2))
    if not halving:
        share_rows = hidden_size // seq_count
        own_new = lax.dynamic_slice_in_dim(own_new, seq_place * share_rows, share_rows, 1)

    def second_attention(part, *done):
        return call(
            second_kernel,
            shape((half * (1 + len(done)), width), BF16),
            (edges, queries_second, near_keep, near_near, far_parts[part],
             prev_second, keys_second, values_second, next_second, *done),
            scalars=1,
            cost=(6 * rows * rows * width, 16 * rows * width),
        )

    normed_second = second_attention(1, second_attention(0))
    return (normed_second, jnp.transpose(own_new, (1, 0, 2))[None])


def solution(mesh):
    return jax.shard_map(
        local,
        mesh=mesh,
        in_specs=(
            P("seq", "head"),
            P("seq", "head"),
            P("seq", "head"),
            P("head", None, None),
            P("seq", "head"),
            P("seq", "head"),
            P("seq", "head"),
            P("head", None, None, None),
            P("head", None),
            P("seq", "head"),
            P("seq", "head"),
            P("seq", "head"),
        ),
        out_specs=(P("seq", "head"), P("head", "seq", None, None)),
        check_vma=False,
    )
```

```python
import functools
import math

import jax
import jax.numpy as jnp
from jax import lax
from jax.experimental import pallas as pl
from jax.experimental.pallas import tpu as pltpu
from jax.sharding import PartitionSpec as P

HALF_WIN = 512
HEAD_DIM = 128
HEADS_GRP = 2
FAST_DIM = 512
FAST_HIDDEN = 512
TILE = 128
QUERY_TILE = 256
VMEM_LIMIT = 24 * 1024 * 1024
VMEM_MOST = 60 * 1024 * 1024

BF16 = jnp.bfloat16
F32 = jnp.float32
INVERSE = 1.0 / math.sqrt(FAST_DIM)


def dot_nn(left, right):
    return lax.dot_general(left, right, (((1,), (0,)), ((), ())), preferred_element_type=F32)


def dot_nt(left, right):
    return lax.dot_general(left, right, (((1,), (1,)), ((), ())), preferred_element_type=F32)


def call(body, out_shapes, operands, scalars=0, anywhere=0, scratch=(), cost=None, limit=VMEM_LIMIT):
    vmem = pl.BlockSpec(memory_space=pltpu.VMEM)
    in_specs = (
        [pl.BlockSpec(memory_space=pltpu.SMEM)] * scalars
        + [vmem] * (len(operands) - scalars - anywhere)
        + [pl.BlockSpec(memory_space=pl.ANY)] * anywhere
    )
    flops, moved = cost or (1000, 1000)
    return pl.pallas_call(
        body,
        out_shape=out_shapes,
        in_specs=in_specs,
        out_specs=jax.tree.map(lambda _: vmem, out_shapes),
        scratch_shapes=scratch,
        compiler_params=pltpu.CompilerParams(vmem_limit_bytes=limit),
        cost_estimate=pl.CostEstimate(flops=flops, bytes_accessed=moved, transcendentals=0),
    )(*operands)


def slot_of(block, order):
    slot = 0
    for bit in order:
        slot = slot * 2 + ((block >> bit) & 1)
    return slot


def gradient_kernel(orders, place_ref, rates_ref, keys_ref, values_ref, weights_ref, *refs):
    out_refs, chunk_refs = refs[:-2], refs[-2:]
    place = place_ref[0, 0]
    rates = rates_ref[...]
    keys = keys_ref[...]
    values = values_ref[...]
    hidden_size = chunk_refs[0].shape[0]
    width = weights_ref.shape[2]
    turn = pl.program_id(0)
    step = weights_ref.shape[1]

    def put(chunk, columns, product):
        order = orders[chunk]
        block_rows = min(step, hidden_size >> len(order))
        for start in range(0, step, block_rows):
            row = turn * step + start
            if order:
                block = turn * (step // block_rows) + start // block_rows
                row = slot_of(block ^ place, order) * block_rows
            row = pl.multiple_of(row, block_rows)
            chunk_refs[chunk][pl.ds(row, block_rows), columns] = product[start:start + block_rows]

    gate = dot_nt(weights_ref[0], keys) * INVERSE
    up = dot_nt(weights_ref[1], keys) * INVERSE
    sigmoid = jax.nn.sigmoid(gate)
    silu = gate * sigmoid
    hidden = (rates * silu * up).astype(BF16)
    backward = rates * dot_nt(weights_ref[2], values)
    d_gate = (backward * up * sigmoid * (1.0 + gate * (1.0 - sigmoid)) * INVERSE).astype(BF16)
    d_up = (backward * silu * INVERSE).astype(BF16)
    up_part = dot_nn(d_up, keys).astype(BF16)
    put(0, slice(0, width), dot_nn(d_gate, keys).astype(BF16))
    put(0, slice(width, width + width // 2), up_part[:, :width // 2])
    put(1, slice(0, width), dot_nn(hidden, values).astype(BF16))
    put(1, slice(width, width + width // 2), up_part[:, width // 2:])

    @pl.when(turn == pl.num_programs(0) - 1)
    def _():
        halves = len(out_refs) // 2
        half_rows = hidden_size // halves
        for index, out_ref in enumerate(out_refs):
            half = index % halves
            out_ref[...] = chunk_refs[index // halves][half * half_rows:(half + 1) * half_rows, :]


def attend_rows(edge_prev, edge_next, query_tile, keys_prev, keys_own, keys_next,
                values_prev, values_own, values_next):
    scale = math.log2(math.e) / math.sqrt(HEAD_DIM)
    row = lax.broadcasted_iota(jnp.int32, (QUERY_TILE, QUERY_TILE), 0)
    col = lax.broadcasted_iota(jnp.int32, (QUERY_TILE, QUERY_TILE), 1)
    minus = jnp.float32(-jnp.inf)
    score_prev = dot_nt(query_tile, keys_prev)
    score_own = dot_nt(query_tile, keys_own)
    score_next = dot_nt(query_tile, keys_next)
    parts = [score_prev[:, :QUERY_TILE] + jnp.where(col >= row, edge_prev, minus)]
    if score_prev.shape[1] > QUERY_TILE:
        parts.append(score_prev[:, QUERY_TILE:] + edge_prev)
    parts.append(score_own)
    if score_next.shape[1] > QUERY_TILE:
        parts.append(score_next[:, :-QUERY_TILE] + edge_next)
    parts.append(score_next[:, -QUERY_TILE:] + jnp.where(col <= row, edge_next, minus))
    scores = jnp.concatenate(parts, axis=1)
    highest = jnp.max(scores, axis=1, keepdims=True)
    weights = jnp.exp2((scores - highest) * scale)
    total = jnp.sum(weights, axis=1, keepdims=True)
    weights = weights.astype(BF16)
    width_prev, width_own = score_prev.shape[1], score_own.shape[1]
    attended = (
        dot_nn(weights[:, :width_prev], values_prev)
        + dot_nn(weights[:, width_prev:width_prev + width_own], values_own)
        + dot_nn(weights[:, width_prev + width_own:], values_next)
    )
    return attended / total


def pack_kernel(side_ref, queries_ref, keys_ref, values_ref, out_ref):
    count = queries_ref.shape[0]
    start = pl.multiple_of((1 - side_ref[0, 0]) * HEAD_DIM, HEAD_DIM)
    for index, ref in enumerate((queries_ref, keys_ref, values_ref)):
        out_ref[index * count:(index + 1) * count, :] = ref[:, pl.ds(start, HEAD_DIM)]


def border_kernel(side_ref, keys_ref, values_ref, other_ref, low_ref, high_ref):
    count = keys_ref.shape[0]
    side = side_ref[0, 0]
    start = pl.multiple_of(side * HEAD_DIM, HEAD_DIM)

    def fill(own_ref, other_out_ref):
        own_ref[:count, :] = keys_ref[:, pl.ds(start, HEAD_DIM)]
        own_ref[count:, :] = values_ref[:, pl.ds(start, HEAD_DIM)]
        other_out_ref[...] = other_ref[count:, :]

    @pl.when(side == 0)
    def _():
        fill(low_ref, high_ref)

    @pl.when(side != 0)
    def _():
        fill(high_ref, low_ref)


def first_kernel(edge_ref, side_ref, queries_ref, other_ref, prev_ref, low_ref, high_ref, next_ref,
                 keep_ref, send_ref, keys_ref, values_ref):
    count = queries_ref.shape[0]
    side = side_ref[0, 0]
    for index, ref in enumerate((prev_ref, low_ref, high_ref, next_ref)):
        rows = slice(index * count, (index + 1) * count)
        keys_ref[rows, :] = ref[:count, :]
        values_ref[rows, :] = ref[count:, :]
    start = pl.multiple_of(side * HEAD_DIM, HEAD_DIM)
    for turn, out_ref in enumerate((keep_ref, send_ref)):
        base = (side if turn == 0 else 1 - side) * count

        def span(ref, low, length):
            return ref[pl.ds(pl.multiple_of(base + low, QUERY_TILE), length), :]

        for index in range(count // QUERY_TILE):
            low, high = index * QUERY_TILE, (index + 1) * QUERY_TILE
            query = queries_ref[low:high, pl.ds(start, HEAD_DIM)] if turn == 0 else other_ref[low:high, :]
            out_ref[low:high, :] = attend_rows(
                edge_ref[turn, 0], edge_ref[turn, 1], query,
                span(keys_ref, low, count - low), span(keys_ref, count, count),
                span(keys_ref, 2 * count, high),
                span(values_ref, low, count - low), span(values_ref, count, count),
                span(values_ref, 2 * count, high),
            ).astype(BF16)


def second_kernel(edge_ref, queries_ref, keep_ref, near_ref, far_ref, prev_ref, keys_ref, values_ref, next_ref,
                  *refs):
    done_refs, out_ref = refs[:-1], refs[-1]
    count = keys_ref.shape[0]
    half = far_ref.shape[0]
    offset = half if done_refs else 0
    if done_refs:
        out_ref[:half, :] = done_refs[0][...]
    for low in range(offset, offset + half, QUERY_TILE):
        high = low + QUERY_TILE
        rows = slice(low, high)
        mixed = (
            keep_ref[rows, :].astype(F32)
            + near_ref[rows, :].astype(F32)
            + far_ref[low - offset:high - offset, :].astype(F32)
        )
        query = (queries_ref[rows, :].astype(F32) + mixed).astype(BF16)
        heads = []
        for head in range(HEADS_GRP):
            cols = slice(head * HEAD_DIM, (head + 1) * HEAD_DIM)
            heads.append(
                attend_rows(
                    edge_ref[0, 0], edge_ref[0, 1], query[:, cols],
                    prev_ref[low:count, cols], keys_ref[:, cols], next_ref[:high, cols],
                    prev_ref[count + low:, cols], values_ref[:, cols], next_ref[count:count + high, cols],
                )
            )
        both = jnp.concatenate(heads, axis=1)
        mean = jnp.mean(both * both, axis=1, keepdims=True)
        out_ref[rows, :] = (both * lax.rsqrt(mean + 1e-05)).astype(BF16)


def renew_kernel(orders, place_ref, side_ref, places_ref, *refs):
    count = (len(refs) - 8) // 2
    sources, own_ref, share_refs = refs[:count], refs[count], refs[count + 1:count + 5]
    loaded, (fast_ref, new_ref, sems) = refs[count + 5:-3], refs[-3:]
    copies = [
        pltpu.make_async_copy(source, target, sems.at[index])
        for index, (source, target) in enumerate(zip(sources, loaded))
    ]
    for copy in copies:
        copy.start()
    pieces, (weights_ref, keep_ref, other_ref, map_ref, output_ref) = loaded[:-5], loaded[-5:]
    place = place_ref[0, 0]
    side = side_ref[0, 0]
    hidden_size, width = weights_ref.shape[1:]
    for copy in copies[:-5]:
        copy.wait()
    limit_norm = math.sqrt(FAST_HIDDEN * FAST_DIM) / 2.0
    step = 64
    square = jnp.zeros((1, pieces[0].shape[1]), F32)
    for piece in pieces:
        for low in range(0, piece.shape[0], step):
            part = piece[low:low + step, :].astype(F32)
            square = square + jnp.sum(part * part, axis=0, keepdims=True)
    square = jnp.sum(square, axis=1, keepdims=True)
    factor = jnp.minimum(1.0, limit_norm * lax.rsqrt(square + 1e-06))
    copies[-5].wait()
    per_chunk = len(pieces) // 2
    piece_rows = pieces[0].shape[0]
    blocks = 1 << len(orders[0])
    block_rows = hidden_size // blocks
    count = min(step, block_rows)
    for block in range(blocks):
        starts = [slot_of(block, order) * block_rows for order in orders]
        for low in range(0, block_rows, count):
            found = []
            for chunk, start in enumerate(starts):
                piece = pieces[chunk * per_chunk + start // piece_rows]
                inside = start % piece_rows + low
                found.append(piece[inside:inside + count, :].astype(F32))
            parts = [
                found[0][:, :width],
                jnp.concatenate([found[0][:, width:], found[1][:, width:]], axis=1),
                found[1][:, :width],
            ]
            rows = slice(low, low + count)
            if blocks > 1:
                rows = pl.ds(pl.multiple_of((block ^ place) * block_rows + low, count), count)
            for matrix, part in enumerate(parts):
                old = weights_ref[matrix, rows, :].astype(F32)
                stepped = old + factor * part
                norm = jnp.sqrt(jnp.sum(old * old, axis=1, keepdims=True))
                size = jnp.sum(stepped * stepped, axis=1, keepdims=True)
                fresh = (stepped * norm * lax.rsqrt(size + 1e-06)).astype(BF16)
                new_ref[matrix, rows, :] = fresh
                if block == 0:
                    own_ref[matrix, low:low + count, :] = fresh
    for copy in copies[-4:-1]:
        copy.wait()
    own_map = map_ref[pl.ds(pl.multiple_of(side * HEAD_DIM, HEAD_DIM), HEAD_DIM), :]
    other_map = map_ref[pl.ds(pl.multiple_of((1 - side) * HEAD_DIM, HEAD_DIM), HEAD_DIM), :]
    for low in range(0, keep_ref.shape[0], TILE):
        rows = slice(low, low + TILE)
        own = keep_ref[rows, :].astype(F32)
        other = other_ref[rows, :].astype(F32)
        total = jnp.sum(own * own + other * other, axis=1, keepdims=True)
        norm = lax.rsqrt(total / (HEADS_GRP * HEAD_DIM) + 1e-05)
        query = (
            dot_nn((own * norm).astype(BF16), own_map) + dot_nn((other * norm).astype(BF16), other_map)
        ).astype(BF16)
        gate = dot_nt(query, new_ref[0]) * INVERSE
        up = dot_nt(query, new_ref[1]) * INVERSE
        hidden = (jax.nn.silu(gate) * up).astype(BF16)
        raw = dot_nn(hidden, new_ref[2])
        mean = jnp.mean(raw * raw, axis=1, keepdims=True)
        fast_ref[rows, :] = (raw * lax.rsqrt(mean + 1e-05)).astype(BF16)
    copies[-1].wait()
    for index, share_ref in enumerate(share_refs):
        width = share_ref.shape[1]
        start = pl.multiple_of(places_ref[0, index] * width, width)
        share_ref[...] = dot_nn(fast_ref[...], output_ref[:, pl.ds(start, width)]).astype(BF16)


def seq_shift(value, step):
    peers = lax.axis_size("seq")
    return lax.ppermute(
        value, "seq", [(i, i + step) for i in range(peers) if 0 <= i + step < peers]
    )


def head_swap(value, bit):
    return lax.ppermute(value, "head", [(i, i ^ bit) for i in range(lax.axis_size("head"))])


def seq_swap(value, bit):
    step = 1 << bit
    return lax.ppermute(value, "seq", [(i, i ^ step) for i in range(lax.axis_size("seq"))])


def after(value, others):
    return lax.optimization_barrier((value, others))[0]


def halving_start(chunks, orders):
    keeps = [keep for keep, _ in chunks]
    return keeps, [seq_swap(send, order[0]) for (_, send), order in zip(chunks, orders)]


def halving_step(keeps, found, orders, turn, wait=()):
    sends, rest = [], []
    for keep, new in zip(keeps, found):
        half = keep.shape[0] // 2
        sends.append((keep[half:].astype(F32) + new[half:].astype(F32)).astype(BF16))
        rest.append(lax.optimization_barrier(keep[:half].astype(F32) + new[:half].astype(F32)))
    sends = after(sends, wait) if wait else sends
    return rest, [seq_swap(send, order[turn]) for send, order in zip(sends, orders)]


def doubling_step(held, orders, turn, wait=()):
    whole = [jnp.concatenate(parts) if len(parts) > 1 else parts[0] for parts in held]
    whole = after(whole, wait) if wait else whole
    return [(own, seq_swap(own, order[turn])) for own, order in zip(whole, orders)]


def local(
    queries_first,
    keys_first,
    values_first,
    input_map,
    fast_keys,
    fast_values,
    step_rates,
    fast_weights,
    output_map,
    queries_second,
    keys_second,
    values_second,
):
    rows, width = queries_first.shape
    seq_count = lax.axis_size("seq")
    seq_place = lax.axis_index("seq")
    head_place = lax.axis_index("head")
    weights = jnp.transpose(fast_weights[0], (1, 0, 2))
    hidden_size, fast_width = weights.shape[1:]
    shape = jax.ShapeDtypeStruct
    minus = jnp.float32(-jnp.inf)
    side = seq_place % 2

    def edges_of(block):
        return [jnp.where(block > 0, 0.0, minus), jnp.where(block < seq_count - 1, 0.0, minus)]

    edges = jnp.stack(edges_of(seq_place) + edges_of(seq_place ^ 1)).reshape(2, 2)
    side_scalar = side.astype(jnp.int32).reshape(1, 1)
    place = seq_place.astype(jnp.int32).reshape(1, 1)

    packed = call(
        pack_kernel,
        shape((3 * rows, HEAD_DIM), BF16),
        (side_scalar, queries_first, keys_first, values_first),
        scalars=1,
    )
    other_first = seq_swap(packed, 0)

    bits = tuple(range(seq_count.bit_length() - 1))
    halving = seq_count == 1 << len(bits) and len(bits) > 1 and hidden_size >> len(bits) >= 16
    orders = (bits, bits[1:] + bits[:1]) if halving else ((), ())
    halves = 2 if halving else 1
    chunk_width = fast_width + fast_width // 2
    out_shapes = [shape((hidden_size // halves, chunk_width), BF16)] * (2 * halves)
    whole = pl.BlockSpec(memory_space=pltpu.VMEM)
    gradients = pl.pallas_call(
        functools.partial(gradient_kernel, orders),
        grid=(hidden_size // TILE,),
        out_shape=out_shapes,
        in_specs=[
            pl.BlockSpec(memory_space=pltpu.SMEM),
            whole,
            whole,
            whole,
            pl.BlockSpec((3, TILE, fast_width), lambda turn: (0, turn, 0)),
        ],
        out_specs=[whole] * len(out_shapes),
        scratch_shapes=[pltpu.VMEM((hidden_size, chunk_width), BF16)] * 2,
        compiler_params=pltpu.CompilerParams(vmem_limit_bytes=VMEM_MOST),
        cost_estimate=pl.CostEstimate(flops=1000, bytes_accessed=1000, transcendentals=0),
    )(place, step_rates.reshape(1, rows), fast_keys, fast_values, weights)

    low_block, high_block = call(
        border_kernel,
        [shape((2 * rows, HEAD_DIM), BF16)] * 2,
        (side_scalar, keys_first, values_first, other_first),
        scalars=1,
    )

    def first_halos(low_block, high_block):
        return seq_shift(high_block, 2), seq_shift(low_block, -2)

    def first_attention(prev_first, next_first):
        keep_first, send_first = call(
            first_kernel,
            [shape((rows, HEAD_DIM), BF16)] * 2,
            (edges, side_scalar, queries_first, other_first, prev_first, low_block, high_block, next_first),
            scalars=2,
            scratch=[pltpu.VMEM((4 * rows, HEAD_DIM), BF16)] * 2,
            cost=(12 * rows * rows * width, 16 * rows * width),
        )
        return keep_first, seq_swap(send_first, 0)

    both_second = jnp.concatenate([keys_second, values_second])

    if halving:
        turns = len(bits)
        keeps, found = halving_start([gradients[:2], gradients[2:]], orders)
        for turn in range(1, turns):
            if turn == turns - 1:
                prev_first, next_first = first_halos(*after((low_block, high_block), found))
                prev_second = seq_shift(after(both_second, found), 1)
            keeps, found = halving_step(keeps, found, orders, turn)
        held = [((keep.astype(F32) + new.astype(F32)).astype(BF16),) for keep, new in zip(keeps, found)]
        for turn in reversed(range(turns)):
            wait = ()
            if turn == 1:
                wait = (prev_first, next_first, prev_second)
            if turn == 0:
                keep_first, back_first = first_attention(prev_first, next_first)
                wait = (keep_first,)
            held = doubling_step(held, orders, turn, wait)
        gathered = [part for parts in held for part in parts]
        next_second = seq_shift(after(both_second, back_first), -1)
    else:
        gathered = lax.psum(gradients, "seq")
        keep_first, back_first = first_attention(*first_halos(low_block, high_block))
        prev_second, next_second = seq_shift(both_second, 1), seq_shift(both_second, -1)
    own_rows = hidden_size >> len(orders[0])
    my_bit, near = head_place % 2, head_place // 2
    places = jnp.stack(
        [2 * pair + bit for pair in (near ^ 1, near) for bit in (1 - my_bit, my_bit)]
    ).astype(jnp.int32).reshape(1, 4)
    share = shape((rows, width), BF16)
    operands = (*gathered, weights, keep_first, back_first, input_map[0], output_map)
    own_new, far_send, far_keep, near_send, near_keep = call(
        functools.partial(renew_kernel, orders),
        [shape((3, own_rows, fast_width), BF16)] + [share] * 4,
        (place, side_scalar, places, *operands),
        scalars=3,
        anywhere=len(operands),
        scratch=[pltpu.VMEM(operand.shape, BF16) for operand in operands]
        + [
            pltpu.VMEM((rows, fast_width), BF16),
            pltpu.VMEM(weights.shape, BF16),
            pltpu.SemaphoreType.DMA((len(operands),)),
        ],
        limit=VMEM_MOST,
    )
    far_near = head_swap(far_send, 1)
    near_near = head_swap(after(near_send, next_second), 1)
    half = rows // 2
    far_parts = []
    for part in (slice(0, half), slice(half, rows)):
        far_sum = far_keep[part].astype(F32) + far_near[part].astype(F32)
        far_parts.append(head_swap(far_sum.astype(BF16), 2))
    if not halving:
        share_rows = hidden_size // seq_count
        own_new = lax.dynamic_slice_in_dim(own_new, seq_place * share_rows, share_rows, 1)

    def second_attention(part, *done):
        return call(
            second_kernel,
            shape((half * (1 + len(done)), width), BF16),
            (edges, queries_second, near_keep, near_near, far_parts[part],
             prev_second, keys_second, values_second, next_second, *done),
            scalars=1,
            cost=(6 * rows * rows * width, 16 * rows * width),
        )

    normed_second = second_attention(1, second_attention(0))
    return (normed_second, jnp.transpose(own_new, (1, 0, 2))[None])


def solution(mesh):
    return jax.shard_map(
        local,
        mesh=mesh,
        in_specs=(
            P("seq", "head"),
            P("seq", "head"),
            P("seq", "head"),
            P("head", None, None),
            P("seq", "head"),
            P("seq", "head"),
            P("seq", "head"),
            P("head", None, None, None),
            P("head", None),
            P("seq", "head"),
            P("seq", "head"),
            P("seq", "head"),
        ),
        out_specs=(P("seq", "head"), P("head", "seq", None, None)),
        check_vma=False,
    )
```

```python
import functools
import math

import jax
import jax.numpy as jnp
from jax import lax
from jax.experimental import pallas as pl
from jax.experimental.pallas import tpu as pltpu
from jax.sharding import PartitionSpec as P

HALF_WIN = 512
HEAD_DIM = 128
HEADS_GRP = 2
FAST_DIM = 512
FAST_HIDDEN = 512
TILE = 128
QUERY_TILE = 256
VMEM_LIMIT = 24 * 1024 * 1024
VMEM_MOST = 60 * 1024 * 1024

BF16 = jnp.bfloat16
F32 = jnp.float32
INVERSE = 1.0 / math.sqrt(FAST_DIM)


def dot_nn(left, right):
    return lax.dot_general(left, right, (((1,), (0,)), ((), ())), preferred_element_type=F32)


def dot_nt(left, right):
    return lax.dot_general(left, right, (((1,), (1,)), ((), ())), preferred_element_type=F32)


def call(body, out_shapes, operands, scalars=0, anywhere=0, scratch=(), cost=None, limit=VMEM_LIMIT):
    vmem = pl.BlockSpec(memory_space=pltpu.VMEM)
    in_specs = (
        [pl.BlockSpec(memory_space=pltpu.SMEM)] * scalars
        + [vmem] * (len(operands) - scalars - anywhere)
        + [pl.BlockSpec(memory_space=pl.ANY)] * anywhere
    )
    flops, moved = cost or (1000, 1000)
    return pl.pallas_call(
        body,
        out_shape=out_shapes,
        in_specs=in_specs,
        out_specs=jax.tree.map(lambda _: vmem, out_shapes),
        scratch_shapes=scratch,
        compiler_params=pltpu.CompilerParams(vmem_limit_bytes=limit),
        cost_estimate=pl.CostEstimate(flops=flops, bytes_accessed=moved, transcendentals=0),
    )(*operands)


def slot_of(block, order):
    slot = 0
    for bit in order:
        slot = slot * 2 + ((block >> bit) & 1)
    return slot


def gradient_kernel(orders, place_ref, rates_ref, keys_ref, values_ref, weights_ref, *refs):
    out_refs, chunk_refs = refs[:-2], refs[-2:]
    place = place_ref[0, 0]
    rates = rates_ref[...]
    keys = keys_ref[...]
    values = values_ref[...]
    hidden_size = chunk_refs[0].shape[0]
    width = weights_ref.shape[2]
    turn = pl.program_id(0)
    step = weights_ref.shape[1]

    def put(chunk, columns, product):
        order = orders[chunk]
        block_rows = min(step, hidden_size >> len(order))
        for start in range(0, step, block_rows):
            row = turn * step + start
            if order:
                block = turn * (step // block_rows) + start // block_rows
                row = slot_of(block ^ place, order) * block_rows
            row = pl.multiple_of(row, block_rows)
            chunk_refs[chunk][pl.ds(row, block_rows), columns] = product[start:start + block_rows]

    gate = dot_nt(weights_ref[0], keys) * INVERSE
    up = dot_nt(weights_ref[1], keys) * INVERSE
    sigmoid = jax.nn.sigmoid(gate)
    silu = gate * sigmoid
    hidden = (rates * silu * up).astype(BF16)
    backward = rates * dot_nt(weights_ref[2], values)
    d_gate = (backward * up * sigmoid * (1.0 + gate * (1.0 - sigmoid)) * INVERSE).astype(BF16)
    d_up = (backward * silu * INVERSE).astype(BF16)
    up_part = dot_nn(d_up, keys).astype(BF16)
    put(0, slice(0, width), dot_nn(d_gate, keys).astype(BF16))
    put(0, slice(width, width + width // 2), up_part[:, :width // 2])
    put(1, slice(0, width), dot_nn(hidden, values).astype(BF16))
    put(1, slice(width, width + width // 2), up_part[:, width // 2:])

    @pl.when(turn == pl.num_programs(0) - 1)
    def _():
        halves = len(out_refs) // 2
        half_rows = hidden_size // halves
        for index, out_ref in enumerate(out_refs):
            half = index % halves
            out_ref[...] = chunk_refs[index // halves][half * half_rows:(half + 1) * half_rows, :]


def attend_rows(edge_prev, edge_next, query_tile, keys_prev, keys_own, keys_next,
                values_prev, values_own, values_next):
    scale = math.log2(math.e) / math.sqrt(HEAD_DIM)
    row = lax.broadcasted_iota(jnp.int32, (QUERY_TILE, QUERY_TILE), 0)
    col = lax.broadcasted_iota(jnp.int32, (QUERY_TILE, QUERY_TILE), 1)
    minus = jnp.float32(-jnp.inf)
    score_prev = dot_nt(query_tile, keys_prev)
    score_own = dot_nt(query_tile, keys_own)
    score_next = dot_nt(query_tile, keys_next)
    parts = [score_prev[:, :QUERY_TILE] + jnp.where(col >= row, edge_prev, minus)]
    if score_prev.shape[1] > QUERY_TILE:
        parts.append(score_prev[:, QUERY_TILE:] + edge_prev)
    parts.append(score_own)
    if score_next.shape[1] > QUERY_TILE:
        parts.append(score_next[:, :-QUERY_TILE] + edge_next)
    parts.append(score_next[:, -QUERY_TILE:] + jnp.where(col <= row, edge_next, minus))
    scores = jnp.concatenate(parts, axis=1)
    highest = jnp.max(scores, axis=1, keepdims=True)
    weights = jnp.exp2((scores - highest) * scale)
    total = jnp.sum(weights, axis=1, keepdims=True)
    weights = weights.astype(BF16)
    width_prev, width_own = score_prev.shape[1], score_own.shape[1]
    attended = (
        dot_nn(weights[:, :width_prev], values_prev)
        + dot_nn(weights[:, width_prev:width_prev + width_own], values_own)
        + dot_nn(weights[:, width_prev + width_own:], values_next)
    )
    return attended / total


def pack_kernel(side_ref, queries_ref, keys_ref, values_ref, out_ref):
    count = queries_ref.shape[0]
    start = pl.multiple_of((1 - side_ref[0, 0]) * HEAD_DIM, HEAD_DIM)
    for index, ref in enumerate((queries_ref, keys_ref, values_ref)):
        out_ref[index * count:(index + 1) * count, :] = ref[:, pl.ds(start, HEAD_DIM)]


def border_kernel(side_ref, keys_ref, values_ref, other_ref, low_ref, high_ref):
    count = keys_ref.shape[0]
    side = side_ref[0, 0]
    start = pl.multiple_of(side * HEAD_DIM, HEAD_DIM)

    def fill(own_ref, other_out_ref):
        own_ref[:count, :] = keys_ref[:, pl.ds(start, HEAD_DIM)]
        own_ref[count:, :] = values_ref[:, pl.ds(start, HEAD_DIM)]
        other_out_ref[...] = other_ref[count:, :]

    @pl.when(side == 0)
    def _():
        fill(low_ref, high_ref)

    @pl.when(side != 0)
    def _():
        fill(high_ref, low_ref)


def first_kernel(edge_ref, side_ref, queries_ref, other_ref, prev_ref, low_ref, high_ref, next_ref,
                 keep_ref, send_ref, keys_ref, values_ref):
    count = queries_ref.shape[0]
    side = side_ref[0, 0]
    for index, ref in enumerate((prev_ref, low_ref, high_ref, next_ref)):
        rows = slice(index * count, (index + 1) * count)
        keys_ref[rows, :] = ref[:count, :]
        values_ref[rows, :] = ref[count:, :]
    start = pl.multiple_of(side * HEAD_DIM, HEAD_DIM)
    for turn, out_ref in enumerate((keep_ref, send_ref)):
        base = (side if turn == 0 else 1 - side) * count

        def span(ref, low, length):
            return ref[pl.ds(pl.multiple_of(base + low, QUERY_TILE), length), :]

        for index in range(count // QUERY_TILE):
            low, high = index * QUERY_TILE, (index + 1) * QUERY_TILE
            query = queries_ref[low:high, pl.ds(start, HEAD_DIM)] if turn == 0 else other_ref[low:high, :]
            out_ref[low:high, :] = attend_rows(
                edge_ref[turn, 0], edge_ref[turn, 1], query,
                span(keys_ref, low, count - low), span(keys_ref, count, count),
                span(keys_ref, 2 * count, high),
                span(values_ref, low, count - low), span(values_ref, count, count),
                span(values_ref, 2 * count, high),
            ).astype(BF16)


def second_kernel(edge_ref, queries_ref, keep_ref, near_ref, far_ref, prev_ref, keys_ref, values_ref, next_ref,
                  *refs):
    done_refs, out_ref = refs[:-1], refs[-1]
    count = keys_ref.shape[0]
    half = far_ref.shape[0]
    offset = half if done_refs else 0
    if done_refs:
        out_ref[:half, :] = done_refs[0][...]
    for low in range(offset, offset + half, QUERY_TILE):
        high = low + QUERY_TILE
        rows = slice(low, high)
        mixed = (
            keep_ref[rows, :].astype(F32)
            + near_ref[rows, :].astype(F32)
            + far_ref[low - offset:high - offset, :].astype(F32)
        )
        query = (queries_ref[rows, :].astype(F32) + mixed).astype(BF16)
        heads = []
        for head in range(HEADS_GRP):
            cols = slice(head * HEAD_DIM, (head + 1) * HEAD_DIM)
            heads.append(
                attend_rows(
                    edge_ref[0, 0], edge_ref[0, 1], query[:, cols],
                    prev_ref[low:count, cols], keys_ref[:, cols], next_ref[:high, cols],
                    prev_ref[count + low:, cols], values_ref[:, cols], next_ref[count:count + high, cols],
                )
            )
        both = jnp.concatenate(heads, axis=1)
        mean = jnp.mean(both * both, axis=1, keepdims=True)
        out_ref[rows, :] = (both * lax.rsqrt(mean + 1e-05)).astype(BF16)


def renew_kernel(orders, place_ref, side_ref, *refs):
    count = (len(refs) - 4) // 2
    sources, (own_ref, fast_ref), loaded = refs[:count], refs[count:count + 2], refs[count + 2:-2]
    new_ref, sems = refs[-2:]
    copies = [
        pltpu.make_async_copy(source, target, sems.at[index])
        for index, (source, target) in enumerate(zip(sources, loaded))
    ]
    for copy in copies:
        copy.start()
    pieces, (weights_ref, keep_ref, other_ref, map_ref) = loaded[:-4], loaded[-4:]
    place = place_ref[0, 0]
    side = side_ref[0, 0]
    hidden_size, width = weights_ref.shape[1:]
    for copy in copies[:-4]:
        copy.wait()
    limit_norm = math.sqrt(FAST_HIDDEN * FAST_DIM) / 2.0
    step = 64
    square = jnp.zeros((1, pieces[0].shape[1]), F32)
    for piece in pieces:
        for low in range(0, piece.shape[0], step):
            part = piece[low:low + step, :].astype(F32)
            square = square + jnp.sum(part * part, axis=0, keepdims=True)
    square = jnp.sum(square, axis=1, keepdims=True)
    factor = jnp.minimum(1.0, limit_norm * lax.rsqrt(square + 1e-06))
    copies[-4].wait()
    per_chunk = len(pieces) // 2
    piece_rows = pieces[0].shape[0]
    blocks = 1 << len(orders[0])
    block_rows = hidden_size // blocks
    count = min(step, block_rows)
    for block in range(blocks):
        starts = [slot_of(block, order) * block_rows for order in orders]
        for low in range(0, block_rows, count):
            found = []
            for chunk, start in enumerate(starts):
                piece = pieces[chunk * per_chunk + start // piece_rows]
                inside = start % piece_rows + low
                found.append(piece[inside:inside + count, :].astype(F32))
            parts = [
                found[0][:, :width],
                jnp.concatenate([found[0][:, width:], found[1][:, width:]], axis=1),
                found[1][:, :width],
            ]
            rows = slice(low, low + count)
            if blocks > 1:
                rows = pl.ds(pl.multiple_of((block ^ place) * block_rows + low, count), count)
            for matrix, part in enumerate(parts):
                old = weights_ref[matrix, rows, :].astype(F32)
                stepped = old + factor * part
                norm = jnp.sqrt(jnp.sum(old * old, axis=1, keepdims=True))
                size = jnp.sum(stepped * stepped, axis=1, keepdims=True)
                fresh = (stepped * norm * lax.rsqrt(size + 1e-06)).astype(BF16)
                new_ref[matrix, rows, :] = fresh
                if block == 0:
                    own_ref[matrix, low:low + count, :] = fresh
    for copy in copies[-3:]:
        copy.wait()
    own_map = map_ref[pl.ds(pl.multiple_of(side * HEAD_DIM, HEAD_DIM), HEAD_DIM), :]
    other_map = map_ref[pl.ds(pl.multiple_of((1 - side) * HEAD_DIM, HEAD_DIM), HEAD_DIM), :]
    for low in range(0, keep_ref.shape[0], TILE):
        rows = slice(low, low + TILE)
        own = keep_ref[rows, :].astype(F32)
        other = other_ref[rows, :].astype(F32)
        total = jnp.sum(own * own + other * other, axis=1, keepdims=True)
        norm = lax.rsqrt(total / (HEADS_GRP * HEAD_DIM) + 1e-05)
        query = (
            dot_nn((own * norm).astype(BF16), own_map) + dot_nn((other * norm).astype(BF16), other_map)
        ).astype(BF16)
        gate = dot_nt(query, new_ref[0]) * INVERSE
        up = dot_nt(query, new_ref[1]) * INVERSE
        hidden = (jax.nn.silu(gate) * up).astype(BF16)
        raw = dot_nn(hidden, new_ref[2])
        mean = jnp.mean(raw * raw, axis=1, keepdims=True)
        fast_ref[rows, :] = (raw * lax.rsqrt(mean + 1e-05)).astype(BF16)


def mix_kernel(pair, places_ref, fast_ref, map_ref, *out_refs):
    for index, out_ref in enumerate(out_refs):
        width = out_ref.shape[1]
        start = pl.multiple_of(places_ref[0, 2 * pair + index] * width, width)
        out_ref[...] = dot_nn(fast_ref[...], map_ref[:, pl.ds(start, width)]).astype(BF16)


def seq_shift(value, step):
    peers = lax.axis_size("seq")
    return lax.ppermute(
        value, "seq", [(i, i + step) for i in range(peers) if 0 <= i + step < peers]
    )


def head_swap(value, bit):
    return lax.ppermute(value, "head", [(i, i ^ bit) for i in range(lax.axis_size("head"))])


def seq_swap(value, bit):
    step = 1 << bit
    return lax.ppermute(value, "seq", [(i, i ^ step) for i in range(lax.axis_size("seq"))])


def after(value, others):
    return lax.optimization_barrier((value, others))[0]


def halving_start(chunks, orders):
    keeps = [keep for keep, _ in chunks]
    return keeps, [seq_swap(send, order[0]) for (_, send), order in zip(chunks, orders)]


def halving_step(keeps, found, orders, turn, wait=()):
    sends, rest = [], []
    for keep, new in zip(keeps, found):
        half = keep.shape[0] // 2
        sends.append((keep[half:].astype(F32) + new[half:].astype(F32)).astype(BF16))
        rest.append(lax.optimization_barrier(keep[:half].astype(F32) + new[:half].astype(F32)))
    sends = after(sends, wait) if wait else sends
    return rest, [seq_swap(send, order[turn]) for send, order in zip(sends, orders)]


def doubling_step(held, orders, turn, wait=()):
    whole = [jnp.concatenate(parts) if len(parts) > 1 else parts[0] for parts in held]
    whole = after(whole, wait) if wait else whole
    return [(own, seq_swap(own, order[turn])) for own, order in zip(whole, orders)]


def local(
    queries_first,
    keys_first,
    values_first,
    input_map,
    fast_keys,
    fast_values,
    step_rates,
    fast_weights,
    output_map,
    queries_second,
    keys_second,
    values_second,
):
    rows, width = queries_first.shape
    seq_count = lax.axis_size("seq")
    seq_place = lax.axis_index("seq")
    head_place = lax.axis_index("head")
    weights = jnp.transpose(fast_weights[0], (1, 0, 2))
    hidden_size, fast_width = weights.shape[1:]
    shape = jax.ShapeDtypeStruct
    minus = jnp.float32(-jnp.inf)
    side = seq_place % 2

    def edges_of(block):
        return [jnp.where(block > 0, 0.0, minus), jnp.where(block < seq_count - 1, 0.0, minus)]

    edges = jnp.stack(edges_of(seq_place) + edges_of(seq_place ^ 1)).reshape(2, 2)
    side_scalar = side.astype(jnp.int32).reshape(1, 1)
    place = seq_place.astype(jnp.int32).reshape(1, 1)

    packed = call(
        pack_kernel,
        shape((3 * rows, HEAD_DIM), BF16),
        (side_scalar, queries_first, keys_first, values_first),
        scalars=1,
    )
    other_first = seq_swap(packed, 0)

    bits = tuple(range(seq_count.bit_length() - 1))
    halving = seq_count == 1 << len(bits) and len(bits) > 1 and hidden_size >> len(bits) >= 16
    orders = (bits, bits[1:] + bits[:1]) if halving else ((), ())
    halves = 2 if halving else 1
    chunk_width = fast_width + fast_width // 2
    out_shapes = [shape((hidden_size // halves, chunk_width), BF16)] * (2 * halves)
    whole = pl.BlockSpec(memory_space=pltpu.VMEM)
    gradients = pl.pallas_call(
        functools.partial(gradient_kernel, orders),
        grid=(hidden_size // TILE,),
        out_shape=out_shapes,
        in_specs=[
            pl.BlockSpec(memory_space=pltpu.SMEM),
            whole,
            whole,
            whole,
            pl.BlockSpec((3, TILE, fast_width), lambda turn: (0, turn, 0)),
        ],
        out_specs=[whole] * len(out_shapes),
        scratch_shapes=[pltpu.VMEM((hidden_size, chunk_width), BF16)] * 2,
        compiler_params=pltpu.CompilerParams(vmem_limit_bytes=VMEM_MOST),
        cost_estimate=pl.CostEstimate(flops=1000, bytes_accessed=1000, transcendentals=0),
    )(place, step_rates.reshape(1, rows), fast_keys, fast_values, weights)

    low_block, high_block = call(
        border_kernel,
        [shape((2 * rows, HEAD_DIM), BF16)] * 2,
        (side_scalar, keys_first, values_first, other_first),
        scalars=1,
    )

    def first_halos(low_block, high_block):
        return seq_shift(high_block, 2), seq_shift(low_block, -2)

    def first_attention(prev_first, next_first):
        keep_first, send_first = call(
            first_kernel,
            [shape((rows, HEAD_DIM), BF16)] * 2,
            (edges, side_scalar, queries_first, other_first, prev_first, low_block, high_block, next_first),
            scalars=2,
            scratch=[pltpu.VMEM((4 * rows, HEAD_DIM), BF16)] * 2,
            cost=(12 * rows * rows * width, 16 * rows * width),
        )
        return keep_first, seq_swap(send_first, 0)

    both_second = jnp.concatenate([keys_second, values_second])

    if halving:
        turns = len(bits)
        keeps, found = halving_start([gradients[:2], gradients[2:]], orders)
        prev_second = seq_shift(both_second, 1)
        for turn in range(1, turns):
            if turn == turns - 1:
                prev_first, next_first = first_halos(*after((low_block, high_block), found))
            keeps, found = halving_step(keeps, found, orders, turn)
        held = [((keep.astype(F32) + new.astype(F32)).astype(BF16),) for keep, new in zip(keeps, found)]
        for turn in reversed(range(turns)):
            wait = ()
            if turn == 1:
                wait = (prev_first, next_first, prev_second)
            if turn == 0:
                keep_first, back_first = first_attention(prev_first, next_first)
                wait = (keep_first,)
            held = doubling_step(held, orders, turn, wait)
        gathered = [part for parts in held for part in parts]
        next_second = seq_shift(after(both_second, back_first), -1)
    else:
        gathered = lax.psum(gradients, "seq")
        keep_first, back_first = first_attention(*first_halos(low_block, high_block))
        prev_second, next_second = seq_shift(both_second, 1), seq_shift(both_second, -1)
    own_rows = hidden_size >> len(orders[0])
    my_bit, near = head_place % 2, head_place // 2
    places = jnp.stack(
        [2 * pair + bit for pair in (near ^ 1, near) for bit in (1 - my_bit, my_bit)]
    ).astype(jnp.int32).reshape(1, 4)
    share = shape((rows, width), BF16)
    operands = (*gathered, weights, keep_first, back_first, input_map[0])
    own_new, fast_out = call(
        functools.partial(renew_kernel, orders),
        [shape((3, own_rows, fast_width), BF16), shape((rows, fast_width), BF16)],
        (place, side_scalar, *operands),
        scalars=2,
        anywhere=len(operands),
        scratch=[pltpu.VMEM(operand.shape, BF16) for operand in operands]
        + [pltpu.VMEM(weights.shape, BF16), pltpu.SemaphoreType.DMA((len(operands),))],
        limit=VMEM_MOST,
    )

    def mixed_for(pair, fast):
        return call(
            functools.partial(mix_kernel, pair), [share, share], (places, fast, output_map), scalars=1
        )

    far_send, far_keep = mixed_for(0, fast_out)
    far_near = head_swap(far_send, 1)
    near_send, near_keep = mixed_for(1, after(fast_out, next_second))
    near_near = head_swap(near_send, 1)
    half = rows // 2
    far_parts = []
    for part in (slice(0, half), slice(half, rows)):
        far_sum = far_keep[part].astype(F32) + far_near[part].astype(F32)
        far_parts.append(head_swap(far_sum.astype(BF16), 2))
    if not halving:
        share_rows = hidden_size // seq_count
        own_new = lax.dynamic_slice_in_dim(own_new, seq_place * share_rows, share_rows, 1)

    def second_attention(part, *done):
        return call(
            second_kernel,
            shape((half * (1 + len(done)), width), BF16),
            (edges, queries_second, near_keep, near_near, far_parts[part],
             prev_second, keys_second, values_second, next_second, *done),
            scalars=1,
            cost=(6 * rows * rows * width, 16 * rows * width),
        )

    normed_second = second_attention(1, second_attention(0))
    return (normed_second, jnp.transpose(own_new, (1, 0, 2))[None])


def solution(mesh):
    return jax.shard_map(
        local,
        mesh=mesh,
        in_specs=(
            P("seq", "head"),
            P("seq", "head"),
            P("seq", "head"),
            P("head", None, None),
            P("seq", "head"),
            P("seq", "head"),
            P("seq", "head"),
            P("head", None, None, None),
            P("head", None),
            P("seq", "head"),
            P("seq", "head"),
            P("seq", "head"),
        ),
        out_specs=(P("seq", "head"), P("head", "seq", None, None)),
        check_vma=False,
    )
```

```python
import functools
import math

import jax
import jax.numpy as jnp
from jax import lax
from jax.experimental import pallas as pl
from jax.experimental.pallas import tpu as pltpu
from jax.sharding import PartitionSpec as P

HALF_WIN = 512
HEAD_DIM = 128
HEADS_GRP = 2
FAST_DIM = 512
FAST_HIDDEN = 512
TILE = 128
QUERY_TILE = 256
VMEM_LIMIT = 24 * 1024 * 1024
VMEM_MOST = 60 * 1024 * 1024

BF16 = jnp.bfloat16
F32 = jnp.float32
INVERSE = 1.0 / math.sqrt(FAST_DIM)


def dot_nn(left, right):
    return lax.dot_general(left, right, (((1,), (0,)), ((), ())), preferred_element_type=F32)


def dot_nt(left, right):
    return lax.dot_general(left, right, (((1,), (1,)), ((), ())), preferred_element_type=F32)


def call(body, out_shapes, operands, scalars=0, anywhere=0, scratch=(), cost=None, limit=VMEM_LIMIT):
    vmem = pl.BlockSpec(memory_space=pltpu.VMEM)
    in_specs = (
        [pl.BlockSpec(memory_space=pltpu.SMEM)] * scalars
        + [vmem] * (len(operands) - scalars - anywhere)
        + [pl.BlockSpec(memory_space=pl.ANY)] * anywhere
    )
    flops, moved = cost or (1000, 1000)
    return pl.pallas_call(
        body,
        out_shape=out_shapes,
        in_specs=in_specs,
        out_specs=jax.tree.map(lambda _: vmem, out_shapes),
        scratch_shapes=scratch,
        compiler_params=pltpu.CompilerParams(vmem_limit_bytes=limit),
        cost_estimate=pl.CostEstimate(flops=flops, bytes_accessed=moved, transcendentals=0),
    )(*operands)


def slot_of(block, order):
    slot = 0
    for bit in order:
        slot = slot * 2 + ((block >> bit) & 1)
    return slot


def gradient_kernel(orders, place_ref, rates_ref, keys_ref, values_ref, weights_ref, *refs):
    out_refs, chunk_refs = refs[:-2], refs[-2:]
    place = place_ref[0, 0]
    rates = rates_ref[...]
    keys = keys_ref[...]
    values = values_ref[...]
    hidden_size = chunk_refs[0].shape[0]
    width = weights_ref.shape[2]
    turn = pl.program_id(0)
    step = weights_ref.shape[1]

    def put(chunk, columns, product):
        order = orders[chunk]
        block_rows = min(step, hidden_size >> len(order))
        for start in range(0, step, block_rows):
            row = turn * step + start
            if order:
                block = turn * (step // block_rows) + start // block_rows
                row = slot_of(block ^ place, order) * block_rows
            row = pl.multiple_of(row, block_rows)
            chunk_refs[chunk][pl.ds(row, block_rows), columns] = product[start:start + block_rows]

    gate = dot_nt(weights_ref[0], keys) * INVERSE
    up = dot_nt(weights_ref[1], keys) * INVERSE
    sigmoid = jax.nn.sigmoid(gate)
    silu = gate * sigmoid
    hidden = (rates * silu * up).astype(BF16)
    backward = rates * dot_nt(weights_ref[2], values)
    d_gate = (backward * up * sigmoid * (1.0 + gate * (1.0 - sigmoid)) * INVERSE).astype(BF16)
    d_up = (backward * silu * INVERSE).astype(BF16)
    up_part = dot_nn(d_up, keys).astype(BF16)
    put(0, slice(0, width), dot_nn(d_gate, keys).astype(BF16))
    put(0, slice(width, width + width // 2), up_part[:, :width // 2])
    put(1, slice(0, width), dot_nn(hidden, values).astype(BF16))
    put(1, slice(width, width + width // 2), up_part[:, width // 2:])

    @pl.when(turn == pl.num_programs(0) - 1)
    def _():
        halves = len(out_refs) // 2
        half_rows = hidden_size // halves
        for index, out_ref in enumerate(out_refs):
            half = index % halves
            out_ref[...] = chunk_refs[index // halves][half * half_rows:(half + 1) * half_rows, :]


def attend_rows(edge_prev, edge_next, query_tile, keys_prev, keys_own, keys_next,
                values_prev, values_own, values_next):
    scale = math.log2(math.e) / math.sqrt(HEAD_DIM)
    row = lax.broadcasted_iota(jnp.int32, (QUERY_TILE, QUERY_TILE), 0)
    col = lax.broadcasted_iota(jnp.int32, (QUERY_TILE, QUERY_TILE), 1)
    minus = jnp.float32(-jnp.inf)
    score_prev = dot_nt(query_tile, keys_prev)
    score_own = dot_nt(query_tile, keys_own)
    score_next = dot_nt(query_tile, keys_next)
    parts = [score_prev[:, :QUERY_TILE] + jnp.where(col >= row, edge_prev, minus)]
    if score_prev.shape[1] > QUERY_TILE:
        parts.append(score_prev[:, QUERY_TILE:] + edge_prev)
    parts.append(score_own)
    if score_next.shape[1] > QUERY_TILE:
        parts.append(score_next[:, :-QUERY_TILE] + edge_next)
    parts.append(score_next[:, -QUERY_TILE:] + jnp.where(col <= row, edge_next, minus))
    scores = jnp.concatenate(parts, axis=1)
    highest = jnp.max(scores, axis=1, keepdims=True)
    weights = jnp.exp2((scores - highest) * scale)
    total = jnp.sum(weights, axis=1, keepdims=True)
    weights = weights.astype(BF16)
    width_prev, width_own = score_prev.shape[1], score_own.shape[1]
    attended = (
        dot_nn(weights[:, :width_prev], values_prev)
        + dot_nn(weights[:, width_prev:width_prev + width_own], values_own)
        + dot_nn(weights[:, width_prev + width_own:], values_next)
    )
    return attended / total


def pack_kernel(side_ref, queries_ref, keys_ref, values_ref, out_ref):
    count = queries_ref.shape[0]
    start = pl.multiple_of((1 - side_ref[0, 0]) * HEAD_DIM, HEAD_DIM)
    for index, ref in enumerate((queries_ref, keys_ref, values_ref)):
        out_ref[index * count:(index + 1) * count, :] = ref[:, pl.ds(start, HEAD_DIM)]


def border_kernel(side_ref, keys_ref, values_ref, other_ref, low_ref, high_ref):
    count = keys_ref.shape[0]
    side = side_ref[0, 0]
    start = pl.multiple_of(side * HEAD_DIM, HEAD_DIM)

    def fill(own_ref, other_out_ref):
        own_ref[:count, :] = keys_ref[:, pl.ds(start, HEAD_DIM)]
        own_ref[count:, :] = values_ref[:, pl.ds(start, HEAD_DIM)]
        other_out_ref[...] = other_ref[count:, :]

    @pl.when(side == 0)
    def _():
        fill(low_ref, high_ref)

    @pl.when(side != 0)
    def _():
        fill(high_ref, low_ref)


def first_kernel(edge_ref, side_ref, queries_ref, other_ref, prev_ref, low_ref, high_ref, next_ref,
                 keep_ref, send_ref, keys_ref, values_ref):
    count = queries_ref.shape[0]
    side = side_ref[0, 0]
    for index, ref in enumerate((prev_ref, low_ref, high_ref, next_ref)):
        rows = slice(index * count, (index + 1) * count)
        keys_ref[rows, :] = ref[:count, :]
        values_ref[rows, :] = ref[count:, :]
    start = pl.multiple_of(side * HEAD_DIM, HEAD_DIM)
    for turn, out_ref in enumerate((keep_ref, send_ref)):
        base = (side if turn == 0 else 1 - side) * count

        def span(ref, low, length):
            return ref[pl.ds(pl.multiple_of(base + low, QUERY_TILE), length), :]

        for index in range(count // QUERY_TILE):
            low, high = index * QUERY_TILE, (index + 1) * QUERY_TILE
            query = queries_ref[low:high, pl.ds(start, HEAD_DIM)] if turn == 0 else other_ref[low:high, :]
            out_ref[low:high, :] = attend_rows(
                edge_ref[turn, 0], edge_ref[turn, 1], query,
                span(keys_ref, low, count - low), span(keys_ref, count, count),
                span(keys_ref, 2 * count, high),
                span(values_ref, low, count - low), span(values_ref, count, count),
                span(values_ref, 2 * count, high),
            ).astype(BF16)


def second_kernel(edge_ref, queries_ref, keep_ref, near_ref, far_ref, prev_ref, keys_ref, values_ref, next_ref,
                  *refs):
    done_refs, out_ref = refs[:-1], refs[-1]
    count = keys_ref.shape[0]
    half = far_ref.shape[0]
    offset = half if done_refs else 0
    if done_refs:
        out_ref[:half, :] = done_refs[0][...]
    for low in range(offset, offset + half, QUERY_TILE):
        high = low + QUERY_TILE
        rows = slice(low, high)
        mixed = (
            keep_ref[rows, :].astype(F32)
            + near_ref[rows, :].astype(F32)
            + far_ref[low - offset:high - offset, :].astype(F32)
        )
        query = (queries_ref[rows, :].astype(F32) + mixed).astype(BF16)
        heads = []
        for head in range(HEADS_GRP):
            cols = slice(head * HEAD_DIM, (head + 1) * HEAD_DIM)
            heads.append(
                attend_rows(
                    edge_ref[0, 0], edge_ref[0, 1], query[:, cols],
                    prev_ref[low:count, cols], keys_ref[:, cols], next_ref[:high, cols],
                    prev_ref[count + low:, cols], values_ref[:, cols], next_ref[count:count + high, cols],
                )
            )
        both = jnp.concatenate(heads, axis=1)
        mean = jnp.mean(both * both, axis=1, keepdims=True)
        out_ref[rows, :] = (both * lax.rsqrt(mean + 1e-05)).astype(BF16)


def renew_kernel(orders, place_ref, side_ref, *refs):
    count = (len(refs) - 4) // 2
    sources, (own_ref, fast_ref), loaded = refs[:count], refs[count:count + 2], refs[count + 2:-2]
    new_ref, sems = refs[-2:]
    copies = [
        pltpu.make_async_copy(source, target, sems.at[index])
        for index, (source, target) in enumerate(zip(sources, loaded))
    ]
    for copy in copies:
        copy.start()
    pieces, (weights_ref, keep_ref, other_ref, map_ref) = loaded[:-4], loaded[-4:]
    place = place_ref[0, 0]
    side = side_ref[0, 0]
    hidden_size, width = weights_ref.shape[1:]
    for copy in copies[:-4]:
        copy.wait()
    limit_norm = math.sqrt(FAST_HIDDEN * FAST_DIM) / 2.0
    step = 64
    square = jnp.zeros((1, pieces[0].shape[1]), F32)
    for piece in pieces:
        for low in range(0, piece.shape[0], step):
            part = piece[low:low + step, :].astype(F32)
            square = square + jnp.sum(part * part, axis=0, keepdims=True)
    square = jnp.sum(square, axis=1, keepdims=True)
    factor = jnp.minimum(1.0, limit_norm * lax.rsqrt(square + 1e-06))
    copies[-4].wait()
    per_chunk = len(pieces) // 2
    piece_rows = pieces[0].shape[0]
    blocks = 1 << len(orders[0])
    block_rows = hidden_size // blocks
    count = min(step, block_rows)
    for block in range(blocks):
        starts = [slot_of(block, order) * block_rows for order in orders]
        for low in range(0, block_rows, count):
            found = []
            for chunk, start in enumerate(starts):
                piece = pieces[chunk * per_chunk + start // piece_rows]
                inside = start % piece_rows + low
                found.append(piece[inside:inside + count, :].astype(F32))
            parts = [
                found[0][:, :width],
                jnp.concatenate([found[0][:, width:], found[1][:, width:]], axis=1),
                found[1][:, :width],
            ]
            rows = slice(low, low + count)
            if blocks > 1:
                rows = pl.ds(pl.multiple_of((block ^ place) * block_rows + low, count), count)
            for matrix, part in enumerate(parts):
                old = weights_ref[matrix, rows, :].astype(F32)
                stepped = old + factor * part
                norm = jnp.sqrt(jnp.sum(old * old, axis=1, keepdims=True))
                size = jnp.sum(stepped * stepped, axis=1, keepdims=True)
                fresh = (stepped * norm * lax.rsqrt(size + 1e-06)).astype(BF16)
                new_ref[matrix, rows, :] = fresh
                if block == 0:
                    own_ref[matrix, low:low + count, :] = fresh
    for copy in copies[-3:]:
        copy.wait()
    own_map = map_ref[pl.ds(pl.multiple_of(side * HEAD_DIM, HEAD_DIM), HEAD_DIM), :]
    other_map = map_ref[pl.ds(pl.multiple_of((1 - side) * HEAD_DIM, HEAD_DIM), HEAD_DIM), :]
    for low in range(0, keep_ref.shape[0], TILE):
        rows = slice(low, low + TILE)
        own = keep_ref[rows, :].astype(F32)
        other = other_ref[rows, :].astype(F32)
        total = jnp.sum(own * own + other * other, axis=1, keepdims=True)
        norm = lax.rsqrt(total / (HEADS_GRP * HEAD_DIM) + 1e-05)
        query = (
            dot_nn((own * norm).astype(BF16), own_map) + dot_nn((other * norm).astype(BF16), other_map)
        ).astype(BF16)
        gate = dot_nt(query, new_ref[0]) * INVERSE
        up = dot_nt(query, new_ref[1]) * INVERSE
        hidden = (jax.nn.silu(gate) * up).astype(BF16)
        raw = dot_nn(hidden, new_ref[2])
        mean = jnp.mean(raw * raw, axis=1, keepdims=True)
        fast_ref[rows, :] = (raw * lax.rsqrt(mean + 1e-05)).astype(BF16)


def mix_kernel(pair, places_ref, fast_ref, map_ref, *out_refs):
    for index, out_ref in enumerate(out_refs):
        width = out_ref.shape[1]
        start = pl.multiple_of(places_ref[0, 2 * pair + index] * width, width)
        out_ref[...] = dot_nn(fast_ref[...], map_ref[:, pl.ds(start, width)]).astype(BF16)


def seq_shift(value, step):
    peers = lax.axis_size("seq")
    return lax.ppermute(
        value, "seq", [(i, i + step) for i in range(peers) if 0 <= i + step < peers]
    )


def head_swap(value, bit):
    return lax.ppermute(value, "head", [(i, i ^ bit) for i in range(lax.axis_size("head"))])


def seq_swap(value, bit):
    step = 1 << bit
    return lax.ppermute(value, "seq", [(i, i ^ step) for i in range(lax.axis_size("seq"))])


def after(value, others):
    return lax.optimization_barrier((value, others))[0]


def halving_start(chunks, orders):
    keeps = [keep for keep, _ in chunks]
    return keeps, [seq_swap(send, order[0]) for (_, send), order in zip(chunks, orders)]


def halving_step(keeps, found, orders, turn, wait=()):
    sends, rest = [], []
    for keep, new in zip(keeps, found):
        half = keep.shape[0] // 2
        sends.append((keep[half:].astype(F32) + new[half:].astype(F32)).astype(BF16))
        rest.append(lax.optimization_barrier(keep[:half].astype(F32) + new[:half].astype(F32)))
    sends = after(sends, wait) if wait else sends
    return rest, [seq_swap(send, order[turn]) for send, order in zip(sends, orders)]


def doubling_step(held, orders, turn, wait=()):
    whole = [jnp.concatenate(parts) if len(parts) > 1 else parts[0] for parts in held]
    whole = after(whole, wait) if wait else whole
    return [(own, seq_swap(own, order[turn])) for own, order in zip(whole, orders)]


def local(
    queries_first,
    keys_first,
    values_first,
    input_map,
    fast_keys,
    fast_values,
    step_rates,
    fast_weights,
    output_map,
    queries_second,
    keys_second,
    values_second,
):
    rows, width = queries_first.shape
    seq_count = lax.axis_size("seq")
    seq_place = lax.axis_index("seq")
    head_place = lax.axis_index("head")
    weights = jnp.transpose(fast_weights[0], (1, 0, 2))
    hidden_size, fast_width = weights.shape[1:]
    shape = jax.ShapeDtypeStruct
    minus = jnp.float32(-jnp.inf)
    side = seq_place % 2

    def edges_of(block):
        return [jnp.where(block > 0, 0.0, minus), jnp.where(block < seq_count - 1, 0.0, minus)]

    edges = jnp.stack(edges_of(seq_place) + edges_of(seq_place ^ 1)).reshape(2, 2)
    side_scalar = side.astype(jnp.int32).reshape(1, 1)
    place = seq_place.astype(jnp.int32).reshape(1, 1)

    packed = call(
        pack_kernel,
        shape((3 * rows, HEAD_DIM), BF16),
        (side_scalar, queries_first, keys_first, values_first),
        scalars=1,
    )
    other_first = seq_swap(packed, 0)

    bits = tuple(range(seq_count.bit_length() - 1))
    halving = seq_count == 1 << len(bits) and len(bits) > 1 and hidden_size >> len(bits) >= 16
    orders = (bits, bits[1:] + bits[:1]) if halving else ((), ())
    halves = 2 if halving else 1
    chunk_width = fast_width + fast_width // 2
    out_shapes = [shape((hidden_size // halves, chunk_width), BF16)] * (2 * halves)
    whole = pl.BlockSpec(memory_space=pltpu.VMEM)
    gradients = pl.pallas_call(
        functools.partial(gradient_kernel, orders),
        grid=(hidden_size // TILE,),
        out_shape=out_shapes,
        in_specs=[
            pl.BlockSpec(memory_space=pltpu.SMEM),
            whole,
            whole,
            whole,
            pl.BlockSpec((3, TILE, fast_width), lambda turn: (0, turn, 0)),
        ],
        out_specs=[whole] * len(out_shapes),
        scratch_shapes=[pltpu.VMEM((hidden_size, chunk_width), BF16)] * 2,
        compiler_params=pltpu.CompilerParams(vmem_limit_bytes=VMEM_MOST),
        cost_estimate=pl.CostEstimate(flops=1000, bytes_accessed=1000, transcendentals=0),
    )(place, step_rates.reshape(1, rows), fast_keys, fast_values, weights)

    low_block, high_block = call(
        border_kernel,
        [shape((2 * rows, HEAD_DIM), BF16)] * 2,
        (side_scalar, keys_first, values_first, other_first),
        scalars=1,
    )

    def first_halos(low_block, high_block):
        return seq_shift(high_block, 2), seq_shift(low_block, -2)

    def first_attention(prev_first, next_first):
        keep_first, send_first = call(
            first_kernel,
            [shape((rows, HEAD_DIM), BF16)] * 2,
            (edges, side_scalar, queries_first, other_first, prev_first, low_block, high_block, next_first),
            scalars=2,
            scratch=[pltpu.VMEM((4 * rows, HEAD_DIM), BF16)] * 2,
            cost=(12 * rows * rows * width, 16 * rows * width),
        )
        return keep_first, seq_swap(send_first, 0)

    both_second = jnp.concatenate([keys_second, values_second])

    if halving:
        turns = len(bits)
        keeps, found = halving_start([gradients[:2], gradients[2:]], orders)
        for turn in range(1, turns):
            if turn == turns - 1:
                prev_first, next_first = first_halos(*after((low_block, high_block), found))
                prev_second = seq_shift(after(both_second, found), 1)
            keeps, found = halving_step(keeps, found, orders, turn)
        held = [((keep.astype(F32) + new.astype(F32)).astype(BF16),) for keep, new in zip(keeps, found)]
        for turn in reversed(range(turns)):
            wait = ()
            if turn == 1:
                wait = (prev_first, next_first, prev_second)
            if turn == 0:
                keep_first, back_first = first_attention(prev_first, next_first)
                wait = (keep_first,)
            held = doubling_step(held, orders, turn, wait)
        gathered = [part for parts in held for part in parts]
        next_second = seq_shift(after(both_second, back_first), -1)
    else:
        gathered = lax.psum(gradients, "seq")
        keep_first, back_first = first_attention(*first_halos(low_block, high_block))
        prev_second, next_second = seq_shift(both_second, 1), seq_shift(both_second, -1)
    own_rows = hidden_size >> len(orders[0])
    my_bit, near = head_place % 2, head_place // 2
    places = jnp.stack(
        [2 * pair + bit for pair in (near ^ 1, near) for bit in (1 - my_bit, my_bit)]
    ).astype(jnp.int32).reshape(1, 4)
    share = shape((rows, width), BF16)
    operands = (*gathered, weights, keep_first, back_first, input_map[0])
    own_new, fast_out = call(
        functools.partial(renew_kernel, orders),
        [shape((3, own_rows, fast_width), BF16), shape((rows, fast_width), BF16)],
        (place, side_scalar, *operands),
        scalars=2,
        anywhere=len(operands),
        scratch=[pltpu.VMEM(operand.shape, BF16) for operand in operands]
        + [pltpu.VMEM(weights.shape, BF16), pltpu.SemaphoreType.DMA((len(operands),))],
        limit=VMEM_MOST - 3 * 1024 * 1024,
    )

    def mixed_for(pair, fast):
        return call(
            functools.partial(mix_kernel, pair), [share, share], (places, fast, output_map), scalars=1
        )

    far_send, far_keep = mixed_for(0, fast_out)
    far_near = head_swap(far_send, 1)
    near_send, near_keep = mixed_for(1, after(fast_out, next_second))
    near_near = head_swap(near_send, 1)
    half = rows // 2
    far_parts = []
    for part in (slice(0, half), slice(half, rows)):
        far_sum = far_keep[part].astype(F32) + far_near[part].astype(F32)
        far_parts.append(head_swap(far_sum.astype(BF16), 2))
    if not halving:
        share_rows = hidden_size // seq_count
        own_new = lax.dynamic_slice_in_dim(own_new, seq_place * share_rows, share_rows, 1)

    def second_attention(part, *done):
        return call(
            second_kernel,
            shape((half * (1 + len(done)), width), BF16),
            (edges, queries_second, near_keep, near_near, far_parts[part],
             prev_second, keys_second, values_second, next_second, *done),
            scalars=1,
            cost=(6 * rows * rows * width, 16 * rows * width),
        )

    normed_second = second_attention(1, second_attention(0))
    return (normed_second, jnp.transpose(own_new, (1, 0, 2))[None])


def solution(mesh):
    return jax.shard_map(
        local,
        mesh=mesh,
        in_specs=(
            P("seq", "head"),
            P("seq", "head"),
            P("seq", "head"),
            P("head", None, None),
            P("seq", "head"),
            P("seq", "head"),
            P("seq", "head"),
            P("head", None, None, None),
            P("head", None),
            P("seq", "head"),
            P("seq", "head"),
            P("seq", "head"),
        ),
        out_specs=(P("seq", "head"), P("head", "seq", None, None)),
        check_vma=False,
    )
```

```python
import functools
import math

import jax
import jax.numpy as jnp
from jax import lax
from jax.experimental import pallas as pl
from jax.experimental.pallas import tpu as pltpu
from jax.sharding import PartitionSpec as P

HALF_WIN = 512
HEAD_DIM = 128
HEADS_GRP = 2
FAST_DIM = 512
FAST_HIDDEN = 512
TILE = 128
ROW_TILE = 256
VMEM_LIMIT = 24 * 1024 * 1024
VMEM_MOST = 60 * 1024 * 1024

BF16 = jnp.bfloat16
F32 = jnp.float32
INVERSE = 1.0 / math.sqrt(FAST_DIM)


def dot_nn(left, right):
    return lax.dot_general(left, right, (((1,), (0,)), ((), ())), preferred_element_type=F32)


def dot_nt(left, right):
    return lax.dot_general(left, right, (((1,), (1,)), ((), ())), preferred_element_type=F32)


def call(body, out_shapes, operands, scalars=0, anywhere=0, scratch=(), cost=None, limit=VMEM_LIMIT):
    vmem = pl.BlockSpec(memory_space=pltpu.VMEM)
    in_specs = (
        [pl.BlockSpec(memory_space=pltpu.SMEM)] * scalars
        + [vmem] * (len(operands) - scalars - anywhere)
        + [pl.BlockSpec(memory_space=pl.ANY)] * anywhere
    )
    flops, moved = cost or (1000, 1000)
    return pl.pallas_call(
        body,
        out_shape=out_shapes,
        in_specs=in_specs,
        out_specs=jax.tree.map(lambda _: vmem, out_shapes),
        scratch_shapes=scratch,
        compiler_params=pltpu.CompilerParams(vmem_limit_bytes=limit),
        cost_estimate=pl.CostEstimate(flops=flops, bytes_accessed=moved, transcendentals=0),
    )(*operands)


def slot_of(block, order):
    slot = 0
    for bit in order:
        slot = slot * 2 + ((block >> bit) & 1)
    return slot


def gradient_kernel(orders, place_ref, rates_ref, keys_ref, values_ref, weights_ref, *refs):
    out_refs, chunk_refs = refs[:-2], refs[-2:]
    place = place_ref[0, 0]
    rates = rates_ref[...]
    keys = keys_ref[...]
    values = values_ref[...]
    hidden_size = chunk_refs[0].shape[0]
    width = weights_ref.shape[2]
    turn = pl.program_id(0)
    step = weights_ref.shape[1]

    def put(chunk, columns, product):
        order = orders[chunk]
        block_rows = min(step, hidden_size >> len(order))
        for start in range(0, step, block_rows):
            row = turn * step + start
            if order:
                block = turn * (step // block_rows) + start // block_rows
                row = slot_of(block ^ place, order) * block_rows
            row = pl.multiple_of(row, block_rows)
            chunk_refs[chunk][pl.ds(row, block_rows), columns] = product[start:start + block_rows]

    gate = dot_nt(weights_ref[0], keys) * INVERSE
    up = dot_nt(weights_ref[1], keys) * INVERSE
    sigmoid = jax.nn.sigmoid(gate)
    silu = gate * sigmoid
    hidden = (rates * silu * up).astype(BF16)
    backward = rates * dot_nt(weights_ref[2], values)
    d_gate = (backward * up * sigmoid * (1.0 + gate * (1.0 - sigmoid)) * INVERSE).astype(BF16)
    d_up = (backward * silu * INVERSE).astype(BF16)
    up_part = dot_nn(d_up, keys).astype(BF16)
    put(0, slice(0, width), dot_nn(d_gate, keys).astype(BF16))
    put(0, slice(width, width + width // 2), up_part[:, :width // 2])
    put(1, slice(0, width), dot_nn(hidden, values).astype(BF16))
    put(1, slice(width, width + width // 2), up_part[:, width // 2:])

    @pl.when(turn == pl.num_programs(0) - 1)
    def _():
        halves = len(out_refs) // 2
        half_rows = hidden_size // halves
        for index, out_ref in enumerate(out_refs):
            half = index % halves
            out_ref[...] = chunk_refs[index // halves][half * half_rows:(half + 1) * half_rows, :]


def attend_rows(edge_prev, edge_next, query_tile, keys_prev, keys_own, keys_next,
                values_prev, values_own, values_next):
    scale = math.log2(math.e) / math.sqrt(HEAD_DIM)
    row = lax.broadcasted_iota(jnp.int32, (ROW_TILE, ROW_TILE), 0)
    col = lax.broadcasted_iota(jnp.int32, (ROW_TILE, ROW_TILE), 1)
    minus = jnp.float32(-jnp.inf)
    score_prev = dot_nt(query_tile, keys_prev)
    score_own = dot_nt(query_tile, keys_own)
    score_next = dot_nt(query_tile, keys_next)
    parts = [score_prev[:, :ROW_TILE] + jnp.where(col >= row, edge_prev, minus)]
    if score_prev.shape[1] > ROW_TILE:
        parts.append(score_prev[:, ROW_TILE:] + edge_prev)
    parts.append(score_own)
    if score_next.shape[1] > ROW_TILE:
        parts.append(score_next[:, :-ROW_TILE] + edge_next)
    parts.append(score_next[:, -ROW_TILE:] + jnp.where(col <= row, edge_next, minus))
    scores = jnp.concatenate(parts, axis=1)
    highest = jnp.max(scores, axis=1, keepdims=True)
    weights = jnp.exp2((scores - highest) * scale)
    total = jnp.sum(weights, axis=1, keepdims=True)
    weights = weights.astype(BF16)
    width_prev, width_own = score_prev.shape[1], score_own.shape[1]
    attended = (
        dot_nn(weights[:, :width_prev], values_prev)
        + dot_nn(weights[:, width_prev:width_prev + width_own], values_own)
        + dot_nn(weights[:, width_prev + width_own:], values_next)
    )
    return attended / total


def pack_kernel(side_ref, queries_ref, keys_ref, values_ref, out_ref):
    count = queries_ref.shape[0]
    start = pl.multiple_of((1 - side_ref[0, 0]) * HEAD_DIM, HEAD_DIM)
    for index, ref in enumerate((queries_ref, keys_ref, values_ref)):
        out_ref[index * count:(index + 1) * count, :] = ref[:, pl.ds(start, HEAD_DIM)]


def border_kernel(side_ref, keys_ref, values_ref, other_ref, low_ref, high_ref):
    count = keys_ref.shape[0]
    side = side_ref[0, 0]
    start = pl.multiple_of(side * HEAD_DIM, HEAD_DIM)

    def fill(own_ref, other_out_ref):
        own_ref[:count, :] = keys_ref[:, pl.ds(start, HEAD_DIM)]
        own_ref[count:, :] = values_ref[:, pl.ds(start, HEAD_DIM)]
        other_out_ref[...] = other_ref[count:, :]

    @pl.when(side == 0)
    def _():
        fill(low_ref, high_ref)

    @pl.when(side != 0)
    def _():
        fill(high_ref, low_ref)


def first_kernel(edge_ref, side_ref, queries_ref, other_ref, prev_ref, low_ref, high_ref, next_ref,
                 keep_ref, send_ref, keys_ref, values_ref):
    count = queries_ref.shape[0]
    side = side_ref[0, 0]
    for index, ref in enumerate((prev_ref, low_ref, high_ref, next_ref)):
        rows = slice(index * count, (index + 1) * count)
        keys_ref[rows, :] = ref[:count, :]
        values_ref[rows, :] = ref[count:, :]
    start = pl.multiple_of(side * HEAD_DIM, HEAD_DIM)
    for turn, out_ref in enumerate((keep_ref, send_ref)):
        base = (side if turn == 0 else 1 - side) * count

        def span(ref, low, length):
            return ref[pl.ds(pl.multiple_of(base + low, ROW_TILE), length), :]

        for index in range(count // ROW_TILE):
            low, high = index * ROW_TILE, (index + 1) * ROW_TILE
            query = queries_ref[low:high, pl.ds(start, HEAD_DIM)] if turn == 0 else other_ref[low:high, :]
            out_ref[low:high, :] = attend_rows(
                edge_ref[turn, 0], edge_ref[turn, 1], query,
                span(keys_ref, low, count - low), span(keys_ref, count, count),
                span(keys_ref, 2 * count, high),
                span(values_ref, low, count - low), span(values_ref, count, count),
                span(values_ref, 2 * count, high),
            ).astype(BF16)


def second_kernel(edge_ref, queries_ref, keep_ref, near_ref, far_ref, prev_ref, keys_ref, values_ref, next_ref,
                  *refs):
    done_refs, out_ref = refs[:-1], refs[-1]
    count = keys_ref.shape[0]
    half = far_ref.shape[0]
    offset = half if done_refs else 0
    if done_refs:
        out_ref[:half, :] = done_refs[0][...]
    for low in range(offset, offset + half, ROW_TILE):
        high = low + ROW_TILE
        rows = slice(low, high)
        mixed = (
            keep_ref[rows, :].astype(F32)
            + near_ref[rows, :].astype(F32)
            + far_ref[low - offset:high - offset, :].astype(F32)
        )
        query = (queries_ref[rows, :].astype(F32) + mixed).astype(BF16)
        heads = []
        for head in range(HEADS_GRP):
            cols = slice(head * HEAD_DIM, (head + 1) * HEAD_DIM)
            heads.append(
                attend_rows(
                    edge_ref[0, 0], edge_ref[0, 1], query[:, cols],
                    prev_ref[low:count, cols], keys_ref[:, cols], next_ref[:high, cols],
                    prev_ref[count + low:, cols], values_ref[:, cols], next_ref[count:count + high, cols],
                )
            )
        both = jnp.concatenate(heads, axis=1)
        mean = jnp.mean(both * both, axis=1, keepdims=True)
        out_ref[rows, :] = (both * lax.rsqrt(mean + 1e-05)).astype(BF16)


def renew_kernel(orders, place_ref, side_ref, *refs):
    count = (len(refs) - 4) // 2
    sources, (own_ref, fast_ref), loaded = refs[:count], refs[count:count + 2], refs[count + 2:-2]
    new_ref, sems = refs[-2:]
    copies = [
        pltpu.make_async_copy(source, target, sems.at[index])
        for index, (source, target) in enumerate(zip(sources, loaded))
    ]
    for copy in copies:
        copy.start()
    pieces, (weights_ref, keep_ref, other_ref, map_ref) = loaded[:-4], loaded[-4:]
    place = place_ref[0, 0]
    side = side_ref[0, 0]
    hidden_size, width = weights_ref.shape[1:]
    for copy in copies[:-4]:
        copy.wait()
    limit_norm = math.sqrt(FAST_HIDDEN * FAST_DIM) / 2.0
    step = 64
    square = jnp.zeros((1, pieces[0].shape[1]), F32)
    for piece in pieces:
        for low in range(0, piece.shape[0], step):
            part = piece[low:low + step, :].astype(F32)
            square = square + jnp.sum(part * part, axis=0, keepdims=True)
    square = jnp.sum(square, axis=1, keepdims=True)
    factor = jnp.minimum(1.0, limit_norm * lax.rsqrt(square + 1e-06))
    copies[-4].wait()
    per_chunk = len(pieces) // 2
    piece_rows = pieces[0].shape[0]
    blocks = 1 << len(orders[0])
    block_rows = hidden_size // blocks
    count = min(step, block_rows)
    for block in range(blocks):
        starts = [slot_of(block, order) * block_rows for order in orders]
        for low in range(0, block_rows, count):
            found = []
            for chunk, start in enumerate(starts):
                piece = pieces[chunk * per_chunk + start // piece_rows]
                inside = start % piece_rows + low
                found.append(piece[inside:inside + count, :].astype(F32))
            parts = [
                found[0][:, :width],
                jnp.concatenate([found[0][:, width:], found[1][:, width:]], axis=1),
                found[1][:, :width],
            ]
            rows = slice(low, low + count)
            if blocks > 1:
                rows = pl.ds(pl.multiple_of((block ^ place) * block_rows + low, count), count)
            for matrix, part in enumerate(parts):
                old = weights_ref[matrix, rows, :].astype(F32)
                stepped = old + factor * part
                norm = jnp.sqrt(jnp.sum(old * old, axis=1, keepdims=True))
                size = jnp.sum(stepped * stepped, axis=1, keepdims=True)
                fresh = (stepped * norm * lax.rsqrt(size + 1e-06)).astype(BF16)
                new_ref[matrix, rows, :] = fresh
                if block == 0:
                    own_ref[matrix, low:low + count, :] = fresh
    for copy in copies[-3:]:
        copy.wait()
    own_map = map_ref[pl.ds(pl.multiple_of(side * HEAD_DIM, HEAD_DIM), HEAD_DIM), :]
    other_map = map_ref[pl.ds(pl.multiple_of((1 - side) * HEAD_DIM, HEAD_DIM), HEAD_DIM), :]
    for low in range(0, keep_ref.shape[0], ROW_TILE):
        rows = slice(low, low + ROW_TILE)
        own = keep_ref[rows, :].astype(F32)
        other = other_ref[rows, :].astype(F32)
        total = jnp.sum(own * own + other * other, axis=1, keepdims=True)
        norm = lax.rsqrt(total / (HEADS_GRP * HEAD_DIM) + 1e-05)
        query = (
            dot_nn((own * norm).astype(BF16), own_map) + dot_nn((other * norm).astype(BF16), other_map)
        ).astype(BF16)
        gate = dot_nt(query, new_ref[0]) * INVERSE
        up = dot_nt(query, new_ref[1]) * INVERSE
        hidden = (jax.nn.silu(gate) * up).astype(BF16)
        raw = dot_nn(hidden, new_ref[2])
        mean = jnp.mean(raw * raw, axis=1, keepdims=True)
        fast_ref[rows, :] = (raw * lax.rsqrt(mean + 1e-05)).astype(BF16)


def mix_kernel(pair, places_ref, fast_ref, map_ref, *out_refs):
    for index, out_ref in enumerate(out_refs):
        width = out_ref.shape[1]
        start = pl.multiple_of(places_ref[0, 2 * pair + index] * width, width)
        out_ref[...] = dot_nn(fast_ref[...], map_ref[:, pl.ds(start, width)]).astype(BF16)


def seq_shift(value, step):
    peers = lax.axis_size("seq")
    return lax.ppermute(
        value, "seq", [(i, i + step) for i in range(peers) if 0 <= i + step < peers]
    )


def head_swap(value, bit):
    return lax.ppermute(value, "head", [(i, i ^ bit) for i in range(lax.axis_size("head"))])


def seq_swap(value, bit):
    step = 1 << bit
    return lax.ppermute(value, "seq", [(i, i ^ step) for i in range(lax.axis_size("seq"))])


def after(value, others):
    return lax.optimization_barrier((value, others))[0]


def halving_start(chunks, orders):
    keeps = [keep for keep, _ in chunks]
    return keeps, [seq_swap(send, order[0]) for (_, send), order in zip(chunks, orders)]


def halving_step(keeps, found, orders, turn, wait=()):
    sends, rest = [], []
    for keep, new in zip(keeps, found):
        half = keep.shape[0] // 2
        sends.append((keep[half:].astype(F32) + new[half:].astype(F32)).astype(BF16))
        rest.append(lax.optimization_barrier(keep[:half].astype(F32) + new[:half].astype(F32)))
    sends = after(sends, wait) if wait else sends
    return rest, [seq_swap(send, order[turn]) for send, order in zip(sends, orders)]


def doubling_step(held, orders, turn, wait=()):
    whole = [jnp.concatenate(parts) if len(parts) > 1 else parts[0] for parts in held]
    whole = after(whole, wait) if wait else whole
    return [(own, seq_swap(own, order[turn])) for own, order in zip(whole, orders)]


def local(
    queries_first,
    keys_first,
    values_first,
    input_map,
    fast_keys,
    fast_values,
    step_rates,
    fast_weights,
    output_map,
    queries_second,
    keys_second,
    values_second,
):
    rows, width = queries_first.shape
    seq_count = lax.axis_size("seq")
    seq_place = lax.axis_index("seq")
    head_place = lax.axis_index("head")
    weights = jnp.transpose(fast_weights[0], (1, 0, 2))
    hidden_size, fast_width = weights.shape[1:]
    shape = jax.ShapeDtypeStruct
    minus = jnp.float32(-jnp.inf)
    side = seq_place % 2

    def edges_of(block):
        return [jnp.where(block > 0, 0.0, minus), jnp.where(block < seq_count - 1, 0.0, minus)]

    edges = jnp.stack(edges_of(seq_place) + edges_of(seq_place ^ 1)).reshape(2, 2)
    side_scalar = side.astype(jnp.int32).reshape(1, 1)
    place = seq_place.astype(jnp.int32).reshape(1, 1)

    packed = call(
        pack_kernel,
        shape((3 * rows, HEAD_DIM), BF16),
        (side_scalar, queries_first, keys_first, values_first),
        scalars=1,
    )
    other_first = seq_swap(packed, 0)

    bits = tuple(range(seq_count.bit_length() - 1))
    halving = seq_count == 1 << len(bits) and len(bits) > 1 and hidden_size >> len(bits) >= 16
    orders = (bits, bits[1:] + bits[:1]) if halving else ((), ())
    halves = 2 if halving else 1
    chunk_width = fast_width + fast_width // 2
    out_shapes = [shape((hidden_size // halves, chunk_width), BF16)] * (2 * halves)
    whole = pl.BlockSpec(memory_space=pltpu.VMEM)
    gradients = pl.pallas_call(
        functools.partial(gradient_kernel, orders),
        grid=(hidden_size // ROW_TILE,),
        out_shape=out_shapes,
        in_specs=[
            pl.BlockSpec(memory_space=pltpu.SMEM),
            whole,
            whole,
            whole,
            pl.BlockSpec((3, ROW_TILE, fast_width), lambda turn: (0, turn, 0)),
        ],
        out_specs=[whole] * len(out_shapes),
        scratch_shapes=[pltpu.VMEM((hidden_size, chunk_width), BF16)] * 2,
        compiler_params=pltpu.CompilerParams(vmem_limit_bytes=VMEM_MOST),
        cost_estimate=pl.CostEstimate(flops=1000, bytes_accessed=1000, transcendentals=0),
    )(place, step_rates.reshape(1, rows), fast_keys, fast_values, weights)

    low_block, high_block = call(
        border_kernel,
        [shape((2 * rows, HEAD_DIM), BF16)] * 2,
        (side_scalar, keys_first, values_first, other_first),
        scalars=1,
    )

    def first_halos(low_block, high_block):
        return seq_shift(high_block, 2), seq_shift(low_block, -2)

    def first_attention(prev_first, next_first):
        keep_first, send_first = call(
            first_kernel,
            [shape((rows, HEAD_DIM), BF16)] * 2,
            (edges, side_scalar, queries_first, other_first, prev_first, low_block, high_block, next_first),
            scalars=2,
            scratch=[pltpu.VMEM((4 * rows, HEAD_DIM), BF16)] * 2,
            cost=(12 * rows * rows * width, 16 * rows * width),
        )
        return keep_first, seq_swap(send_first, 0)

    both_second = jnp.concatenate([keys_second, values_second])

    if halving:
        turns = len(bits)
        keeps, found = halving_start([gradients[:2], gradients[2:]], orders)
        for turn in range(1, turns):
            if turn == turns - 1:
                prev_first, next_first = first_halos(*after((low_block, high_block), found))
                prev_second = seq_shift(after(both_second, found), 1)
            keeps, found = halving_step(keeps, found, orders, turn)
        held = [((keep.astype(F32) + new.astype(F32)).astype(BF16),) for keep, new in zip(keeps, found)]
        for turn in reversed(range(turns)):
            wait = ()
            if turn == 1:
                wait = (prev_first, next_first, prev_second)
            if turn == 0:
                keep_first, back_first = first_attention(prev_first, next_first)
                wait = (keep_first,)
            held = doubling_step(held, orders, turn, wait)
        gathered = [part for parts in held for part in parts]
        next_second = seq_shift(after(both_second, back_first), -1)
    else:
        gathered = lax.psum(gradients, "seq")
        keep_first, back_first = first_attention(*first_halos(low_block, high_block))
        prev_second, next_second = seq_shift(both_second, 1), seq_shift(both_second, -1)
    own_rows = hidden_size >> len(orders[0])
    my_bit, near = head_place % 2, head_place // 2
    places = jnp.stack(
        [2 * pair + bit for pair in (near ^ 1, near) for bit in (1 - my_bit, my_bit)]
    ).astype(jnp.int32).reshape(1, 4)
    share = shape((rows, width), BF16)
    operands = (*gathered, weights, keep_first, back_first, input_map[0])
    own_new, fast_out = call(
        functools.partial(renew_kernel, orders),
        [shape((3, own_rows, fast_width), BF16), shape((rows, fast_width), BF16)],
        (place, side_scalar, *operands),
        scalars=2,
        anywhere=len(operands),
        scratch=[pltpu.VMEM(operand.shape, BF16) for operand in operands]
        + [pltpu.VMEM(weights.shape, BF16), pltpu.SemaphoreType.DMA((len(operands),))],
        limit=VMEM_MOST - 3 * 1024 * 1024,
    )

    def mixed_for(pair, fast):
        return call(
            functools.partial(mix_kernel, pair), [share, share], (places, fast, output_map), scalars=1
        )

    far_send, far_keep = mixed_for(0, fast_out)
    far_near = head_swap(far_send, 1)
    near_send, near_keep = mixed_for(1, after(fast_out, next_second))
    near_near = head_swap(near_send, 1)
    half = rows // 2
    far_parts = []
    for part in (slice(0, half), slice(half, rows)):
        far_sum = far_keep[part].astype(F32) + far_near[part].astype(F32)
        far_parts.append(head_swap(far_sum.astype(BF16), 2))
    if not halving:
        share_rows = hidden_size // seq_count
        own_new = lax.dynamic_slice_in_dim(own_new, seq_place * share_rows, share_rows, 1)

    def second_attention(part, *done):
        return call(
            second_kernel,
            shape((half * (1 + len(done)), width), BF16),
            (edges, queries_second, near_keep, near_near, far_parts[part],
             prev_second, keys_second, values_second, next_second, *done),
            scalars=1,
            cost=(6 * rows * rows * width, 16 * rows * width),
        )

    normed_second = second_attention(1, second_attention(0))
    return (normed_second, jnp.transpose(own_new, (1, 0, 2))[None])


def solution(mesh):
    return jax.shard_map(
        local,
        mesh=mesh,
        in_specs=(
            P("seq", "head"),
            P("seq", "head"),
            P("seq", "head"),
            P("head", None, None),
            P("seq", "head"),
            P("seq", "head"),
            P("seq", "head"),
            P("head", None, None, None),
            P("head", None),
            P("seq", "head"),
            P("seq", "head"),
            P("seq", "head"),
        ),
        out_specs=(P("seq", "head"), P("head", "seq", None, None)),
        check_vma=False,
    )
```

```python
import functools
import math

import jax
import jax.numpy as jnp
from jax import lax
from jax.experimental import pallas as pl
from jax.experimental.pallas import tpu as pltpu
from jax.sharding import PartitionSpec as P

HALF_WIN = 512
HEAD_DIM = 128
HEADS_GRP = 2
FAST_DIM = 512
FAST_HIDDEN = 512
TILE = 128
ROW_TILE = 256
VMEM_LIMIT = 24 * 1024 * 1024
VMEM_MOST = 60 * 1024 * 1024

BF16 = jnp.bfloat16
F32 = jnp.float32
INVERSE = 1.0 / math.sqrt(FAST_DIM)


def dot_nn(left, right):
    return lax.dot_general(left, right, (((1,), (0,)), ((), ())), preferred_element_type=F32)


def dot_nt(left, right):
    return lax.dot_general(left, right, (((1,), (1,)), ((), ())), preferred_element_type=F32)


def call(body, out_shapes, operands, scalars=0, anywhere=0, scratch=(), cost=None, limit=VMEM_LIMIT):
    vmem = pl.BlockSpec(memory_space=pltpu.VMEM)
    in_specs = (
        [pl.BlockSpec(memory_space=pltpu.SMEM)] * scalars
        + [vmem] * (len(operands) - scalars - anywhere)
        + [pl.BlockSpec(memory_space=pl.ANY)] * anywhere
    )
    flops, moved = cost or (1000, 1000)
    return pl.pallas_call(
        body,
        out_shape=out_shapes,
        in_specs=in_specs,
        out_specs=jax.tree.map(lambda _: vmem, out_shapes),
        scratch_shapes=scratch,
        compiler_params=pltpu.CompilerParams(vmem_limit_bytes=limit),
        cost_estimate=pl.CostEstimate(flops=flops, bytes_accessed=moved, transcendentals=0),
    )(*operands)


def slot_of(block, order):
    slot = 0
    for bit in order:
        slot = slot * 2 + ((block >> bit) & 1)
    return slot


def gradient_kernel(orders, place_ref, rates_ref, keys_ref, values_ref, weights_ref, *refs):
    out_refs, chunk_refs = refs[:-2], refs[-2:]
    place = place_ref[0, 0]
    rates = rates_ref[...]
    keys = keys_ref[...]
    values = values_ref[...]
    hidden_size = chunk_refs[0].shape[0]
    width = weights_ref.shape[2]
    turn = pl.program_id(0)
    step = weights_ref.shape[1]

    def put(chunk, columns, product):
        order = orders[chunk]
        block_rows = min(step, hidden_size >> len(order))
        for start in range(0, step, block_rows):
            row = turn * step + start
            if order:
                block = turn * (step // block_rows) + start // block_rows
                row = slot_of(block ^ place, order) * block_rows
            row = pl.multiple_of(row, block_rows)
            chunk_refs[chunk][pl.ds(row, block_rows), columns] = product[start:start + block_rows]

    gate = dot_nt(weights_ref[0], keys) * INVERSE
    up = dot_nt(weights_ref[1], keys) * INVERSE
    sigmoid = jax.nn.sigmoid(gate)
    silu = gate * sigmoid
    hidden = (rates * silu * up).astype(BF16)
    backward = rates * dot_nt(weights_ref[2], values)
    d_gate = (backward * up * sigmoid * (1.0 + gate * (1.0 - sigmoid)) * INVERSE).astype(BF16)
    d_up = (backward * silu * INVERSE).astype(BF16)
    up_part = dot_nn(d_up, keys).astype(BF16)
    put(0, slice(0, width), dot_nn(d_gate, keys).astype(BF16))
    put(0, slice(width, width + width // 2), up_part[:, :width // 2])
    put(1, slice(0, width), dot_nn(hidden, values).astype(BF16))
    put(1, slice(width, width + width // 2), up_part[:, width // 2:])

    @pl.when(turn == pl.num_programs(0) - 1)
    def _():
        halves = len(out_refs) // 2
        half_rows = hidden_size // halves
        for index, out_ref in enumerate(out_refs):
            half = index % halves
            out_ref[...] = chunk_refs[index // halves][half * half_rows:(half + 1) * half_rows, :]


def attend_rows(edge_prev, edge_next, query_tile, keys_prev, keys_own, keys_next,
                values_prev, values_own, values_next):
    scale = math.log2(math.e) / math.sqrt(HEAD_DIM)
    row = lax.broadcasted_iota(jnp.int32, (ROW_TILE, ROW_TILE), 0)
    col = lax.broadcasted_iota(jnp.int32, (ROW_TILE, ROW_TILE), 1)
    minus = jnp.float32(-jnp.inf)
    score_prev = dot_nt(query_tile, keys_prev)
    score_own = dot_nt(query_tile, keys_own)
    score_next = dot_nt(query_tile, keys_next)
    parts = [score_prev[:, :ROW_TILE] + jnp.where(col >= row, edge_prev, minus)]
    if score_prev.shape[1] > ROW_TILE:
        parts.append(score_prev[:, ROW_TILE:] + edge_prev)
    parts.append(score_own)
    if score_next.shape[1] > ROW_TILE:
        parts.append(score_next[:, :-ROW_TILE] + edge_next)
    parts.append(score_next[:, -ROW_TILE:] + jnp.where(col <= row, edge_next, minus))
    scores = jnp.concatenate(parts, axis=1)
    highest = jnp.max(scores, axis=1, keepdims=True)
    weights = jnp.exp2((scores - highest) * scale)
    total = jnp.sum(weights, axis=1, keepdims=True)
    weights = weights.astype(BF16)
    width_prev, width_own = score_prev.shape[1], score_own.shape[1]
    attended = (
        dot_nn(weights[:, :width_prev], values_prev)
        + dot_nn(weights[:, width_prev:width_prev + width_own], values_own)
        + dot_nn(weights[:, width_prev + width_own:], values_next)
    )
    return attended / total


def pack_kernel(side_ref, queries_ref, keys_ref, values_ref, out_ref):
    count = queries_ref.shape[0]
    start = pl.multiple_of((1 - side_ref[0, 0]) * HEAD_DIM, HEAD_DIM)
    for index, ref in enumerate((queries_ref, keys_ref, values_ref)):
        out_ref[index * count:(index + 1) * count, :] = ref[:, pl.ds(start, HEAD_DIM)]


def border_kernel(side_ref, keys_ref, values_ref, other_ref, low_ref, high_ref):
    count = keys_ref.shape[0]
    side = side_ref[0, 0]
    start = pl.multiple_of(side * HEAD_DIM, HEAD_DIM)

    def fill(own_ref, other_out_ref):
        own_ref[:count, :] = keys_ref[:, pl.ds(start, HEAD_DIM)]
        own_ref[count:, :] = values_ref[:, pl.ds(start, HEAD_DIM)]
        other_out_ref[...] = other_ref[count:, :]

    @pl.when(side == 0)
    def _():
        fill(low_ref, high_ref)

    @pl.when(side != 0)
    def _():
        fill(high_ref, low_ref)


def first_kernel(edge_ref, side_ref, queries_ref, other_ref, prev_ref, low_ref, high_ref, next_ref,
                 keep_ref, send_ref, keys_ref, values_ref):
    count = queries_ref.shape[0]
    side = side_ref[0, 0]
    for index, ref in enumerate((prev_ref, low_ref, high_ref, next_ref)):
        rows = slice(index * count, (index + 1) * count)
        keys_ref[rows, :] = ref[:count, :]
        values_ref[rows, :] = ref[count:, :]
    start = pl.multiple_of(side * HEAD_DIM, HEAD_DIM)
    for turn, out_ref in enumerate((keep_ref, send_ref)):
        base = (side if turn == 0 else 1 - side) * count

        def span(ref, low, length):
            return ref[pl.ds(pl.multiple_of(base + low, ROW_TILE), length), :]

        for index in range(count // ROW_TILE):
            low, high = index * ROW_TILE, (index + 1) * ROW_TILE
            query = queries_ref[low:high, pl.ds(start, HEAD_DIM)] if turn == 0 else other_ref[low:high, :]
            out_ref[low:high, :] = attend_rows(
                edge_ref[turn, 0], edge_ref[turn, 1], query,
                span(keys_ref, low, count - low), span(keys_ref, count, count),
                span(keys_ref, 2 * count, high),
                span(values_ref, low, count - low), span(values_ref, count, count),
                span(values_ref, 2 * count, high),
            ).astype(BF16)


def second_kernel(edge_ref, queries_ref, keep_ref, near_ref, far_ref, prev_ref, keys_ref, values_ref, next_ref,
                  *refs):
    done_refs, out_ref = refs[:-1], refs[-1]
    count = keys_ref.shape[0]
    half = far_ref.shape[0]
    offset = half if done_refs else 0
    if done_refs:
        out_ref[:half, :] = done_refs[0][...]
    for low in range(offset, offset + half, ROW_TILE):
        high = low + ROW_TILE
        rows = slice(low, high)
        mixed = (
            keep_ref[rows, :].astype(F32)
            + near_ref[rows, :].astype(F32)
            + far_ref[low - offset:high - offset, :].astype(F32)
        )
        query = (queries_ref[rows, :].astype(F32) + mixed).astype(BF16)
        heads = []
        for head in range(HEADS_GRP):
            cols = slice(head * HEAD_DIM, (head + 1) * HEAD_DIM)
            heads.append(
                attend_rows(
                    edge_ref[0, 0], edge_ref[0, 1], query[:, cols],
                    prev_ref[low:count, cols], keys_ref[:, cols], next_ref[:high, cols],
                    prev_ref[count + low:, cols], values_ref[:, cols], next_ref[count:count + high, cols],
                )
            )
        both = jnp.concatenate(heads, axis=1)
        mean = jnp.mean(both * both, axis=1, keepdims=True)
        out_ref[rows, :] = (both * lax.rsqrt(mean + 1e-05)).astype(BF16)


def renew_kernel(orders, place_ref, side_ref, places_ref, *refs):
    count = (len(refs) - 8) // 2
    sources, own_ref, share_refs = refs[:count], refs[count], refs[count + 1:count + 5]
    loaded, (fast_ref, new_ref, sems) = refs[count + 5:-3], refs[-3:]
    copies = [
        pltpu.make_async_copy(source, target, sems.at[index])
        for index, (source, target) in enumerate(zip(sources, loaded))
    ]
    for copy in copies:
        copy.start()
    pieces, (weights_ref, keep_ref, other_ref, map_ref, output_ref) = loaded[:-5], loaded[-5:]
    place = place_ref[0, 0]
    side = side_ref[0, 0]
    hidden_size, width = weights_ref.shape[1:]
    for copy in copies[:-5]:
        copy.wait()
    limit_norm = math.sqrt(FAST_HIDDEN * FAST_DIM) / 2.0
    step = 64
    square = jnp.zeros((1, pieces[0].shape[1]), F32)
    for piece in pieces:
        for low in range(0, piece.shape[0], step):
            part = piece[low:low + step, :].astype(F32)
            square = square + jnp.sum(part * part, axis=0, keepdims=True)
    square = jnp.sum(square, axis=1, keepdims=True)
    factor = jnp.minimum(1.0, limit_norm * lax.rsqrt(square + 1e-06))
    copies[-5].wait()
    per_chunk = len(pieces) // 2
    piece_rows = pieces[0].shape[0]
    blocks = 1 << len(orders[0])
    block_rows = hidden_size // blocks
    count = min(step, block_rows)
    for block in range(blocks):
        starts = [slot_of(block, order) * block_rows for order in orders]
        for low in range(0, block_rows, count):
            found = []
            for chunk, start in enumerate(starts):
                piece = pieces[chunk * per_chunk + start // piece_rows]
                inside = start % piece_rows + low
                found.append(piece[inside:inside + count, :].astype(F32))
            parts = [
                found[0][:, :width],
                jnp.concatenate([found[0][:, width:], found[1][:, width:]], axis=1),
                found[1][:, :width],
            ]
            rows = slice(low, low + count)
            if blocks > 1:
                rows = pl.ds(pl.multiple_of((block ^ place) * block_rows + low, count), count)
            for matrix, part in enumerate(parts):
                old = weights_ref[matrix, rows, :].astype(F32)
                stepped = old + factor * part
                norm = jnp.sqrt(jnp.sum(old * old, axis=1, keepdims=True))
                size = jnp.sum(stepped * stepped, axis=1, keepdims=True)
                fresh = (stepped * norm * lax.rsqrt(size + 1e-06)).astype(BF16)
                new_ref[matrix, rows, :] = fresh
                if block == 0:
                    own_ref[matrix, low:low + count, :] = fresh
    for copy in copies[-4:-1]:
        copy.wait()
    own_map = map_ref[pl.ds(pl.multiple_of(side * HEAD_DIM, HEAD_DIM), HEAD_DIM), :]
    other_map = map_ref[pl.ds(pl.multiple_of((1 - side) * HEAD_DIM, HEAD_DIM), HEAD_DIM), :]
    step = keep_ref.shape[0]
    for low in range(0, keep_ref.shape[0], step):
        rows = slice(low, low + step)
        own = keep_ref[rows, :].astype(F32)
        other = other_ref[rows, :].astype(F32)
        total = jnp.sum(own * own + other * other, axis=1, keepdims=True)
        norm = lax.rsqrt(total / (HEADS_GRP * HEAD_DIM) + 1e-05)
        query = (
            dot_nn((own * norm).astype(BF16), own_map) + dot_nn((other * norm).astype(BF16), other_map)
        ).astype(BF16)
        gate = dot_nt(query, new_ref[0]) * INVERSE
        up = dot_nt(query, new_ref[1]) * INVERSE
        hidden = (jax.nn.silu(gate) * up).astype(BF16)
        raw = dot_nn(hidden, new_ref[2])
        mean = jnp.mean(raw * raw, axis=1, keepdims=True)
        fast_ref[rows, :] = (raw * lax.rsqrt(mean + 1e-05)).astype(BF16)
    copies[-1].wait()
    for index, share_ref in enumerate(share_refs):
        width = share_ref.shape[1]
        start = pl.multiple_of(places_ref[0, index] * width, width)
        share_ref[...] = dot_nn(fast_ref[...], output_ref[:, pl.ds(start, width)]).astype(BF16)


def seq_shift(value, step):
    peers = lax.axis_size("seq")
    return lax.ppermute(
        value, "seq", [(i, i + step) for i in range(peers) if 0 <= i + step < peers]
    )


def head_swap(value, bit):
    return lax.ppermute(value, "head", [(i, i ^ bit) for i in range(lax.axis_size("head"))])


def seq_swap(value, bit):
    step = 1 << bit
    return lax.ppermute(value, "seq", [(i, i ^ step) for i in range(lax.axis_size("seq"))])


def after(value, others):
    return lax.optimization_barrier((value, others))[0]


def halving_start(chunks, orders):
    keeps = [keep for keep, _ in chunks]
    return keeps, [seq_swap(send, order[0]) for (_, send), order in zip(chunks, orders)]


def halving_step(keeps, found, orders, turn, wait=()):
    sends, rest = [], []
    for keep, new in zip(keeps, found):
        half = keep.shape[0] // 2
        sends.append((keep[half:].astype(F32) + new[half:].astype(F32)).astype(BF16))
        rest.append(lax.optimization_barrier(keep[:half].astype(F32) + new[:half].astype(F32)))
    sends = after(sends, wait) if wait else sends
    return rest, [seq_swap(send, order[turn]) for send, order in zip(sends, orders)]


def doubling_step(held, orders, turn, wait=()):
    whole = [jnp.concatenate(parts) if len(parts) > 1 else parts[0] for parts in held]
    whole = after(whole, wait) if wait else whole
    return [(own, seq_swap(own, order[turn])) for own, order in zip(whole, orders)]


def local(
    queries_first,
    keys_first,
    values_first,
    input_map,
    fast_keys,
    fast_values,
    step_rates,
    fast_weights,
    output_map,
    queries_second,
    keys_second,
    values_second,
):
    rows, width = queries_first.shape
    seq_count = lax.axis_size("seq")
    seq_place = lax.axis_index("seq")
    head_place = lax.axis_index("head")
    weights = jnp.transpose(fast_weights[0], (1, 0, 2))
    hidden_size, fast_width = weights.shape[1:]
    shape = jax.ShapeDtypeStruct
    minus = jnp.float32(-jnp.inf)
    side = seq_place % 2

    def edges_of(block):
        return [jnp.where(block > 0, 0.0, minus), jnp.where(block < seq_count - 1, 0.0, minus)]

    edges = jnp.stack(edges_of(seq_place) + edges_of(seq_place ^ 1)).reshape(2, 2)
    side_scalar = side.astype(jnp.int32).reshape(1, 1)
    place = seq_place.astype(jnp.int32).reshape(1, 1)

    packed = call(
        pack_kernel,
        shape((3 * rows, HEAD_DIM), BF16),
        (side_scalar, queries_first, keys_first, values_first),
        scalars=1,
    )
    other_first = seq_swap(packed, 0)

    bits = tuple(range(seq_count.bit_length() - 1))
    halving = seq_count == 1 << len(bits) and len(bits) > 1 and hidden_size >> len(bits) >= 16
    orders = (bits, bits[1:] + bits[:1]) if halving else ((), ())
    halves = 2 if halving else 1
    chunk_width = fast_width + fast_width // 2
    out_shapes = [shape((hidden_size // halves, chunk_width), BF16)] * (2 * halves)
    whole = pl.BlockSpec(memory_space=pltpu.VMEM)
    gradients = pl.pallas_call(
        functools.partial(gradient_kernel, orders),
        grid=(hidden_size // ROW_TILE,),
        out_shape=out_shapes,
        in_specs=[
            pl.BlockSpec(memory_space=pltpu.SMEM),
            whole,
            whole,
            whole,
            pl.BlockSpec((3, ROW_TILE, fast_width), lambda turn: (0, turn, 0)),
        ],
        out_specs=[whole] * len(out_shapes),
        scratch_shapes=[pltpu.VMEM((hidden_size, chunk_width), BF16)] * 2,
        compiler_params=pltpu.CompilerParams(vmem_limit_bytes=VMEM_MOST),
        cost_estimate=pl.CostEstimate(flops=1000, bytes_accessed=1000, transcendentals=0),
    )(place, step_rates.reshape(1, rows), fast_keys, fast_values, weights)

    low_block, high_block = call(
        border_kernel,
        [shape((2 * rows, HEAD_DIM), BF16)] * 2,
        (side_scalar, keys_first, values_first, other_first),
        scalars=1,
    )

    def first_halos(low_block, high_block):
        return seq_shift(high_block, 2), seq_shift(low_block, -2)

    def first_attention(prev_first, next_first):
        keep_first, send_first = call(
            first_kernel,
            [shape((rows, HEAD_DIM), BF16)] * 2,
            (edges, side_scalar, queries_first, other_first, prev_first, low_block, high_block, next_first),
            scalars=2,
            scratch=[pltpu.VMEM((4 * rows, HEAD_DIM), BF16)] * 2,
            cost=(12 * rows * rows * width, 16 * rows * width),
        )
        return keep_first, seq_swap(send_first, 0)

    both_second = jnp.concatenate([keys_second, values_second])

    if halving:
        turns = len(bits)
        keeps, found = halving_start([gradients[:2], gradients[2:]], orders)
        for turn in range(1, turns):
            if turn == turns - 1:
                prev_first, next_first = first_halos(*after((low_block, high_block), found))
                prev_second = seq_shift(after(both_second, found), 1)
            keeps, found = halving_step(keeps, found, orders, turn)
        held = [((keep.astype(F32) + new.astype(F32)).astype(BF16),) for keep, new in zip(keeps, found)]
        for turn in reversed(range(turns)):
            wait = ()
            if turn == 1:
                wait = (prev_first, next_first, prev_second)
            if turn == 0:
                keep_first, back_first = first_attention(prev_first, next_first)
                wait = (keep_first,)
            held = doubling_step(held, orders, turn, wait)
        gathered = [part for parts in held for part in parts]
        next_second = seq_shift(after(both_second, back_first), -1)
    else:
        gathered = lax.psum(gradients, "seq")
        keep_first, back_first = first_attention(*first_halos(low_block, high_block))
        prev_second, next_second = seq_shift(both_second, 1), seq_shift(both_second, -1)
    own_rows = hidden_size >> len(orders[0])
    my_bit, near = head_place % 2, head_place // 2
    places = jnp.stack(
        [2 * pair + bit for pair in (near ^ 1, near) for bit in (1 - my_bit, my_bit)]
    ).astype(jnp.int32).reshape(1, 4)
    share = shape((rows, width), BF16)
    operands = (*gathered, weights, keep_first, back_first, input_map[0], output_map)
    own_new, far_send, far_keep, near_send, near_keep = call(
        functools.partial(renew_kernel, orders),
        [shape((3, own_rows, fast_width), BF16)] + [share] * 4,
        (place, side_scalar, places, *operands),
        scalars=3,
        anywhere=len(operands),
        scratch=[pltpu.VMEM(operand.shape, BF16) for operand in operands]
        + [
            pltpu.VMEM((rows, fast_width), BF16),
            pltpu.VMEM(weights.shape, BF16),
            pltpu.SemaphoreType.DMA((len(operands),)),
        ],
        limit=VMEM_MOST - 3 * 1024 * 1024,
    )
    far_near = head_swap(far_send, 1)
    far_keep = lax.optimization_barrier(far_keep.astype(F32))
    near_near = head_swap(after(near_send, next_second), 1)
    half = rows // 2
    far_parts = []
    for part in (slice(0, half), slice(half, rows)):
        far_sum = far_keep[part] + far_near[part].astype(F32)
        far_parts.append(head_swap(far_sum.astype(BF16), 2))
    if not halving:
        share_rows = hidden_size // seq_count
        own_new = lax.dynamic_slice_in_dim(own_new, seq_place * share_rows, share_rows, 1)

    def second_attention(part, *done):
        return call(
            second_kernel,
            shape((half * (1 + len(done)), width), BF16),
            (edges, queries_second, near_keep, near_near, far_parts[part],
             prev_second, keys_second, values_second, next_second, *done),
            scalars=1,
            cost=(6 * rows * rows * width, 16 * rows * width),
        )

    normed_second = second_attention(1, second_attention(0))
    return (normed_second, jnp.transpose(own_new, (1, 0, 2))[None])


def solution(mesh):
    return jax.shard_map(
        local,
        mesh=mesh,
        in_specs=(
            P("seq", "head"),
            P("seq", "head"),
            P("seq", "head"),
            P("head", None, None),
            P("seq", "head"),
            P("seq", "head"),
            P("seq", "head"),
            P("head", None, None, None),
            P("head", None),
            P("seq", "head"),
            P("seq", "head"),
            P("seq", "head"),
        ),
        out_specs=(P("seq", "head"), P("head", "seq", None, None)),
        check_vma=False,
    )
```

```python
import functools
import math

import jax
import jax.numpy as jnp
from jax import lax
from jax.experimental import pallas as pl
from jax.experimental.pallas import tpu as pltpu
from jax.sharding import PartitionSpec as P

HALF_WIN = 512
HEAD_DIM = 128
HEADS_GRP = 2
FAST_DIM = 512
FAST_HIDDEN = 512
TILE = 128
ROW_TILE = 256
VMEM_LIMIT = 24 * 1024 * 1024
VMEM_MOST = 60 * 1024 * 1024

BF16 = jnp.bfloat16
F32 = jnp.float32
INVERSE = 1.0 / math.sqrt(FAST_DIM)


def dot_nn(left, right):
    return lax.dot_general(left, right, (((1,), (0,)), ((), ())), preferred_element_type=F32)


def dot_nt(left, right):
    return lax.dot_general(left, right, (((1,), (1,)), ((), ())), preferred_element_type=F32)


def call(body, out_shapes, operands, scalars=0, anywhere=0, scratch=(), cost=None, limit=VMEM_LIMIT):
    vmem = pl.BlockSpec(memory_space=pltpu.VMEM)
    in_specs = (
        [pl.BlockSpec(memory_space=pltpu.SMEM)] * scalars
        + [vmem] * (len(operands) - scalars - anywhere)
        + [pl.BlockSpec(memory_space=pl.ANY)] * anywhere
    )
    flops, moved = cost or (1000, 1000)
    return pl.pallas_call(
        body,
        out_shape=out_shapes,
        in_specs=in_specs,
        out_specs=jax.tree.map(lambda _: vmem, out_shapes),
        scratch_shapes=scratch,
        compiler_params=pltpu.CompilerParams(vmem_limit_bytes=limit),
        cost_estimate=pl.CostEstimate(flops=flops, bytes_accessed=moved, transcendentals=0),
    )(*operands)


def slot_of(block, order):
    slot = 0
    for bit in order:
        slot = slot * 2 + ((block >> bit) & 1)
    return slot


def gradient_kernel(orders, place_ref, rates_ref, keys_ref, values_ref, weights_ref, *refs):
    out_refs, chunk_refs = refs[:-2], refs[-2:]
    place = place_ref[0, 0]
    rates = rates_ref[...]
    keys = keys_ref[...]
    values = values_ref[...]
    hidden_size = chunk_refs[0].shape[0]
    width = weights_ref.shape[2]
    turn = pl.program_id(0)
    step = weights_ref.shape[1]

    def put(chunk, columns, product):
        order = orders[chunk]
        block_rows = min(step, hidden_size >> len(order))
        for start in range(0, step, block_rows):
            row = turn * step + start
            if order:
                block = turn * (step // block_rows) + start // block_rows
                row = slot_of(block ^ place, order) * block_rows
            row = pl.multiple_of(row, block_rows)
            chunk_refs[chunk][pl.ds(row, block_rows), columns] = product[start:start + block_rows]

    gate = dot_nt(weights_ref[0], keys) * INVERSE
    up = dot_nt(weights_ref[1], keys) * INVERSE
    sigmoid = jax.nn.sigmoid(gate)
    silu = gate * sigmoid
    hidden = (rates * silu * up).astype(BF16)
    backward = rates * dot_nt(weights_ref[2], values)
    d_gate = (backward * up * sigmoid * (1.0 + gate * (1.0 - sigmoid)) * INVERSE).astype(BF16)
    d_up = (backward * silu * INVERSE).astype(BF16)
    up_part = dot_nn(d_up, keys).astype(BF16)
    put(0, slice(0, width), dot_nn(d_gate, keys).astype(BF16))
    put(0, slice(width, width + width // 2), up_part[:, :width // 2])
    put(1, slice(0, width), dot_nn(hidden, values).astype(BF16))
    put(1, slice(width, width + width // 2), up_part[:, width // 2:])

    @pl.when(turn == pl.num_programs(0) - 1)
    def _():
        halves = len(out_refs) // 2
        half_rows = hidden_size // halves
        for index, out_ref in enumerate(out_refs):
            half = index % halves
            out_ref[...] = chunk_refs[index // halves][half * half_rows:(half + 1) * half_rows, :]


def attend_rows(edge_prev, edge_next, query_tile, keys_prev, keys_own, keys_next,
                values_prev, values_own, values_next):
    scale = math.log2(math.e) / math.sqrt(HEAD_DIM)
    row = lax.broadcasted_iota(jnp.int32, (ROW_TILE, ROW_TILE), 0)
    col = lax.broadcasted_iota(jnp.int32, (ROW_TILE, ROW_TILE), 1)
    minus = jnp.float32(-jnp.inf)
    score_prev = dot_nt(query_tile, keys_prev)
    score_own = dot_nt(query_tile, keys_own)
    score_next = dot_nt(query_tile, keys_next)
    parts = [score_prev[:, :ROW_TILE] + jnp.where(col >= row, edge_prev, minus)]
    if score_prev.shape[1] > ROW_TILE:
        parts.append(score_prev[:, ROW_TILE:] + edge_prev)
    parts.append(score_own)
    if score_next.shape[1] > ROW_TILE:
        parts.append(score_next[:, :-ROW_TILE] + edge_next)
    parts.append(score_next[:, -ROW_TILE:] + jnp.where(col <= row, edge_next, minus))
    scores = jnp.concatenate(parts, axis=1)
    highest = jnp.max(scores, axis=1, keepdims=True)
    weights = jnp.exp2((scores - highest) * scale)
    total = jnp.sum(weights, axis=1, keepdims=True)
    weights = weights.astype(BF16)
    width_prev, width_own = score_prev.shape[1], score_own.shape[1]
    attended = (
        dot_nn(weights[:, :width_prev], values_prev)
        + dot_nn(weights[:, width_prev:width_prev + width_own], values_own)
        + dot_nn(weights[:, width_prev + width_own:], values_next)
    )
    return attended / total


def pack_kernel(side_ref, queries_ref, keys_ref, values_ref, out_ref):
    count = queries_ref.shape[0]
    start = pl.multiple_of((1 - side_ref[0, 0]) * HEAD_DIM, HEAD_DIM)
    for index, ref in enumerate((queries_ref, keys_ref, values_ref)):
        out_ref[index * count:(index + 1) * count, :] = ref[:, pl.ds(start, HEAD_DIM)]


def border_kernel(side_ref, keys_ref, values_ref, other_ref, low_ref, high_ref):
    count = keys_ref.shape[0]
    side = side_ref[0, 0]
    start = pl.multiple_of(side * HEAD_DIM, HEAD_DIM)

    def fill(own_ref, other_out_ref):
        own_ref[:count, :] = keys_ref[:, pl.ds(start, HEAD_DIM)]
        own_ref[count:, :] = values_ref[:, pl.ds(start, HEAD_DIM)]
        other_out_ref[...] = other_ref[count:, :]

    @pl.when(side == 0)
    def _():
        fill(low_ref, high_ref)

    @pl.when(side != 0)
    def _():
        fill(high_ref, low_ref)


def first_kernel(edge_ref, side_ref, queries_ref, other_ref, prev_ref, low_ref, high_ref, next_ref,
                 keep_ref, send_ref, keys_ref, values_ref):
    count = queries_ref.shape[0]
    side = side_ref[0, 0]
    for index, ref in enumerate((prev_ref, low_ref, high_ref, next_ref)):
        rows = slice(index * count, (index + 1) * count)
        keys_ref[rows, :] = ref[:count, :]
        values_ref[rows, :] = ref[count:, :]
    start = pl.multiple_of(side * HEAD_DIM, HEAD_DIM)
    for turn, out_ref in enumerate((keep_ref, send_ref)):
        base = (side if turn == 0 else 1 - side) * count

        def span(ref, low, length):
            return ref[pl.ds(pl.multiple_of(base + low, ROW_TILE), length), :]

        for index in range(count // ROW_TILE):
            low, high = index * ROW_TILE, (index + 1) * ROW_TILE
            query = queries_ref[low:high, pl.ds(start, HEAD_DIM)] if turn == 0 else other_ref[low:high, :]
            out_ref[low:high, :] = attend_rows(
                edge_ref[turn, 0], edge_ref[turn, 1], query,
                span(keys_ref, low, count - low), span(keys_ref, count, count),
                span(keys_ref, 2 * count, high),
                span(values_ref, low, count - low), span(values_ref, count, count),
                span(values_ref, 2 * count, high),
            ).astype(BF16)


def second_kernel(edge_ref, queries_ref, keep_ref, near_ref, far_ref, prev_ref, keys_ref, values_ref, next_ref,
                  out_ref):
    count = keys_ref.shape[0]
    for low in range(0, count, ROW_TILE):
        high = low + ROW_TILE
        rows = slice(low, high)
        mixed = (
            keep_ref[rows, :].astype(F32)
            + near_ref[rows, :].astype(F32)
            + far_ref[rows, :].astype(F32)
        )
        query = (queries_ref[rows, :].astype(F32) + mixed).astype(BF16)
        heads = []
        for head in range(HEADS_GRP):
            cols = slice(head * HEAD_DIM, (head + 1) * HEAD_DIM)
            heads.append(
                attend_rows(
                    edge_ref[0, 0], edge_ref[0, 1], query[:, cols],
                    prev_ref[low:count, cols], keys_ref[:, cols], next_ref[:high, cols],
                    prev_ref[count + low:, cols], values_ref[:, cols], next_ref[count:count + high, cols],
                )
            )
        both = jnp.concatenate(heads, axis=1)
        mean = jnp.mean(both * both, axis=1, keepdims=True)
        out_ref[rows, :] = (both * lax.rsqrt(mean + 1e-05)).astype(BF16)


def renew_kernel(orders, place_ref, side_ref, places_ref, *refs):
    count = (len(refs) - 8) // 2
    sources, own_ref, share_refs = refs[:count], refs[count], refs[count + 1:count + 5]
    loaded, (fast_ref, new_ref, sems) = refs[count + 5:-3], refs[-3:]
    copies = [
        pltpu.make_async_copy(source, target, sems.at[index])
        for index, (source, target) in enumerate(zip(sources, loaded))
    ]
    for copy in copies:
        copy.start()
    pieces, (weights_ref, keep_ref, other_ref, map_ref, output_ref) = loaded[:-5], loaded[-5:]
    place = place_ref[0, 0]
    side = side_ref[0, 0]
    hidden_size, width = weights_ref.shape[1:]
    for copy in copies[:-5]:
        copy.wait()
    limit_norm = math.sqrt(FAST_HIDDEN * FAST_DIM) / 2.0
    step = 64
    square = jnp.zeros((1, pieces[0].shape[1]), F32)
    for piece in pieces:
        for low in range(0, piece.shape[0], step):
            part = piece[low:low + step, :].astype(F32)
            square = square + jnp.sum(part * part, axis=0, keepdims=True)
    square = jnp.sum(square, axis=1, keepdims=True)
    factor = jnp.minimum(1.0, limit_norm * lax.rsqrt(square + 1e-06))
    copies[-5].wait()
    per_chunk = len(pieces) // 2
    piece_rows = pieces[0].shape[0]
    blocks = 1 << len(orders[0])
    block_rows = hidden_size // blocks
    count = min(step, block_rows)
    for block in range(blocks):
        starts = [slot_of(block, order) * block_rows for order in orders]
        for low in range(0, block_rows, count):
            found = []
            for chunk, start in enumerate(starts):
                piece = pieces[chunk * per_chunk + start // piece_rows]
                inside = start % piece_rows + low
                found.append(piece[inside:inside + count, :].astype(F32))
            parts = [
                found[0][:, :width],
                jnp.concatenate([found[0][:, width:], found[1][:, width:]], axis=1),
                found[1][:, :width],
            ]
            rows = slice(low, low + count)
            if blocks > 1:
                rows = pl.ds(pl.multiple_of((block ^ place) * block_rows + low, count), count)
            for matrix, part in enumerate(parts):
                old = weights_ref[matrix, rows, :].astype(F32)
                stepped = old + factor * part
                norm = jnp.sqrt(jnp.sum(old * old, axis=1, keepdims=True))
                size = jnp.sum(stepped * stepped, axis=1, keepdims=True)
                fresh = (stepped * norm * lax.rsqrt(size + 1e-06)).astype(BF16)
                new_ref[matrix, rows, :] = fresh
                if block == 0:
                    own_ref[matrix, low:low + count, :] = fresh
    for copy in copies[-4:-1]:
        copy.wait()
    own_map = map_ref[pl.ds(pl.multiple_of(side * HEAD_DIM, HEAD_DIM), HEAD_DIM), :]
    other_map = map_ref[pl.ds(pl.multiple_of((1 - side) * HEAD_DIM, HEAD_DIM), HEAD_DIM), :]
    step = keep_ref.shape[0]
    for low in range(0, keep_ref.shape[0], step):
        rows = slice(low, low + step)
        own = keep_ref[rows, :].astype(F32)
        other = other_ref[rows, :].astype(F32)
        total = jnp.sum(own * own + other * other, axis=1, keepdims=True)
        norm = lax.rsqrt(total / (HEADS_GRP * HEAD_DIM) + 1e-05)
        query = (
            dot_nn((own * norm).astype(BF16), own_map) + dot_nn((other * norm).astype(BF16), other_map)
        ).astype(BF16)
        gate = dot_nt(query, new_ref[0]) * INVERSE
        up = dot_nt(query, new_ref[1]) * INVERSE
        hidden = (jax.nn.silu(gate) * up).astype(BF16)
        raw = dot_nn(hidden, new_ref[2])
        mean = jnp.mean(raw * raw, axis=1, keepdims=True)
        fast_ref[rows, :] = (raw * lax.rsqrt(mean + 1e-05)).astype(BF16)
    copies[-1].wait()
    for index, share_ref in enumerate(share_refs):
        width = share_ref.shape[1]
        start = pl.multiple_of(places_ref[0, index] * width, width)
        share_ref[...] = dot_nn(fast_ref[...], output_ref[:, pl.ds(start, width)]).astype(BF16)


def seq_shift(value, step):
    peers = lax.axis_size("seq")
    return lax.ppermute(
        value, "seq", [(i, i + step) for i in range(peers) if 0 <= i + step < peers]
    )


def head_swap(value, bit):
    return lax.ppermute(value, "head", [(i, i ^ bit) for i in range(lax.axis_size("head"))])


def seq_swap(value, bit):
    step = 1 << bit
    return lax.ppermute(value, "seq", [(i, i ^ step) for i in range(lax.axis_size("seq"))])


def after(value, others):
    return lax.optimization_barrier((value, others))[0]


def halving_start(chunks, orders):
    keeps = [keep for keep, _ in chunks]
    return keeps, [seq_swap(send, order[0]) for (_, send), order in zip(chunks, orders)]


def halving_step(keeps, found, orders, turn, wait=()):
    sends, rest = [], []
    for keep, new in zip(keeps, found):
        half = keep.shape[0] // 2
        sends.append((keep[half:].astype(F32) + new[half:].astype(F32)).astype(BF16))
        rest.append(lax.optimization_barrier(keep[:half].astype(F32) + new[:half].astype(F32)))
    sends = after(sends, wait) if wait else sends
    return rest, [seq_swap(send, order[turn]) for send, order in zip(sends, orders)]


def doubling_step(held, orders, turn, wait=()):
    whole = [jnp.concatenate(parts) if len(parts) > 1 else parts[0] for parts in held]
    whole = after(whole, wait) if wait else whole
    return [(own, seq_swap(own, order[turn])) for own, order in zip(whole, orders)]


def local(
    queries_first,
    keys_first,
    values_first,
    input_map,
    fast_keys,
    fast_values,
    step_rates,
    fast_weights,
    output_map,
    queries_second,
    keys_second,
    values_second,
):
    rows, width = queries_first.shape
    seq_count = lax.axis_size("seq")
    seq_place = lax.axis_index("seq")
    head_place = lax.axis_index("head")
    weights = jnp.transpose(fast_weights[0], (1, 0, 2))
    hidden_size, fast_width = weights.shape[1:]
    shape = jax.ShapeDtypeStruct
    minus = jnp.float32(-jnp.inf)
    side = seq_place % 2

    def edges_of(block):
        return [jnp.where(block > 0, 0.0, minus), jnp.where(block < seq_count - 1, 0.0, minus)]

    edges = jnp.stack(edges_of(seq_place) + edges_of(seq_place ^ 1)).reshape(2, 2)
    side_scalar = side.astype(jnp.int32).reshape(1, 1)
    place = seq_place.astype(jnp.int32).reshape(1, 1)

    packed = call(
        pack_kernel,
        shape((3 * rows, HEAD_DIM), BF16),
        (side_scalar, queries_first, keys_first, values_first),
        scalars=1,
    )
    other_first = seq_swap(packed, 0)

    bits = tuple(range(seq_count.bit_length() - 1))
    halving = seq_count == 1 << len(bits) and len(bits) > 1 and hidden_size >> len(bits) >= 16
    orders = (bits, bits[1:] + bits[:1]) if halving else ((), ())
    halves = 2 if halving else 1
    chunk_width = fast_width + fast_width // 2
    out_shapes = [shape((hidden_size // halves, chunk_width), BF16)] * (2 * halves)
    whole = pl.BlockSpec(memory_space=pltpu.VMEM)
    gradients = pl.pallas_call(
        functools.partial(gradient_kernel, orders),
        grid=(hidden_size // ROW_TILE,),
        out_shape=out_shapes,
        in_specs=[
            pl.BlockSpec(memory_space=pltpu.SMEM),
            whole,
            whole,
            whole,
            pl.BlockSpec((3, ROW_TILE, fast_width), lambda turn: (0, turn, 0)),
        ],
        out_specs=[whole] * len(out_shapes),
        scratch_shapes=[pltpu.VMEM((hidden_size, chunk_width), BF16)] * 2,
        compiler_params=pltpu.CompilerParams(vmem_limit_bytes=VMEM_MOST),
        cost_estimate=pl.CostEstimate(flops=1000, bytes_accessed=1000, transcendentals=0),
    )(place, step_rates.reshape(1, rows), fast_keys, fast_values, weights)

    low_block, high_block = call(
        border_kernel,
        [shape((2 * rows, HEAD_DIM), BF16)] * 2,
        (side_scalar, keys_first, values_first, other_first),
        scalars=1,
    )

    def first_halos(low_block, high_block):
        return seq_shift(high_block, 2), seq_shift(low_block, -2)

    def first_attention(prev_first, next_first):
        keep_first, send_first = call(
            first_kernel,
            [shape((rows, HEAD_DIM), BF16)] * 2,
            (edges, side_scalar, queries_first, other_first, prev_first, low_block, high_block, next_first),
            scalars=2,
            scratch=[pltpu.VMEM((4 * rows, HEAD_DIM), BF16)] * 2,
            cost=(12 * rows * rows * width, 16 * rows * width),
        )
        return keep_first, seq_swap(send_first, 0)

    both_second = jnp.concatenate([keys_second, values_second])

    if halving:
        turns = len(bits)
        keeps, found = halving_start([gradients[:2], gradients[2:]], orders)
        for turn in range(1, turns):
            if turn == turns - 1:
                prev_first, next_first = first_halos(*after((low_block, high_block), found))
                prev_second = seq_shift(after(both_second, found), 1)
            keeps, found = halving_step(keeps, found, orders, turn)
        held = [((keep.astype(F32) + new.astype(F32)).astype(BF16),) for keep, new in zip(keeps, found)]
        for turn in reversed(range(turns)):
            wait = ()
            if turn == 1:
                wait = (prev_first, next_first, prev_second)
            if turn == 0:
                keep_first, back_first = first_attention(prev_first, next_first)
                wait = (keep_first,)
            held = doubling_step(held, orders, turn, wait)
        gathered = [part for parts in held for part in parts]
        next_second = seq_shift(after(both_second, back_first), -1)
    else:
        gathered = lax.psum(gradients, "seq")
        keep_first, back_first = first_attention(*first_halos(low_block, high_block))
        prev_second, next_second = seq_shift(both_second, 1), seq_shift(both_second, -1)
    own_rows = hidden_size >> len(orders[0])
    my_bit, near = head_place % 2, head_place // 2
    places = jnp.stack(
        [2 * pair + bit for pair in (near ^ 1, near) for bit in (1 - my_bit, my_bit)]
    ).astype(jnp.int32).reshape(1, 4)
    share = shape((rows, width), BF16)
    operands = (*gathered, weights, keep_first, back_first, input_map[0], output_map)
    own_new, far_send, far_keep, near_send, near_keep = call(
        functools.partial(renew_kernel, orders),
        [shape((3, own_rows, fast_width), BF16)] + [share] * 4,
        (place, side_scalar, places, *operands),
        scalars=3,
        anywhere=len(operands),
        scratch=[pltpu.VMEM(operand.shape, BF16) for operand in operands]
        + [
            pltpu.VMEM((rows, fast_width), BF16),
            pltpu.VMEM(weights.shape, BF16),
            pltpu.SemaphoreType.DMA((len(operands),)),
        ],
        limit=VMEM_MOST - 3 * 1024 * 1024,
    )
    far_near = head_swap(far_send, 1)
    far_keep = lax.optimization_barrier(far_keep.astype(F32))
    near_near = head_swap(after(near_send, next_second), 1)
    far_far = head_swap((far_keep + far_near.astype(F32)).astype(BF16), 2)
    if not halving:
        share_rows = hidden_size // seq_count
        own_new = lax.dynamic_slice_in_dim(own_new, seq_place * share_rows, share_rows, 1)

    normed_second = call(
        second_kernel,
        share,
        (edges, queries_second, near_keep, near_near, far_far,
         prev_second, keys_second, values_second, next_second),
        scalars=1,
        cost=(12 * rows * rows * width, 16 * rows * width),
    )
    return (normed_second, jnp.transpose(own_new, (1, 0, 2))[None])


def solution(mesh):
    return jax.shard_map(
        local,
        mesh=mesh,
        in_specs=(
            P("seq", "head"),
            P("seq", "head"),
            P("seq", "head"),
            P("head", None, None),
            P("seq", "head"),
            P("seq", "head"),
            P("seq", "head"),
            P("head", None, None, None),
            P("head", None),
            P("seq", "head"),
            P("seq", "head"),
            P("seq", "head"),
        ),
        out_specs=(P("seq", "head"), P("head", "seq", None, None)),
        check_vma=False,
    )
```

```python
import functools
import math

import jax
import jax.numpy as jnp
from jax import lax
from jax.experimental import pallas as pl
from jax.experimental.pallas import tpu as pltpu
from jax.sharding import PartitionSpec as P

HALF_WIN = 512
HEAD_DIM = 128
HEADS_GRP = 2
FAST_DIM = 512
FAST_HIDDEN = 512
TILE = 128
ROW_TILE = 256
VMEM_LIMIT = 24 * 1024 * 1024
VMEM_MOST = 60 * 1024 * 1024

BF16 = jnp.bfloat16
F32 = jnp.float32
INVERSE = 1.0 / math.sqrt(FAST_DIM)


def dot_nn(left, right):
    return lax.dot_general(left, right, (((1,), (0,)), ((), ())), preferred_element_type=F32)


def dot_nt(left, right):
    return lax.dot_general(left, right, (((1,), (1,)), ((), ())), preferred_element_type=F32)


def call(body, out_shapes, operands, scalars=0, anywhere=0, scratch=(), cost=None, limit=VMEM_LIMIT):
    vmem = pl.BlockSpec(memory_space=pltpu.VMEM)
    in_specs = (
        [pl.BlockSpec(memory_space=pltpu.SMEM)] * scalars
        + [vmem] * (len(operands) - scalars - anywhere)
        + [pl.BlockSpec(memory_space=pl.ANY)] * anywhere
    )
    flops, moved = cost or (1000, 1000)
    return pl.pallas_call(
        body,
        out_shape=out_shapes,
        in_specs=in_specs,
        out_specs=jax.tree.map(lambda _: vmem, out_shapes),
        scratch_shapes=scratch,
        compiler_params=pltpu.CompilerParams(vmem_limit_bytes=limit),
        cost_estimate=pl.CostEstimate(flops=flops, bytes_accessed=moved, transcendentals=0),
    )(*operands)


def slot_of(block, order):
    slot = 0
    for bit in order:
        slot = slot * 2 + ((block >> bit) & 1)
    return slot


def gradient_kernel(orders, place_ref, rates_ref, keys_ref, values_ref, weights_ref, *refs):
    out_refs, chunk_refs = refs[:-2], refs[-2:]
    place = place_ref[0, 0]
    rates = rates_ref[...]
    keys = keys_ref[...]
    values = values_ref[...]
    hidden_size = chunk_refs[0].shape[0]
    width = weights_ref.shape[2]
    turn = pl.program_id(0)
    step = weights_ref.shape[1]

    def put(chunk, columns, product):
        order = orders[chunk]
        block_rows = min(step, hidden_size >> len(order))
        for start in range(0, step, block_rows):
            row = turn * step + start
            if order:
                block = turn * (step // block_rows) + start // block_rows
                row = slot_of(block ^ place, order) * block_rows
            row = pl.multiple_of(row, block_rows)
            chunk_refs[chunk][pl.ds(row, block_rows), columns] = product[start:start + block_rows]

    gate = dot_nt(weights_ref[0], keys) * INVERSE
    up = dot_nt(weights_ref[1], keys) * INVERSE
    sigmoid = jax.nn.sigmoid(gate)
    silu = gate * sigmoid
    hidden = (rates * silu * up).astype(BF16)
    backward = rates * dot_nt(weights_ref[2], values)
    d_gate = (backward * up * sigmoid * (1.0 + gate * (1.0 - sigmoid)) * INVERSE).astype(BF16)
    d_up = (backward * silu * INVERSE).astype(BF16)
    up_part = dot_nn(d_up, keys).astype(BF16)
    put(0, slice(0, width), dot_nn(d_gate, keys).astype(BF16))
    put(0, slice(width, width + width // 2), up_part[:, :width // 2])
    put(1, slice(0, width), dot_nn(hidden, values).astype(BF16))
    put(1, slice(width, width + width // 2), up_part[:, width // 2:])

    @pl.when(turn == pl.num_programs(0) - 1)
    def _():
        halves = len(out_refs) // 2
        half_rows = hidden_size // halves
        for index, out_ref in enumerate(out_refs):
            half = index % halves
            out_ref[...] = chunk_refs[index // halves][half * half_rows:(half + 1) * half_rows, :]


def attend_rows(edge_prev, edge_next, query_tile, keys_prev, keys_own, keys_next,
                values_prev, values_own, values_next):
    scale = math.log2(math.e) / math.sqrt(HEAD_DIM)
    row = lax.broadcasted_iota(jnp.int32, (ROW_TILE, ROW_TILE), 0)
    col = lax.broadcasted_iota(jnp.int32, (ROW_TILE, ROW_TILE), 1)
    minus = jnp.float32(-jnp.inf)
    score_prev = dot_nt(query_tile, keys_prev)
    score_own = dot_nt(query_tile, keys_own)
    score_next = dot_nt(query_tile, keys_next)
    parts = [score_prev[:, :ROW_TILE] + jnp.where(col >= row, edge_prev, minus)]
    if score_prev.shape[1] > ROW_TILE:
        parts.append(score_prev[:, ROW_TILE:] + edge_prev)
    parts.append(score_own)
    if score_next.shape[1] > ROW_TILE:
        parts.append(score_next[:, :-ROW_TILE] + edge_next)
    parts.append(score_next[:, -ROW_TILE:] + jnp.where(col <= row, edge_next, minus))
    scores = jnp.concatenate(parts, axis=1)
    highest = jnp.max(scores, axis=1, keepdims=True)
    weights = jnp.exp2((scores - highest) * scale)
    total = jnp.sum(weights, axis=1, keepdims=True)
    weights = weights.astype(BF16)
    width_prev, width_own = score_prev.shape[1], score_own.shape[1]
    attended = (
        dot_nn(weights[:, :width_prev], values_prev)
        + dot_nn(weights[:, width_prev:width_prev + width_own], values_own)
        + dot_nn(weights[:, width_prev + width_own:], values_next)
    )
    return attended / total


def pack_kernel(side_ref, queries_ref, keys_ref, values_ref, out_ref):
    count = queries_ref.shape[0]
    start = pl.multiple_of((1 - side_ref[0, 0]) * HEAD_DIM, HEAD_DIM)
    for index, ref in enumerate((queries_ref, keys_ref, values_ref)):
        out_ref[index * count:(index + 1) * count, :] = ref[:, pl.ds(start, HEAD_DIM)]


def border_kernel(side_ref, keys_ref, values_ref, other_ref, low_ref, high_ref):
    count = keys_ref.shape[0]
    side = side_ref[0, 0]
    start = pl.multiple_of(side * HEAD_DIM, HEAD_DIM)

    def fill(own_ref, other_out_ref):
        own_ref[:count, :] = keys_ref[:, pl.ds(start, HEAD_DIM)]
        own_ref[count:, :] = values_ref[:, pl.ds(start, HEAD_DIM)]
        other_out_ref[...] = other_ref[count:, :]

    @pl.when(side == 0)
    def _():
        fill(low_ref, high_ref)

    @pl.when(side != 0)
    def _():
        fill(high_ref, low_ref)


def first_kernel(edge_ref, side_ref, queries_ref, other_ref, prev_ref, low_ref, high_ref, next_ref,
                 keep_ref, send_ref, keys_ref, values_ref):
    count = queries_ref.shape[0]
    side = side_ref[0, 0]
    for index, ref in enumerate((prev_ref, low_ref, high_ref, next_ref)):
        rows = slice(index * count, (index + 1) * count)
        keys_ref[rows, :] = ref[:count, :]
        values_ref[rows, :] = ref[count:, :]
    start = pl.multiple_of(side * HEAD_DIM, HEAD_DIM)
    for turn, out_ref in enumerate((keep_ref, send_ref)):
        base = (side if turn == 0 else 1 - side) * count

        def span(ref, low, length):
            return ref[pl.ds(pl.multiple_of(base + low, ROW_TILE), length), :]

        for index in range(count // ROW_TILE):
            low, high = index * ROW_TILE, (index + 1) * ROW_TILE
            query = queries_ref[low:high, pl.ds(start, HEAD_DIM)] if turn == 0 else other_ref[low:high, :]
            out_ref[low:high, :] = attend_rows(
                edge_ref[turn, 0], edge_ref[turn, 1], query,
                span(keys_ref, low, count - low), span(keys_ref, count, count),
                span(keys_ref, 2 * count, high),
                span(values_ref, low, count - low), span(values_ref, count, count),
                span(values_ref, 2 * count, high),
            ).astype(BF16)


def second_kernel(edge_ref, queries_ref, keep_ref, near_ref, far_ref, prev_ref, keys_ref, values_ref, next_ref,
                  *refs):
    done_refs, out_ref = refs[:-1], refs[-1]
    count = keys_ref.shape[0]
    half = far_ref.shape[0]
    offset = half if done_refs else 0
    if done_refs:
        out_ref[:half, :] = done_refs[0][...]
    for low in range(offset, offset + half, ROW_TILE):
        high = low + ROW_TILE
        rows = slice(low, high)
        mixed = (
            keep_ref[rows, :].astype(F32)
            + near_ref[rows, :].astype(F32)
            + far_ref[low - offset:high - offset, :].astype(F32)
        )
        query = (queries_ref[rows, :].astype(F32) + mixed).astype(BF16)
        heads = []
        for head in range(HEADS_GRP):
            cols = slice(head * HEAD_DIM, (head + 1) * HEAD_DIM)
            heads.append(
                attend_rows(
                    edge_ref[0, 0], edge_ref[0, 1], query[:, cols],
                    prev_ref[low:count, cols], keys_ref[:, cols], next_ref[:high, cols],
                    prev_ref[count + low:, cols], values_ref[:, cols], next_ref[count:count + high, cols],
                )
            )
        both = jnp.concatenate(heads, axis=1)
        mean = jnp.mean(both * both, axis=1, keepdims=True)
        out_ref[rows, :] = (both * lax.rsqrt(mean + 1e-05)).astype(BF16)


def renew_kernel(orders, place_ref, side_ref, places_ref, *refs):
    count = (len(refs) - 8) // 2
    sources, own_ref, share_refs = refs[:count], refs[count], refs[count + 1:count + 5]
    loaded, (fast_ref, new_ref, sems) = refs[count + 5:-3], refs[-3:]
    copies = [
        pltpu.make_async_copy(source, target, sems.at[index])
        for index, (source, target) in enumerate(zip(sources, loaded))
    ]
    for copy in copies:
        copy.start()
    pieces, (weights_ref, keep_ref, other_ref, map_ref, output_ref) = loaded[:-5], loaded[-5:]
    place = place_ref[0, 0]
    side = side_ref[0, 0]
    hidden_size, width = weights_ref.shape[1:]
    for copy in copies[:-5]:
        copy.wait()
    limit_norm = math.sqrt(FAST_HIDDEN * FAST_DIM) / 2.0
    step = 64
    square = jnp.zeros((1, pieces[0].shape[1]), F32)
    for piece in pieces:
        for low in range(0, piece.shape[0], step):
            part = piece[low:low + step, :].astype(F32)
            square = square + jnp.sum(part * part, axis=0, keepdims=True)
    square = jnp.sum(square, axis=1, keepdims=True)
    factor = jnp.minimum(1.0, limit_norm * lax.rsqrt(square + 1e-06))
    copies[-5].wait()
    per_chunk = len(pieces) // 2
    piece_rows = pieces[0].shape[0]
    blocks = 1 << len(orders[0])
    block_rows = hidden_size // blocks
    count = min(step, block_rows)
    for block in range(blocks):
        starts = [slot_of(block, order) * block_rows for order in orders]
        for low in range(0, block_rows, count):
            found = []
            for chunk, start in enumerate(starts):
                piece = pieces[chunk * per_chunk + start // piece_rows]
                inside = start % piece_rows + low
                found.append(piece[inside:inside + count, :].astype(F32))
            parts = [
                found[0][:, :width],
                jnp.concatenate([found[0][:, width:], found[1][:, width:]], axis=1),
                found[1][:, :width],
            ]
            rows = slice(low, low + count)
            if blocks > 1:
                rows = pl.ds(pl.multiple_of((block ^ place) * block_rows + low, count), count)
            for matrix, part in enumerate(parts):
                old = weights_ref[matrix, rows, :].astype(F32)
                stepped = old + factor * part
                norm = jnp.sqrt(jnp.sum(old * old, axis=1, keepdims=True))
                size = jnp.sum(stepped * stepped, axis=1, keepdims=True)
                fresh = (stepped * norm * lax.rsqrt(size + 1e-06)).astype(BF16)
                new_ref[matrix, rows, :] = fresh
                if block == 0:
                    own_ref[matrix, low:low + count, :] = fresh
    for copy in copies[-4:-1]:
        copy.wait()
    own_map = map_ref[pl.ds(pl.multiple_of(side * HEAD_DIM, HEAD_DIM), HEAD_DIM), :]
    other_map = map_ref[pl.ds(pl.multiple_of((1 - side) * HEAD_DIM, HEAD_DIM), HEAD_DIM), :]
    step = keep_ref.shape[0]
    for low in range(0, keep_ref.shape[0], step):
        rows = slice(low, low + step)
        own = keep_ref[rows, :].astype(F32)
        other = other_ref[rows, :].astype(F32)
        total = jnp.sum(own * own + other * other, axis=1, keepdims=True)
        norm = lax.rsqrt(total / (HEADS_GRP * HEAD_DIM) + 1e-05)
        query = (
            dot_nn((own * norm).astype(BF16), own_map) + dot_nn((other * norm).astype(BF16), other_map)
        ).astype(BF16)
        gate = dot_nt(query, new_ref[0]) * INVERSE
        up = dot_nt(query, new_ref[1]) * INVERSE
        hidden = (jax.nn.silu(gate) * up).astype(BF16)
        raw = dot_nn(hidden, new_ref[2])
        mean = jnp.mean(raw * raw, axis=1, keepdims=True)
        fast_ref[rows, :] = (raw * lax.rsqrt(mean + 1e-05)).astype(BF16)
    copies[-1].wait()
    for index, share_ref in enumerate(share_refs):
        width = share_ref.shape[1]
        start = pl.multiple_of(places_ref[0, index] * width, width)
        share_ref[...] = dot_nn(fast_ref[...], output_ref[:, pl.ds(start, width)]).astype(BF16)


def seq_shift(value, step):
    peers = lax.axis_size("seq")
    return lax.ppermute(
        value, "seq", [(i, i + step) for i in range(peers) if 0 <= i + step < peers]
    )


def head_swap(value, bit):
    return lax.ppermute(value, "head", [(i, i ^ bit) for i in range(lax.axis_size("head"))])


def seq_swap(value, bit):
    step = 1 << bit
    return lax.ppermute(value, "seq", [(i, i ^ step) for i in range(lax.axis_size("seq"))])


def after(value, others):
    return lax.optimization_barrier((value, others))[0]


def halving_start(chunks, orders):
    keeps = [keep for keep, _ in chunks]
    return keeps, [seq_swap(send, order[0]) for (_, send), order in zip(chunks, orders)]


def halving_step(keeps, found, orders, turn, wait=()):
    sends, rest = [], []
    for keep, new in zip(keeps, found):
        half = keep.shape[0] // 2
        sends.append((keep[half:].astype(F32) + new[half:].astype(F32)).astype(BF16))
        rest.append(lax.optimization_barrier(keep[:half].astype(F32) + new[:half].astype(F32)))
    sends = after(sends, wait) if wait else sends
    return rest, [seq_swap(send, order[turn]) for send, order in zip(sends, orders)]


def doubling_step(held, orders, turn, wait=()):
    whole = [jnp.concatenate(parts) if len(parts) > 1 else parts[0] for parts in held]
    whole = after(whole, wait) if wait else whole
    return [(own, seq_swap(own, order[turn])) for own, order in zip(whole, orders)]


def local(
    queries_first,
    keys_first,
    values_first,
    input_map,
    fast_keys,
    fast_values,
    step_rates,
    fast_weights,
    output_map,
    queries_second,
    keys_second,
    values_second,
):
    rows, width = queries_first.shape
    seq_count = lax.axis_size("seq")
    seq_place = lax.axis_index("seq")
    head_place = lax.axis_index("head")
    weights = jnp.transpose(fast_weights[0], (1, 0, 2))
    hidden_size, fast_width = weights.shape[1:]
    shape = jax.ShapeDtypeStruct
    minus = jnp.float32(-jnp.inf)
    side = seq_place % 2

    def edges_of(block):
        return [jnp.where(block > 0, 0.0, minus), jnp.where(block < seq_count - 1, 0.0, minus)]

    edges = jnp.stack(edges_of(seq_place) + edges_of(seq_place ^ 1)).reshape(2, 2)
    side_scalar = side.astype(jnp.int32).reshape(1, 1)
    place = seq_place.astype(jnp.int32).reshape(1, 1)

    packed = call(
        pack_kernel,
        shape((3 * rows, HEAD_DIM), BF16),
        (side_scalar, queries_first, keys_first, values_first),
        scalars=1,
    )
    other_first = seq_swap(packed, 0)

    bits = tuple(range(seq_count.bit_length() - 1))
    halving = seq_count == 1 << len(bits) and len(bits) > 1 and hidden_size >> len(bits) >= 16
    orders = (bits, bits[1:] + bits[:1]) if halving else ((), ())
    halves = 2 if halving else 1
    chunk_width = fast_width + fast_width // 2
    out_shapes = [shape((hidden_size // halves, chunk_width), BF16)] * (2 * halves)
    whole = pl.BlockSpec(memory_space=pltpu.VMEM)
    gradients = pl.pallas_call(
        functools.partial(gradient_kernel, orders),
        grid=(1,),
        out_shape=out_shapes,
        in_specs=[
            pl.BlockSpec(memory_space=pltpu.SMEM),
            whole,
            whole,
            whole,
            pl.BlockSpec((3, hidden_size, fast_width), lambda turn: (0, turn, 0)),
        ],
        out_specs=[whole] * len(out_shapes),
        scratch_shapes=[pltpu.VMEM((hidden_size, chunk_width), BF16)] * 2,
        compiler_params=pltpu.CompilerParams(vmem_limit_bytes=VMEM_MOST),
        cost_estimate=pl.CostEstimate(flops=1000, bytes_accessed=1000, transcendentals=0),
    )(place, step_rates.reshape(1, rows), fast_keys, fast_values, weights)

    low_block, high_block = call(
        border_kernel,
        [shape((2 * rows, HEAD_DIM), BF16)] * 2,
        (side_scalar, keys_first, values_first, other_first),
        scalars=1,
    )

    def first_halos(low_block, high_block):
        return seq_shift(high_block, 2), seq_shift(low_block, -2)

    def first_attention(prev_first, next_first):
        keep_first, send_first = call(
            first_kernel,
            [shape((rows, HEAD_DIM), BF16)] * 2,
            (edges, side_scalar, queries_first, other_first, prev_first, low_block, high_block, next_first),
            scalars=2,
            scratch=[pltpu.VMEM((4 * rows, HEAD_DIM), BF16)] * 2,
            cost=(12 * rows * rows * width, 16 * rows * width),
        )
        return keep_first, seq_swap(send_first, 0)

    both_second = jnp.concatenate([keys_second, values_second])

    if halving:
        turns = len(bits)
        keeps, found = halving_start([gradients[:2], gradients[2:]], orders)
        for turn in range(1, turns):
            if turn == turns - 1:
                prev_first, next_first = first_halos(*after((low_block, high_block), found))
                prev_second = seq_shift(after(both_second, found), 1)
            keeps, found = halving_step(keeps, found, orders, turn)
        held = [((keep.astype(F32) + new.astype(F32)).astype(BF16),) for keep, new in zip(keeps, found)]
        for turn in reversed(range(turns)):
            wait = ()
            if turn == 1:
                wait = (prev_first, next_first, prev_second)
            if turn == 0:
                keep_first, back_first = first_attention(prev_first, next_first)
                wait = (keep_first,)
            held = doubling_step(held, orders, turn, wait)
        gathered = [part for parts in held for part in parts]
        next_second = seq_shift(after(both_second, back_first), -1)
    else:
        gathered = lax.psum(gradients, "seq")
        keep_first, back_first = first_attention(*first_halos(low_block, high_block))
        prev_second, next_second = seq_shift(both_second, 1), seq_shift(both_second, -1)
    own_rows = hidden_size >> len(orders[0])
    my_bit, near = head_place % 2, head_place // 2
    places = jnp.stack(
        [2 * pair + bit for pair in (near ^ 1, near) for bit in (1 - my_bit, my_bit)]
    ).astype(jnp.int32).reshape(1, 4)
    share = shape((rows, width), BF16)
    operands = (*gathered, weights, keep_first, back_first, input_map[0], output_map)
    own_new, far_send, far_keep, near_send, near_keep = call(
        functools.partial(renew_kernel, orders),
        [shape((3, own_rows, fast_width), BF16)] + [share] * 4,
        (place, side_scalar, places, *operands),
        scalars=3,
        anywhere=len(operands),
        scratch=[pltpu.VMEM(operand.shape, BF16) for operand in operands]
        + [
            pltpu.VMEM((rows, fast_width), BF16),
            pltpu.VMEM(weights.shape, BF16),
            pltpu.SemaphoreType.DMA((len(operands),)),
        ],
        limit=VMEM_MOST - 3 * 1024 * 1024,
    )
    far_near = head_swap(far_send, 1)
    far_keep = lax.optimization_barrier(far_keep.astype(F32))
    near_near = head_swap(after(near_send, next_second), 1)
    half = rows // 2
    far_parts = []
    for part in (slice(0, half), slice(half, rows)):
        far_sum = far_keep[part] + far_near[part].astype(F32)
        far_parts.append(head_swap(far_sum.astype(BF16), 2))
    if not halving:
        share_rows = hidden_size // seq_count
        own_new = lax.dynamic_slice_in_dim(own_new, seq_place * share_rows, share_rows, 1)

    def second_attention(part, *done):
        return call(
            second_kernel,
            shape((half * (1 + len(done)), width), BF16),
            (edges, queries_second, near_keep, near_near, far_parts[part],
             prev_second, keys_second, values_second, next_second, *done),
            scalars=1,
            cost=(6 * rows * rows * width, 16 * rows * width),
        )

    normed_second = second_attention(1, second_attention(0))
    return (normed_second, jnp.transpose(own_new, (1, 0, 2))[None])


def solution(mesh):
    return jax.shard_map(
        local,
        mesh=mesh,
        in_specs=(
            P("seq", "head"),
            P("seq", "head"),
            P("seq", "head"),
            P("head", None, None),
            P("seq", "head"),
            P("seq", "head"),
            P("seq", "head"),
            P("head", None, None, None),
            P("head", None),
            P("seq", "head"),
            P("seq", "head"),
            P("seq", "head"),
        ),
        out_specs=(P("seq", "head"), P("head", "seq", None, None)),
        check_vma=False,
    )
```

```python
import functools
import math

import jax
import jax.numpy as jnp
from jax import lax
from jax.experimental import pallas as pl
from jax.experimental.pallas import tpu as pltpu
from jax.sharding import PartitionSpec as P

HALF_WIN = 512
HEAD_DIM = 128
HEADS_GRP = 2
FAST_DIM = 512
FAST_HIDDEN = 512
TILE = 128
ROW_TILE = 256
VMEM_LIMIT = 24 * 1024 * 1024
VMEM_MOST = 60 * 1024 * 1024

BF16 = jnp.bfloat16
F32 = jnp.float32
INVERSE = 1.0 / math.sqrt(FAST_DIM)


def dot_nn(left, right):
    return lax.dot_general(left, right, (((1,), (0,)), ((), ())), preferred_element_type=F32)


def dot_nt(left, right):
    return lax.dot_general(left, right, (((1,), (1,)), ((), ())), preferred_element_type=F32)


def call(body, out_shapes, operands, scalars=0, anywhere=0, scratch=(), cost=None, limit=VMEM_LIMIT):
    vmem = pl.BlockSpec(memory_space=pltpu.VMEM)
    in_specs = (
        [pl.BlockSpec(memory_space=pltpu.SMEM)] * scalars
        + [vmem] * (len(operands) - scalars - anywhere)
        + [pl.BlockSpec(memory_space=pl.ANY)] * anywhere
    )
    flops, moved = cost or (1000, 1000)
    return pl.pallas_call(
        body,
        out_shape=out_shapes,
        in_specs=in_specs,
        out_specs=jax.tree.map(lambda _: vmem, out_shapes),
        scratch_shapes=scratch,
        compiler_params=pltpu.CompilerParams(vmem_limit_bytes=limit),
        cost_estimate=pl.CostEstimate(flops=flops, bytes_accessed=moved, transcendentals=0),
    )(*operands)


def slot_of(block, order):
    slot = 0
    for bit in order:
        slot = slot * 2 + ((block >> bit) & 1)
    return slot


def gradient_kernel(orders, place_ref, rates_ref, keys_hbm, values_hbm, weights_hbm, *refs):
    out_refs, chunk_refs = refs[:-7], refs[-7:-5]
    keys_ref, values_ref, weights_ref, load_sems, store_sems = refs[-5:]
    place = place_ref[0, 0]
    rates = rates_ref[...]
    hidden_size, width = weights_ref.shape[1:]
    loads = [
        pltpu.make_async_copy(source, target, load_sems.at[index])
        for index, (source, target) in enumerate(
            [
                (keys_hbm, keys_ref),
                (weights_hbm.at[0], weights_ref.at[0]),
                (weights_hbm.at[1], weights_ref.at[1]),
                (values_hbm, values_ref),
                (weights_hbm.at[2], weights_ref.at[2]),
            ]
        )
    ]
    for load in loads:
        load.start()

    def put(chunk, columns, product):
        order = orders[chunk]
        block_rows = hidden_size >> len(order)
        for block in range(1 << len(order)):
            row = pl.multiple_of(slot_of(block ^ place, order) * block_rows, block_rows) if order else 0
            chunk_refs[chunk][pl.ds(row, block_rows), columns] = product[
                block * block_rows:(block + 1) * block_rows
            ]

    def stores_of(chunk):
        halves = len(out_refs) // 2
        half_rows = hidden_size // halves
        stores = []
        for half in reversed(range(halves)):
            index = chunk * halves + half
            stores.append(
                pltpu.make_async_copy(
                    chunk_refs[chunk].at[pl.ds(half * half_rows, half_rows), :],
                    out_refs[index],
                    store_sems.at[index],
                )
            )
        for store in stores:
            store.start()
        return stores

    loads[0].wait()
    loads[1].wait()
    keys = keys_ref[...]
    gate = dot_nt(weights_ref[0], keys) * INVERSE
    sigmoid = jax.nn.sigmoid(gate)
    silu = gate * sigmoid
    loads[2].wait()
    up = dot_nt(weights_ref[1], keys) * INVERSE
    hidden = (rates * silu * up).astype(BF16)
    loads[3].wait()
    values = values_ref[...]
    put(1, slice(0, width), dot_nn(hidden, values).astype(BF16))
    loads[4].wait()
    backward = rates * dot_nt(weights_ref[2], values)
    d_up = (backward * silu * INVERSE).astype(BF16)
    up_part = dot_nn(d_up, keys).astype(BF16)
    put(1, slice(width, width + width // 2), up_part[:, width // 2:])
    stores = stores_of(1)
    put(0, slice(width, width + width // 2), up_part[:, :width // 2])
    d_gate = (backward * up * sigmoid * (1.0 + gate * (1.0 - sigmoid)) * INVERSE).astype(BF16)
    put(0, slice(0, width), dot_nn(d_gate, keys).astype(BF16))
    for store in stores + stores_of(0):
        store.wait()


def attend_rows(edge_prev, edge_next, query_tile, keys_prev, keys_own, keys_next,
                values_prev, values_own, values_next):
    scale = math.log2(math.e) / math.sqrt(HEAD_DIM)
    row = lax.broadcasted_iota(jnp.int32, (ROW_TILE, ROW_TILE), 0)
    col = lax.broadcasted_iota(jnp.int32, (ROW_TILE, ROW_TILE), 1)
    minus = jnp.float32(-jnp.inf)
    score_prev = dot_nt(query_tile, keys_prev)
    score_own = dot_nt(query_tile, keys_own)
    score_next = dot_nt(query_tile, keys_next)
    parts = [score_prev[:, :ROW_TILE] + jnp.where(col >= row, edge_prev, minus)]
    if score_prev.shape[1] > ROW_TILE:
        parts.append(score_prev[:, ROW_TILE:] + edge_prev)
    parts.append(score_own)
    if score_next.shape[1] > ROW_TILE:
        parts.append(score_next[:, :-ROW_TILE] + edge_next)
    parts.append(score_next[:, -ROW_TILE:] + jnp.where(col <= row, edge_next, minus))
    scores = jnp.concatenate(parts, axis=1)
    highest = jnp.max(scores, axis=1, keepdims=True)
    weights = jnp.exp2((scores - highest) * scale)
    total = jnp.sum(weights, axis=1, keepdims=True)
    weights = weights.astype(BF16)
    width_prev, width_own = score_prev.shape[1], score_own.shape[1]
    attended = (
        dot_nn(weights[:, :width_prev], values_prev)
        + dot_nn(weights[:, width_prev:width_prev + width_own], values_own)
        + dot_nn(weights[:, width_prev + width_own:], values_next)
    )
    return attended / total


def pack_kernel(side_ref, queries_ref, keys_ref, values_ref, out_ref):
    count = queries_ref.shape[0]
    start = pl.multiple_of((1 - side_ref[0, 0]) * HEAD_DIM, HEAD_DIM)
    for index, ref in enumerate((queries_ref, keys_ref, values_ref)):
        out_ref[index * count:(index + 1) * count, :] = ref[:, pl.ds(start, HEAD_DIM)]


def border_kernel(side_ref, keys_ref, values_ref, other_ref, low_ref, high_ref):
    count = keys_ref.shape[0]
    side = side_ref[0, 0]
    start = pl.multiple_of(side * HEAD_DIM, HEAD_DIM)

    def fill(own_ref, other_out_ref):
        own_ref[:count, :] = keys_ref[:, pl.ds(start, HEAD_DIM)]
        own_ref[count:, :] = values_ref[:, pl.ds(start, HEAD_DIM)]
        other_out_ref[...] = other_ref[count:, :]

    @pl.when(side == 0)
    def _():
        fill(low_ref, high_ref)

    @pl.when(side != 0)
    def _():
        fill(high_ref, low_ref)


def first_kernel(edge_ref, side_ref, queries_ref, other_ref, prev_ref, low_ref, high_ref, next_ref,
                 keep_ref, send_ref, keys_ref, values_ref):
    count = queries_ref.shape[0]
    side = side_ref[0, 0]
    for index, ref in enumerate((prev_ref, low_ref, high_ref, next_ref)):
        rows = slice(index * count, (index + 1) * count)
        keys_ref[rows, :] = ref[:count, :]
        values_ref[rows, :] = ref[count:, :]
    start = pl.multiple_of(side * HEAD_DIM, HEAD_DIM)
    for turn, out_ref in enumerate((keep_ref, send_ref)):
        base = (side if turn == 0 else 1 - side) * count

        def span(ref, low, length):
            return ref[pl.ds(pl.multiple_of(base + low, ROW_TILE), length), :]

        for index in range(count // ROW_TILE):
            low, high = index * ROW_TILE, (index + 1) * ROW_TILE
            query = queries_ref[low:high, pl.ds(start, HEAD_DIM)] if turn == 0 else other_ref[low:high, :]
            out_ref[low:high, :] = attend_rows(
                edge_ref[turn, 0], edge_ref[turn, 1], query,
                span(keys_ref, low, count - low), span(keys_ref, count, count),
                span(keys_ref, 2 * count, high),
                span(values_ref, low, count - low), span(values_ref, count, count),
                span(values_ref, 2 * count, high),
            ).astype(BF16)


def second_kernel(edge_ref, queries_ref, keep_ref, near_ref, far_ref, prev_ref, keys_ref, values_ref, next_ref,
                  *refs):
    done_refs, out_ref = refs[:-1], refs[-1]
    count = keys_ref.shape[0]
    half = far_ref.shape[0]
    offset = half if done_refs else 0
    if done_refs:
        out_ref[:half, :] = done_refs[0][...]
    for low in range(offset, offset + half, ROW_TILE):
        high = low + ROW_TILE
        rows = slice(low, high)
        mixed = (
            keep_ref[rows, :].astype(F32)
            + near_ref[rows, :].astype(F32)
            + far_ref[low - offset:high - offset, :].astype(F32)
        )
        query = (queries_ref[rows, :].astype(F32) + mixed).astype(BF16)
        heads = []
        for head in range(HEADS_GRP):
            cols = slice(head * HEAD_DIM, (head + 1) * HEAD_DIM)
            heads.append(
                attend_rows(
                    edge_ref[0, 0], edge_ref[0, 1], query[:, cols],
                    prev_ref[low:count, cols], keys_ref[:, cols], next_ref[:high, cols],
                    prev_ref[count + low:, cols], values_ref[:, cols], next_ref[count:count + high, cols],
                )
            )
        both = jnp.concatenate(heads, axis=1)
        mean = jnp.mean(both * both, axis=1, keepdims=True)
        out_ref[rows, :] = (both * lax.rsqrt(mean + 1e-05)).astype(BF16)


def renew_kernel(orders, place_ref, side_ref, places_ref, *refs):
    count = (len(refs) - 8) // 2
    sources, own_ref, share_refs = refs[:count], refs[count], refs[count + 1:count + 5]
    loaded, (fast_ref, new_ref, sems) = refs[count + 5:-3], refs[-3:]
    copies = [
        pltpu.make_async_copy(source, target, sems.at[index])
        for index, (source, target) in enumerate(zip(sources, loaded))
    ]
    for copy in copies[:-4]:
        copy.start()
    pieces, (weights_ref, keep_ref, other_ref, map_ref, output_ref) = loaded[:-5], loaded[-5:]
    place = place_ref[0, 0]
    side = side_ref[0, 0]
    hidden_size, width = weights_ref.shape[1:]
    for copy in copies[:-5]:
        copy.wait()
    for copy in copies[-4:]:
        copy.start()
    limit_norm = math.sqrt(FAST_HIDDEN * FAST_DIM) / 2.0
    step = 64
    square = jnp.zeros((1, pieces[0].shape[1]), F32)
    for piece in pieces:
        for low in range(0, piece.shape[0], step):
            part = piece[low:low + step, :].astype(F32)
            square = square + jnp.sum(part * part, axis=0, keepdims=True)
    square = jnp.sum(square, axis=1, keepdims=True)
    factor = jnp.minimum(1.0, limit_norm * lax.rsqrt(square + 1e-06))
    copies[-5].wait()
    per_chunk = len(pieces) // 2
    piece_rows = pieces[0].shape[0]
    blocks = 1 << len(orders[0])
    block_rows = hidden_size // blocks
    count = min(step, block_rows)
    for block in range(blocks):
        starts = [slot_of(block, order) * block_rows for order in orders]
        for low in range(0, block_rows, count):
            found = []
            for chunk, start in enumerate(starts):
                piece = pieces[chunk * per_chunk + start // piece_rows]
                inside = start % piece_rows + low
                found.append(piece[inside:inside + count, :].astype(F32))
            parts = [
                found[0][:, :width],
                jnp.concatenate([found[0][:, width:], found[1][:, width:]], axis=1),
                found[1][:, :width],
            ]
            rows = slice(low, low + count)
            if blocks > 1:
                rows = pl.ds(pl.multiple_of((block ^ place) * block_rows + low, count), count)
            for matrix, part in enumerate(parts):
                old = weights_ref[matrix, rows, :].astype(F32)
                stepped = old + factor * part
                norm = jnp.sqrt(jnp.sum(old * old, axis=1, keepdims=True))
                size = jnp.sum(stepped * stepped, axis=1, keepdims=True)
                fresh = (stepped * norm * lax.rsqrt(size + 1e-06)).astype(BF16)
                new_ref[matrix, rows, :] = fresh
                if block == 0:
                    own_ref[matrix, low:low + count, :] = fresh
    for copy in copies[-4:-1]:
        copy.wait()
    own_map = map_ref[pl.ds(pl.multiple_of(side * HEAD_DIM, HEAD_DIM), HEAD_DIM), :]
    other_map = map_ref[pl.ds(pl.multiple_of((1 - side) * HEAD_DIM, HEAD_DIM), HEAD_DIM), :]
    step = keep_ref.shape[0]
    for low in range(0, keep_ref.shape[0], step):
        rows = slice(low, low + step)
        own = keep_ref[rows, :].astype(F32)
        other = other_ref[rows, :].astype(F32)
        total = jnp.sum(own * own + other * other, axis=1, keepdims=True)
        norm = lax.rsqrt(total / (HEADS_GRP * HEAD_DIM) + 1e-05)
        query = (
            dot_nn((own * norm).astype(BF16), own_map) + dot_nn((other * norm).astype(BF16), other_map)
        ).astype(BF16)
        gate = dot_nt(query, new_ref[0]) * INVERSE
        up = dot_nt(query, new_ref[1]) * INVERSE
        hidden = (jax.nn.silu(gate) * up).astype(BF16)
        raw = dot_nn(hidden, new_ref[2])
        mean = jnp.mean(raw * raw, axis=1, keepdims=True)
        fast_ref[rows, :] = (raw * lax.rsqrt(mean + 1e-05)).astype(BF16)
    copies[-1].wait()
    for index, share_ref in enumerate(share_refs):
        width = share_ref.shape[1]
        start = pl.multiple_of(places_ref[0, index] * width, width)
        share_ref[...] = dot_nn(fast_ref[...], output_ref[:, pl.ds(start, width)]).astype(BF16)


def seq_shift(value, step):
    peers = lax.axis_size("seq")
    return lax.ppermute(
        value, "seq", [(i, i + step) for i in range(peers) if 0 <= i + step < peers]
    )


def head_swap(value, bit):
    return lax.ppermute(value, "head", [(i, i ^ bit) for i in range(lax.axis_size("head"))])


def seq_swap(value, bit):
    step = 1 << bit
    return lax.ppermute(value, "seq", [(i, i ^ step) for i in range(lax.axis_size("seq"))])


def after(value, others):
    return lax.optimization_barrier((value, others))[0]


def halving_start(chunks, orders):
    keeps = [keep for keep, _ in chunks]
    return keeps, [seq_swap(send, order[0]) for (_, send), order in zip(chunks, orders)]


def halving_step(keeps, found, orders, turn, wait=()):
    sends, rest = [], []
    for keep, new in zip(keeps, found):
        half = keep.shape[0] // 2
        sends.append((keep[half:].astype(F32) + new[half:].astype(F32)).astype(BF16))
        rest.append(lax.optimization_barrier(keep[:half].astype(F32) + new[:half].astype(F32)))
    sends = after(sends, wait) if wait else sends
    return rest, [seq_swap(send, order[turn]) for send, order in zip(sends, orders)]


def doubling_step(held, orders, turn, wait=()):
    whole = [jnp.concatenate(parts) if len(parts) > 1 else parts[0] for parts in held]
    whole = after(whole, wait) if wait else whole
    return [(own, seq_swap(own, order[turn])) for own, order in zip(whole, orders)]


def local(
    queries_first,
    keys_first,
    values_first,
    input_map,
    fast_keys,
    fast_values,
    step_rates,
    fast_weights,
    output_map,
    queries_second,
    keys_second,
    values_second,
):
    rows, width = queries_first.shape
    seq_count = lax.axis_size("seq")
    seq_place = lax.axis_index("seq")
    head_place = lax.axis_index("head")
    weights = jnp.transpose(fast_weights[0], (1, 0, 2))
    hidden_size, fast_width = weights.shape[1:]
    shape = jax.ShapeDtypeStruct
    minus = jnp.float32(-jnp.inf)
    side = seq_place % 2

    def edges_of(block):
        return [jnp.where(block > 0, 0.0, minus), jnp.where(block < seq_count - 1, 0.0, minus)]

    edges = jnp.stack(edges_of(seq_place) + edges_of(seq_place ^ 1)).reshape(2, 2)
    side_scalar = side.astype(jnp.int32).reshape(1, 1)
    place = seq_place.astype(jnp.int32).reshape(1, 1)

    packed = call(
        pack_kernel,
        shape((3 * rows, HEAD_DIM), BF16),
        (side_scalar, queries_first, keys_first, values_first),
        scalars=1,
    )
    other_first = seq_swap(packed, 0)

    bits = tuple(range(seq_count.bit_length() - 1))
    halving = seq_count == 1 << len(bits) and len(bits) > 1 and hidden_size >> len(bits) >= 16
    orders = (bits, bits[1:] + bits[:1]) if halving else ((), ())
    halves = 2 if halving else 1
    chunk_width = fast_width + fast_width // 2
    out_shapes = [shape((hidden_size // halves, chunk_width), BF16)] * (2 * halves)
    anywhere = pl.BlockSpec(memory_space=pl.ANY)
    gradients = pl.pallas_call(
        functools.partial(gradient_kernel, orders),
        out_shape=out_shapes,
        in_specs=[
            pl.BlockSpec(memory_space=pltpu.SMEM),
            pl.BlockSpec(memory_space=pltpu.VMEM),
            anywhere,
            anywhere,
            anywhere,
        ],
        out_specs=[anywhere] * len(out_shapes),
        scratch_shapes=[pltpu.VMEM((hidden_size, chunk_width), BF16)] * 2
        + [
            pltpu.VMEM(fast_keys.shape, BF16),
            pltpu.VMEM(fast_values.shape, BF16),
            pltpu.VMEM(weights.shape, BF16),
            pltpu.SemaphoreType.DMA((5,)),
            pltpu.SemaphoreType.DMA((len(out_shapes),)),
        ],
        compiler_params=pltpu.CompilerParams(vmem_limit_bytes=VMEM_MOST),
        cost_estimate=pl.CostEstimate(flops=1000, bytes_accessed=1000, transcendentals=0),
    )(place, step_rates.reshape(1, rows), fast_keys, fast_values, weights)

    low_block, high_block = call(
        border_kernel,
        [shape((2 * rows, HEAD_DIM), BF16)] * 2,
        (side_scalar, keys_first, values_first, other_first),
        scalars=1,
    )

    def first_halos(low_block, high_block):
        return seq_shift(high_block, 2), seq_shift(low_block, -2)

    def first_attention(prev_first, next_first):
        keep_first, send_first = call(
            first_kernel,
            [shape((rows, HEAD_DIM), BF16)] * 2,
            (edges, side_scalar, queries_first, other_first, prev_first, low_block, high_block, next_first),
            scalars=2,
            scratch=[pltpu.VMEM((4 * rows, HEAD_DIM), BF16)] * 2,
            cost=(12 * rows * rows * width, 16 * rows * width),
        )
        return keep_first, seq_swap(send_first, 0)

    both_second = jnp.concatenate([keys_second, values_second])

    if halving:
        turns = len(bits)
        keeps, found = halving_start([gradients[:2], gradients[2:]], orders)
        for turn in range(1, turns):
            if turn == turns - 1:
                prev_first, next_first = first_halos(*after((low_block, high_block), found))
                prev_second = seq_shift(after(both_second, found), 1)
            keeps, found = halving_step(keeps, found, orders, turn)
        held = [((keep.astype(F32) + new.astype(F32)).astype(BF16),) for keep, new in zip(keeps, found)]
        for turn in reversed(range(turns)):
            wait = ()
            if turn == 1:
                wait = (prev_first, next_first, prev_second)
            if turn == 0:
                keep_first, back_first = first_attention(prev_first, next_first)
                wait = (keep_first,)
            held = doubling_step(held, orders, turn, wait)
        gathered = [part for parts in held for part in parts]
        next_second = seq_shift(after(both_second, back_first), -1)
    else:
        gathered = lax.psum(gradients, "seq")
        keep_first, back_first = first_attention(*first_halos(low_block, high_block))
        prev_second, next_second = seq_shift(both_second, 1), seq_shift(both_second, -1)
    own_rows = hidden_size >> len(orders[0])
    my_bit, near = head_place % 2, head_place // 2
    places = jnp.stack(
        [2 * pair + bit for pair in (near ^ 1, near) for bit in (1 - my_bit, my_bit)]
    ).astype(jnp.int32).reshape(1, 4)
    share = shape((rows, width), BF16)
    operands = (*gathered, weights, keep_first, back_first, input_map[0], output_map)
    own_new, far_send, far_keep, near_send, near_keep = call(
        functools.partial(renew_kernel, orders),
        [shape((3, own_rows, fast_width), BF16)] + [share] * 4,
        (place, side_scalar, places, *operands),
        scalars=3,
        anywhere=len(operands),
        scratch=[pltpu.VMEM(operand.shape, BF16) for operand in operands]
        + [
            pltpu.VMEM((rows, fast_width), BF16),
            pltpu.VMEM(weights.shape, BF16),
            pltpu.SemaphoreType.DMA((len(operands),)),
        ],
        limit=VMEM_MOST - 3 * 1024 * 1024,
    )
    far_near = head_swap(far_send, 1)
    far_keep = lax.optimization_barrier(far_keep.astype(F32))
    near_near = head_swap(after(near_send, next_second), 1)
    half = rows // 2
    far_parts = []
    for part in (slice(0, half), slice(half, rows)):
        far_sum = far_keep[part] + far_near[part].astype(F32)
        far_parts.append(head_swap(far_sum.astype(BF16), 2))
    if not halving:
        share_rows = hidden_size // seq_count
        own_new = lax.dynamic_slice_in_dim(own_new, seq_place * share_rows, share_rows, 1)

    def second_attention(part, *done):
        return call(
            second_kernel,
            shape((half * (1 + len(done)), width), BF16),
            (edges, queries_second, near_keep, near_near, far_parts[part],
             prev_second, keys_second, values_second, next_second, *done),
            scalars=1,
            cost=(6 * rows * rows * width, 16 * rows * width),
        )

    normed_second = second_attention(1, second_attention(0))
    return (normed_second, jnp.transpose(own_new, (1, 0, 2))[None])


def solution(mesh):
    return jax.shard_map(
        local,
        mesh=mesh,
        in_specs=(
            P("seq", "head"),
            P("seq", "head"),
            P("seq", "head"),
            P("head", None, None),
            P("seq", "head"),
            P("seq", "head"),
            P("seq", "head"),
            P("head", None, None, None),
            P("head", None),
            P("seq", "head"),
            P("seq", "head"),
            P("seq", "head"),
        ),
        out_specs=(P("seq", "head"), P("head", "seq", None, None)),
        check_vma=False,
    )
```

```python
import functools
import math

import jax
import jax.numpy as jnp
from jax import lax
from jax.experimental import pallas as pl
from jax.experimental.pallas import tpu as pltpu
from jax.sharding import PartitionSpec as P

HALF_WIN = 512
HEAD_DIM = 128
HEADS_GRP = 2
FAST_DIM = 512
FAST_HIDDEN = 512
TILE = 128
ROW_TILE = 256
VMEM_LIMIT = 24 * 1024 * 1024
VMEM_MOST = 60 * 1024 * 1024

BF16 = jnp.bfloat16
F32 = jnp.float32
INVERSE = 1.0 / math.sqrt(FAST_DIM)


def dot_nn(left, right):
    return lax.dot_general(left, right, (((1,), (0,)), ((), ())), preferred_element_type=F32)


def dot_nt(left, right):
    return lax.dot_general(left, right, (((1,), (1,)), ((), ())), preferred_element_type=F32)


def call(body, out_shapes, operands, scalars=0, anywhere=0, scratch=(), cost=None, limit=VMEM_LIMIT):
    vmem = pl.BlockSpec(memory_space=pltpu.VMEM)
    in_specs = (
        [pl.BlockSpec(memory_space=pltpu.SMEM)] * scalars
        + [vmem] * (len(operands) - scalars - anywhere)
        + [pl.BlockSpec(memory_space=pl.ANY)] * anywhere
    )
    flops, moved = cost or (1000, 1000)
    return pl.pallas_call(
        body,
        out_shape=out_shapes,
        in_specs=in_specs,
        out_specs=jax.tree.map(lambda _: vmem, out_shapes),
        scratch_shapes=scratch,
        compiler_params=pltpu.CompilerParams(vmem_limit_bytes=limit),
        cost_estimate=pl.CostEstimate(flops=flops, bytes_accessed=moved, transcendentals=0),
    )(*operands)


def slot_of(block, order):
    slot = 0
    for bit in order:
        slot = slot * 2 + ((block >> bit) & 1)
    return slot


def gradient_kernel(orders, place_ref, rates_ref, keys_ref, values_ref, weights_ref, *refs):
    out_refs, chunk_refs = refs[:-2], refs[-2:]
    place = place_ref[0, 0]
    rates = rates_ref[...]
    keys = keys_ref[...]
    values = values_ref[...]
    hidden_size = chunk_refs[0].shape[0]
    width = weights_ref.shape[2]
    turn = pl.program_id(0)
    step = weights_ref.shape[1]

    def put(chunk, columns, product):
        order = orders[chunk]
        block_rows = min(step, hidden_size >> len(order))
        for start in range(0, step, block_rows):
            row = turn * step + start
            if order:
                block = turn * (step // block_rows) + start // block_rows
                row = slot_of(block ^ place, order) * block_rows
            row = pl.multiple_of(row, block_rows)
            chunk_refs[chunk][pl.ds(row, block_rows), columns] = product[start:start + block_rows]

    gate = dot_nt(weights_ref[0], keys) * INVERSE
    up = dot_nt(weights_ref[1], keys) * INVERSE
    sigmoid = jax.nn.sigmoid(gate)
    silu = gate * sigmoid
    hidden = (rates * silu * up).astype(BF16)
    backward = rates * dot_nt(weights_ref[2], values)
    d_gate = (backward * up * sigmoid * (1.0 + gate * (1.0 - sigmoid)) * INVERSE).astype(BF16)
    d_up = (backward * silu * INVERSE).astype(BF16)
    up_part = dot_nn(d_up, keys).astype(BF16)
    put(0, slice(0, width), dot_nn(d_gate, keys).astype(BF16))
    put(0, slice(width, width + width // 2), up_part[:, :width // 2])
    put(1, slice(0, width), dot_nn(hidden, values).astype(BF16))
    put(1, slice(width, width + width // 2), up_part[:, width // 2:])

    @pl.when(turn == pl.num_programs(0) - 1)
    def _():
        halves = len(out_refs) // 2
        half_rows = hidden_size // halves
        for index, out_ref in enumerate(out_refs):
            half = index % halves
            out_ref[...] = chunk_refs[index // halves][half * half_rows:(half + 1) * half_rows, :]


def attend_rows(edge_prev, edge_next, query_tile, keys_prev, keys_own, keys_next,
                values_prev, values_own, values_next):
    scale = math.log2(math.e) / math.sqrt(HEAD_DIM)
    row = lax.broadcasted_iota(jnp.int32, (ROW_TILE, ROW_TILE), 0)
    col = lax.broadcasted_iota(jnp.int32, (ROW_TILE, ROW_TILE), 1)
    minus = jnp.float32(-jnp.inf)
    score_prev = dot_nt(query_tile, keys_prev)
    score_own = dot_nt(query_tile, keys_own)
    score_next = dot_nt(query_tile, keys_next)
    parts = [score_prev[:, :ROW_TILE] + jnp.where(col >= row, edge_prev, minus)]
    if score_prev.shape[1] > ROW_TILE:
        parts.append(score_prev[:, ROW_TILE:] + edge_prev)
    parts.append(score_own)
    if score_next.shape[1] > ROW_TILE:
        parts.append(score_next[:, :-ROW_TILE] + edge_next)
    parts.append(score_next[:, -ROW_TILE:] + jnp.where(col <= row, edge_next, minus))
    scores = jnp.concatenate(parts, axis=1)
    highest = jnp.max(scores, axis=1, keepdims=True)
    weights = jnp.exp2((scores - highest) * scale)
    total = jnp.sum(weights, axis=1, keepdims=True)
    weights = weights.astype(BF16)
    width_prev, width_own = score_prev.shape[1], score_own.shape[1]
    attended = (
        dot_nn(weights[:, :width_prev], values_prev)
        + dot_nn(weights[:, width_prev:width_prev + width_own], values_own)
        + dot_nn(weights[:, width_prev + width_own:], values_next)
    )
    return attended / total


def pack_kernel(side_ref, queries_ref, keys_ref, values_ref, out_ref):
    count = queries_ref.shape[0]
    start = pl.multiple_of((1 - side_ref[0, 0]) * HEAD_DIM, HEAD_DIM)
    for index, ref in enumerate((queries_ref, keys_ref, values_ref)):
        out_ref[index * count:(index + 1) * count, :] = ref[:, pl.ds(start, HEAD_DIM)]


def border_kernel(side_ref, keys_ref, values_ref, other_ref, low_ref, high_ref):
    count = keys_ref.shape[0]
    side = side_ref[0, 0]
    start = pl.multiple_of(side * HEAD_DIM, HEAD_DIM)

    def fill(own_ref, other_out_ref):
        own_ref[:count, :] = keys_ref[:, pl.ds(start, HEAD_DIM)]
        own_ref[count:, :] = values_ref[:, pl.ds(start, HEAD_DIM)]
        other_out_ref[...] = other_ref[count:, :]

    @pl.when(side == 0)
    def _():
        fill(low_ref, high_ref)

    @pl.when(side != 0)
    def _():
        fill(high_ref, low_ref)


def first_kernel(edge_ref, side_ref, queries_ref, other_ref, prev_ref, low_ref, high_ref, next_ref,
                 keep_ref, send_ref, keys_ref, values_ref):
    count = queries_ref.shape[0]
    side = side_ref[0, 0]
    for index, ref in enumerate((prev_ref, low_ref, high_ref, next_ref)):
        rows = slice(index * count, (index + 1) * count)
        keys_ref[rows, :] = ref[:count, :]
        values_ref[rows, :] = ref[count:, :]
    start = pl.multiple_of(side * HEAD_DIM, HEAD_DIM)
    for turn, out_ref in enumerate((keep_ref, send_ref)):
        base = (side if turn == 0 else 1 - side) * count

        def span(ref, low, length):
            return ref[pl.ds(pl.multiple_of(base + low, ROW_TILE), length), :]

        for index in range(count // ROW_TILE):
            low, high = index * ROW_TILE, (index + 1) * ROW_TILE
            query = queries_ref[low:high, pl.ds(start, HEAD_DIM)] if turn == 0 else other_ref[low:high, :]
            out_ref[low:high, :] = attend_rows(
                edge_ref[turn, 0], edge_ref[turn, 1], query,
                span(keys_ref, low, count - low), span(keys_ref, count, count),
                span(keys_ref, 2 * count, high),
                span(values_ref, low, count - low), span(values_ref, count, count),
                span(values_ref, 2 * count, high),
            ).astype(BF16)


def second_kernel(edge_ref, queries_ref, keep_ref, near_ref, far_ref, prev_ref, keys_ref, values_ref, next_ref,
                  *refs):
    done_refs, out_ref = refs[:-1], refs[-1]
    count = keys_ref.shape[0]
    half = far_ref.shape[0]
    offset = half if done_refs else 0
    if done_refs:
        out_ref[:half, :] = done_refs[0][...]
    for low in range(offset, offset + half, ROW_TILE):
        high = low + ROW_TILE
        rows = slice(low, high)
        mixed = (
            keep_ref[rows, :].astype(F32)
            + near_ref[rows, :].astype(F32)
            + far_ref[low - offset:high - offset, :].astype(F32)
        )
        query = (queries_ref[rows, :].astype(F32) + mixed).astype(BF16)
        heads = []
        for head in range(HEADS_GRP):
            cols = slice(head * HEAD_DIM, (head + 1) * HEAD_DIM)
            heads.append(
                attend_rows(
                    edge_ref[0, 0], edge_ref[0, 1], query[:, cols],
                    prev_ref[low:count, cols], keys_ref[:, cols], next_ref[:high, cols],
                    prev_ref[count + low:, cols], values_ref[:, cols], next_ref[count:count + high, cols],
                )
            )
        both = jnp.concatenate(heads, axis=1)
        mean = jnp.mean(both * both, axis=1, keepdims=True)
        out_ref[rows, :] = (both * lax.rsqrt(mean + 1e-05)).astype(BF16)


def renew_kernel(orders, place_ref, side_ref, places_ref, *refs):
    count = (len(refs) - 8) // 2
    sources, own_ref, share_refs = refs[:count], refs[count], refs[count + 1:count + 5]
    loaded, (fast_ref, new_ref, sems) = refs[count + 5:-3], refs[-3:]
    copies = [
        pltpu.make_async_copy(source, target, sems.at[index])
        for index, (source, target) in enumerate(zip(sources, loaded))
    ]
    for copy in copies:
        copy.start()
    pieces, (weights_ref, keep_ref, other_ref, map_ref, output_ref) = loaded[:-5], loaded[-5:]
    place = place_ref[0, 0]
    side = side_ref[0, 0]
    hidden_size, width = weights_ref.shape[1:]
    for copy in copies[:-5]:
        copy.wait()
    limit_norm = math.sqrt(FAST_HIDDEN * FAST_DIM) / 2.0
    step = 64
    square = jnp.zeros((1, pieces[0].shape[1]), F32)
    for piece in pieces:
        for low in range(0, piece.shape[0], step):
            part = piece[low:low + step, :].astype(F32)
            square = square + jnp.sum(part * part, axis=0, keepdims=True)
    square = jnp.sum(square, axis=1, keepdims=True)
    factor = jnp.minimum(1.0, limit_norm * lax.rsqrt(square + 1e-06))
    copies[-5].wait()
    per_chunk = len(pieces) // 2
    piece_rows = pieces[0].shape[0]
    blocks = 1 << len(orders[0])
    block_rows = hidden_size // blocks
    count = min(step, block_rows)
    for block in range(blocks):
        starts = [slot_of(block, order) * block_rows for order in orders]
        for low in range(0, block_rows, count):
            found = []
            for chunk, start in enumerate(starts):
                piece = pieces[chunk * per_chunk + start // piece_rows]
                inside = start % piece_rows + low
                found.append(piece[inside:inside + count, :].astype(F32))
            parts = [
                found[0][:, :width],
                jnp.concatenate([found[0][:, width:], found[1][:, width:]], axis=1),
                found[1][:, :width],
            ]
            rows = slice(low, low + count)
            if blocks > 1:
                rows = pl.ds(pl.multiple_of((block ^ place) * block_rows + low, count), count)
            for matrix, part in enumerate(parts):
                old = weights_ref[matrix, rows, :].astype(F32)
                stepped = old + factor * part
                norm = jnp.sqrt(jnp.sum(old * old, axis=1, keepdims=True))
                size = jnp.sum(stepped * stepped, axis=1, keepdims=True)
                fresh = (stepped * norm * lax.rsqrt(size + 1e-06)).astype(BF16)
                new_ref[matrix, rows, :] = fresh
                if block == 0:
                    own_ref[matrix, low:low + count, :] = fresh
    for copy in copies[-4:-1]:
        copy.wait()
    own_map = map_ref[pl.ds(pl.multiple_of(side * HEAD_DIM, HEAD_DIM), HEAD_DIM), :]
    other_map = map_ref[pl.ds(pl.multiple_of((1 - side) * HEAD_DIM, HEAD_DIM), HEAD_DIM), :]
    step = keep_ref.shape[0]
    for low in range(0, keep_ref.shape[0], step):
        rows = slice(low, low + step)
        own = keep_ref[rows, :].astype(F32)
        other = other_ref[rows, :].astype(F32)
        total = jnp.sum(own * own + other * other, axis=1, keepdims=True)
        norm = lax.rsqrt(total / (HEADS_GRP * HEAD_DIM) + 1e-05)
        query = (
            dot_nn((own * norm).astype(BF16), own_map) + dot_nn((other * norm).astype(BF16), other_map)
        ).astype(BF16)
        gate = dot_nt(query, new_ref[0]) * INVERSE
        up = dot_nt(query, new_ref[1]) * INVERSE
        hidden = (jax.nn.silu(gate) * up).astype(BF16)
        raw = dot_nn(hidden, new_ref[2])
        mean = jnp.mean(raw * raw, axis=1, keepdims=True)
        fast_ref[rows, :] = (raw * lax.rsqrt(mean + 1e-05)).astype(BF16)
    copies[-1].wait()
    for index, share_ref in enumerate(share_refs):
        width = share_ref.shape[1]
        start = pl.multiple_of(places_ref[0, index] * width, width)
        share_ref[...] = dot_nn(fast_ref[...], output_ref[:, pl.ds(start, width)]).astype(BF16)


def seq_shift(value, step):
    peers = lax.axis_size("seq")
    return lax.ppermute(
        value, "seq", [(i, i + step) for i in range(peers) if 0 <= i + step < peers]
    )


def head_swap(value, bit):
    return lax.ppermute(value, "head", [(i, i ^ bit) for i in range(lax.axis_size("head"))])


def seq_swap(value, bit):
    step = 1 << bit
    return lax.ppermute(value, "seq", [(i, i ^ step) for i in range(lax.axis_size("seq"))])


def after(value, others):
    return lax.optimization_barrier((value, others))[0]


def halving_start(chunks, orders):
    keeps = [keep for keep, _ in chunks]
    return keeps, [seq_swap(send, order[0]) for (_, send), order in zip(chunks, orders)]


def halving_step(keeps, found, orders, turn, wait=()):
    sends, rest = [], []
    for keep, new in zip(keeps, found):
        half = keep.shape[0] // 2
        sends.append((keep[half:].astype(F32) + new[half:].astype(F32)).astype(BF16))
        rest.append(lax.optimization_barrier(keep[:half].astype(F32) + new[:half].astype(F32)))
    sends = after(sends, wait) if wait else sends
    return rest, [seq_swap(send, order[turn]) for send, order in zip(sends, orders)]


def doubling_step(held, orders, turn, wait=()):
    whole = [jnp.concatenate(parts) if len(parts) > 1 else parts[0] for parts in held]
    whole = after(whole, wait) if wait else whole
    return [(own, seq_swap(own, order[turn])) for own, order in zip(whole, orders)]


def local(
    queries_first,
    keys_first,
    values_first,
    input_map,
    fast_keys,
    fast_values,
    step_rates,
    fast_weights,
    output_map,
    queries_second,
    keys_second,
    values_second,
):
    rows, width = queries_first.shape
    seq_count = lax.axis_size("seq")
    seq_place = lax.axis_index("seq")
    head_place = lax.axis_index("head")
    weights = jnp.transpose(fast_weights[0], (1, 0, 2))
    hidden_size, fast_width = weights.shape[1:]
    shape = jax.ShapeDtypeStruct
    minus = jnp.float32(-jnp.inf)
    side = seq_place % 2

    def edges_of(block):
        return [jnp.where(block > 0, 0.0, minus), jnp.where(block < seq_count - 1, 0.0, minus)]

    edges = jnp.stack(edges_of(seq_place) + edges_of(seq_place ^ 1)).reshape(2, 2)
    side_scalar = side.astype(jnp.int32).reshape(1, 1)
    place = seq_place.astype(jnp.int32).reshape(1, 1)

    packed = call(
        pack_kernel,
        shape((3 * rows, HEAD_DIM), BF16),
        (side_scalar, queries_first, keys_first, values_first),
        scalars=1,
    )
    other_first = seq_swap(packed, 0)

    bits = tuple(range(seq_count.bit_length() - 1))
    halving = seq_count == 1 << len(bits) and len(bits) > 1 and hidden_size >> len(bits) >= 16
    orders = (bits, bits[1:] + bits[:1]) if halving else ((), ())
    halves = 2 if halving else 1
    chunk_width = fast_width + fast_width // 2
    out_shapes = [shape((hidden_size // halves, chunk_width), BF16)] * (2 * halves)
    whole = pl.BlockSpec(memory_space=pltpu.VMEM)
    gradients = pl.pallas_call(
        functools.partial(gradient_kernel, orders),
        grid=(1,),
        out_shape=out_shapes,
        in_specs=[
            pl.BlockSpec(memory_space=pltpu.SMEM),
            whole,
            whole,
            whole,
            pl.BlockSpec((3, hidden_size, fast_width), lambda turn: (0, turn, 0)),
        ],
        out_specs=[whole] * len(out_shapes),
        scratch_shapes=[pltpu.VMEM((hidden_size, chunk_width), BF16)] * 2,
        compiler_params=pltpu.CompilerParams(vmem_limit_bytes=VMEM_MOST),
        cost_estimate=pl.CostEstimate(flops=1000, bytes_accessed=1000, transcendentals=0),
    )(place, step_rates.reshape(1, rows), fast_keys, fast_values, weights)

    low_block, high_block = call(
        border_kernel,
        [shape((2 * rows, HEAD_DIM), BF16)] * 2,
        (side_scalar, keys_first, values_first, other_first),
        scalars=1,
    )

    def first_halos(low_block, high_block):
        return seq_shift(high_block, 2), seq_shift(low_block, -2)

    def first_attention(prev_first, next_first):
        keep_first, send_first = call(
            first_kernel,
            [shape((rows, HEAD_DIM), BF16)] * 2,
            (edges, side_scalar, queries_first, other_first, prev_first, low_block, high_block, next_first),
            scalars=2,
            scratch=[pltpu.VMEM((4 * rows, HEAD_DIM), BF16)] * 2,
            cost=(12 * rows * rows * width, 16 * rows * width),
        )
        return keep_first, seq_swap(send_first, 0)

    both_second = jnp.concatenate([keys_second, values_second])

    if halving:
        turns = len(bits)
        keeps, found = halving_start([gradients[:2], gradients[2:]], orders)
        for turn in range(1, turns):
            if turn == turns - 1:
                prev_first, next_first = first_halos(*after((low_block, high_block), found))
                prev_second = seq_shift(after(both_second, found), 1)
            keeps, found = halving_step(keeps, found, orders, turn)
        held = [((keep.astype(F32) + new.astype(F32)).astype(BF16),) for keep, new in zip(keeps, found)]
        for turn in reversed(range(turns)):
            wait = ()
            if turn == 1:
                wait = (prev_first, next_first, prev_second)
            if turn == 0:
                keep_first, back_first = first_attention(prev_first, next_first)
                wait = (keep_first,)
            held = doubling_step(held, orders, turn, wait)
        gathered = [part for parts in held for part in parts]
        next_second = seq_shift(after(both_second, back_first), -1)
    else:
        gathered = lax.psum(gradients, "seq")
        keep_first, back_first = first_attention(*first_halos(low_block, high_block))
        prev_second, next_second = seq_shift(both_second, 1), seq_shift(both_second, -1)
    own_rows = hidden_size >> len(orders[0])
    my_bit, near = head_place % 2, head_place // 2
    places = jnp.stack(
        [2 * pair + bit for pair in (near ^ 1, near) for bit in (1 - my_bit, my_bit)]
    ).astype(jnp.int32).reshape(1, 4)
    share = shape((rows, width), BF16)
    operands = (*gathered, weights, keep_first, back_first, input_map[0], output_map)
    own_new, far_send, far_keep, near_send, near_keep = call(
        functools.partial(renew_kernel, orders),
        [shape((3, own_rows, fast_width), BF16)] + [share] * 4,
        (place, side_scalar, places, *operands),
        scalars=3,
        anywhere=len(operands),
        scratch=[pltpu.VMEM(operand.shape, BF16) for operand in operands]
        + [
            pltpu.VMEM((rows, fast_width), BF16),
            pltpu.VMEM(weights.shape, BF16),
            pltpu.SemaphoreType.DMA((len(operands),)),
        ],
    )
    far_near = head_swap(far_send, 1)
    far_keep = lax.optimization_barrier(far_keep.astype(F32))
    near_near = head_swap(after(near_send, next_second), 1)
    half = rows // 2
    far_parts = []
    for part in (slice(0, half), slice(half, rows)):
        far_sum = far_keep[part] + far_near[part].astype(F32)
        far_parts.append(head_swap(far_sum.astype(BF16), 2))
    if not halving:
        share_rows = hidden_size // seq_count
        own_new = lax.dynamic_slice_in_dim(own_new, seq_place * share_rows, share_rows, 1)

    def second_attention(part, *done):
        return call(
            second_kernel,
            shape((half * (1 + len(done)), width), BF16),
            (edges, queries_second, near_keep, near_near, far_parts[part],
             prev_second, keys_second, values_second, next_second, *done),
            scalars=1,
            cost=(6 * rows * rows * width, 16 * rows * width),
        )

    normed_second = second_attention(1, second_attention(0))
    return (normed_second, jnp.transpose(own_new, (1, 0, 2))[None])


def solution(mesh):
    return jax.shard_map(
        local,
        mesh=mesh,
        in_specs=(
            P("seq", "head"),
            P("seq", "head"),
            P("seq", "head"),
            P("head", None, None),
            P("seq", "head"),
            P("seq", "head"),
            P("seq", "head"),
            P("head", None, None, None),
            P("head", None),
            P("seq", "head"),
            P("seq", "head"),
            P("seq", "head"),
        ),
        out_specs=(P("seq", "head"), P("head", "seq", None, None)),
        check_vma=False,
    )
```

```python
import functools
import math

import jax
import jax.numpy as jnp
from jax import lax
from jax.experimental import pallas as pl
from jax.experimental.pallas import tpu as pltpu
from jax.sharding import PartitionSpec as P

HALF_WIN = 512
HEAD_DIM = 128
HEADS_GRP = 2
FAST_DIM = 512
FAST_HIDDEN = 512
TILE = 128
ROW_TILE = 256
VMEM_LIMIT = 24 * 1024 * 1024
VMEM_MOST = 60 * 1024 * 1024

BF16 = jnp.bfloat16
F32 = jnp.float32
INVERSE = 1.0 / math.sqrt(FAST_DIM)


def dot_nn(left, right):
    return lax.dot_general(left, right, (((1,), (0,)), ((), ())), preferred_element_type=F32)


def dot_nt(left, right):
    return lax.dot_general(left, right, (((1,), (1,)), ((), ())), preferred_element_type=F32)


def call(body, out_shapes, operands, scalars=0, anywhere=0, scratch=(), cost=None, limit=VMEM_LIMIT):
    vmem = pl.BlockSpec(memory_space=pltpu.VMEM)
    in_specs = (
        [pl.BlockSpec(memory_space=pltpu.SMEM)] * scalars
        + [vmem] * (len(operands) - scalars - anywhere)
        + [pl.BlockSpec(memory_space=pl.ANY)] * anywhere
    )
    flops, moved = cost or (1000, 1000)
    return pl.pallas_call(
        body,
        out_shape=out_shapes,
        in_specs=in_specs,
        out_specs=jax.tree.map(lambda _: vmem, out_shapes),
        scratch_shapes=scratch,
        compiler_params=pltpu.CompilerParams(vmem_limit_bytes=limit),
        cost_estimate=pl.CostEstimate(flops=flops, bytes_accessed=moved, transcendentals=0),
    )(*operands)


def slot_of(block, order):
    slot = 0
    for bit in order:
        slot = slot * 2 + ((block >> bit) & 1)
    return slot


def gradient_kernel(orders, place_ref, rates_ref, keys_ref, values_ref, weights_ref, *refs):
    out_refs, chunk_refs = refs[:-2], refs[-2:]
    place = place_ref[0, 0]
    rates = rates_ref[...]
    keys = keys_ref[...]
    values = values_ref[...]
    hidden_size = chunk_refs[0].shape[0]
    width = weights_ref.shape[2]
    turn = pl.program_id(0)
    step = weights_ref.shape[1]

    def put(chunk, columns, product):
        order = orders[chunk]
        block_rows = min(step, hidden_size >> len(order))
        for start in range(0, step, block_rows):
            row = turn * step + start
            if order:
                block = turn * (step // block_rows) + start // block_rows
                row = slot_of(block ^ place, order) * block_rows
            row = pl.multiple_of(row, block_rows)
            chunk_refs[chunk][pl.ds(row, block_rows), columns] = product[start:start + block_rows]

    gate = dot_nt(weights_ref[0], keys) * INVERSE
    up = dot_nt(weights_ref[1], keys) * INVERSE
    sigmoid = jax.nn.sigmoid(gate)
    silu = gate * sigmoid
    hidden = (rates * silu * up).astype(BF16)
    backward = rates * dot_nt(weights_ref[2], values)
    d_gate = (backward * up * sigmoid * (1.0 + gate * (1.0 - sigmoid)) * INVERSE).astype(BF16)
    d_up = (backward * silu * INVERSE).astype(BF16)
    up_part = dot_nn(d_up, keys).astype(BF16)
    put(0, slice(0, width), dot_nn(d_gate, keys).astype(BF16))
    put(0, slice(width, width + width // 2), up_part[:, :width // 2])
    put(1, slice(0, width), dot_nn(hidden, values).astype(BF16))
    put(1, slice(width, width + width // 2), up_part[:, width // 2:])

    @pl.when(turn == pl.num_programs(0) - 1)
    def _():
        halves = len(out_refs) // 2
        half_rows = hidden_size // halves
        for index, out_ref in enumerate(out_refs):
            half = index % halves
            out_ref[...] = chunk_refs[index // halves][half * half_rows:(half + 1) * half_rows, :]


def attend_rows(edge_prev, edge_next, query_tile, keys_prev, keys_own, keys_next,
                values_prev, values_own, values_next):
    scale = math.log2(math.e) / math.sqrt(HEAD_DIM)
    row = lax.broadcasted_iota(jnp.int32, (ROW_TILE, ROW_TILE), 0)
    col = lax.broadcasted_iota(jnp.int32, (ROW_TILE, ROW_TILE), 1)
    minus = jnp.float32(-jnp.inf)
    score_prev = dot_nt(query_tile, keys_prev)
    score_own = dot_nt(query_tile, keys_own)
    score_next = dot_nt(query_tile, keys_next)
    parts = [score_prev[:, :ROW_TILE] + jnp.where(col >= row, edge_prev, minus)]
    if score_prev.shape[1] > ROW_TILE:
        parts.append(score_prev[:, ROW_TILE:] + edge_prev)
    parts.append(score_own)
    if score_next.shape[1] > ROW_TILE:
        parts.append(score_next[:, :-ROW_TILE] + edge_next)
    parts.append(score_next[:, -ROW_TILE:] + jnp.where(col <= row, edge_next, minus))
    scores = jnp.concatenate(parts, axis=1)
    highest = jnp.max(scores, axis=1, keepdims=True)
    weights = jnp.exp2((scores - highest) * scale)
    total = jnp.sum(weights, axis=1, keepdims=True)
    weights = weights.astype(BF16)
    width_prev, width_own = score_prev.shape[1], score_own.shape[1]
    attended = (
        dot_nn(weights[:, :width_prev], values_prev)
        + dot_nn(weights[:, width_prev:width_prev + width_own], values_own)
        + dot_nn(weights[:, width_prev + width_own:], values_next)
    )
    return attended / total


def pack_kernel(side_ref, queries_ref, keys_ref, values_ref, out_ref):
    count = queries_ref.shape[0]
    start = pl.multiple_of((1 - side_ref[0, 0]) * HEAD_DIM, HEAD_DIM)
    for index, ref in enumerate((queries_ref, keys_ref, values_ref)):
        out_ref[index * count:(index + 1) * count, :] = ref[:, pl.ds(start, HEAD_DIM)]


def border_kernel(side_ref, keys_ref, values_ref, other_ref, low_ref, high_ref):
    count = keys_ref.shape[0]
    side = side_ref[0, 0]
    start = pl.multiple_of(side * HEAD_DIM, HEAD_DIM)

    def fill(own_ref, other_out_ref):
        own_ref[:count, :] = keys_ref[:, pl.ds(start, HEAD_DIM)]
        own_ref[count:, :] = values_ref[:, pl.ds(start, HEAD_DIM)]
        other_out_ref[...] = other_ref[count:, :]

    @pl.when(side == 0)
    def _():
        fill(low_ref, high_ref)

    @pl.when(side != 0)
    def _():
        fill(high_ref, low_ref)


def first_kernel(edge_ref, side_ref, queries_ref, other_ref, prev_ref, low_ref, high_ref, next_ref,
                 keep_ref, send_ref, keys_ref, values_ref):
    count = queries_ref.shape[0]
    side = side_ref[0, 0]
    for index, ref in enumerate((prev_ref, low_ref, high_ref, next_ref)):
        rows = slice(index * count, (index + 1) * count)
        keys_ref[rows, :] = ref[:count, :]
        values_ref[rows, :] = ref[count:, :]
    start = pl.multiple_of(side * HEAD_DIM, HEAD_DIM)
    for turn, out_ref in enumerate((keep_ref, send_ref)):
        base = (side if turn == 0 else 1 - side) * count

        def span(ref, low, length):
            return ref[pl.ds(pl.multiple_of(base + low, ROW_TILE), length), :]

        for index in range(count // ROW_TILE):
            low, high = index * ROW_TILE, (index + 1) * ROW_TILE
            query = queries_ref[low:high, pl.ds(start, HEAD_DIM)] if turn == 0 else other_ref[low:high, :]
            out_ref[low:high, :] = attend_rows(
                edge_ref[turn, 0], edge_ref[turn, 1], query,
                span(keys_ref, low, count - low), span(keys_ref, count, count),
                span(keys_ref, 2 * count, high),
                span(values_ref, low, count - low), span(values_ref, count, count),
                span(values_ref, 2 * count, high),
            ).astype(BF16)


def second_kernel(edge_ref, queries_ref, keep_ref, near_ref, far_ref, prev_ref, keys_ref, values_ref, next_ref,
                  *refs):
    done_refs, out_ref = refs[:-1], refs[-1]
    count = keys_ref.shape[0]
    half = far_ref.shape[0]
    offset = half if done_refs else 0
    if done_refs:
        out_ref[:half, :] = done_refs[0][...]
    for low in range(offset, offset + half, ROW_TILE):
        high = low + ROW_TILE
        rows = slice(low, high)
        mixed = (
            keep_ref[rows, :].astype(F32)
            + near_ref[rows, :].astype(F32)
            + far_ref[low - offset:high - offset, :].astype(F32)
        )
        query = (queries_ref[rows, :].astype(F32) + mixed).astype(BF16)
        heads = []
        for head in range(HEADS_GRP):
            cols = slice(head * HEAD_DIM, (head + 1) * HEAD_DIM)
            heads.append(
                attend_rows(
                    edge_ref[0, 0], edge_ref[0, 1], query[:, cols],
                    prev_ref[low:count, cols], keys_ref[:, cols], next_ref[:high, cols],
                    prev_ref[count + low:, cols], values_ref[:, cols], next_ref[count:count + high, cols],
                )
            )
        both = jnp.concatenate(heads, axis=1)
        mean = jnp.mean(both * both, axis=1, keepdims=True)
        out_ref[rows, :] = (both * lax.rsqrt(mean + 1e-05)).astype(BF16)


def renew_kernel(orders, place_ref, side_ref, places_ref, *refs):
    count = (len(refs) - 8) // 2
    sources, own_ref, share_refs = refs[:count], refs[count], refs[count + 1:count + 5]
    loaded, (fast_ref, new_ref, sems) = refs[count + 5:-3], refs[-3:]
    copies = [
        pltpu.make_async_copy(source, target, sems.at[index])
        for index, (source, target) in enumerate(zip(sources, loaded))
    ]
    for copy in copies:
        copy.start()
    pieces, (weights_ref, keep_ref, other_ref, map_ref, output_ref) = loaded[:-5], loaded[-5:]
    place = place_ref[0, 0]
    side = side_ref[0, 0]
    hidden_size, width = weights_ref.shape[1:]
    for copy in copies[:-5]:
        copy.wait()
    limit_norm = math.sqrt(FAST_HIDDEN * FAST_DIM) / 2.0
    step = 64
    square = jnp.zeros((8, pieces[0].shape[1]), F32)
    for piece in pieces:
        for low in range(0, piece.shape[0], step):
            part = piece[low:low + step, :].astype(F32)
            square = square + jnp.sum((part * part).reshape(step // 8, 8, -1), axis=0)
    square = jnp.sum(jnp.sum(square, axis=0, keepdims=True), axis=1, keepdims=True)
    factor = jnp.minimum(1.0, limit_norm * lax.rsqrt(square + 1e-06))
    copies[-5].wait()
    per_chunk = len(pieces) // 2
    piece_rows = pieces[0].shape[0]
    blocks = 1 << len(orders[0])
    block_rows = hidden_size // blocks
    count = min(step, block_rows)
    for block in range(blocks):
        starts = [slot_of(block, order) * block_rows for order in orders]
        for low in range(0, block_rows, count):
            found = []
            for chunk, start in enumerate(starts):
                piece = pieces[chunk * per_chunk + start // piece_rows]
                inside = start % piece_rows + low
                found.append(piece[inside:inside + count, :].astype(F32))
            parts = [
                found[0][:, :width],
                jnp.concatenate([found[0][:, width:], found[1][:, width:]], axis=1),
                found[1][:, :width],
            ]
            rows = slice(low, low + count)
            if blocks > 1:
                rows = pl.ds(pl.multiple_of((block ^ place) * block_rows + low, count), count)
            for matrix, part in enumerate(parts):
                old = weights_ref[matrix, rows, :].astype(F32)
                stepped = old + factor * part
                norm = jnp.sqrt(jnp.sum(old * old, axis=1, keepdims=True))
                size = jnp.sum(stepped * stepped, axis=1, keepdims=True)
                fresh = (stepped * norm * lax.rsqrt(size + 1e-06)).astype(BF16)
                new_ref[matrix, rows, :] = fresh
                if block == 0:
                    own_ref[matrix, low:low + count, :] = fresh
    for copy in copies[-4:-1]:
        copy.wait()
    own_map = map_ref[pl.ds(pl.multiple_of(side * HEAD_DIM, HEAD_DIM), HEAD_DIM), :]
    other_map = map_ref[pl.ds(pl.multiple_of((1 - side) * HEAD_DIM, HEAD_DIM), HEAD_DIM), :]
    step = keep_ref.shape[0]
    for low in range(0, keep_ref.shape[0], step):
        rows = slice(low, low + step)
        own = keep_ref[rows, :].astype(F32)
        other = other_ref[rows, :].astype(F32)
        total = jnp.sum(own * own + other * other, axis=1, keepdims=True)
        norm = lax.rsqrt(total / (HEADS_GRP * HEAD_DIM) + 1e-05)
        query = (
            dot_nn((own * norm).astype(BF16), own_map) + dot_nn((other * norm).astype(BF16), other_map)
        ).astype(BF16)
        gate = dot_nt(query, new_ref[0]) * INVERSE
        up = dot_nt(query, new_ref[1]) * INVERSE
        hidden = (jax.nn.silu(gate) * up).astype(BF16)
        raw = dot_nn(hidden, new_ref[2])
        mean = jnp.mean(raw * raw, axis=1, keepdims=True)
        fast_ref[rows, :] = (raw * lax.rsqrt(mean + 1e-05)).astype(BF16)
    copies[-1].wait()
    for index, share_ref in enumerate(share_refs):
        width = share_ref.shape[1]
        start = pl.multiple_of(places_ref[0, index] * width, width)
        share_ref[...] = dot_nn(fast_ref[...], output_ref[:, pl.ds(start, width)]).astype(BF16)


def seq_shift(value, step):
    peers = lax.axis_size("seq")
    return lax.ppermute(
        value, "seq", [(i, i + step) for i in range(peers) if 0 <= i + step < peers]
    )


def head_swap(value, bit):
    return lax.ppermute(value, "head", [(i, i ^ bit) for i in range(lax.axis_size("head"))])


def seq_swap(value, bit):
    step = 1 << bit
    return lax.ppermute(value, "seq", [(i, i ^ step) for i in range(lax.axis_size("seq"))])


def after(value, others):
    return lax.optimization_barrier((value, others))[0]


def halving_start(chunks, orders):
    keeps = [keep for keep, _ in chunks]
    return keeps, [seq_swap(send, order[0]) for (_, send), order in zip(chunks, orders)]


def halving_step(keeps, found, orders, turn, wait=()):
    sends, rest = [], []
    for keep, new in zip(keeps, found):
        half = keep.shape[0] // 2
        sends.append((keep[half:].astype(F32) + new[half:].astype(F32)).astype(BF16))
        rest.append(lax.optimization_barrier(keep[:half].astype(F32) + new[:half].astype(F32)))
    sends = after(sends, wait) if wait else sends
    return rest, [seq_swap(send, order[turn]) for send, order in zip(sends, orders)]


def doubling_step(held, orders, turn, wait=()):
    whole = [jnp.concatenate(parts) if len(parts) > 1 else parts[0] for parts in held]
    whole = after(whole, wait) if wait else whole
    return [(own, seq_swap(own, order[turn])) for own, order in zip(whole, orders)]


def local(
    queries_first,
    keys_first,
    values_first,
    input_map,
    fast_keys,
    fast_values,
    step_rates,
    fast_weights,
    output_map,
    queries_second,
    keys_second,
    values_second,
):
    rows, width = queries_first.shape
    seq_count = lax.axis_size("seq")
    seq_place = lax.axis_index("seq")
    head_place = lax.axis_index("head")
    weights = jnp.transpose(fast_weights[0], (1, 0, 2))
    hidden_size, fast_width = weights.shape[1:]
    shape = jax.ShapeDtypeStruct
    minus = jnp.float32(-jnp.inf)
    side = seq_place % 2

    def edges_of(block):
        return [jnp.where(block > 0, 0.0, minus), jnp.where(block < seq_count - 1, 0.0, minus)]

    edges = jnp.stack(edges_of(seq_place) + edges_of(seq_place ^ 1)).reshape(2, 2)
    side_scalar = side.astype(jnp.int32).reshape(1, 1)
    place = seq_place.astype(jnp.int32).reshape(1, 1)

    packed = call(
        pack_kernel,
        shape((3 * rows, HEAD_DIM), BF16),
        (side_scalar, queries_first, keys_first, values_first),
        scalars=1,
    )
    other_first = seq_swap(packed, 0)

    bits = tuple(range(seq_count.bit_length() - 1))
    halving = seq_count == 1 << len(bits) and len(bits) > 1 and hidden_size >> len(bits) >= 16
    orders = (bits, bits[1:] + bits[:1]) if halving else ((), ())
    halves = 2 if halving else 1
    chunk_width = fast_width + fast_width // 2
    out_shapes = [shape((hidden_size // halves, chunk_width), BF16)] * (2 * halves)
    whole = pl.BlockSpec(memory_space=pltpu.VMEM)
    gradients = pl.pallas_call(
        functools.partial(gradient_kernel, orders),
        grid=(1,),
        out_shape=out_shapes,
        in_specs=[
            pl.BlockSpec(memory_space=pltpu.SMEM),
            whole,
            whole,
            whole,
            pl.BlockSpec((3, hidden_size, fast_width), lambda turn: (0, turn, 0)),
        ],
        out_specs=[whole] * len(out_shapes),
        scratch_shapes=[pltpu.VMEM((hidden_size, chunk_width), BF16)] * 2,
        compiler_params=pltpu.CompilerParams(vmem_limit_bytes=VMEM_MOST),
        cost_estimate=pl.CostEstimate(flops=1000, bytes_accessed=1000, transcendentals=0),
    )(place, step_rates.reshape(1, rows), fast_keys, fast_values, weights)

    low_block, high_block = call(
        border_kernel,
        [shape((2 * rows, HEAD_DIM), BF16)] * 2,
        (side_scalar, keys_first, values_first, other_first),
        scalars=1,
    )

    def first_halos(low_block, high_block):
        return seq_shift(high_block, 2), seq_shift(low_block, -2)

    def first_attention(prev_first, next_first):
        keep_first, send_first = call(
            first_kernel,
            [shape((rows, HEAD_DIM), BF16)] * 2,
            (edges, side_scalar, queries_first, other_first, prev_first, low_block, high_block, next_first),
            scalars=2,
            scratch=[pltpu.VMEM((4 * rows, HEAD_DIM), BF16)] * 2,
            cost=(12 * rows * rows * width, 16 * rows * width),
        )
        return keep_first, seq_swap(send_first, 0)

    both_second = jnp.concatenate([keys_second, values_second])

    if halving:
        turns = len(bits)
        keeps, found = halving_start([gradients[:2], gradients[2:]], orders)
        for turn in range(1, turns):
            if turn == turns - 1:
                prev_first, next_first = first_halos(*after((low_block, high_block), found))
                prev_second = seq_shift(after(both_second, found), 1)
            keeps, found = halving_step(keeps, found, orders, turn)
        held = [((keep.astype(F32) + new.astype(F32)).astype(BF16),) for keep, new in zip(keeps, found)]
        for turn in reversed(range(turns)):
            wait = ()
            if turn == 1:
                wait = (prev_first, next_first, prev_second)
            if turn == 0:
                keep_first, back_first = first_attention(prev_first, next_first)
                wait = (keep_first,)
            held = doubling_step(held, orders, turn, wait)
        gathered = [part for parts in held for part in parts]
        next_second = seq_shift(after(both_second, back_first), -1)
    else:
        gathered = lax.psum(gradients, "seq")
        keep_first, back_first = first_attention(*first_halos(low_block, high_block))
        prev_second, next_second = seq_shift(both_second, 1), seq_shift(both_second, -1)
    own_rows = hidden_size >> len(orders[0])
    my_bit, near = head_place % 2, head_place // 2
    places = jnp.stack(
        [2 * pair + bit for pair in (near ^ 1, near) for bit in (1 - my_bit, my_bit)]
    ).astype(jnp.int32).reshape(1, 4)
    share = shape((rows, width), BF16)
    operands = (*gathered, weights, keep_first, back_first, input_map[0], output_map)
    own_new, far_send, far_keep, near_send, near_keep = call(
        functools.partial(renew_kernel, orders),
        [shape((3, own_rows, fast_width), BF16)] + [share] * 4,
        (place, side_scalar, places, *operands),
        scalars=3,
        anywhere=len(operands),
        scratch=[pltpu.VMEM(operand.shape, BF16) for operand in operands]
        + [
            pltpu.VMEM((rows, fast_width), BF16),
            pltpu.VMEM(weights.shape, BF16),
            pltpu.SemaphoreType.DMA((len(operands),)),
        ],
        limit=VMEM_MOST - 3 * 1024 * 1024,
    )
    far_near = head_swap(far_send, 1)
    far_keep = lax.optimization_barrier(far_keep.astype(F32))
    near_near = head_swap(after(near_send, next_second), 1)
    half = rows // 2
    far_parts = []
    for part in (slice(0, half), slice(half, rows)):
        far_sum = far_keep[part] + far_near[part].astype(F32)
        far_parts.append(head_swap(far_sum.astype(BF16), 2))
    if not halving:
        share_rows = hidden_size // seq_count
        own_new = lax.dynamic_slice_in_dim(own_new, seq_place * share_rows, share_rows, 1)

    def second_attention(part, *done):
        return call(
            second_kernel,
            shape((half * (1 + len(done)), width), BF16),
            (edges, queries_second, near_keep, near_near, far_parts[part],
             prev_second, keys_second, values_second, next_second, *done),
            scalars=1,
            cost=(6 * rows * rows * width, 16 * rows * width),
        )

    normed_second = second_attention(1, second_attention(0))
    return (normed_second, jnp.transpose(own_new, (1, 0, 2))[None])


def solution(mesh):
    return jax.shard_map(
        local,
        mesh=mesh,
        in_specs=(
            P("seq", "head"),
            P("seq", "head"),
            P("seq", "head"),
            P("head", None, None),
            P("seq", "head"),
            P("seq", "head"),
            P("seq", "head"),
            P("head", None, None, None),
            P("head", None),
            P("seq", "head"),
            P("seq", "head"),
            P("seq", "head"),
        ),
        out_specs=(P("seq", "head"), P("head", "seq", None, None)),
        check_vma=False,
    )
```
